32 devices in a mesh: section: 2 (over core), ctx: 4 (over y, x), fsdp: 4 (over z).
Axes of the slice: x: 2, y: 2, z: 4, core: 2. Of those that a mesh axis runs over, the one named last changes fastest.
Arguments:
- tokens: bfloat16 [2, 4, 1024, 1024], P(None, 'fsdp', 'ctx'), may hold values from -6 to 6
- targets: bfloat16 [2, 4, 1024, 1024], P(None, 'fsdp', 'ctx'), may hold values from -6 to 6
- lengths: int32 [2, 4], replicated, may hold values from 256 to 1024, as said below
- routes: int32 [2, 2, 4, 1024, 8], P('section', None, 'fsdp', 'ctx'), may hold values from 0 to 31, all different within a row; in each aligned block of 256 rows (0 to 255, 256 to 511, ..., all dimensions but the last counted through in order) at most 72 rows name the same one
- attention_gain: bfloat16 [2, 1024], P('section', ('ctx', 'fsdp')), may hold values from 0.5 to 1.5
- query_weight: bfloat16 [2, 1024, 1024], P('section', ('ctx', 'fsdp')), may hold values from -0.1875 to 0.1875
- memory_weight: bfloat16 [2, 1024, 1024], P('section', ('ctx', 'fsdp')), may hold values from -0.1875 to 0.1875
- output_weight: bfloat16 [2, 1024, 1024], P('section', ('ctx', 'fsdp')), may hold values from -0.75 to 0.75
- mixture_gain: bfloat16 [2, 1024], P('section', ('ctx', 'fsdp')), may hold values from 0.5 to 1.5
- router_weight: bfloat16 [2, 1024, 32], P('section', ('ctx', 'fsdp')), may hold values from -0.099609375 to 0.099609375
- gate_up_weight: bfloat16 [2, 32, 1024, 1024], P('section', 'ctx', 'fsdp'), may hold values from -0.1875 to 0.1875
- down_weight: bfloat16 [2, 32, 512, 1024], P('section', 'ctx', 'fsdp'), may hold values from -1 to 1
Outputs:
- hidden_states: bfloat16 [2, 2, 4, 1024, 1024], P('section', None, 'fsdp', 'ctx')
- input_grads: float32 [2, 2, 4, 1024, 1024], P('section', None, 'fsdp', 'ctx')
- loss_value: float32 [], replicated
- attention_gain_grad: float32 [2, 1024], P('section', ('ctx', 'fsdp'))
- query_grad: float32 [2, 1024, 1024], P('section', ('ctx', 'fsdp'))
- memory_grad: float32 [2, 1024, 1024], P('section', ('ctx', 'fsdp'))
- output_grad: float32 [2, 1024, 1024], P('section', ('ctx', 'fsdp'))
- mixture_gain_grad: float32 [2, 1024], P('section', ('ctx', 'fsdp'))
- router_grad: float32 [2, 1024, 32], P('section', ('ctx', 'fsdp'))
- gate_up_grad: float32 [2, 32, 1024, 1024], P('section', 'ctx', 'fsdp')
- down_grad: float32 [2, 32, 512, 1024], P('section', 'ctx', 'fsdp')
The draws below stay inside these ranges and needn't reach their ends.
Inputs may be any that keep to these rules, and one draw needn't show every extreme that they name: `lengths`: for every sequence index, the sequence of one micro-batch has all 1024 positions valid. `routes`: each row names 8 different experts. In every layer, micro-batch and sequence, the 256 stored rows of one device name one expert at most 72 times.
All inputs are finite; a program needn't handle non-finite values.
Results may differ from the reference program's by a relative error of at most 0.02.
Values may be sent and summed in bfloat16 or wider, within the bound.
No kernel may reach another device: no remote copies, remote signals or barrier semaphores. Data moves between devices by JAX's collectives and lax.ppermute only.
A program may use at most 384 MiB of HBM per device.

```python
import math
import jax
import jax.numpy as jnp
import numpy as np
from jax import lax

D = 1024
QH = 16
KVH = 8
HD = 64
EXPERTS = 32
FF_E = 512
TOPK = 8
CTX_TOK = 256
MICRO = 2
LAYERS = 2
SEQS = 4
L = 1024
CAP = 72
N_CTX = 4


def draw_lengths(key, part):
    key = jax.random.fold_in(key, 7)
    first, second = jax.random.split(key)
    base = jax.random.randint(first, (MICRO, SEQS), L // 4, L + 1)
    chosen = jax.random.randint(second, (SEQS,), 0, MICRO)
    full_rows = jnp.arange(MICRO)[:, None] == chosen[None, :]
    return jnp.where(full_rows, L, base).astype(jnp.int32)


def block_levels(stream_key, shape, cuts, smallest, largest):
    loudness = 1.0
    for dim, parts in cuts:
        steps = jax.random.uniform(jax.random.fold_in(jax.random.fold_in(stream_key, 6), dim), (parts,), jnp.float32, smallest / len(cuts), largest / len(cuts))
        loudness = loudness * jnp.repeat(jnp.exp(steps), shape[dim] // parts).reshape((-1,) + (1,) * (len(shape) - 1 - dim))
    return loudness


def assign_block(key, own, number, rows, amount, top, bound, skew):
    sequence = jax.random.permutation(key, amount)
    packed, ordinary = portions_of(amount, rows * top, bound, skew, True), portions_of(amount, rows * top, bound, skew, False)
    places = jnp.arange(amount)

    def named(sizes, offset_by):
        used = int((sizes > 0).sum())
        fixed = max(1, used // 4)
        moved = fixed + (places - fixed + offset_by * (used - fixed)) % max(1, amount - fixed)
        return jnp.zeros((amount,), jnp.int32).at[sequence[jnp.where(places < fixed, places, moved)]].set(jnp.asarray(sizes, jnp.int32))

    sizes = jnp.where(number % 4 == 0, named(packed, number // 4), named(ordinary, number - number // 4 - 1))
    mixed = jax.random.permutation(jax.random.fold_in(own, 3), amount)
    giver, taker = mixed[0:amount // 2 * 2:2], mixed[1:amount // 2 * 2:2]
    slack = jnp.minimum(sizes[giver] - 1, bound - sizes[taker]) // 2
    slack = jnp.where((giver == sequence[0]) | (taker == sequence[0]) | (sizes[taker] == 0), 0, jnp.maximum(slack, 0))
    moved = jax.random.randint(jax.random.fold_in(own, 4), (amount // 2,), 0, 1 << 20) % (slack + 1)
    sizes = sizes.at[giver].add(-moved).at[taker].add(moved)
    members = jnp.searchsorted(jnp.cumsum(sizes), jnp.arange(rows * top), side="right").astype(jnp.int32)
    grid = members.reshape(top, rows).T
    grid = grid[jax.random.permutation(jax.random.fold_in(own, 1), rows)]
    offset_by = jax.random.randint(jax.random.fold_in(own, 2), (rows, 1), 0, top)
    return jnp.take_along_axis(grid, (jnp.arange(top)[None, :] + offset_by) % top, axis=1)


def portions_of(amount, total, bound, skew, full):
    loads = [(1 << 20) // math.isqrt(grade ** skew) + 1 for grade in range(1, amount + 1)]
    largest = bound if full else min(bound, max(-(-total // amount), total * loads[0] // sum(loads)))
    least = 1 if total - largest >= amount - 1 else 0
    counts, spare = [largest] + [least] * (amount - 1), total - largest - least * (amount - 1)
    while spare > 0:
        free = [i for i in range(1, amount) if counts[i] < largest] or [i for i in range(1, amount) if counts[i] < bound]
        whole, left = sum([loads[i] for i in free]), spare
        for i in free:
            more = min(bound - counts[i], max(1, left * loads[i] // whole), spare)
            counts[i] = counts[i] + more
            spare = spare - more
    return np.array(counts)


def centred(stream_key, extent, width, most, cuts=(), held_as=jnp.bfloat16):
    values = jax.random.normal(stream_key, extent, jnp.float32) * width
    if len(cuts) > 0:
        values = block_levels(stream_key, extent, cuts, -0.22, 0.18) * values
    return jnp.clip(values, min=-most, max=most).astype(held_as)


def setup_inputs(seed: int = 0) -> dict:
    splits = jax.random.split(jax.random.key(seed), 13)
    tokens = centred(splits[0], (MICRO, SEQS, L, D), 1.0, 6.0, ((1, 4), (2, 4)))
    targets = centred(splits[1], (MICRO, SEQS, L, D), 1.0, 6.0, ((1, 4), (2, 4)))
    lengths = draw_lengths(jax.random.fold_in(splits[12], 71), 0)
    routes_keys = jax.random.split(jax.random.fold_in(splits[3], 1), LAYERS * MICRO * SEQS * L // CTX_TOK)
    routes_turns = jax.random.permutation(jax.random.fold_in(splits[3], 3), LAYERS * MICRO * SEQS * L // CTX_TOK)
    routes = jax.vmap(lambda own, number: assign_block(jax.random.fold_in(splits[3], 2), own, number, CTX_TOK, EXPERTS, TOPK, CAP, 1))(routes_keys, routes_turns).reshape((LAYERS, MICRO, SEQS, L, TOPK))
    attention_gain = jnp.clip(1.0 + 0.1 * jax.random.normal(splits[4], (LAYERS, D), jnp.float32), 0.5, 1.5).astype(jnp.bfloat16)
    query_weight = centred(splits[5], (LAYERS, D, QH * HD), D ** -0.5, 0.1875, ((0, 2), (1, 16)))
    memory_weight = centred(splits[6], (LAYERS, D, 2 * KVH * HD), D ** -0.5, 0.1875, ((0, 2), (1, 16)))
    output_weight = centred(splits[7], (LAYERS, QH * HD, D), (QH * HD // 16) ** -0.5, 0.75, ((0, 2), (1, 16)))
    mixture_gain = jnp.clip(1.0 + 0.1 * jax.random.normal(splits[8], (LAYERS, D), jnp.float32), 0.5, 1.5).astype(jnp.bfloat16)
    router_weight = centred(splits[9], (LAYERS, D, EXPERTS), 0.015625, 0.099609375, ((0, 2), (1, 16)))
    gate_up_weight = centred(splits[10], (LAYERS, EXPERTS, D, 2 * FF_E), D ** -0.5, 0.1875, ((0, 2), (1, 4), (2, 4)))
    down_weight = centred(splits[11], (LAYERS, EXPERTS, FF_E, D), (FF_E // 16) ** -0.5, 1.0, ((0, 2), (1, 4), (2, 4)))
    return dict(tokens=tokens, targets=targets, lengths=lengths, routes=routes, attention_gain=attention_gain, query_weight=query_weight, memory_weight=memory_weight, output_weight=output_weight, mixture_gain=mixture_gain, router_weight=router_weight, gate_up_weight=gate_up_weight, down_weight=down_weight)


epsilon = 1e-06
rope_base = 10000.0
negative = -1e+30
HIGHEST = lax.Precision.HIGHEST

@jax.custom_vjp
def low(v):
    return lax.optimization_barrier(v.astype(jnp.bfloat16)).astype(jnp.float32)

@jax.custom_vjp
def low_back(v):
    return v

def low_keep(v):
    return (low(v), None)

def low_pass(kept, grad):
    return (grad,)

def back_keep(v):
    return (v, None)

def back_low(kept, grad):
    return (low(grad),)
low.defvjp(low_keep, low_pass)
low_back.defvjp(back_keep, back_low)

def rotary_tables(positions, head_width):
    half = head_width // 2
    inverse = rope_base ** (-2.0 * jnp.arange(half, dtype=jnp.float32) / head_width)
    angles = positions.astype(jnp.float32)[:, None] * inverse[None, :]
    angles = jnp.concatenate([angles, angles], axis=1)
    return (jnp.cos(angles)[:, None, :], jnp.sin(angles)[:, None, :])

def rotate(values, cosine, sine):
    half = values.shape[-1] // 2
    turned = jnp.concatenate([-values[..., half:], values[..., :half]], axis=-1)
    return values * cosine + turned * sine

def norm_apply(values, gain):
    return values * lax.rsqrt(lax.optimization_barrier(jnp.mean(values * values, axis=-1, keepdims=True)) + epsilon) * gain

def dot_high(left, right):
    return jnp.dot(left, right, precision=HIGHEST)

def stored_positions(first_row, count, row_count, devices):
    rows_index = first_row + jnp.arange(count, dtype=jnp.int32)
    device = rows_index // row_count
    within = rows_index % row_count
    half = row_count // 2
    return jnp.where(within < half, device * half + within, (2 * devices - 1 - device) * half + within - half).astype(jnp.int32)

def natural_rows():
    half = CTX_TOK // 2
    position = jnp.arange(L, dtype=jnp.int32)
    block = position // half
    inner = position % half
    device = jnp.where(block < N_CTX, block, 2 * N_CTX - 1 - block)
    second = jnp.where(block < N_CTX, 0, 1)
    return (device * CTX_TOK + second * half + inner).astype(jnp.int32)

def layer_sequence(params, inputs, route_rows, length):
    attention_gain, query_weight, memory_weight, output_weight, mixture_gain, router_weight, gate_up_weight, down_weight = params
    key_width = KVH * HD
    score_scale = 1.0 / math.sqrt(HD)
    positions = jnp.arange(L, dtype=jnp.int32)
    cosine, sine = rotary_tables(positions, HD)
    normed = low(norm_apply(inputs, attention_gain))
    query_raw = low_back(dot_high(normed, query_weight))
    memory_raw = low_back(dot_high(normed, memory_weight))
    query = low(rotate(query_raw.reshape(L, QH, HD), cosine, sine)).reshape(L, KVH, 2, HD)
    keys = low(rotate(memory_raw[:, :key_width].reshape(L, KVH, HD), cosine, sine))
    values = low(memory_raw[:, key_width:].reshape(L, KVH, HD))
    query_block = min(512, L)

    def attend(block):
        block_query, block_pos = block
        raw = low_back(jnp.einsum('rgjd,kgd->gjrk', block_query, keys, precision=HIGHEST) * score_scale)
        valid = (positions[None, :] <= block_pos[:, None]) & (positions[None, :] < length)
        probs = low(jax.nn.softmax(jnp.where(valid[None, None], raw, negative), axis=-1))
        return jnp.einsum('gjrk,kgd->rgjd', probs, values, precision=HIGHEST)
    attended = lax.map(jax.checkpoint(attend), (query.reshape(L // query_block, query_block, KVH, 2, HD), positions.reshape(L // query_block, query_block)))
    attended = low(low_back(attended.reshape(L, QH * HD)))
    middle = inputs + low_back(dot_high(attended, output_weight))
    normed_mix = low(norm_apply(middle, mixture_gain))
    logits = dot_high(normed_mix, router_weight)
    gates = jax.nn.softmax(jnp.take_along_axis(logits, route_rows, axis=1), axis=-1)
    capacity = N_CTX * CAP
    flat = route_rows.reshape(-1)
    onehot = (flat[:, None] == jnp.arange(EXPERTS, dtype=jnp.int32)[None, :]).astype(jnp.int32)
    rank = lax.optimization_barrier(jnp.sum((jnp.cumsum(onehot, axis=0) - onehot) * onehot, axis=1))
    slot_of = (flat * capacity + rank).astype(jnp.int32)
    owner = jnp.full((EXPERTS * capacity,), L * TOPK, jnp.int32).at[slot_of].set(jnp.arange(L * TOPK, dtype=jnp.int32))
    padded = jnp.concatenate([normed_mix, jnp.zeros((1, D), jnp.float32)], axis=0)
    dispatched = low_back(padded[owner // TOPK]).reshape(EXPERTS, capacity, D)
    gate_up = low_back(jnp.einsum('erd,edf->erf', dispatched, gate_up_weight, precision=HIGHEST))
    activated = low(jax.nn.silu(gate_up[..., :FF_E]) * gate_up[..., FF_E:])
    expert_out = low(low_back(jnp.einsum('erf,efd->erd', activated, down_weight, precision=HIGHEST))).reshape(EXPERTS * capacity, D)
    picked = expert_out[slot_of].reshape(L, TOPK, D)
    mixed = jnp.einsum('rk,rkd->rd', gates, picked, precision=HIGHEST)
    return middle + mixed

def reference(tokens, targets, lengths, routes, attention_gain, query_weight, memory_weight, output_weight, mixture_gain, router_weight, gate_up_weight, down_weight):
    count = MICRO * SEQS
    to_natural = natural_rows()
    to_stored = stored_positions(0, L, CTX_TOK, N_CTX)

    def natural(array):
        return array.reshape((count, L) + array.shape[3:])[:, to_natural]

    def stored(array):
        return array[:, to_stored].reshape((MICRO, SEQS, L) + array.shape[2:])
    start = natural(tokens.astype(jnp.float32))
    goals = natural(targets.astype(jnp.float32))
    layer_routes = [natural(routes[layer]) for layer in range(LAYERS)]
    sequence_lengths = lengths.reshape(count)
    valid = (jnp.arange(L, dtype=jnp.int32)[None, :] < sequence_lengths[:, None]).astype(jnp.float32)[:, :, None]
    weights = (attention_gain, query_weight, memory_weight, output_weight, mixture_gain, router_weight, gate_up_weight, down_weight)
    all_params = [tuple((weight[layer].astype(jnp.float32) for weight in weights)) for layer in range(LAYERS)]
    shifts = [jnp.zeros_like(start) for layer in range(LAYERS - 1)]

    def run_layer(params, layer_input, route_rows):

        def one(item):
            return layer_sequence(params, item[0], item[1], item[2])
        return lax.map(jax.checkpoint(one), (layer_input, route_rows, sequence_lengths))

    def objective(params_list, first_input, shift_list):
        current = first_input
        links = []
        result = first_input
        for layer in range(LAYERS):
            if layer > 0:
                current = links[layer - 1] + shift_list[layer - 1]
            result = run_layer(params_list[layer], current, layer_routes[layer])
            if layer < LAYERS - 1:
                links.append(low(low_back(result)))
        error = 0.5 * jnp.sum(valid * (result - goals) ** 2)
        return (error, (links, result))
    error, pullback, extras = jax.vjp(objective, all_params, start, shifts, has_aux=True)
    links, result = extras
    params_grad, start_grad, shift_grad = pullback(jnp.ones((), jnp.float32))
    hidden_states = jnp.stack([stored(link) for link in links] + [stored(result)]).astype(jnp.bfloat16)
    input_grads = jnp.stack([stored(start_grad)] + [stored(item) for item in shift_grad])
    loss_value = error / jnp.sum(lengths).astype(jnp.float32)
    grads = [jnp.stack([params_grad[layer][member] for layer in range(LAYERS)]) for member in range(8)]
    return (hidden_states, input_grads, loss_value, grads[0], grads[1], grads[2], grads[3], grads[4], grads[5], grads[6], grads[7])
```

```python
import functools
import math

import jax
import jax.numpy as jnp
from jax import lax
from jax.experimental import pallas as pl
from jax.experimental.pallas import tpu as pltpu
from jax.sharding import PartitionSpec as P

QH = 16
KVH = 8
HD = 64
EXPERTS = 32
FF_E = 512
TOPK = 8
KW = KVH * HD
EXT = 16

epsilon = 1e-06
rope_base = 10000.0
negative = -1e30
F32 = jnp.float32
BF16 = jnp.bfloat16
VMEM_LIMIT = 60 * 1024 * 1024


def params(grid_dims=0):
    return pltpu.CompilerParams(
        vmem_limit_bytes=VMEM_LIMIT,
        dimension_semantics=("arbitrary",) * grid_dims if grid_dims else None,
    )


def cost(flops, moved, exps=0):
    return pl.CostEstimate(flops=int(flops), bytes_accessed=int(moved), transcendentals=int(exps))


def mm(a, b):
    return jnp.dot(a, b, preferred_element_type=F32)


def mm_nt(a, b):
    return lax.dot_general(a, b, (((1,), (1,)), ((), ())), preferred_element_type=F32)


def mm_tn(a, b):
    return lax.dot_general(a, b, (((0,), (0,)), ((), ())), preferred_element_type=F32)


def fixed(shape):
    return pl.BlockSpec(shape, lambda *_: (0,) * len(shape), pipeline_mode=pl.Buffered(1))


def resident(shape):
    return pl.BlockSpec(shape, lambda *_: (0,) * len(shape))


def lane_index(shape):
    return lax.broadcasted_iota(jnp.int32, shape, len(shape) - 1)


def turn(block, cosine, sine):
    low_half = lane_index(block.shape) % HD < HD // 2
    swapped = jnp.where(
        low_half, pltpu.roll(block, 128 - HD // 2, axis=1), pltpu.roll(block, HD // 2, axis=1)
    )
    return block * cosine + swapped * sine


def rolled(block):
    return pltpu.roll(block.astype(F32), HD, axis=1).astype(BF16)


def key_positions(device, half, devices, shape, dim):
    within = lax.broadcasted_iota(jnp.int32, shape, dim)
    return jnp.where(
        within < half, device * half + within, (2 * devices - 1 - device) * half + within - half
    )


def fill_bias(bias, scal, devices, rows):
    context, length = scal[0], scal[1]
    query_pos = key_positions(context, rows // 2, devices, (rows, rows), 1)
    for k in range(devices):
        key_pos = key_positions(context ^ k, rows // 2, devices, (rows, rows), 0)
        taken = (key_pos <= query_pos) & (key_pos < length)
        bias[k * rows : (k + 1) * rows, :] = jnp.where(taken, 0.0, negative)


def two_heads(block):
    even = lane_index(block.shape) < HD
    zero = jnp.zeros((), block.dtype)
    return jnp.concatenate([jnp.where(even, block, zero), jnp.where(even, zero, block)], axis=0)


def two_heads_doubled(block):
    even = lane_index(block.shape) < HD
    other = rolled(block)
    return jnp.concatenate([jnp.where(even, block, other), jnp.where(even, other, block)], axis=0)


def doubled(block, odd):
    even = lane_index(block.shape) < HD
    other = rolled(block)
    return jnp.where(even, other, block) if odd else jnp.where(even, block, other)


def one_hot(rank_row, slots):
    rows = rank_row.shape[-1]
    index = lax.broadcasted_iota(jnp.int32, (slots, rows), 0).astype(F32)
    return rank_row == index


def project_kernel(x, gain, wq, wm, cosine, sine, q_out, kv_out):
    values = x[...].astype(F32)
    factor = lax.rsqrt(jnp.mean(values * values, axis=-1, keepdims=True) + epsilon)
    normed = (values * factor * gain[...]).astype(BF16)
    cos, sin = cosine[...], sine[...]
    q0 = mm(normed, wq[...])
    for b in range(QH * HD // 128):
        at = slice(b * 128, (b + 1) * 128)
        q_out[:, at] = turn(q0[:, at], cos, sin).astype(BF16)
    kv0 = mm(normed, wm[...])
    for b in range(KW // 128):
        at = slice(b * 128, (b + 1) * 128)
        kv_out[0, :, at] = turn(kv0[:, at], cos, sin).astype(BF16)
    kv_out[1] = kv0[:, KW:].astype(BF16)


def project(x, gain, shared, cosine, sine):
    rows, width = x.shape
    return pl.pallas_call(
        project_kernel,
        name="project",
        grid=(1,),
        in_specs=[
            fixed((rows, width)),
            fixed((1, width)),
            pl.BlockSpec((width, QH * HD), lambda i: (0, 0), pipeline_mode=pl.Buffered(1)),
            pl.BlockSpec((width, 2 * KW), lambda i: (0, 1), pipeline_mode=pl.Buffered(1)),
            fixed((rows, 128)),
            fixed((rows, 128)),
        ],
        out_specs=[resident((rows, QH * HD)), resident((2, rows, KW))],
        out_shape=[
            jax.ShapeDtypeStruct((rows, QH * HD), BF16),
            jax.ShapeDtypeStruct((2, rows, KW), BF16),
        ],
        compiler_params=params(1),
        cost_estimate=cost(2 * rows * width * 2048, 2 * width * 2048 + 8 * rows * width),
    )(x, gain, shared, shared, cosine, sine)


def attend_kernel(devices, scal, x, q, *rest):
    ks, vs, rest = rest[:devices], rest[devices : 2 * devices], rest[2 * devices :]
    wo, gain, router, mask, o_out, lse_out, mid_out, msg_out, bias, held = rest
    rows = x.shape[0]
    step = pl.program_id(0)

    @pl.when(step == 0)
    def _():
        fill_bias(bias, scal, devices, rows)

    keys = jnp.concatenate([r[0] for r in ks], axis=0)
    values = jnp.concatenate([r[0] for r in vs], axis=0)
    block_bias = bias[...]
    both_bias = jnp.concatenate([block_bias, block_bias], axis=1)
    for i in range(2):
        query = two_heads(q[:, i * 128 : (i + 1) * 128])
        scores = mm_nt(doubled(keys, i), query) * (1.0 / math.sqrt(HD)) + both_bias
        top = jnp.max(scores, axis=0, keepdims=True)
        raised = jnp.exp(scores - top)
        total = jnp.sum(raised, axis=0, keepdims=True)
        probs = (raised * (1.0 / total)).astype(BF16)
        lse_out[0, i : i + 1, :] = top + jnp.log(total)
        mixed = mm_tn(values, probs)[i * HD : (i + 1) * HD]
        pair = jnp.concatenate([mixed[:, :rows], mixed[:, rows:]], axis=0)
        at = pl.multiple_of(step * 256 + i * 128, 128)
        held[:, pl.ds(at, 128)] = jnp.transpose(pair).astype(BF16)

    @pl.when(step == pl.num_programs(0) - 1)
    def _():
        attended = held[...]
        o_out[...] = attended
        middle = x[...].astype(F32) + mm(attended, wo[...])
        mid_out[...] = middle
        factor = lax.rsqrt(jnp.mean(middle * middle, axis=-1, keepdims=True) + epsilon)
        normed = (middle * factor * gain[...]).astype(BF16)
        msg_out[:rows, :] = normed
        logits = mm_nt(router[...], normed)
        chosen = mask[...] > 0.5
        top = jnp.max(jnp.where(chosen, logits, negative), axis=0, keepdims=True)
        raised = jnp.where(chosen, jnp.exp(jnp.where(chosen, logits - top, 0.0)), 0.0)
        gates = raised / jnp.sum(raised, axis=0, keepdims=True)
        high = gates.astype(BF16)
        low = (gates - high.astype(F32)).astype(BF16)
        ext = [high[:EXT], high[EXT:], low[:EXT], low[EXT:]]
        if 4 * rows < x.shape[1]:
            ext.append(jnp.zeros((EXT, x.shape[1] - 4 * rows), BF16))
        msg_out[rows:, :] = jnp.concatenate(ext, axis=1)


def attend(scal, x, q, kvs, shared, gain, router, mask):
    rows, width = x.shape
    devices = len(kvs)
    keys = devices * rows
    kv_specs = [pl.BlockSpec((1, rows, 128), lambda h: (0, 0, h)) for _ in kvs] + [
        pl.BlockSpec((1, rows, 128), lambda h: (1, 0, h)) for _ in kvs
    ]
    return pl.pallas_call(
        functools.partial(attend_kernel, devices),
        name="attend",
        grid=(KVH // 2,),
        in_specs=[
            pl.BlockSpec(memory_space=pltpu.SMEM),
            fixed((rows, width)),
            pl.BlockSpec((rows, 256), lambda h: (0, h)),
            *kv_specs,
            pl.BlockSpec((QH * HD, width), lambda h: (0, 2), pipeline_mode=pl.Buffered(1)),
            fixed((1, width)),
            fixed((EXPERTS, width)),
            fixed((EXPERTS, rows)),
        ],
        out_specs=[
            resident((rows, QH * HD)),
            pl.BlockSpec((1, 2, 2 * rows), lambda h: (h, 0, 0)),
            resident((rows, width)),
            resident((rows + EXT, width)),
        ],
        out_shape=[
            jax.ShapeDtypeStruct((rows, QH * HD), BF16),
            jax.ShapeDtypeStruct((KVH // 2, 2, 2 * rows), F32),
            jax.ShapeDtypeStruct((rows, width), F32),
            jax.ShapeDtypeStruct((rows + EXT, width), BF16),
        ],
        scratch_shapes=[pltpu.VMEM((keys, rows), F32), pltpu.VMEM((rows, QH * HD), BF16)],
        compiler_params=params(1),
        cost_estimate=cost(
            4 * rows * keys * QH * HD * 2 + 2 * rows * width * width,
            2 * width * width + 4 * keys * width + 12 * rows * width,
            rows * keys * QH,
        ),
    )(scal, x, q, *kvs, *kvs, shared, gain, router, mask)


def experts_kernel(sources, slots, scal, *rest):
    msgs, rest = rest[:sources], rest[sources:]
    rank, w1, w2, x_out, gu_out, y_out, gate_out, own_out, other_out, xs, ys = rest
    local = rank.shape[1]
    rows = rank.shape[2]
    step = pl.program_id(0)
    half = sources // 2

    @pl.when(step == 0)
    def _():
        first = scal[0]
        pick_row = lax.broadcasted_iota(jnp.int32, (EXT, 4 * rows), 0)
        for j in range(sources):
            hot = jnp.concatenate(
                [
                    jnp.where(one_hot(rank[j, i : i + 1, :], slots), 1.0, 0.0).astype(BF16)
                    for i in range(local)
                ],
                axis=0,
            )
            picked = mm(hot, msgs[j][:rows, :]).astype(BF16)
            ext = msgs[j][rows:, : 4 * rows].astype(F32)
            for i in range(local):
                xs[i, j] = picked[i * slots : (i + 1) * slots]
                expert = first + i
                row = jnp.sum(jnp.where(pick_row == expert % EXT, ext, 0.0), axis=0, keepdims=True)
                high = jnp.where(expert < EXT, row[:, :rows], row[:, rows : 2 * rows])
                low = jnp.where(expert < EXT, row[:, 2 * rows : 3 * rows], row[:, 3 * rows :])
                gate_out[j, i : i + 1, :] = high + low

    width = xs.shape[-1]
    taken = xs[step].reshape(sources * slots, width)
    x_out[0] = taken
    gate_up = mm(taken, w1[0])
    gu_out[0] = gate_up
    gate, up = gate_up[:, :FF_E], gate_up[:, FF_E:]
    activated = (gate * jax.nn.sigmoid(gate) * up).astype(BF16)
    out = mm(activated, w2[0]).astype(BF16)
    y_out[0] = out
    ys[step] = out.reshape(sources, slots, width)

    @pl.when(step == pl.num_programs(0) - 1)
    def _():
        for j in range(sources):
            spread = jnp.concatenate(
                [
                    jnp.where(one_hot(rank[j, i : i + 1, :], slots), gate_out[j, i : i + 1, :], 0.0)
                    for i in range(local)
                ],
                axis=0,
            )
            high = spread.astype(BF16)
            low = (spread - high.astype(F32)).astype(BF16)
            given = ys[:, j].reshape(local * slots, width)
            part = (mm_tn(high, given) + mm_tn(low, given)).astype(BF16)
            if j < half:
                own_out[j] = part
            else:
                other_out[j - half] = part


def experts_forward(scal, msgs, rank, w1, w2, slots):
    sources, local, rows = rank.shape
    width = msgs[0].shape[1]
    count = sources * slots
    each = lambda shape: pl.BlockSpec((1,) + shape, lambda e: (e, 0, 0))
    return pl.pallas_call(
        functools.partial(experts_kernel, sources, slots),
        name="experts_forward",
        grid=(local,),
        in_specs=[
            pl.BlockSpec(memory_space=pltpu.SMEM),
            *[fixed((rows + EXT, width)) for _ in msgs],
            fixed((sources, local, rows)),
            each((width, 2 * FF_E)),
            each((FF_E, width)),
        ],
        out_specs=[
            each((count, width)),
            each((count, 2 * FF_E)),
            each((count, width)),
            resident((sources, local, rows)),
            resident((sources // 2, rows, width)),
            resident((sources // 2, rows, width)),
        ],
        out_shape=[
            jax.ShapeDtypeStruct((local, count, width), BF16),
            jax.ShapeDtypeStruct((local, count, 2 * FF_E), F32),
            jax.ShapeDtypeStruct((local, count, width), BF16),
            jax.ShapeDtypeStruct((sources, local, rows), F32),
            jax.ShapeDtypeStruct((sources // 2, rows, width), BF16),
            jax.ShapeDtypeStruct((sources // 2, rows, width), BF16),
        ],
        scratch_shapes=[
            pltpu.VMEM((local, sources, slots, width), BF16),
            pltpu.VMEM((local, sources, slots, width), BF16),
        ],
        compiler_params=params(1),
        cost_estimate=cost(
            2 * local * count * width * 3 * FF_E * 1.3, 8 * local * count * width, local * count * FF_E
        ),
    )(scal, *msgs, rank, w1, w2)


def experts_back_kernel(sources, slots, *rest):
    msgs, rest = rest[:sources], rest[sources:]
    rank, gates, xs, gu, ys, w1, w2, router = rest[:8]
    g1_out, g2_out, router_out, own_out, other_out, held = rest[8:]
    local = rank.shape[1]
    rows = rank.shape[2]
    width = held.shape[-1]
    step = pl.program_id(0)
    half = sources // 2

    @pl.when(step == 0)
    def _():
        for j in range(sources):
            hot = jnp.concatenate(
                [
                    jnp.where(one_hot(rank[j, i : i + 1, :], slots), 1.0, 0.0).astype(BF16)
                    for i in range(local)
                ],
                axis=0,
            )
            picked = mm(hot, msgs[j][:rows, :]).astype(BF16)
            for i in range(local):
                held[i, j] = picked[i * slots : (i + 1) * slots]

    gate_columns, inner_columns = [], []
    for j in range(sources):
        hot = one_hot(rank[j, pl.ds(step, 1), :], slots)
        ext = msgs[j][rows:, :rows].astype(F32)
        inner = ext[0:1, :] + ext[1:2, :]
        gate_columns.append(
            jnp.sum(jnp.where(hot, gates[j, pl.ds(step, 1), :], 0.0), axis=1, keepdims=True)
        )
        inner_columns.append(jnp.sum(jnp.where(hot, inner, 0.0), axis=1, keepdims=True))
    gate_column = jnp.concatenate(gate_columns, axis=0)
    inner_column = jnp.concatenate(inner_columns, axis=0)
    grad_out = held[step].reshape(sources * slots, width).astype(F32)
    grad_y = (gate_column * grad_out).astype(BF16)
    given = jnp.sum(grad_out * ys[0].astype(F32), axis=1, keepdims=True)
    grad_logit = gate_column * (given - inner_column)
    gate, up = gu[0, :, :FF_E], gu[0, :, FF_E:]
    sigmoid = jax.nn.sigmoid(gate)
    silu = gate * sigmoid
    activated = (silu * up).astype(BF16)
    g2_out[0] = mm_tn(activated, grad_y).astype(BF16)
    grad_act = mm_nt(grad_y, w2[0])
    grad_gate = grad_act * up * sigmoid * (1.0 + gate * (1.0 - sigmoid))
    grad_up = grad_act * silu
    grad_gate_up = jnp.concatenate([grad_gate.astype(BF16), grad_up.astype(BF16)], axis=1)
    taken = xs[0]
    g1_out[0] = mm_tn(taken, grad_gate_up).astype(BF16)
    router_out[0] = jnp.sum(taken.astype(F32) * grad_logit, axis=0, keepdims=True)
    grad_rows = mm_nt(grad_gate_up, w1[0]) + grad_logit * router[0]
    held[step] = grad_rows.astype(BF16).reshape(sources, slots, width)

    @pl.when(step == pl.num_programs(0) - 1)
    def _():
        for j in range(sources):
            hot = jnp.concatenate(
                [
                    jnp.where(one_hot(rank[j, i : i + 1, :], slots), 1.0, 0.0)
                    for i in range(local)
                ],
                axis=0,
            ).astype(BF16)
            part = mm_tn(hot, held[:, j].reshape(local * slots, width)).astype(BF16)
            if j < half:
                own_out[j] = part
            else:
                other_out[j - half] = part


def experts_backward(msgs, rank, gates, xs, gu, ys, w1, w2, router, slots):
    sources, local, rows = rank.shape
    width = msgs[0].shape[1]
    count = sources * slots
    each = lambda shape: pl.BlockSpec((1,) + shape, lambda e: (e, 0, 0))
    return pl.pallas_call(
        functools.partial(experts_back_kernel, sources, slots),
        name="experts_backward",
        grid=(local,),
        in_specs=[
            *[fixed((rows + EXT, width)) for _ in msgs],
            fixed((sources, local, rows)),
            fixed((sources, local, rows)),
            each((count, width)),
            each((count, 2 * FF_E)),
            each((count, width)),
            each((width, 2 * FF_E)),
            each((FF_E, width)),
            each((1, width)),
        ],
        out_specs=[
            each((width, 2 * FF_E)),
            each((FF_E, width)),
            each((1, width)),
            resident((sources // 2, rows, width)),
            resident((sources // 2, rows, width)),
        ],
        out_shape=[
            jax.ShapeDtypeStruct((local, width, 2 * FF_E), BF16),
            jax.ShapeDtypeStruct((local, FF_E, width), BF16),
            jax.ShapeDtypeStruct((local, 1, width), F32),
            jax.ShapeDtypeStruct((sources // 2, rows, width), BF16),
            jax.ShapeDtypeStruct((sources // 2, rows, width), BF16),
        ],
        scratch_shapes=[pltpu.VMEM((local, sources, slots, width), BF16)],
        compiler_params=params(1),
        cost_estimate=cost(
            2 * local * count * width * 3 * FF_E * 2.3, 14 * local * count * width, local * count * FF_E
        ),
    )(*msgs, rank, gates, xs, gu, ys, w1, w2, router)


def attend_back_kernel(devices, arrived, scal, *rest):
    parts, rest = rest[:arrived], rest[arrived:]
    grad_out, middle, gain, attended, wo, q, lse, cosine, sine = rest[:9]
    ks, vs, rest = rest[9 : 9 + devices], rest[9 + devices : 9 + 2 * devices], rest[9 + 2 * devices :]
    mid_out, wo_grad, gain_grad, dq_out = rest[:4]
    dkv_outs, (bias, held) = rest[4 : 4 + devices], rest[4 + devices :]
    rows = middle.shape[0]
    scale = 1.0 / math.sqrt(HD)
    step = pl.program_id(0)

    @pl.when(step == 0)
    def _():
        fill_bias(bias, scal, devices, rows)
        grad_mix = parts[0][...].astype(F32)
        for part in parts[1:]:
            grad_mix = grad_mix + part[...].astype(F32)
        mid = middle[...]
        factor = lax.rsqrt(jnp.mean(mid * mid, axis=-1, keepdims=True) + epsilon)
        scaled = grad_mix * gain[...]
        inner = jnp.mean(mid * scaled, axis=-1, keepdims=True)
        gain_grad[...] = jnp.sum(grad_mix * mid * factor, axis=0, keepdims=True)
        grad_mid = grad_out[...] + factor * scaled - mid * (factor * factor * factor * inner)
        mid_out[...] = grad_mid
        branch = grad_mid.astype(BF16)
        wo_grad[...] = mm_tn(attended[...], branch).astype(BF16)
        held[...] = mm_nt(branch, wo[...]).astype(BF16)

    keys = jnp.concatenate([r[0] for r in ks], axis=0)
    values = jnp.concatenate([r[0] for r in vs], axis=0)
    block_bias = bias[...]
    both_bias = jnp.concatenate([block_bias, block_bias], axis=1)
    key_parts, value_parts = [], []
    for i in range(2):
        block = q[:, i * 128 : (i + 1) * 128]
        at = pl.multiple_of(step * 256 + i * 128, 128)
        grads = held[:, pl.ds(at, 128)]
        scores = mm_nt(doubled(keys, i), two_heads(block)) * scale + both_bias
        probs = jnp.exp(scores - lse[0, i : i + 1, :])
        grad_probs = mm_nt(doubled(values, i), two_heads(grads))
        product = probs * grad_probs
        dots = jnp.sum(product, axis=0, keepdims=True)
        grad_scores = (product - probs * dots).astype(BF16)
        key_parts.append(mm(grad_scores, two_heads_doubled(block)) * scale)
        value_parts.append(mm(probs.astype(BF16), two_heads_doubled(grads)))
        moved = mm_tn(keys, grad_scores)[i * HD : (i + 1) * HD] * scale
        pair = jnp.concatenate([moved[:, :rows], moved[:, rows:]], axis=0)
        dq_out[:, i * 128 : (i + 1) * 128] = turn(
            jnp.transpose(pair), cosine[...], sine[...]
        ).astype(BF16)
    even = lane_index(key_parts[0].shape) < HD
    grad_keys = jnp.where(even, key_parts[0], key_parts[1]).astype(BF16)
    grad_values = jnp.where(even, value_parts[0], value_parts[1]).astype(BF16)
    for k in range(devices):
        dkv_outs[k][0] = grad_keys[k * rows : (k + 1) * rows]
        dkv_outs[k][1] = grad_values[k * rows : (k + 1) * rows]


def attend_backward(scal, parts, grad_out, middle, gain, attended, shared, q, lse, cosine, sine, kvs):
    rows, width = middle.shape
    devices = len(kvs)
    keys = devices * rows
    kv_specs = [pl.BlockSpec((1, rows, 128), lambda h: (0, 0, h)) for _ in kvs] + [
        pl.BlockSpec((1, rows, 128), lambda h: (1, 0, h)) for _ in kvs
    ]
    return pl.pallas_call(
        functools.partial(attend_back_kernel, devices, len(parts)),
        name="attend_backward",
        grid=(KVH // 2,),
        in_specs=[
            pl.BlockSpec(memory_space=pltpu.SMEM),
            *[fixed((rows, width)) for _ in parts],
            fixed((rows, width)),
            fixed((rows, width)),
            fixed((1, width)),
            fixed((rows, QH * HD)),
            pl.BlockSpec((QH * HD, width), lambda h: (0, 2), pipeline_mode=pl.Buffered(1)),
            pl.BlockSpec((rows, 256), lambda h: (0, h)),
            pl.BlockSpec((1, 2, 2 * rows), lambda h: (h, 0, 0)),
            fixed((rows, 128)),
            fixed((rows, 128)),
            *kv_specs,
        ],
        out_specs=[
            resident((rows, width)),
            resident((QH * HD, width)),
            resident((1, width)),
            pl.BlockSpec((rows, 256), lambda h: (0, h)),
            *[pl.BlockSpec((2, rows, 128), lambda h: (0, 0, h)) for _ in kvs],
        ],
        out_shape=[
            jax.ShapeDtypeStruct((rows, width), F32),
            jax.ShapeDtypeStruct((QH * HD, width), BF16),
            jax.ShapeDtypeStruct((1, width), F32),
            jax.ShapeDtypeStruct((rows, QH * HD), BF16),
            *[jax.ShapeDtypeStruct((2, rows, KW), BF16) for _ in kvs],
        ],
        scratch_shapes=[pltpu.VMEM((keys, rows), F32), pltpu.VMEM((rows, QH * HD), BF16)],
        compiler_params=params(1),
        cost_estimate=cost(
            10 * rows * keys * QH * HD * 2 + 4 * rows * width * width,
            6 * width * width + 8 * keys * width + 20 * rows * width,
            rows * keys * QH,
        ),
    )(
        scal, *parts, grad_out, middle, gain, attended, shared, q, lse, cosine, sine, *kvs, *kvs
    )


def project_back_kernel(devices, x, gain, dq, *rest):
    parts, rest = rest[:devices], rest[devices:]
    grad_mid, wq, wm, cosine, sine, dx_out, wq_grad, wm_grad, gain_grad = rest
    values = x[...].astype(F32)
    factor = lax.rsqrt(jnp.mean(values * values, axis=-1, keepdims=True) + epsilon)
    normed = (values * factor * gain[...]).astype(BF16)
    summed = parts[0][...].astype(F32)
    for part in parts[1:]:
        summed = summed + part[...].astype(F32)
    grad_keys = [
        turn(summed[0, :, b * 128 : (b + 1) * 128], cosine[...], sine[...]).astype(BF16)
        for b in range(KW // 128)
    ]
    grad_memory = jnp.concatenate(grad_keys + [summed[1].astype(BF16)], axis=1)
    grad_query = dq[...]
    wq_grad[...] = mm_tn(normed, grad_query).astype(BF16)
    wm_grad[...] = mm_tn(normed, grad_memory).astype(BF16)
    grad_normed = mm_nt(grad_query, wq[...]) + mm_nt(grad_memory, wm[...])
    scaled = grad_normed * gain[...]
    inner = jnp.mean(values * scaled, axis=-1, keepdims=True)
    gain_grad[...] = jnp.sum(grad_normed * values * factor, axis=0, keepdims=True)
    dx_out[...] = (
        grad_mid[...] + factor * scaled - values * (factor * factor * factor * inner)
    )


def project_backward(x, gain, dq, parts, grad_mid, shared, cosine, sine):
    rows, width = x.shape
    return pl.pallas_call(
        functools.partial(project_back_kernel, len(parts)),
        name="project_backward",
        grid=(1,),
        in_specs=[
            fixed((rows, width)),
            fixed((1, width)),
            fixed((rows, QH * HD)),
            *[fixed((2, rows, KW)) for _ in parts],
            fixed((rows, width)),
            pl.BlockSpec((width, QH * HD), lambda i: (0, 0), pipeline_mode=pl.Buffered(1)),
            pl.BlockSpec((width, 2 * KW), lambda i: (0, 1), pipeline_mode=pl.Buffered(1)),
            fixed((rows, 128)),
            fixed((rows, 128)),
        ],
        out_specs=[
            resident((rows, width)),
            resident((width, QH * HD)),
            resident((width, 2 * KW)),
            resident((1, width)),
        ],
        out_shape=[
            jax.ShapeDtypeStruct((rows, width), F32),
            jax.ShapeDtypeStruct((width, QH * HD), BF16),
            jax.ShapeDtypeStruct((width, 2 * KW), BF16),
            jax.ShapeDtypeStruct((1, width), F32),
        ],
        compiler_params=params(1),
        cost_estimate=cost(8 * rows * width * 2048, 8 * width * 2048 + 16 * rows * width),
    )(x, gain, dq, *parts, grad_mid, shared, shared, cosine, sine)


def pairs_within(axis, by, sections=(0, 1)):
    count = lax.axis_size(axis)
    return [(s * count + i, s * count + (i ^ by)) for s in sections for i in range(count)]


def exchanged(value, axis, by, sections=(0, 1)):
    return lax.ppermute(value, ("section", axis), pairs_within(axis, by, sections))


def swapped(value):
    return lax.ppermute(value, "section", [(0, 1), (1, 0)])


def from_all(value, axis, sections=(0, 1)):
    count = lax.axis_size(axis)
    return [value] + [exchanged(value, axis, k, sections) for k in range(1, count)]


def in_order(blocks, me):
    size = blocks[0].shape[0]
    whole = jnp.zeros((size * len(blocks),) + blocks[0].shape[1:], blocks[0].dtype)
    for k, block in enumerate(blocks):
        whole = lax.dynamic_update_slice_in_dim(whole, block, (me ^ k) * size, 0)
    return whole


def scattered_sum(value, axis, me, sections):
    count = lax.axis_size(axis)
    size = value.shape[0] // count
    block = lambda k: lax.dynamic_slice_in_dim(value, (me ^ k) * size, size, 0)
    total = block(0).astype(F32)
    for arrived in [exchanged(block(k), axis, k, sections) for k in range(1, count)]:
        total = total + arrived.astype(F32)
    return total


def shards(
    tokens,
    targets,
    lengths,
    routes,
    attention_gain,
    query_weight,
    memory_weight,
    output_weight,
    mixture_gain,
    router_weight,
    gate_up_weight,
    down_weight,
):
    section = lax.axis_index("section")
    context = lax.axis_index("ctx")
    line = lax.axis_index("fsdp")
    devices = lax.axis_size("ctx")
    depth = lax.axis_size("fsdp")
    first_core = section == 0
    rows, width = tokens.shape[2:]
    layers = 2
    held_experts = gate_up_weight.shape[1]
    local = held_experts // 2
    sources = 2 * devices
    capacity = rows * TOPK * 9 // (EXPERTS * 8)
    slots = -(-capacity // 16) * 16
    first_expert = context * held_experts + section * local

    def both_layers(weight):
        mine = lax.dynamic_slice_in_dim(weight, section * local, local, 0)
        theirs = lax.dynamic_slice_in_dim(weight, (1 - section) * local, local, 0)
        arrived = swapped(theirs)
        return (jnp.where(first_core, mine, arrived), jnp.where(first_core, arrived, mine))

    up_shards = both_layers(gate_up_weight[0])
    down_shards = both_layers(down_weight[0])
    experts = []
    for layer in range(layers):
        experts.append(
            (
                lax.all_gather(up_shards[layer], "fsdp", axis=1, tiled=True),
                lax.all_gather(down_shards[layer], "fsdp", axis=1, tiled=True),
            )
        )

    pack = jnp.concatenate(
        [
            query_weight[0],
            memory_weight[0],
            output_weight[0],
            router_weight[0],
            attention_gain[0][:, None],
            mixture_gain[0][:, None],
            jnp.zeros((query_weight.shape[1], 128 - EXPERTS - 2), BF16),
        ],
        axis=1,
    )

    def gathered_shared(layer):
        plane = in_order(from_all(pack, "fsdp", (layer,)), line)
        whole = in_order(from_all(plane, "ctx", (layer,)), context)
        arrived = lax.ppermute(whole, "section", [(layer, 1 - layer)])
        return jnp.where(section == layer, whole, arrived)

    def small_parts(whole):
        small = whole[:, 3 * width :].T
        return (
            small[:EXPERTS],
            small[EXPERTS : EXPERTS + 1].astype(F32),
            small[EXPERTS + 1 : EXPERTS + 2].astype(F32),
        )

    my_routes = jnp.swapaxes(routes[0, :, 0], 1, 2)
    other_routes = swapped(my_routes)
    layer_routes = jnp.where(
        first_core,
        jnp.stack([my_routes, other_routes]),
        jnp.stack([other_routes, my_routes])[:, ::-1],
    )
    all_routes = jnp.stack(from_all(layer_routes, "ctx"), axis=2).reshape(
        layers, sources, TOPK, rows
    )
    ids = first_expert + jnp.arange(local, dtype=jnp.int32)
    named = jnp.any(all_routes[:, :, None] == ids[None, None, :, None, None], axis=3)
    earlier = (
        lax.broadcasted_iota(jnp.int32, (rows, rows), 0)
        < lax.broadcasted_iota(jnp.int32, (rows, rows), 1)
    ).astype(BF16)
    before = jnp.dot(
        named.astype(BF16).reshape(-1, rows), earlier, preferred_element_type=F32
    ).reshape(named.shape)
    ranks = jnp.where(named, before, -1.0)
    masks = jnp.any(
        layer_routes[:, 0, None] == jnp.arange(EXPERTS, dtype=jnp.int32)[None, :, None, None], axis=2
    ).astype(F32)

    half = rows // 2
    within = jnp.arange(rows, dtype=jnp.int32)
    positions = jnp.where(
        within < half, context * half + within, (2 * devices - 1 - context) * half + within - half
    )
    inverse = rope_base ** (-2.0 * jnp.arange(HD // 2, dtype=F32) / HD)
    angles = positions.astype(F32)[:, None] * inverse[None, :]
    sine, cosine = jnp.sin(angles), jnp.cos(angles)
    cos_table = jnp.concatenate([cosine] * 4, axis=1)
    sin_table = jnp.concatenate([-sine, sine, -sine, sine], axis=1)
    length = lengths[section, line]
    attend_scalars = jnp.stack([context, length]).astype(jnp.int32)
    expert_scalars = first_expert.astype(jnp.int32).reshape(1)

    def dispatched(message):
        plane = from_all(message, "ctx")
        return plane + [swapped(block) for block in plane]

    def returned(own, other):
        crossed = [swapped(other[k]) for k in range(devices)]
        terms = [own[0], crossed[0]]
        for k in range(1, devices):
            chip = (own[k].astype(F32) + crossed[k].astype(F32)).astype(BF16)
            terms.append(exchanged(chip, "ctx", k))
        return terms

    my_targets = lax.dynamic_index_in_dim(targets[:, 0], section, 0, keepdims=False)
    layer_input = lax.dynamic_index_in_dim(tokens[:, 0], section, 0, keepdims=False)
    saved, hidden = [], []
    for layer in range(layers):
        shared = gathered_shared(layer)
        router, gain_first, gain_second = small_parts(shared)
        w1, w2 = experts[layer]
        q, kv = project(layer_input, gain_first, shared, cos_table, sin_table)
        kvs = from_all(kv, "ctx")
        attended, lse, middle, message = attend(
            attend_scalars, layer_input, q, kvs, shared, gain_second, router, masks[layer]
        )
        messages = dispatched(message)
        xs, gate_up, ys, gates, own, other = experts_forward(
            expert_scalars, messages, ranks[layer], w1, w2, slots
        )
        mixed = functools.reduce(lambda a, b: a + b, [t.astype(F32) for t in returned(own, other)])
        output = middle + mixed
        hidden.append(output.astype(BF16))
        saved.append(
            dict(
                x=layer_input,
                shared=shared,
                router=router,
                gain_first=gain_first,
                gain_second=gain_second,
                q=q,
                kvs=kvs,
                attended=attended,
                lse=lse,
                middle=middle,
                xs=xs,
                gate_up=gate_up,
                ys=ys,
                gates=gates,
                mixed=mixed,
            )
        )
        layer_input = hidden[-1]

    valid = (positions < length).astype(F32)[:, None]
    grad_output = (output - my_targets.astype(F32)) * valid
    error = 0.5 * jnp.sum(grad_output * grad_output)
    for axis in ("section", "ctx", "fsdp"):
        by = 1
        while by < lax.axis_size(axis):
            error = error + lax.ppermute(
                error, axis, [(i, i ^ by) for i in range(lax.axis_size(axis))]
            )
            by *= 2
    loss_value = error / jnp.sum(lengths).astype(F32)

    input_grads, shared_grads, expert_grads = [None] * layers, [None] * layers, [None] * layers
    small_grads = [None] * layers
    for layer in reversed(range(layers)):
        kept = saved[layer]
        w1, w2 = experts[layer]
        inner = jnp.sum(grad_output * kept["mixed"], axis=1)
        inner_high = inner.astype(BF16)
        inner_low = (inner - inner_high.astype(F32)).astype(BF16)
        ext = jnp.pad(jnp.stack([inner_high, inner_low]), ((0, EXT - 2), (0, width - rows)))
        message = jnp.concatenate([grad_output.astype(BF16), ext], axis=0)
        own_router = lax.dynamic_slice_in_dim(kept["router"], first_expert, local, 0).astype(F32)
        g1, g2, router_grad, own, other = experts_backward(
            dispatched(message),
            ranks[layer],
            kept["gates"],
            kept["xs"],
            kept["gate_up"],
            kept["ys"],
            w1,
            w2,
            own_router[:, None, :],
            slots,
        )
        expert_grads[layer] = (
            lax.psum_scatter(g2, "fsdp", scatter_dimension=1, tiled=True),
            lax.psum_scatter(g1, "fsdp", scatter_dimension=1, tiled=True),
        )
        back = attend_backward(
            attend_scalars,
            returned(own, other),
            grad_output,
            kept["middle"],
            kept["gain_second"],
            kept["attended"],
            kept["shared"],
            kept["q"],
            kept["lse"],
            cos_table,
            -sin_table,
            kept["kvs"],
        )
        grad_mid, wo_grad, gain_second_grad, dq = back[:4]
        dkv = back[4:]
        parts = [dkv[0]] + [exchanged(dkv[k], "ctx", k) for k in range(1, devices)]
        dx, wq_grad, wm_grad, gain_first_grad = project_backward(
            kept["x"], kept["gain_first"], dq, parts, grad_mid, kept["shared"], cos_table, -sin_table
        )
        input_grads[layer] = dx
        grad_output = dx.astype(BF16).astype(F32)

        router_rows = lax.dynamic_update_slice_in_dim(
            jnp.zeros((EXPERTS, width), F32), router_grad[:, 0], first_expert, 0
        )
        small = jnp.concatenate(
            [
                router_rows,
                gain_first_grad,
                gain_second_grad,
                jnp.zeros((128 - EXPERTS - 2, width), F32),
            ],
            axis=0,
        ).astype(BF16)
        packed = jnp.concatenate([wq_grad, wm_grad, wo_grad, small.T], axis=1)
        arrived = lax.ppermute(packed, "section", [(1 - layer, layer)])
        chip = (packed.astype(F32) + arrived.astype(F32)).astype(BF16)
        plane = scattered_sum(chip, "ctx", context, (layer,)).astype(BF16)
        shared_grads[layer] = scattered_sum(plane, "fsdp", line, (layer,))

    def placed_experts(which):
        home = jnp.where(first_core, expert_grads[0][which], expert_grads[1][which])
        away = jnp.where(first_core, expert_grads[1][which], expert_grads[0][which])
        arrived = swapped(away)
        return jnp.concatenate(
            [jnp.where(first_core, home, arrived), jnp.where(first_core, arrived, home)], axis=0
        ).astype(F32)

    def placed_rows(values):
        home = jnp.where(first_core, values[0], values[1])
        arrived = swapped(jnp.where(first_core, values[1], values[0]))
        return jnp.stack(
            [jnp.where(first_core, home, arrived), jnp.where(first_core, arrived, home)]
        )

    total = jnp.where(first_core, shared_grads[0], shared_grads[1])
    at = 3 * width
    return (
        placed_rows(hidden)[None, :, None],
        placed_rows(input_grads)[None, :, None],
        loss_value,
        total[:, at + EXPERTS][None],
        total[:, :width][None],
        total[:, width : 2 * width][None],
        total[:, 2 * width : 3 * width][None],
        total[:, at + EXPERTS + 1][None],
        total[:, at : at + EXPERTS][None],
        placed_experts(1)[None],
        placed_experts(0)[None],
    )


def solution(mesh):
    placed = (
        P(None, "fsdp", "ctx", None),
        P(None, "fsdp", "ctx", None),
        P(),
        P("section", None, "fsdp", "ctx", None),
        P("section", ("ctx", "fsdp")),
        P("section", ("ctx", "fsdp"), None),
        P("section", ("ctx", "fsdp"), None),
        P("section", ("ctx", "fsdp"), None),
        P("section", ("ctx", "fsdp")),
        P("section", ("ctx", "fsdp"), None),
        P("section", "ctx", "fsdp", None),
        P("section", "ctx", "fsdp", None),
    )
    return jax.shard_map(
        shards,
        mesh=mesh,
        in_specs=placed,
        out_specs=(
            P("section", None, "fsdp", "ctx", None),
            P("section", None, "fsdp", "ctx", None),
            P(),
            P("section", ("ctx", "fsdp")),
            P("section", ("ctx", "fsdp"), None),
            P("section", ("ctx", "fsdp"), None),
            P("section", ("ctx", "fsdp"), None),
            P("section", ("ctx", "fsdp")),
            P("section", ("ctx", "fsdp"), None),
            P("section", "ctx", "fsdp", None),
            P("section", "ctx", "fsdp", None),
        ),
        check_vma=False,
    )
```

```python
import functools
import math

import jax
import jax.numpy as jnp
from jax import lax
from jax.experimental import pallas as pl
from jax.experimental.pallas import tpu as pltpu
from jax.sharding import PartitionSpec as P

QH = 16
KVH = 8
HD = 64
EXPERTS = 32
FF_E = 512
TOPK = 8
KW = KVH * HD
EXT = 16

epsilon = 1e-06
rope_base = 10000.0
negative = -1e30
F32 = jnp.float32
BF16 = jnp.bfloat16
VMEM_LIMIT = 60 * 1024 * 1024


def params(grid_dims=0):
    return pltpu.CompilerParams(
        vmem_limit_bytes=VMEM_LIMIT,
        dimension_semantics=("arbitrary",) * grid_dims if grid_dims else None,
    )


def cost(flops, moved, exps=0):
    return pl.CostEstimate(flops=int(flops), bytes_accessed=int(moved), transcendentals=int(exps))


def mm(a, b):
    return jnp.dot(a, b, preferred_element_type=F32)


def mm_nt(a, b):
    return lax.dot_general(a, b, (((1,), (1,)), ((), ())), preferred_element_type=F32)


def mm_tn(a, b):
    return lax.dot_general(a, b, (((0,), (0,)), ((), ())), preferred_element_type=F32)


def fixed(shape):
    return pl.BlockSpec(shape, lambda *_: (0,) * len(shape), pipeline_mode=pl.Buffered(1))


def resident(shape):
    return pl.BlockSpec(shape, lambda *_: (0,) * len(shape))


def lane_index(shape):
    return lax.broadcasted_iota(jnp.int32, shape, len(shape) - 1)


def turn(block, cosine, sine):
    low_half = lane_index(block.shape) % HD < HD // 2
    swapped = jnp.where(
        low_half, pltpu.roll(block, 128 - HD // 2, axis=1), pltpu.roll(block, HD // 2, axis=1)
    )
    return block * cosine + swapped * sine


def rolled(block):
    return pltpu.roll(block.astype(F32), HD, axis=1).astype(BF16)


def key_positions(device, half, devices, shape, dim):
    within = lax.broadcasted_iota(jnp.int32, shape, dim)
    return jnp.where(
        within < half, device * half + within, (2 * devices - 1 - device) * half + within - half
    )


def fill_bias(bias, scal, devices, rows):
    context, length = scal[0], scal[1]
    query_pos = key_positions(context, rows // 2, devices, (rows, rows), 1)
    for k in range(devices):
        key_pos = key_positions(context ^ k, rows // 2, devices, (rows, rows), 0)
        taken = (key_pos <= query_pos) & (key_pos < length)
        bias[k * rows : (k + 1) * rows, :] = jnp.where(taken, 0.0, negative)


def two_heads(block):
    even = lane_index(block.shape) < HD
    zero = jnp.zeros((), block.dtype)
    return jnp.concatenate([jnp.where(even, block, zero), jnp.where(even, zero, block)], axis=0)


def two_heads_doubled(block):
    even = lane_index(block.shape) < HD
    other = rolled(block)
    return jnp.concatenate([jnp.where(even, block, other), jnp.where(even, other, block)], axis=0)


def doubled(block, odd):
    even = lane_index(block.shape) < HD
    other = rolled(block)
    return jnp.where(even, other, block) if odd else jnp.where(even, block, other)


def one_hot(rank_row, slots):
    rows = rank_row.shape[-1]
    index = lax.broadcasted_iota(jnp.int32, (slots, rows), 0).astype(F32)
    return rank_row == index


def project_kernel(x, gain, wq, wm, cosine, sine, q_out, kv_out):
    values = x[...].astype(F32)
    factor = lax.rsqrt(jnp.mean(values * values, axis=-1, keepdims=True) + epsilon)
    normed = (values * factor * gain[...]).astype(BF16)
    cos, sin = cosine[...], sine[...]
    q0 = mm(normed, wq[...])
    for b in range(QH * HD // 128):
        at = slice(b * 128, (b + 1) * 128)
        q_out[:, at] = turn(q0[:, at], cos, sin).astype(BF16)
    kv0 = mm(normed, wm[...])
    for b in range(KW // 128):
        at = slice(b * 128, (b + 1) * 128)
        kv_out[0, :, at] = turn(kv0[:, at], cos, sin).astype(BF16)
    kv_out[1] = kv0[:, KW:].astype(BF16)


def project(x, gain, shared, cosine, sine):
    rows, width = x.shape
    return pl.pallas_call(
        project_kernel,
        name="project",
        grid=(1,),
        in_specs=[
            fixed((rows, width)),
            fixed((1, width)),
            pl.BlockSpec((width, QH * HD), lambda i: (0, 0), pipeline_mode=pl.Buffered(1)),
            pl.BlockSpec((width, 2 * KW), lambda i: (0, 1), pipeline_mode=pl.Buffered(1)),
            fixed((rows, 128)),
            fixed((rows, 128)),
        ],
        out_specs=[resident((rows, QH * HD)), resident((2, rows, KW))],
        out_shape=[
            jax.ShapeDtypeStruct((rows, QH * HD), BF16),
            jax.ShapeDtypeStruct((2, rows, KW), BF16),
        ],
        compiler_params=params(1),
        cost_estimate=cost(2 * rows * width * 2048, 2 * width * 2048 + 8 * rows * width),
    )(x, gain, shared, shared, cosine, sine)


def attend_kernel(devices, scal, x, q, *rest):
    ks, vs, rest = rest[:devices], rest[devices : 2 * devices], rest[2 * devices :]
    wo, gain, router, mask, o_out, lse_out, mid_out, msg_out, bias, held = rest
    rows = x.shape[0]
    step = pl.program_id(0)

    @pl.when(step == 0)
    def _():
        fill_bias(bias, scal, devices, rows)

    keys = jnp.concatenate([r[0] for r in ks], axis=0)
    values = jnp.concatenate([r[0] for r in vs], axis=0)
    block_bias = bias[...]
    both_bias = jnp.concatenate([block_bias, block_bias], axis=1)
    for i in range(2):
        query = two_heads(q[:, i * 128 : (i + 1) * 128])
        scores = mm_nt(doubled(keys, i), query) * (1.0 / math.sqrt(HD)) + both_bias
        top = jnp.max(scores, axis=0, keepdims=True)
        raised = jnp.exp(scores - top)
        total = jnp.sum(raised, axis=0, keepdims=True)
        probs = (raised * (1.0 / total)).astype(BF16)
        lse_out[0, i : i + 1, :] = top + jnp.log(total)
        mixed = mm_tn(values, probs)[i * HD : (i + 1) * HD]
        pair = jnp.concatenate([mixed[:, :rows], mixed[:, rows:]], axis=0)
        at = pl.multiple_of(step * 256 + i * 128, 128)
        held[:, pl.ds(at, 128)] = jnp.transpose(pair).astype(BF16)

    @pl.when(step == pl.num_programs(0) - 1)
    def _():
        attended = held[...]
        o_out[...] = attended
        middle = x[...].astype(F32) + mm(attended, wo[...])
        mid_out[...] = middle
        factor = lax.rsqrt(jnp.mean(middle * middle, axis=-1, keepdims=True) + epsilon)
        normed = (middle * factor * gain[...]).astype(BF16)
        msg_out[:rows, :] = normed
        logits = mm_nt(router[...], normed)
        chosen = mask[...] > 0.5
        top = jnp.max(jnp.where(chosen, logits, negative), axis=0, keepdims=True)
        raised = jnp.where(chosen, jnp.exp(jnp.where(chosen, logits - top, 0.0)), 0.0)
        gates = raised / jnp.sum(raised, axis=0, keepdims=True)
        high = gates.astype(BF16)
        low = (gates - high.astype(F32)).astype(BF16)
        ext = [high[:EXT], high[EXT:], low[:EXT], low[EXT:]]
        if 4 * rows < x.shape[1]:
            ext.append(jnp.zeros((EXT, x.shape[1] - 4 * rows), BF16))
        msg_out[rows:, :] = jnp.concatenate(ext, axis=1)


def attend(scal, x, q, kvs, shared, gain, router, mask):
    rows, width = x.shape
    devices = len(kvs)
    keys = devices * rows
    kv_specs = [pl.BlockSpec((1, rows, 128), lambda h: (0, 0, h)) for _ in kvs] + [
        pl.BlockSpec((1, rows, 128), lambda h: (1, 0, h)) for _ in kvs
    ]
    return pl.pallas_call(
        functools.partial(attend_kernel, devices),
        name="attend",
        grid=(KVH // 2,),
        in_specs=[
            pl.BlockSpec(memory_space=pltpu.SMEM),
            fixed((rows, width)),
            pl.BlockSpec((rows, 256), lambda h: (0, h)),
            *kv_specs,
            pl.BlockSpec((QH * HD, width), lambda h: (0, 2), pipeline_mode=pl.Buffered(1)),
            fixed((1, width)),
            fixed((EXPERTS, width)),
            fixed((EXPERTS, rows)),
        ],
        out_specs=[
            resident((rows, QH * HD)),
            pl.BlockSpec((1, 2, 2 * rows), lambda h: (h, 0, 0)),
            resident((rows, width)),
            resident((rows + EXT, width)),
        ],
        out_shape=[
            jax.ShapeDtypeStruct((rows, QH * HD), BF16),
            jax.ShapeDtypeStruct((KVH // 2, 2, 2 * rows), F32),
            jax.ShapeDtypeStruct((rows, width), F32),
            jax.ShapeDtypeStruct((rows + EXT, width), BF16),
        ],
        scratch_shapes=[pltpu.VMEM((keys, rows), F32), pltpu.VMEM((rows, QH * HD), BF16)],
        compiler_params=params(1),
        cost_estimate=cost(
            4 * rows * keys * QH * HD * 2 + 2 * rows * width * width,
            2 * width * width + 4 * keys * width + 12 * rows * width,
            rows * keys * QH,
        ),
    )(scal, x, q, *kvs, *kvs, shared, gain, router, mask)


def hot_rows(rank, j, slots):
    local = rank.shape[1]
    return jnp.concatenate(
        [
            jnp.where(one_hot(rank[j, i : i + 1, :], slots), 1.0, 0.0).astype(BF16)
            for i in range(local)
        ],
        axis=0,
    )


def combine(rank, held, prior, outs, buffers, slots):
    held = held if isinstance(held, list) else [held]
    prior_buffer, out_buffer, prior_sems, out_sems = buffers
    width = held[0].shape[-1]
    depth = out_buffer.shape[0]
    count = len(outs)
    fetch = lambda j: pltpu.make_async_copy(
        prior[j], prior_buffer.at[j % depth], prior_sems.at[j % depth]
    )
    send = lambda j: pltpu.make_async_copy(
        out_buffer.at[j % depth], outs[j], out_sems.at[j % depth]
    )
    for j in range(min(depth - 1, count) if prior else 0):
        fetch(j).start()
    for j in range(count):
        rows = [part[:, j].reshape(part.shape[0] * slots, width) for part in held]
        rows = rows[0] if len(rows) == 1 else jnp.concatenate(rows, axis=0)
        total = mm_tn(hot_rows(rank, j, slots), rows)
        if prior:
            if j + depth - 1 < count:
                fetch(j + depth - 1).start()
            fetch(j).wait()
            total = total + prior_buffer[j % depth].astype(F32)
        if j >= depth:
            send(j - depth).wait()
        out_buffer[j % depth] = total.astype(BF16)
        send(j).start()
    for j in range(max(0, count - depth), count):
        send(j).wait()


def gate_columns(rank, values, step, sources, slots):
    columns = []
    for j in sources:
        hot = one_hot(rank[j, pl.ds(step, 1), :], slots)
        columns.append(jnp.sum(jnp.where(hot, values(j), 0.0), axis=1, keepdims=True))
    return jnp.concatenate(columns, axis=0)


def finish_kernel(count, *refs):
    terms, (middle, goal, valid, hidden, mixed_out, grad_out, message, error) = (
        refs[:count],
        refs[count:],
    )
    rows, width = middle.shape
    mixed = terms[0][...].astype(F32)
    for term in terms[1:]:
        mixed = mixed + term[...].astype(F32)
    output = middle[...] + mixed
    hidden[...] = output.astype(BF16)
    mixed_out[...] = mixed
    grad = (output - goal[...].astype(F32)) * valid[...]
    grad_out[...] = grad
    error[...] = 0.5 * jnp.sum(
        jnp.sum(grad * grad, axis=1, keepdims=True), axis=0, keepdims=True
    )
    fill_message(message, grad, mixed)


def fill_message(message, grad, mixed):
    rows, width = grad.shape
    message[:rows, :] = grad.astype(BF16)
    inner = jnp.transpose(
        jnp.broadcast_to(jnp.sum(grad * mixed, axis=1, keepdims=True), (rows, 128))
    )[:EXT]
    high = inner.astype(BF16)
    low = (inner - high.astype(F32)).astype(BF16)
    first = lax.broadcasted_iota(jnp.int32, (EXT, rows), 0) == 0
    message[rows:, :rows] = jnp.where(first, high, low)
    message[rows:, rows:] = jnp.zeros((EXT, width - rows), BF16)


def finish(terms, middle, goal, valid):
    rows, width = middle.shape
    return pl.pallas_call(
        functools.partial(finish_kernel, len(terms)),
        name="finish",
        out_shape=[
            jax.ShapeDtypeStruct((rows, width), BF16),
            jax.ShapeDtypeStruct((rows, width), F32),
            jax.ShapeDtypeStruct((rows, width), F32),
            jax.ShapeDtypeStruct((rows + EXT, width), BF16),
            jax.ShapeDtypeStruct((1, 1), F32),
        ],
        compiler_params=params(),
        cost_estimate=cost(8 * rows * width, 24 * rows * width),
    )(*terms, middle, goal, valid)


def message_kernel(grad, mixed, message):
    fill_message(message, grad[...], mixed[...])


def grad_message(grad, mixed):
    rows, width = grad.shape
    return pl.pallas_call(
        message_kernel,
        name="grad_message",
        out_shape=jax.ShapeDtypeStruct((rows + EXT, width), BF16),
        compiler_params=params(),
        cost_estimate=cost(4 * rows * width, 10 * rows * width),
    )(grad, mixed)


def dispatch_kernel(sources, slots, backward, scal, *rest):
    msgs, (rank, x_out, side_out, arrived, picked, in_sems, out_sems) = (
        rest[:sources],
        rest[sources:],
    )
    local, rows = rank.shape[1:]
    fetch = lambda j: pltpu.make_async_copy(msgs[j], arrived.at[j], in_sems.at[j])
    send = lambda j: pltpu.make_async_copy(picked.at[j], x_out.at[:, j], out_sems.at[j])
    for j in range(sources):
        fetch(j).start()
    pick_row = lax.broadcasted_iota(jnp.int32, (EXT, 4 * rows), 0)
    for j in range(sources):
        fetch(j).wait()
        taken = mm(hot_rows(rank, j, slots), arrived[j, :rows, :]).astype(BF16)
        for i in range(local):
            picked[j, i] = taken[i * slots : (i + 1) * slots]
        send(j).start()
        if backward:
            ext = arrived[j, rows:, :rows].astype(F32)
            side_out[j] = ext[0:1, :] + ext[1:2, :]
        else:
            ext = arrived[j, rows:, : 4 * rows].astype(F32)
            for i in range(local):
                expert = scal[0] + i
                row = jnp.sum(jnp.where(pick_row == expert % EXT, ext, 0.0), axis=0, keepdims=True)
                high = jnp.where(expert < EXT, row[:, :rows], row[:, rows : 2 * rows])
                low = jnp.where(expert < EXT, row[:, 2 * rows : 3 * rows], row[:, 3 * rows :])
                side_out[j, i : i + 1, :] = high + low
    for j in range(sources):
        send(j).wait()


def dispatch(scal, msgs, rank, slots, backward):
    sources, local, rows = rank.shape
    width = msgs[0].shape[1]
    anywhere = pl.BlockSpec(memory_space=pl.ANY)
    side = (sources, 1 if backward else local, rows)
    taken, beside = pl.pallas_call(
        functools.partial(dispatch_kernel, sources, slots, backward),
        name="dispatch",
        grid=(1,),
        in_specs=[
            pl.BlockSpec(memory_space=pltpu.SMEM),
            *[anywhere for _ in msgs],
            fixed(rank.shape),
        ],
        out_specs=[anywhere, resident(side)],
        out_shape=[
            jax.ShapeDtypeStruct((local, sources, slots, width), BF16),
            jax.ShapeDtypeStruct(side, F32),
        ],
        scratch_shapes=[
            pltpu.VMEM((sources, rows + EXT, width), BF16),
            pltpu.VMEM((sources, local, slots, width), BF16),
            pltpu.SemaphoreType.DMA((sources,)),
            pltpu.SemaphoreType.DMA((sources,)),
        ],
        compiler_params=params(1),
        cost_estimate=cost(
            2 * local * sources * slots * rows * width, 2 * sources * width * (rows + local * slots)
        ),
    )(scal, *msgs, rank)
    return taken.reshape(local, sources * slots, width), beside


def fill_weights(scal, blocks, w1, w2):
    up = w1.shape[0] // len(blocks)
    down = w2.shape[0] // len(blocks)
    for k, block in enumerate(blocks):
        at = scal[1 + k]
        w1[pl.ds(pl.multiple_of(at * up, up), up), :] = block[0, :up]
        w2[pl.ds(pl.multiple_of(at * down, down), down), :] = block[0, up:]


def experts_kernel(sources, depth, slots, chained, scal, *rest):
    prior = ()
    if chained:
        prior, rest = rest[:sources], rest[sources:]
    rank, gates, xs, rest = *rest[:3], rest[3:]
    blocks, rest = rest[:depth], rest[depth:]
    gu_out, y_out, rest = *rest[:2], rest[2:]
    outs, rest = rest[:sources], rest[sources:]
    held, w1, w2 = rest[:3]
    width = held.shape[-1]
    step, part = pl.program_id(0), pl.program_id(1)
    portions = sources // (xs.shape[1] // slots)
    portion = sources // portions

    @pl.when(part == 0)
    def _():
        fill_weights(scal, blocks, w1, w2)

    gate_up = mm(xs[0], w1[...])
    gu_out[0] = gate_up
    gate, up = gate_up[:, :FF_E], gate_up[:, FF_E:]
    activated = (gate * jax.nn.sigmoid(gate) * up).astype(BF16)
    out = mm(activated, w2[...]).astype(BF16)
    y_out[0] = out
    column = gate_columns(
        rank,
        lambda j: gates[j, pl.ds(step, 1), :],
        step,
        [part * portion + n for n in range(portion)],
        slots,
    )
    held[step, pl.ds(part * portion, portion)] = (
        (column * out.astype(F32)).astype(BF16).reshape(portion, slots, width)
    )

    @pl.when((step == pl.num_programs(0) - 1) & (part == portions - 1))
    def _():
        combine(rank, held, prior, outs, rest[3:], slots)


def weight_specs(blocks, depth):
    arrays = blocks if len(blocks) == depth else blocks * depth
    rows = arrays[0].shape[1] // (depth // len(blocks))
    width = arrays[0].shape[2]
    specs = [
        pl.BlockSpec((1, rows, width), lambda e, r, f=(k if len(blocks) == 1 else 0): (e, f, 0))
        for k in range(depth)
    ]
    return arrays, specs


def stream_scratch(rows, width):
    return [
        pltpu.VMEM((4, rows, width), BF16),
        pltpu.VMEM((4, rows, width), BF16),
        pltpu.SemaphoreType.DMA((4,)),
        pltpu.SemaphoreType.DMA((4,)),
    ]


def experts_forward(scal, xs, rank, gates, blocks, depth, slots, first, prior=()):
    sources, local, rows = rank.shape
    width = xs.shape[2]
    portions = max(1, sources // 8)
    count = sources * slots
    arrays, specs = weight_specs(blocks, depth)
    anywhere = pl.BlockSpec(memory_space=pl.ANY)
    each = lambda shape, base=0: pl.BlockSpec((1,) + shape, lambda e, r: (e + base, r, 0))
    outs = pl.pallas_call(
        functools.partial(experts_kernel, sources, depth, slots, bool(prior)),
        name="experts_forward",
        grid=(local, portions),
        in_specs=[
            pl.BlockSpec(memory_space=pltpu.SMEM),
            *[anywhere for _ in prior],
            fixed((sources, local, rows)),
            fixed((sources, local, rows)),
            each((count // portions, width), first),
            *specs,
        ],
        out_specs=[
            each((count // portions, 2 * FF_E)),
            each((count // portions, width)),
            *[anywhere for _ in range(sources)],
        ],
        out_shape=[
            jax.ShapeDtypeStruct((local, count, 2 * FF_E), F32),
            jax.ShapeDtypeStruct((local, count, width), BF16),
            *[jax.ShapeDtypeStruct((rows, width), BF16) for _ in range(sources)],
        ],
        scratch_shapes=[
            pltpu.VMEM((local, sources, slots, width), BF16),
            pltpu.VMEM((width, 2 * FF_E), BF16),
            pltpu.VMEM((FF_E, width), BF16),
            *stream_scratch(rows, width),
        ],
        compiler_params=params(2),
        cost_estimate=cost(
            2 * local * count * width * 3 * FF_E * 1.3, 8 * local * count * width, local * count * FF_E
        ),
    )(scal, *prior, rank, gates, xs, *arrays)
    return outs[:2], list(outs[2:])


def experts_back_kernel(sources, depth, slots, mode, scal, *rest):
    last, order = mode
    earlier = ()
    if last:
        full_rank, rest = rest[0], rest[1:]
        earlier, rest = rest[: len(order) - 1], rest[len(order) - 1 :]
    rank, gates, inners, grads, xs, gu, ys, router, rest = *rest[:8], rest[8:]
    blocks, rest = rest[:depth], rest[depth:]
    grad_out_ref, router_out, rest = *rest[:2], rest[2:]
    outs, rest = (rest[:sources], rest[sources:]) if last else (rest[:1], rest[1:])
    held, w1, w2, sum1, sum2 = rest[:5]
    width = w1.shape[0]
    step, part = pl.program_id(0), pl.program_id(1)
    portions = sources // (xs.shape[1] // slots)
    portion = sources // portions

    @pl.when(part == 0)
    def _():
        fill_weights(scal, blocks, w1, w2)

    mine = [part * portion + n for n in range(portion)]
    gate_column = gate_columns(rank, lambda j: gates[j, pl.ds(step, 1), :], step, mine, slots)
    inner_column = gate_columns(rank, lambda j: inners[j], step, mine, slots)
    grad_out = grads[0].astype(F32)
    grad_y = (gate_column * grad_out).astype(BF16)
    given = jnp.sum(grad_out * ys[0].astype(F32), axis=1, keepdims=True)
    grad_logit = gate_column * (given - inner_column)
    gate, up = gu[0, :, :FF_E], gu[0, :, FF_E:]
    sigmoid = jax.nn.sigmoid(gate)
    silu = gate * sigmoid
    activated = (silu * up).astype(BF16)
    down_part = mm_tn(activated, grad_y)
    grad_act = mm_nt(grad_y, w2[...])
    grad_gate = grad_act * up * sigmoid * (1.0 + gate * (1.0 - sigmoid))
    grad_up = grad_act * silu
    grad_gate_up = jnp.concatenate([grad_gate.astype(BF16), grad_up.astype(BF16)], axis=1)
    taken = xs[0]
    up_part = mm_tn(taken, grad_gate_up)
    router_part = jnp.sum(taken.astype(F32) * grad_logit, axis=0, keepdims=True)
    grad_rows = mm_nt(grad_gate_up, w1[...]) + grad_logit * router[0]
    if last:
        held[step, pl.ds(part * portion, portion)] = grad_rows.astype(BF16).reshape(
            portion, slots, width
        )
    else:
        outs[0][0] = grad_rows.astype(BF16)

    def write(up_total, down_total):
        up_rows, down_rows = width // depth, FF_E // depth
        for f in range(depth):
            top = f * (up_rows + down_rows)
            grad_out_ref[0, top : top + up_rows, :] = up_total[
                f * up_rows : (f + 1) * up_rows
            ].astype(BF16)
            grad_out_ref[0, top + up_rows : top + up_rows + down_rows, :] = down_total[
                f * down_rows : (f + 1) * down_rows
            ].astype(BF16)

    if sum1 is None:
        write(up_part, down_part)
        router_out[0] = router_part
    else:

        @pl.when(part == 0)
        def _():
            sum1[...] = up_part
            sum2[...] = down_part
            router_out[0] = router_part

        @pl.when(part > 0)
        def _():
            sum1[...] += up_part
            sum2[...] += down_part
            router_out[0] += router_part

        @pl.when(part == portions - 1)
        def _():
            write(sum1, sum2)

    if last:

        @pl.when((step == pl.num_programs(0) - 1) & (part == portions - 1))
        def _():
            pieces = list(earlier) + [held]
            combine(full_rank, [pieces[o] for o in order], (), outs, rest[5:], slots)


def experts_backward(
    scal, grads, rank, gates, inners, xs, kept, router, blocks, depth, slots, first, last
):
    sources, local, rows = rank.shape
    width = xs.shape[2]
    portions = max(1, sources // 8)
    count = sources * slots
    gu, ys = kept
    arrays, specs = weight_specs(blocks, depth)
    merged = width + FF_E
    anywhere = pl.BlockSpec(memory_space=pl.ANY)
    each = lambda shape, base=0: pl.BlockSpec((1,) + shape, lambda e, r: (e + base, r, 0))
    whole = lambda shape: pl.BlockSpec((1,) + shape, lambda e, r: (e, 0, 0))
    before = []
    if last:
        before = [last[0]] + [
            part.reshape(part.shape[0], sources, slots, width) for part in last[1]
        ]
    mode = (bool(last), last[2] if last else ())

    def kernel(*refs):
        refs = list(refs)
        if portions == 1:
            at = len(refs) - (4 if last else 0)
            refs[at:at] = [None, None]
        if not last:
            refs[-4:-4] = [None]
        experts_back_kernel(sources, depth, slots, mode, *refs)

    sums = [pltpu.VMEM((width, 2 * FF_E), F32), pltpu.VMEM((FF_E, width), F32)]
    outs = pl.pallas_call(
        kernel,
        name="experts_backward",
        grid=(local, portions),
        in_specs=[
            pl.BlockSpec(memory_space=pltpu.SMEM),
            *[fixed(part.shape) for part in before],
            fixed((sources, local, rows)),
            fixed((sources, local, rows)),
            fixed((sources, 1, rows)),
            each((count // portions, width)),
            each((count // portions, width), first),
            each((count // portions, 2 * FF_E)),
            each((count // portions, width)),
            whole((1, width)),
            *specs,
        ],
        out_specs=[
            whole((merged, width)),
            whole((1, width)),
            *([anywhere] * sources if last else [each((count // portions, width))]),
        ],
        out_shape=[
            jax.ShapeDtypeStruct((local, merged, width), BF16),
            jax.ShapeDtypeStruct((local, 1, width), F32),
            *(
                [jax.ShapeDtypeStruct((rows, width), BF16)] * sources
                if last
                else [jax.ShapeDtypeStruct((local, count, width), BF16)]
            ),
        ],
        scratch_shapes=[
            *([pltpu.VMEM((local, sources, slots, width), BF16)] if last else []),
            pltpu.VMEM((width, 2 * FF_E), BF16),
            pltpu.VMEM((FF_E, width), BF16),
            *(sums if portions > 1 else []),
            *(stream_scratch(rows, width) if last else []),
        ],
        compiler_params=params(2),
        cost_estimate=cost(
            2 * local * count * width * 3 * FF_E * 2.3, 14 * local * count * width, local * count * FF_E
        ),
    )(scal, *before, rank, gates, inners, grads, xs, gu, ys, router, *arrays)
    return outs[0], outs[1], list(outs[2:])


def place_base(place, scal):
    return jnp.where(scal[1] == 0, place[1], place[2])


def place_kernel(places, number, aliased, scal, *refs):
    parts, (up_out, down_out) = refs[: -2 - aliased], refs[-2:]
    step = number(pl.program_id(0))
    up_rows = up_out.shape[1]

    def put(blocks):
        total = blocks[0][0].astype(F32)
        for block in blocks[1:]:
            total = total + block[0].astype(F32)
        up_out[0] = total[:up_rows]
        down_out[0] = total[up_rows:]

    at = 0
    for place in places:
        base, count, terms = place_base(place, scal), place[3], place[4]
        pl.when((scal[0] == place[0]) & (step >= base) & (step < base + count))(
            functools.partial(put, parts[at : at + terms])
        )
        at += terms


def place_experts(scal, pieces, held_experts, up_rows, experts, into=()):
    rows, width = pieces[0][3][0].shape[1:]
    places, specs, arrays = [], [], []
    run = next((i for i in range(1, len(experts)) if experts[i] != experts[0] + i), len(experts))
    skip = experts[run] - experts[run - 1] if run < len(experts) else 1
    number = lambda i: experts[0] + (i // run) * (run - 1 + skip) + i % run
    assert [number(i) for i in range(len(experts))] == list(experts)
    for core, even_base, odd_base, terms in pieces:
        place = (core, even_base, odd_base, terms[0].shape[0], len(terms))
        places.append(place)
        for term in terms:
            arrays.append(term)
            specs.append(
                pl.BlockSpec(
                    (1, rows, width),
                    lambda i, scal, place=place: (
                        jnp.clip(number(i) - place_base(place, scal), 0, place[3] - 1),
                        0,
                        0,
                    ),
                )
            )
    specs += [pl.BlockSpec(memory_space=pl.ANY) for _ in into]
    return pl.pallas_call(
        functools.partial(place_kernel, places, number, len(into)),
        name="place_experts",
        grid_spec=pltpu.PrefetchScalarGridSpec(
            num_scalar_prefetch=1,
            grid=(len(experts),),
            in_specs=specs,
            out_specs=[
                pl.BlockSpec((1, up_rows, width), lambda i, scal: (number(i), 0, 0)),
                pl.BlockSpec((1, rows - up_rows, width), lambda i, scal: (number(i), 0, 0)),
            ],
        ),
        out_shape=[
            jax.ShapeDtypeStruct((held_experts, up_rows, width), F32),
            jax.ShapeDtypeStruct((held_experts, rows - up_rows, width), F32),
        ],
        input_output_aliases={1 + len(arrays) + i: i for i in range(len(into))},
        compiler_params=params(1),
        cost_estimate=cost(0, 8 * len(experts) * rows * width),
    )(scal, *arrays, *into)


def assemble_kernel(devices, depth, scal, *refs):
    owns, others, whole, sem = refs[:devices], refs[devices : 2 * devices], refs[-2], refs[-1]
    piece = whole.shape[0] // (devices * depth)
    for home, blocks in ((1, owns), (0, others)):

        @pl.when(scal[0] == home)
        def _(blocks=blocks):
            for k in range(devices):
                for i in range(depth):
                    to = pl.multiple_of(((scal[1] ^ k) * depth + (scal[2] ^ i)) * piece, piece)
                    pltpu.make_async_copy(
                        blocks[k].at[pl.ds(i * piece, piece)], whole.at[pl.ds(to, piece)], sem
                    ).start()
            pltpu.make_async_copy(whole, whole, sem).wait()


def assemble(scal, owns, others, depth):
    devices = len(owns)
    rows, columns = owns[0].shape
    return pl.pallas_call(
        functools.partial(assemble_kernel, devices, depth),
        name="assemble",
        in_specs=[pl.BlockSpec(memory_space=pltpu.SMEM)]
        + [pl.BlockSpec(memory_space=pl.ANY)] * (2 * devices),
        out_specs=pl.BlockSpec(memory_space=pltpu.VMEM),
        out_shape=jax.ShapeDtypeStruct((rows * devices, columns), owns[0].dtype),
        scratch_shapes=[pltpu.SemaphoreType.DMA(())],
        compiler_params=params(),
        cost_estimate=cost(0, 4 * rows * devices * columns),
    )(scal, *owns, *others)


def attend_back_kernel(devices, arrived, scal, *rest):
    parts, rest = rest[:arrived], rest[arrived:]
    grad_out, middle, gain, attended, wo, q, lse, cosine, sine, x, gain_first = rest[:11]
    ks, vs, rest = rest[11 : 11 + devices], rest[11 + devices : 11 + 2 * devices], rest[11 + 2 * devices :]
    mid_out, weight_grads, gain_grad, dq_out = rest[:4]
    dkv_outs, (bias, held) = rest[4 : 4 + devices], rest[4 + devices :]
    width = middle.shape[1]
    rows = middle.shape[0]
    scale = 1.0 / math.sqrt(HD)
    step = pl.program_id(0)

    @pl.when(step == 0)
    def _():
        fill_bias(bias, scal, devices, rows)
        grad_mix = parts[0][...].astype(F32)
        for part in parts[1:]:
            grad_mix = grad_mix + part[...].astype(F32)
        mid = middle[...]
        factor = lax.rsqrt(jnp.mean(mid * mid, axis=-1, keepdims=True) + epsilon)
        scaled = grad_mix * gain[...]
        inner = jnp.mean(mid * scaled, axis=-1, keepdims=True)
        gain_grad[...] = jnp.sum(grad_mix * mid * factor, axis=0, keepdims=True)
        grad_mid = grad_out[...] + factor * scaled - mid * (factor * factor * factor * inner)
        mid_out[...] = grad_mid
        branch = grad_mid.astype(BF16)
        weight_grads[:, :width] = mm_tn(attended[...], branch).astype(BF16)
        held[...] = mm_nt(branch, wo[...]).astype(BF16)

    keys = jnp.concatenate([r[0] for r in ks], axis=0)
    values = jnp.concatenate([r[0] for r in vs], axis=0)
    block_bias = bias[...]
    both_bias = jnp.concatenate([block_bias, block_bias], axis=1)
    key_parts, value_parts = [], []
    for i in range(2):
        block = q[:, i * 128 : (i + 1) * 128]
        at = pl.multiple_of(step * 256 + i * 128, 128)
        grads = held[:, pl.ds(at, 128)]
        scores = mm_nt(doubled(keys, i), two_heads(block)) * scale + both_bias
        probs = jnp.exp(scores - lse[0, i : i + 1, :])
        grad_probs = mm_nt(doubled(values, i), two_heads(grads))
        product = probs * grad_probs
        dots = jnp.sum(product, axis=0, keepdims=True)
        grad_scores = (product - probs * dots).astype(BF16)
        key_parts.append(mm(grad_scores, two_heads_doubled(block)) * scale)
        value_parts.append(mm(probs.astype(BF16), two_heads_doubled(grads)))
        moved = mm_tn(keys, grad_scores)[i * HD : (i + 1) * HD] * scale
        pair = jnp.concatenate([moved[:, :rows], moved[:, rows:]], axis=0)
        dq_out[:, pl.ds(at, 128)] = turn(jnp.transpose(pair), cosine[...], sine[...]).astype(BF16)
    even = lane_index(key_parts[0].shape) < HD
    grad_keys = jnp.where(even, key_parts[0], key_parts[1]).astype(BF16)
    grad_values = jnp.where(even, value_parts[0], value_parts[1]).astype(BF16)
    for k in range(devices):
        dkv_outs[k][0] = grad_keys[k * rows : (k + 1) * rows]
        dkv_outs[k][1] = grad_values[k * rows : (k + 1) * rows]

    @pl.when(step == pl.num_programs(0) - 1)
    def _():
        values = x[...].astype(F32)
        factor = lax.rsqrt(jnp.mean(values * values, axis=-1, keepdims=True) + epsilon)
        normed = (values * factor * gain_first[...]).astype(BF16)
        weight_grads[:, width:] = mm_tn(normed, dq_out[...]).astype(BF16)


def attend_backward(
    scal, parts, grad_out, middle, gain, attended, shared, q, lse, cosine, sine, x, gain_first, kvs
):
    rows, width = middle.shape
    devices = len(kvs)
    keys = devices * rows
    kv_specs = [pl.BlockSpec((1, rows, 128), lambda h: (0, 0, h)) for _ in kvs] + [
        pl.BlockSpec((1, rows, 128), lambda h: (1, 0, h)) for _ in kvs
    ]
    return pl.pallas_call(
        functools.partial(attend_back_kernel, devices, len(parts)),
        name="attend_backward",
        grid=(KVH // 2,),
        in_specs=[
            pl.BlockSpec(memory_space=pltpu.SMEM),
            *[fixed((rows, width)) for _ in parts],
            fixed((rows, width)),
            fixed((rows, width)),
            fixed((1, width)),
            fixed((rows, QH * HD)),
            pl.BlockSpec((QH * HD, width), lambda h: (0, 2), pipeline_mode=pl.Buffered(1)),
            pl.BlockSpec((rows, 256), lambda h: (0, h)),
            pl.BlockSpec((1, 2, 2 * rows), lambda h: (h, 0, 0)),
            fixed((rows, 128)),
            fixed((rows, 128)),
            fixed((rows, width)),
            fixed((1, width)),
            *kv_specs,
        ],
        out_specs=[
            resident((rows, width)),
            resident((width, width + QH * HD)),
            resident((1, width)),
            resident((rows, QH * HD)),
            *[pl.BlockSpec((2, rows, 128), lambda h: (0, 0, h)) for _ in kvs],
        ],
        out_shape=[
            jax.ShapeDtypeStruct((rows, width), F32),
            jax.ShapeDtypeStruct((width, width + QH * HD), BF16),
            jax.ShapeDtypeStruct((1, width), F32),
            jax.ShapeDtypeStruct((rows, QH * HD), BF16),
            *[jax.ShapeDtypeStruct((2, rows, KW), BF16) for _ in kvs],
        ],
        scratch_shapes=[pltpu.VMEM((keys, rows), F32), pltpu.VMEM((rows, QH * HD), BF16)],
        compiler_params=params(1),
        cost_estimate=cost(
            10 * rows * keys * QH * HD * 2 + 4 * rows * width * width,
            6 * width * width + 8 * keys * width + 20 * rows * width,
            rows * keys * QH,
        ),
    )(
        scal,
        *parts,
        grad_out,
        middle,
        gain,
        attended,
        shared,
        q,
        lse,
        cosine,
        sine,
        x,
        gain_first,
        *kvs,
        *kvs,
    )


def project_back_kernel(devices, x, gain, dq, *rest):
    parts, rest = rest[:devices], rest[devices:]
    grad_mid, wq, wm, cosine, sine, small, dx_out, packed = rest
    values = x[...].astype(F32)
    width = values.shape[1]
    factor = lax.rsqrt(jnp.mean(values * values, axis=-1, keepdims=True) + epsilon)
    normed = (values * factor * gain[...]).astype(BF16)
    summed = parts[0][...].astype(F32)
    for part in parts[1:]:
        summed = summed + part[...].astype(F32)
    grad_keys = [
        turn(summed[0, :, b * 128 : (b + 1) * 128], cosine[...], sine[...]).astype(BF16)
        for b in range(KW // 128)
    ]
    grad_memory = jnp.concatenate(grad_keys + [summed[1].astype(BF16)], axis=1)
    grad_query = dq[...]
    packed[:, : 2 * KW] = mm_tn(normed, grad_memory).astype(BF16)
    grad_normed = mm_nt(grad_query, wq[...]) + mm_nt(grad_memory, wm[...])
    scaled = grad_normed * gain[...]
    inner = jnp.mean(values * scaled, axis=-1, keepdims=True)
    gain_grad = jnp.sum(grad_normed * values * factor, axis=0, keepdims=True)
    row = lax.broadcasted_iota(jnp.int32, (128, width), 0)
    packed[:, 2 * KW :] = jnp.transpose(
        jnp.where(row == EXPERTS, gain_grad, small[...])
    ).astype(BF16)
    dx_out[...] = (
        grad_mid[...] + factor * scaled - values * (factor * factor * factor * inner)
    )


def project_backward(x, gain, dq, parts, grad_mid, shared, cosine, sine, small):
    rows, width = x.shape
    columns = 2 * KW + 128
    return pl.pallas_call(
        functools.partial(project_back_kernel, len(parts)),
        name="project_backward",
        grid=(1,),
        in_specs=[
            fixed((rows, width)),
            fixed((1, width)),
            fixed((rows, QH * HD)),
            *[fixed((2, rows, KW)) for _ in parts],
            fixed((rows, width)),
            pl.BlockSpec((width, QH * HD), lambda i: (0, 0), pipeline_mode=pl.Buffered(1)),
            pl.BlockSpec((width, 2 * KW), lambda i: (0, 1), pipeline_mode=pl.Buffered(1)),
            fixed((rows, 128)),
            fixed((rows, 128)),
            fixed((128, width)),
        ],
        out_specs=[resident((rows, width)), resident((width, columns))],
        out_shape=[
            jax.ShapeDtypeStruct((rows, width), F32),
            jax.ShapeDtypeStruct((width, columns), BF16),
        ],
        compiler_params=params(1),
        cost_estimate=cost(8 * rows * width * 2048, 8 * width * 2048 + 16 * rows * width),
    )(x, gain, dq, *parts, grad_mid, shared, shared, cosine, sine, small)


def pairs_within(axis, by, sections=(0, 1)):
    count = lax.axis_size(axis)
    return [(s * count + i, s * count + (i ^ by)) for s in sections for i in range(count)]


def exchanged(value, axis, by, sections=(0, 1)):
    return lax.ppermute(value, ("section", axis), pairs_within(axis, by, sections))


def swapped(value):
    return lax.ppermute(value, "section", [(0, 1), (1, 0)])


def from_all(value, axis, sections=(0, 1)):
    count = lax.axis_size(axis)
    return [value] + [exchanged(value, axis, k, sections) for k in range(1, count)]


def after(value, other):
    return lax.optimization_barrier((value, other))[0]


def scattered_sum(blocks, axis, sections):
    total = blocks[0].astype(F32)
    for k in range(1, len(blocks)):
        total = total + exchanged(blocks[k], axis, k, sections).astype(F32)
    return total


def shards(
    tokens,
    targets,
    lengths,
    routes,
    attention_gain,
    query_weight,
    memory_weight,
    output_weight,
    mixture_gain,
    router_weight,
    gate_up_weight,
    down_weight,
):
    section = lax.axis_index("section")
    context = lax.axis_index("ctx")
    line = lax.axis_index("fsdp")
    devices = lax.axis_size("ctx")
    depth = lax.axis_size("fsdp")
    first_core = section == 0
    rows, width = tokens.shape[2:]
    layers = 2
    held_experts = gate_up_weight.shape[1]
    half_held = held_experts // 2
    quarter = held_experts // 4
    side = line % 2
    alternate = [list(range(parity, depth, 2)) for parity in range(2)]
    paired = False
    capacity = rows * TOPK * 9 // (EXPERTS * 8)
    slots = -(-capacity // 16) * 16
    up_rows, down_rows = gate_up_weight.shape[2], down_weight.shape[2]
    shard_rows = up_rows + down_rows

    column = context * held_experts
    plain = (column + section * half_held, half_held, 2 * devices)
    pair = (column + side * half_held + section * quarter, quarter, 4 * devices)
    places = [pair if paired else plain, plain]

    pack = jnp.concatenate(
        [
            query_weight[0],
            memory_weight[0],
            output_weight[0],
            router_weight[0],
            attention_gain[0][:, None],
            mixture_gain[0][:, None],
            jnp.zeros((query_weight.shape[1], 128 - EXPERTS - 2), BF16),
        ],
        axis=1,
    )

    def shared_of_line(layer, ahead):
        mine = pack if ahead is None else after(pack, ahead)
        return jnp.concatenate(from_all(mine, "fsdp", (layer,)), axis=0)

    def shared_of_plane(layer, block, ahead):
        mine = block if ahead is None else after(block, ahead)
        owns = from_all(mine, "ctx", (layer,))
        others = [lax.ppermute(own, "section", [(layer, 1 - layer)]) for own in owns]
        scal = jnp.stack([(section == layer).astype(jnp.int32), context, line])
        whole = assemble(scal, owns, others, depth)
        small = whole[:, 3 * width :].T
        return (
            whole,
            small[:EXPERTS],
            small[EXPERTS : EXPERTS + 1].astype(F32),
            small[EXPERTS + 1 : EXPERTS + 2].astype(F32),
        )

    my_routes = jnp.swapaxes(routes[0, :, 0], 1, 2)
    other_routes = swapped(my_routes)
    layer_routes = jnp.where(
        first_core,
        jnp.stack([my_routes, other_routes]),
        jnp.stack([other_routes, my_routes])[:, ::-1],
    )
    all_routes = jnp.stack(from_all(layer_routes, "ctx"), axis=2).reshape(
        layers, 2 * devices, TOPK, rows
    )
    source_routes = [all_routes[0], all_routes[1]]
    if paired:
        source_routes[0] = jnp.concatenate(
            [all_routes[0], exchanged(all_routes[0], "fsdp", 1)], axis=0
        )
    earlier = (
        lax.broadcasted_iota(jnp.int32, (rows, rows), 0)
        < lax.broadcasted_iota(jnp.int32, (rows, rows), 1)
    ).astype(BF16)

    def ranked(layer):
        first, local, _ = places[layer]
        ids = first + jnp.arange(local, dtype=jnp.int32)
        named = jnp.any(source_routes[layer][:, None] == ids[None, :, None, None], axis=2)
        before = jnp.dot(
            named.astype(BF16).reshape(-1, rows), earlier, preferred_element_type=F32
        ).reshape(named.shape)
        return jnp.where(named, before, -1.0)

    ranks = [ranked(layer) for layer in range(layers)]
    masks = jnp.any(
        layer_routes[:, 0, None] == jnp.arange(EXPERTS, dtype=jnp.int32)[None, :, None, None], axis=2
    ).astype(F32)

    line_blocks = [after(shared_of_line(0, None), (ranks, masks)), None]

    merged = jnp.concatenate([gate_up_weight[0], down_weight[0]], axis=1)
    if paired:
        taken = lambda parity, core: lax.dynamic_slice_in_dim(
            merged, parity * half_held + core * quarter, quarter, 0
        )
        arrived = swapped(
            jnp.where(
                first_core,
                jnp.concatenate([taken(side, 1), taken(1 - side, 1)], axis=0),
                merged[:half_held],
            )
        )
        same = jnp.where(first_core, taken(side, 0), arrived[:quarter])
        differ = jnp.where(first_core, taken(1 - side, 0), arrived[quarter:])
        late = jnp.where(first_core, arrived, merged[half_held:])
        early = None
    else:
        mine = lax.dynamic_slice_in_dim(merged, section * half_held, half_held, 0)
        arrived = swapped(
            lax.dynamic_slice_in_dim(merged, (1 - section) * half_held, half_held, 0)
        )
        early = jnp.where(first_core, mine, arrived)
        late = jnp.where(first_core, arrived, mine)

    split = [(0, half_held - 1), (half_held - 1, 1)] if half_held > 1 else [(0, half_held)]
    runs = [[(0, quarter)] if paired else split, split]
    gathered_experts = lambda shard: [
        [lax.all_gather(shard[a : a + n], "fsdp", axis=1, tiled=True)] for a, n in split
    ]

    half = rows // 2
    within = jnp.arange(rows, dtype=jnp.int32)
    positions = jnp.where(
        within < half, context * half + within, (2 * devices - 1 - context) * half + within - half
    )
    inverse = rope_base ** (-2.0 * jnp.arange(HD // 2, dtype=F32) / HD)
    angles = positions.astype(F32)[:, None] * inverse[None, :]
    sine, cosine = jnp.sin(angles), jnp.cos(angles)
    cos_table = jnp.concatenate([cosine] * 4, axis=1)
    sin_table = jnp.concatenate([-sine, sine, -sine, sine], axis=1)
    length = lengths[section, line]
    attend_scalars = jnp.stack([context, length]).astype(jnp.int32)

    def dispatched(message, wide):
        plane = from_all(message, "ctx")
        blocks = plane + [swapped(block) for block in plane]
        if wide:
            blocks = blocks + dispatched(exchanged(message, "fsdp", 1), False)
        return blocks

    def returned(outs):
        terms = []
        if len(outs) > 2 * devices:
            far = returned(outs[2 * devices :])
            total = functools.reduce(lambda a, b: a + b, [t.astype(F32) for t in far])
            terms = [exchanged(total.astype(BF16), "fsdp", 1)]
        own, other = outs[:devices], outs[devices : 2 * devices]
        crossed = [swapped(block) for block in other]
        near = [own[0], crossed[0]]
        for k in range(1, devices):
            chip = (own[k].astype(F32) + crossed[k].astype(F32)).astype(BF16)
            near.append(exchanged(chip, "ctx", k))
        return near + terms

    my_targets = lax.dynamic_index_in_dim(targets[:, 0], section, 0, keepdims=False)
    layer_input = lax.dynamic_index_in_dim(tokens[:, 0], section, 0, keepdims=False)
    valid = (positions < length).astype(F32)[:, None]
    saved, hidden = [], []
    if paired:
        arrived = exchanged(differ, "fsdp", 1)
        both = jnp.where(
            side == 0,
            jnp.concatenate([same, arrived], axis=1),
            jnp.concatenate([arrived, same], axis=1),
        )
        early_experts = [
            [
                lax.all_gather(
                    both, "fsdp", axis=1, tiled=True, axis_index_groups=alternate
                )
            ]
        ]
    else:
        early_experts = gathered_experts(early)
    ahead = None
    for layer in range(layers):
        first, local, sources = places[layer]
        shared, router, gain_first, gain_second = shared_of_plane(
            layer, line_blocks[layer], ahead
        )
        wide = sources > 2 * devices
        q, kv = project(layer_input, gain_first, shared, cos_table, sin_table)
        if layer == 0:
            line_blocks[1] = shared_of_line(1, kv)
        kvs = from_all(kv, "ctx")
        attended, lse, middle, message = attend(
            attend_scalars, layer_input, q, kvs, shared, gain_second, router, masks[layer]
        )
        messages = dispatched(message, sources > 2 * devices)
        if layer == 0:
            ahead = messages
            weights = early_experts
            late_experts = gathered_experts(after(late, message))
        else:
            weights = late_experts
        kept, outs = [], ()
        xs, gates = dispatch(
            first.astype(jnp.int32).reshape(1), messages, ranks[layer], slots, False
        )
        for (a, n), blocks in zip(runs[layer], weights):
            order = [line ^ k for k in range(depth)] if len(blocks) > 1 else range(depth)
            scal = jnp.stack([first + a, *[jnp.asarray(o) for o in order]]).astype(jnp.int32)
            run, outs = experts_forward(
                scal,
                xs,
                ranks[layer][:, a : a + n],
                gates[:, a : a + n],
                blocks,
                depth,
                slots,
                a,
                outs,
            )
            kept.append((scal, run, blocks))
        if layer == layers - 1:
            hidden_rows, mixed, grad_output, message, error = finish(
                returned(outs), middle, my_targets, valid
            )
            hidden.append(hidden_rows)
        else:
            mixed = functools.reduce(lambda a, b: a + b, [t.astype(F32) for t in returned(outs)])
            hidden.append((middle + mixed).astype(BF16))
        saved.append(
            dict(
                x=layer_input,
                shared=shared,
                router=router,
                gain_first=gain_first,
                gain_second=gain_second,
                q=q,
                kvs=kvs,
                attended=attended,
                lse=lse,
                middle=middle,
                kept=kept,
                xs=xs,
                gates=gates,
                mixed=mixed,
            )
        )
        layer_input = hidden[-1]

    error = error[0, 0]
    for axis in ("section", "ctx", "fsdp"):
        by = 1
        while by < lax.axis_size(axis):
            error = error + lax.ppermute(
                error, axis, [(i, i ^ by) for i in range(lax.axis_size(axis))]
            )
            by *= 2
    loss_value = error / jnp.sum(lengths).astype(F32)

    def home_blocks(packed, layer):
        arrived = lax.ppermute(packed, "section", [(1 - layer, layer)])
        size = packed.shape[0] // devices
        return [
            (
                lax.dynamic_slice_in_dim(packed, (context ^ k) * size, size, 0).astype(F32)
                + lax.dynamic_slice_in_dim(arrived, (context ^ k) * size, size, 0).astype(F32)
            ).astype(BF16)
            for k in range(devices)
        ]

    def home_plane(blocks, layer):
        return scattered_sum(blocks, "ctx", (layer,)).astype(BF16)

    def home_line(plane, layer):
        size = plane.shape[0] // depth
        return scattered_sum(
            [
                lax.dynamic_slice_in_dim(plane, (line ^ k) * size, size, 0)
                for k in range(depth)
            ],
            "fsdp",
            (layer,),
        )

    def placed_rows(values):
        home = jnp.where(first_core, values[0], values[1])
        arrived = swapped(jnp.where(first_core, values[1], values[0]))
        return jnp.stack(
            [jnp.where(first_core, home, arrived), jnp.where(first_core, arrived, home)]
        )

    hidden_out = placed_rows(hidden)
    input_grads, expert_grads = [None] * layers, [None] * layers
    shared_grads = [None] * layers
    waiting = None
    summed = {}
    for layer in reversed(range(layers)):
        held = saved[layer]
        first, local, sources = places[layer]
        wide = sources > 2 * devices
        if layer < layers - 1:
            message = grad_message(grad_output, held["mixed"])
        messages = dispatched(message, sources > 2 * devices)
        if waiting is not None:
            blocks_1 = [home_blocks(part, 1) for part in waiting]
            messages = after(messages, blocks_1)
            blocks_1 = after(blocks_1, messages)
            planes = [home_plane(blocks, 1) for blocks in blocks_1]
        own_router = lax.dynamic_slice_in_dim(held["router"], first, local, 0).astype(F32)
        small = jnp.zeros((128, width), F32)
        outs = ()
        gathered = []
        steps = list(zip(runs[layer], held["kept"]))
        if layer == 1:
            steps = steps[::-1]
        spans = [a for (a, _), _ in steps]
        for at, ((a, n), (scal, run, blocks)) in enumerate(steps):
            last = None
            if at == len(steps) - 1:
                order = tuple(sorted(range(len(spans)), key=lambda i: spans[i]))
                last = (ranks[layer], [rows_of for rows_of in outs], order)
            grad_rows, inners = dispatch(
                scal[:1], messages, ranks[layer][:, a : a + n], slots, True
            )
            grads, router_grad, rows_out = experts_backward(
                scal,
                grad_rows,
                ranks[layer][:, a : a + n],
                held["gates"][:, a : a + n],
                inners,
                held["xs"],
                run,
                own_router[a : a + n, None, :],
                blocks,
                depth,
                slots,
                a,
                last,
            )
            outs = rows_out if last else list(outs) + rows_out
            small = lax.dynamic_update_slice_in_dim(small, router_grad[:, 0], first + a, 0)
            gathered.append(grads)
        if wide:
            pieces = []
            for at in range(quarter):
                pair_sum = lax.psum_scatter(
                    gathered[0][at : at + 1],
                    "fsdp",
                    scatter_dimension=1,
                    tiled=True,
                    axis_index_groups=alternate,
                )
                mine = lax.dynamic_slice_in_dim(pair_sum, side * shard_rows, shard_rows, 1)
                theirs = lax.dynamic_slice_in_dim(pair_sum, (1 - side) * shard_rows, shard_rows, 1)
                for core in range(2):
                    near, far = mine, theirs
                    if core:
                        near = lax.ppermute(mine, "section", [(1, 0)])
                    far = lax.ppermute(
                        far, ("section", "fsdp"), [(core * depth + i, i ^ 1) for i in range(depth)]
                    )
                    low = core * quarter + at
                    pieces.append((0, low, half_held + low, [near]))
                    pieces.append((0, half_held + low, low, [far]))
            expert_grads[0] = pieces
        else:
            summed[layer] = [
                lax.psum_scatter(grads, "fsdp", scatter_dimension=1, tiled=True)
                for grads in gathered
            ]
            expert_grads[layer] = []
            for at, part in zip(spans, summed[layer]):
                arrived = lax.ppermute(part, "section", [(1 - layer, layer)])
                for half_at, term in ((layer, part), (1 - layer, arrived)):
                    base = half_at * half_held + at
                    expert_grads[layer].append((layer, base, base, [term]))
        if layer == 1:
            grad_output = after(grad_output, (summed[1][0], loss_value))
        else:
            grad_output = after(grad_output, summed[1][-1])
            outs = after(outs, planes)
            shared_grads[1] = [home_line(part, 1) for part in planes]
        back = attend_backward(
            attend_scalars,
            returned(outs),
            grad_output,
            held["middle"],
            held["gain_second"],
            held["attended"],
            held["shared"],
            held["q"],
            held["lse"],
            cos_table,
            -sin_table,
            held["x"],
            held["gain_first"],
            held["kvs"],
        )
        grad_mid, weight_grads, gain_second_grad, dq = back[:4]
        dkv = back[4:]
        parts = [dkv[0]] + [exchanged(dkv[k], "ctx", k) for k in range(1, devices)]
        if layer == 0:
            outward = home_blocks(weight_grads, 0)
            grad_mid = after(grad_mid, (outward, shared_grads[1]))
        else:
            grad_mid = after(grad_mid, hidden_out)
        small = lax.dynamic_update_slice_in_dim(small, gain_second_grad, EXPERTS + 1, 0)
        dx, packed = project_backward(
            held["x"],
            held["gain_first"],
            dq,
            parts,
            grad_mid,
            held["shared"],
            cos_table,
            -sin_table,
            small,
        )
        input_grads[layer] = dx
        grad_output = dx.astype(BF16).astype(F32)
        if layer == 1:
            waiting = (weight_grads, packed)
        else:
            shared_grads[0] = [
                home_line(home_plane(blocks, 0), 0) for blocks in (outward, home_blocks(packed, 0))
            ]

    pick = lambda values: jnp.where(first_core, values[0], values[1])
    outward, inward = (pick([shared_grads[0][i], shared_grads[1][i]]) for i in range(2))
    input_out = placed_rows(input_grads)
    pieces = expert_grads[0] + expert_grads[1]
    numbers = range(held_experts)
    last = [e for e in numbers if len(runs[0]) > 1 and e % half_held >= runs[0][-1][0]]
    touches = lambda piece, experts: any(
        0 <= e - base < piece[3][0].shape[0] for e in experts for base in piece[1:3]
    )
    place_scalars = jnp.stack([section, side]).astype(jnp.int32)
    placed = ()
    for experts in ([e for e in numbers if e not in last], last):
        if experts:
            placed = place_experts(
                place_scalars,
                [piece for piece in pieces if touches(piece, experts)],
                held_experts,
                up_rows,
                experts,
                placed,
            )
    up_sum, down_sum = placed
    at = 2 * KW
    return (
        hidden_out[None, :, None],
        input_out[None, :, None],
        loss_value,
        inward[:, at + EXPERTS][None],
        outward[:, width:][None],
        inward[:, :at][None],
        outward[:, :width][None],
        inward[:, at + EXPERTS + 1][None],
        inward[:, at : at + EXPERTS][None],
        up_sum[None],
        down_sum[None],
    )


def solution(mesh):
    placed = (
        P(None, "fsdp", "ctx", None),
        P(None, "fsdp", "ctx", None),
        P(),
        P("section", None, "fsdp", "ctx", None),
        P("section", ("ctx", "fsdp")),
        P("section", ("ctx", "fsdp"), None),
        P("section", ("ctx", "fsdp"), None),
        P("section", ("ctx", "fsdp"), None),
        P("section", ("ctx", "fsdp")),
        P("section", ("ctx", "fsdp"), None),
        P("section", "ctx", "fsdp", None),
        P("section", "ctx", "fsdp", None),
    )
    return jax.shard_map(
        shards,
        mesh=mesh,
        in_specs=placed,
        out_specs=(
            P("section", None, "fsdp", "ctx", None),
            P("section", None, "fsdp", "ctx", None),
            P(),
            P("section", ("ctx", "fsdp")),
            P("section", ("ctx", "fsdp"), None),
            P("section", ("ctx", "fsdp"), None),
            P("section", ("ctx", "fsdp"), None),
            P("section", ("ctx", "fsdp")),
            P("section", ("ctx", "fsdp"), None),
            P("section", "ctx", "fsdp", None),
            P("section", "ctx", "fsdp", None),
        ),
        check_vma=False,
    )
```

```python
import functools
import math

import jax
import jax.numpy as jnp
from jax import lax
from jax.experimental import pallas as pl
from jax.experimental.pallas import tpu as pltpu
from jax.sharding import PartitionSpec as P

QH = 16
KVH = 8
HD = 64
EXPERTS = 32
FF_E = 512
TOPK = 8
KW = KVH * HD
EXT = 16

epsilon = 1e-06
rope_base = 10000.0
negative = -1e30
F32 = jnp.float32
BF16 = jnp.bfloat16
VMEM_LIMIT = 60 * 1024 * 1024


def params(grid_dims=0):
    return pltpu.CompilerParams(
        vmem_limit_bytes=VMEM_LIMIT,
        dimension_semantics=("arbitrary",) * grid_dims if grid_dims else None,
    )


def cost(flops, moved, exps=0):
    return pl.CostEstimate(flops=int(flops), bytes_accessed=int(moved), transcendentals=int(exps))


def mm(a, b):
    return jnp.dot(a, b, preferred_element_type=F32)


def mm_nt(a, b):
    return lax.dot_general(a, b, (((1,), (1,)), ((), ())), preferred_element_type=F32)


def mm_tn(a, b):
    return lax.dot_general(a, b, (((0,), (0,)), ((), ())), preferred_element_type=F32)


def fixed(shape):
    return pl.BlockSpec(shape, lambda *_: (0,) * len(shape), pipeline_mode=pl.Buffered(1))


def resident(shape):
    return pl.BlockSpec(shape, lambda *_: (0,) * len(shape))


def lane_index(shape):
    return lax.broadcasted_iota(jnp.int32, shape, len(shape) - 1)


def turn(block, cosine, sine):
    low_half = lane_index(block.shape) % HD < HD // 2
    swapped = jnp.where(
        low_half, pltpu.roll(block, 128 - HD // 2, axis=1), pltpu.roll(block, HD // 2, axis=1)
    )
    return block * cosine + swapped * sine


def rolled(block):
    return pltpu.roll(block.astype(F32), HD, axis=1).astype(BF16)


def key_positions(device, half, devices, shape, dim):
    within = lax.broadcasted_iota(jnp.int32, shape, dim)
    return jnp.where(
        within < half, device * half + within, (2 * devices - 1 - device) * half + within - half
    )


def fill_bias(bias, scal, devices, rows):
    context, length = scal[0], scal[1]
    query_pos = key_positions(context, rows // 2, devices, (rows, rows), 1)
    for k in range(devices):
        key_pos = key_positions(context ^ k, rows // 2, devices, (rows, rows), 0)
        taken = (key_pos <= query_pos) & (key_pos < length)
        bias[k * rows : (k + 1) * rows, :] = jnp.where(taken, 0.0, negative)


def two_heads(block):
    even = lane_index(block.shape) < HD
    zero = jnp.zeros((), block.dtype)
    return jnp.concatenate([jnp.where(even, block, zero), jnp.where(even, zero, block)], axis=0)


def two_heads_doubled(block):
    even = lane_index(block.shape) < HD
    other = rolled(block)
    return jnp.concatenate([jnp.where(even, block, other), jnp.where(even, other, block)], axis=0)


def doubled(block, odd):
    even = lane_index(block.shape) < HD
    other = rolled(block)
    return jnp.where(even, other, block) if odd else jnp.where(even, block, other)


def one_hot(rank_row, slots):
    rows = rank_row.shape[-1]
    index = lax.broadcasted_iota(jnp.int32, (slots, rows), 0).astype(F32)
    return rank_row == index


def project_kernel(x, gain, wq, wm, cosine, sine, q_out, kv_out):
    values = x[...].astype(F32)
    factor = lax.rsqrt(jnp.mean(values * values, axis=-1, keepdims=True) + epsilon)
    normed = (values * factor * gain[...]).astype(BF16)
    cos, sin = cosine[...], sine[...]
    q0 = mm(normed, wq[...])
    for b in range(QH * HD // 128):
        at = slice(b * 128, (b + 1) * 128)
        q_out[:, at] = turn(q0[:, at], cos, sin).astype(BF16)
    kv0 = mm(normed, wm[...])
    for b in range(KW // 128):
        at = slice(b * 128, (b + 1) * 128)
        kv_out[0, :, at] = turn(kv0[:, at], cos, sin).astype(BF16)
    kv_out[1] = kv0[:, KW:].astype(BF16)


def project(x, gain, shared, cosine, sine):
    rows, width = x.shape
    return pl.pallas_call(
        project_kernel,
        name="project",
        grid=(1,),
        in_specs=[
            fixed((rows, width)),
            fixed((1, width)),
            pl.BlockSpec((width, QH * HD), lambda i: (0, 0), pipeline_mode=pl.Buffered(1)),
            pl.BlockSpec((width, 2 * KW), lambda i: (0, 1), pipeline_mode=pl.Buffered(1)),
            fixed((rows, 128)),
            fixed((rows, 128)),
        ],
        out_specs=[resident((rows, QH * HD)), resident((2, rows, KW))],
        out_shape=[
            jax.ShapeDtypeStruct((rows, QH * HD), BF16),
            jax.ShapeDtypeStruct((2, rows, KW), BF16),
        ],
        compiler_params=params(1),
        cost_estimate=cost(2 * rows * width * 2048, 2 * width * 2048 + 8 * rows * width),
    )(x, gain, shared, shared, cosine, sine)


def attend_kernel(devices, scal, x, q, *rest):
    ks, vs, rest = rest[:devices], rest[devices : 2 * devices], rest[2 * devices :]
    wo, gain, router, mask, o_out, lse_out, mid_out, msg_out, bias, held = rest
    rows = x.shape[0]
    step = pl.program_id(0)

    @pl.when(step == 0)
    def _():
        fill_bias(bias, scal, devices, rows)

    keys = jnp.concatenate([r[0] for r in ks], axis=0)
    values = jnp.concatenate([r[0] for r in vs], axis=0)
    block_bias = bias[...]
    both_bias = jnp.concatenate([block_bias, block_bias], axis=1)
    for i in range(2):
        query = two_heads(q[:, i * 128 : (i + 1) * 128])
        scores = mm_nt(doubled(keys, i), query) * (1.0 / math.sqrt(HD)) + both_bias
        top = jnp.max(scores, axis=0, keepdims=True)
        raised = jnp.exp(scores - top)
        total = jnp.sum(raised, axis=0, keepdims=True)
        probs = (raised * (1.0 / total)).astype(BF16)
        lse_out[0, i : i + 1, :] = top + jnp.log(total)
        mixed = mm_tn(values, probs)[i * HD : (i + 1) * HD]
        pair = jnp.concatenate([mixed[:, :rows], mixed[:, rows:]], axis=0)
        at = pl.multiple_of(step * 256 + i * 128, 128)
        held[:, pl.ds(at, 128)] = jnp.transpose(pair).astype(BF16)

    @pl.when(step == pl.num_programs(0) - 1)
    def _():
        attended = held[...]
        o_out[...] = attended
        middle = x[...].astype(F32) + mm(attended, wo[...])
        mid_out[...] = middle
        factor = lax.rsqrt(jnp.mean(middle * middle, axis=-1, keepdims=True) + epsilon)
        normed = (middle * factor * gain[...]).astype(BF16)
        msg_out[:rows, :] = normed
        logits = mm_nt(router[...], normed)
        chosen = mask[...] > 0.5
        top = jnp.max(jnp.where(chosen, logits, negative), axis=0, keepdims=True)
        raised = jnp.where(chosen, jnp.exp(jnp.where(chosen, logits - top, 0.0)), 0.0)
        gates = raised / jnp.sum(raised, axis=0, keepdims=True)
        high = gates.astype(BF16)
        low = (gates - high.astype(F32)).astype(BF16)
        ext = [high[:EXT], high[EXT:], low[:EXT], low[EXT:]]
        if 4 * rows < x.shape[1]:
            ext.append(jnp.zeros((EXT, x.shape[1] - 4 * rows), BF16))
        msg_out[rows:, :] = jnp.concatenate(ext, axis=1)


def attend(scal, x, q, kvs, shared, gain, router, mask):
    rows, width = x.shape
    devices = len(kvs)
    keys = devices * rows
    kv_specs = [pl.BlockSpec((1, rows, 128), lambda h: (0, 0, h)) for _ in kvs] + [
        pl.BlockSpec((1, rows, 128), lambda h: (1, 0, h)) for _ in kvs
    ]
    return pl.pallas_call(
        functools.partial(attend_kernel, devices),
        name="attend",
        grid=(KVH // 2,),
        in_specs=[
            pl.BlockSpec(memory_space=pltpu.SMEM),
            fixed((rows, width)),
            pl.BlockSpec((rows, 256), lambda h: (0, h)),
            *kv_specs,
            pl.BlockSpec((QH * HD, width), lambda h: (0, 2), pipeline_mode=pl.Buffered(1)),
            fixed((1, width)),
            fixed((EXPERTS, width)),
            fixed((EXPERTS, rows)),
        ],
        out_specs=[
            resident((rows, QH * HD)),
            pl.BlockSpec((1, 2, 2 * rows), lambda h: (h, 0, 0)),
            resident((rows, width)),
            resident((rows + EXT, width)),
        ],
        out_shape=[
            jax.ShapeDtypeStruct((rows, QH * HD), BF16),
            jax.ShapeDtypeStruct((KVH // 2, 2, 2 * rows), F32),
            jax.ShapeDtypeStruct((rows, width), F32),
            jax.ShapeDtypeStruct((rows + EXT, width), BF16),
        ],
        scratch_shapes=[pltpu.VMEM((keys, rows), F32), pltpu.VMEM((rows, QH * HD), BF16)],
        compiler_params=params(1),
        cost_estimate=cost(
            4 * rows * keys * QH * HD * 2 + 2 * rows * width * width,
            2 * width * width + 4 * keys * width + 12 * rows * width,
            rows * keys * QH,
        ),
    )(scal, x, q, *kvs, *kvs, shared, gain, router, mask)


def hot_rows(rank, j, slots):
    local = rank.shape[1]
    return jnp.concatenate(
        [
            jnp.where(one_hot(rank[j, i : i + 1, :], slots), 1.0, 0.0).astype(BF16)
            for i in range(local)
        ],
        axis=0,
    )


def combine(rank, held, prior, outs, buffers, slots):
    held = held if isinstance(held, list) else [held]
    prior_buffer, out_buffer, prior_sems, out_sems = buffers
    width = held[0].shape[-1]
    depth = out_buffer.shape[0]
    count = len(outs)
    fetch = lambda j: pltpu.make_async_copy(
        prior[j], prior_buffer.at[j % depth], prior_sems.at[j % depth]
    )
    send = lambda j: pltpu.make_async_copy(
        out_buffer.at[j % depth], outs[j], out_sems.at[j % depth]
    )
    for j in range(min(depth - 1, count) if prior else 0):
        fetch(j).start()
    for j in range(count):
        rows = [part[:, j].reshape(part.shape[0] * slots, width) for part in held]
        rows = rows[0] if len(rows) == 1 else jnp.concatenate(rows, axis=0)
        total = mm_tn(hot_rows(rank, j, slots), rows)
        if prior:
            if j + depth - 1 < count:
                fetch(j + depth - 1).start()
            fetch(j).wait()
            total = total + prior_buffer[j % depth].astype(F32)
        if j >= depth:
            send(j - depth).wait()
        out_buffer[j % depth] = total.astype(BF16)
        send(j).start()
    for j in range(max(0, count - depth), count):
        send(j).wait()


def gate_columns(rank, values, step, sources, slots):
    columns = []
    for j in sources:
        hot = one_hot(rank[j, pl.ds(step, 1), :], slots)
        columns.append(jnp.sum(jnp.where(hot, values(j), 0.0), axis=1, keepdims=True))
    return jnp.concatenate(columns, axis=0)


def finish_kernel(count, *refs):
    terms, (middle, goal, valid, hidden, mixed_out, grad_out, message) = (
        refs[:count],
        refs[count:],
    )
    rows, width = middle.shape
    mixed = terms[0][...].astype(F32)
    for term in terms[1:]:
        mixed = mixed + term[...].astype(F32)
    output = middle[...] + mixed
    hidden[...] = output.astype(BF16)
    mixed_out[...] = mixed
    grad = (output - goal[...].astype(F32)) * valid[...]
    grad_out[...] = grad
    error = 0.5 * jnp.sum(jnp.sum(grad * grad, axis=1, keepdims=True), axis=0, keepdims=True)
    fill_message(message, grad, mixed, error)


def fill_message(message, grad, mixed, error):
    rows, width = grad.shape
    message[:rows, :] = grad.astype(BF16)
    inner = jnp.transpose(
        jnp.broadcast_to(jnp.sum(grad * mixed, axis=1, keepdims=True), (rows, 128))
    )[:EXT]
    high = inner.astype(BF16)
    low = (inner - high.astype(F32)).astype(BF16)
    row = lax.broadcasted_iota(jnp.int32, (EXT, rows), 0)
    ext = jnp.where(row == 0, high.astype(F32), jnp.where(row == 1, low.astype(F32), 0.0))
    for at in range(2, 5):
        term = error.astype(BF16).astype(F32)
        ext = jnp.where(row == at, term, ext)
        error = error - term
    message[rows:, :rows] = ext.astype(BF16)
    message[rows:, rows:] = jnp.zeros((EXT, width - rows), BF16)


def finish(terms, middle, goal, valid):
    rows, width = middle.shape
    return pl.pallas_call(
        functools.partial(finish_kernel, len(terms)),
        name="finish",
        out_shape=[
            jax.ShapeDtypeStruct((rows, width), BF16),
            jax.ShapeDtypeStruct((rows, width), F32),
            jax.ShapeDtypeStruct((rows, width), F32),
            jax.ShapeDtypeStruct((rows + EXT, width), BF16),
        ],
        compiler_params=params(),
        cost_estimate=cost(8 * rows * width, 24 * rows * width),
    )(*terms, middle, goal, valid)


def message_kernel(grad, mixed, message):
    fill_message(message, grad[...], mixed[...], jnp.zeros((1, 1), F32))


def grad_message(grad, mixed):
    rows, width = grad.shape
    return pl.pallas_call(
        message_kernel,
        name="grad_message",
        out_shape=jax.ShapeDtypeStruct((rows + EXT, width), BF16),
        compiler_params=params(),
        cost_estimate=cost(4 * rows * width, 10 * rows * width),
    )(grad, mixed)


def dispatch_kernel(sources, slots, backward, scal, *rest):
    msgs, (rank, x_out, side_out, arrived, picked, in_sems, out_sems) = (
        rest[:sources],
        rest[sources:],
    )
    local, rows = rank.shape[1:]
    fetch = lambda j: pltpu.make_async_copy(msgs[j], arrived.at[j], in_sems.at[j])
    send = lambda j: pltpu.make_async_copy(picked.at[j], x_out.at[:, j], out_sems.at[j])
    for j in range(sources):
        fetch(j).start()
    pick_row = lax.broadcasted_iota(jnp.int32, (EXT, 4 * rows), 0)
    for j in range(sources):
        fetch(j).wait()
        taken = mm(hot_rows(rank, j, slots), arrived[j, :rows, :]).astype(BF16)
        for i in range(local):
            picked[j, i] = taken[i * slots : (i + 1) * slots]
        send(j).start()
        if backward:
            ext = arrived[j, rows:, :rows].astype(F32)
            side_out[j, 0:1, :] = ext[0:1, :] + ext[1:2, :]
            side_out[j, 1:2, :] = ext[2:3, :] + ext[3:4, :] + ext[4:5, :]
        else:
            ext = arrived[j, rows:, : 4 * rows].astype(F32)
            for i in range(local):
                expert = scal[0] + i
                row = jnp.sum(jnp.where(pick_row == expert % EXT, ext, 0.0), axis=0, keepdims=True)
                high = jnp.where(expert < EXT, row[:, :rows], row[:, rows : 2 * rows])
                low = jnp.where(expert < EXT, row[:, 2 * rows : 3 * rows], row[:, 3 * rows :])
                side_out[j, i : i + 1, :] = high + low
    for j in range(sources):
        send(j).wait()


def dispatch(scal, msgs, rank, slots, backward):
    sources, local, rows = rank.shape
    width = msgs[0].shape[1]
    anywhere = pl.BlockSpec(memory_space=pl.ANY)
    side = (sources, 2 if backward else local, rows)
    taken, beside = pl.pallas_call(
        functools.partial(dispatch_kernel, sources, slots, backward),
        name="dispatch",
        grid=(1,),
        in_specs=[
            pl.BlockSpec(memory_space=pltpu.SMEM),
            *[anywhere for _ in msgs],
            fixed(rank.shape),
        ],
        out_specs=[anywhere, resident(side)],
        out_shape=[
            jax.ShapeDtypeStruct((local, sources, slots, width), BF16),
            jax.ShapeDtypeStruct(side, F32),
        ],
        scratch_shapes=[
            pltpu.VMEM((sources, rows + EXT, width), BF16),
            pltpu.VMEM((sources, local, slots, width), BF16),
            pltpu.SemaphoreType.DMA((sources,)),
            pltpu.SemaphoreType.DMA((sources,)),
        ],
        compiler_params=params(1),
        cost_estimate=cost(
            2 * local * sources * slots * rows * width, 2 * sources * width * (rows + local * slots)
        ),
    )(scal, *msgs, rank)
    return taken.reshape(local, sources * slots, width), beside


def fill_weights(scal, blocks, w1, w2):
    up = w1.shape[0] // len(blocks)
    down = w2.shape[0] // len(blocks)
    for k, block in enumerate(blocks):
        at = scal[1 + k]
        w1[pl.ds(pl.multiple_of(at * up, up), up), :] = block[0, :up]
        w2[pl.ds(pl.multiple_of(at * down, down), down), :] = block[0, up:]


def experts_kernel(sources, depth, slots, chained, scal, *rest):
    prior = ()
    if chained:
        prior, rest = rest[:sources], rest[sources:]
    rank, gates, xs, rest = *rest[:3], rest[3:]
    blocks, rest = rest[:depth], rest[depth:]
    gu_out, y_out, rest = *rest[:2], rest[2:]
    outs, rest = rest[:sources], rest[sources:]
    held, w1, w2 = rest[:3]
    width = held.shape[-1]
    step, part = pl.program_id(0), pl.program_id(1)
    portions = sources // (xs.shape[1] // slots)
    portion = sources // portions

    @pl.when(part == 0)
    def _():
        fill_weights(scal, blocks, w1, w2)

    gate_up = mm(xs[0], w1[...])
    gu_out[0] = gate_up
    gate, up = gate_up[:, :FF_E], gate_up[:, FF_E:]
    activated = (gate * jax.nn.sigmoid(gate) * up).astype(BF16)
    out = mm(activated, w2[...]).astype(BF16)
    y_out[0] = out
    column = gate_columns(
        rank,
        lambda j: gates[j, pl.ds(step, 1), :],
        step,
        [part * portion + n for n in range(portion)],
        slots,
    )
    held[step, pl.ds(part * portion, portion)] = (
        (column * out.astype(F32)).astype(BF16).reshape(portion, slots, width)
    )

    @pl.when((step == pl.num_programs(0) - 1) & (part == portions - 1))
    def _():
        combine(rank, held, prior, outs, rest[3:], slots)


def weight_specs(blocks, depth, base=0):
    arrays = blocks if len(blocks) == depth else blocks * depth
    rows = arrays[0].shape[1] // (depth // len(blocks))
    width = arrays[0].shape[2]
    specs = [
        pl.BlockSpec((1, rows, width), lambda e, r, f=(k if len(blocks) == 1 else 0): (e + base, f, 0))
        for k in range(depth)
    ]
    return arrays, specs


def stream_scratch(rows, width):
    return [
        pltpu.VMEM((4, rows, width), BF16),
        pltpu.VMEM((4, rows, width), BF16),
        pltpu.SemaphoreType.DMA((4,)),
        pltpu.SemaphoreType.DMA((4,)),
    ]


def experts_forward(scal, xs, rank, gates, blocks, depth, slots, first, prior=()):
    sources, local, rows = rank.shape
    width = xs.shape[2]
    portions = max(1, sources // 8)
    count = sources * slots
    arrays, specs = weight_specs(blocks, depth)
    anywhere = pl.BlockSpec(memory_space=pl.ANY)
    each = lambda shape, base=0: pl.BlockSpec((1,) + shape, lambda e, r: (e + base, r, 0))
    outs = pl.pallas_call(
        functools.partial(experts_kernel, sources, depth, slots, bool(prior)),
        name="experts_forward",
        grid=(local, portions),
        in_specs=[
            pl.BlockSpec(memory_space=pltpu.SMEM),
            *[anywhere for _ in prior],
            fixed((sources, local, rows)),
            fixed((sources, local, rows)),
            each((count // portions, width), first),
            *specs,
        ],
        out_specs=[
            each((count // portions, 2 * FF_E)),
            each((count // portions, width)),
            *[anywhere for _ in range(sources)],
        ],
        out_shape=[
            jax.ShapeDtypeStruct((local, count, 2 * FF_E), F32),
            jax.ShapeDtypeStruct((local, count, width), BF16),
            *[jax.ShapeDtypeStruct((rows, width), BF16) for _ in range(sources)],
        ],
        scratch_shapes=[
            pltpu.VMEM((local, sources, slots, width), BF16),
            pltpu.VMEM((width, 2 * FF_E), BF16),
            pltpu.VMEM((FF_E, width), BF16),
            *stream_scratch(rows, width),
        ],
        compiler_params=params(2),
        cost_estimate=cost(
            2 * local * count * width * 3 * FF_E * 1.3, 8 * local * count * width, local * count * FF_E
        ),
    )(scal, *prior, rank, gates, xs, *arrays)
    return outs[:2], list(outs[2:])


def experts_back_kernel(sources, depth, slots, mode, scal, *rest):
    last, order = mode
    earlier = ()
    if last:
        full_rank, rest = rest[0], rest[1:]
        earlier, rest = rest[: len(order) - 1], rest[len(order) - 1 :]
    rank, gates, inners, grads, xs, gu, ys, router, rest = *rest[:8], rest[8:]
    blocks, rest = rest[:depth], rest[depth:]
    grad_out_ref, router_out, rest = *rest[:2], rest[2:]
    outs, rest = (rest[:sources], rest[sources:]) if last else (rest[:1], rest[1:])
    held, w1, w2, sum1, sum2 = rest[:5]
    width = w1.shape[0]
    step, part = pl.program_id(0), pl.program_id(1)
    portions = sources // (xs.shape[1] // slots)
    portion = sources // portions

    @pl.when(part == 0)
    def _():
        fill_weights(scal, blocks, w1, w2)

    mine = [part * portion + n for n in range(portion)]
    gate_column = gate_columns(rank, lambda j: gates[j, pl.ds(step, 1), :], step, mine, slots)
    inner_column = gate_columns(rank, lambda j: inners[j, 0:1, :], step, mine, slots)
    grad_out = grads[0].astype(F32)
    grad_y = (gate_column * grad_out).astype(BF16)
    given = jnp.sum(grad_out * ys[0].astype(F32), axis=1, keepdims=True)
    grad_logit = gate_column * (given - inner_column)
    gate, up = gu[0, :, :FF_E], gu[0, :, FF_E:]
    sigmoid = jax.nn.sigmoid(gate)
    silu = gate * sigmoid
    activated = (silu * up).astype(BF16)
    down_part = mm_tn(activated, grad_y)
    grad_act = mm_nt(grad_y, w2[...])
    grad_gate = grad_act * up * sigmoid * (1.0 + gate * (1.0 - sigmoid))
    grad_up = grad_act * silu
    grad_gate_up = jnp.concatenate([grad_gate.astype(BF16), grad_up.astype(BF16)], axis=1)
    taken = xs[0]
    up_part = mm_tn(taken, grad_gate_up)
    router_part = jnp.sum(taken.astype(F32) * grad_logit, axis=0, keepdims=True)
    grad_rows = mm_nt(grad_gate_up, w1[...]) + grad_logit * router[0]
    if last:
        held[step, pl.ds(part * portion, portion)] = grad_rows.astype(BF16).reshape(
            portion, slots, width
        )
    else:
        outs[0][0] = grad_rows.astype(BF16)

    def write(up_total, down_total):
        up_rows, down_rows = width // depth, FF_E // depth
        for f in range(depth):
            top = f * (up_rows + down_rows)
            grad_out_ref[0, top : top + up_rows, :] = up_total[
                f * up_rows : (f + 1) * up_rows
            ].astype(BF16)
            grad_out_ref[0, top + up_rows : top + up_rows + down_rows, :] = down_total[
                f * down_rows : (f + 1) * down_rows
            ].astype(BF16)

    if sum1 is None:
        write(up_part, down_part)
        router_out[0] = router_part
    else:

        @pl.when(part == 0)
        def _():
            sum1[...] = up_part
            sum2[...] = down_part
            router_out[0] = router_part

        @pl.when(part > 0)
        def _():
            sum1[...] += up_part
            sum2[...] += down_part
            router_out[0] += router_part

        @pl.when(part == portions - 1)
        def _():
            write(sum1, sum2)

    if last:

        @pl.when((step == pl.num_programs(0) - 1) & (part == portions - 1))
        def _():
            pieces = list(earlier) + [held]
            combine(full_rank, [pieces[o] for o in order], (), outs, rest[5:], slots)


def experts_backward(
    scal, grads, rank, gates, inners, xs, kept, router, blocks, depth, slots, first, base, last
):
    sources, local, rows = rank.shape
    width = xs.shape[2]
    portions = max(1, sources // 8)
    count = sources * slots
    gu, ys = kept
    arrays, specs = weight_specs(blocks, depth, base)
    merged = width + FF_E
    anywhere = pl.BlockSpec(memory_space=pl.ANY)
    each = lambda shape, base=0: pl.BlockSpec((1,) + shape, lambda e, r: (e + base, r, 0))
    whole = lambda shape: pl.BlockSpec((1,) + shape, lambda e, r: (e, 0, 0))
    before = []
    if last:
        before = [last[0]] + [
            part.reshape(part.shape[0], sources, slots, width) for part in last[1]
        ]
    mode = (bool(last), last[2] if last else ())

    def kernel(*refs):
        refs = list(refs)
        if portions == 1:
            at = len(refs) - (4 if last else 0)
            refs[at:at] = [None, None]
        if not last:
            refs[-4:-4] = [None]
        experts_back_kernel(sources, depth, slots, mode, *refs)

    sums = [pltpu.VMEM((width, 2 * FF_E), F32), pltpu.VMEM((FF_E, width), F32)]
    outs = pl.pallas_call(
        kernel,
        name="experts_backward",
        grid=(local, portions),
        in_specs=[
            pl.BlockSpec(memory_space=pltpu.SMEM),
            *[fixed(part.shape) for part in before],
            fixed((sources, local, rows)),
            fixed((sources, local, rows)),
            fixed((sources, 2, rows)),
            each((count // portions, width)),
            each((count // portions, width), first),
            each((count // portions, 2 * FF_E), base),
            each((count // portions, width), base),
            whole((1, width)),
            *specs,
        ],
        out_specs=[
            whole((merged, width)),
            whole((1, width)),
            *([anywhere] * sources if last else [each((count // portions, width))]),
        ],
        out_shape=[
            jax.ShapeDtypeStruct((local, merged, width), BF16),
            jax.ShapeDtypeStruct((local, 1, width), F32),
            *(
                [jax.ShapeDtypeStruct((rows, width), BF16)] * sources
                if last
                else [jax.ShapeDtypeStruct((local, count, width), BF16)]
            ),
        ],
        scratch_shapes=[
            *([pltpu.VMEM((local, sources, slots, width), BF16)] if last else []),
            pltpu.VMEM((width, 2 * FF_E), BF16),
            pltpu.VMEM((FF_E, width), BF16),
            *(sums if portions > 1 else []),
            *(stream_scratch(rows, width) if last else []),
        ],
        compiler_params=params(2),
        cost_estimate=cost(
            2 * local * count * width * 3 * FF_E * 2.3, 14 * local * count * width, local * count * FF_E
        ),
    )(scal, *before, rank, gates, inners, grads, xs, gu, ys, router, *arrays)
    return outs[0], outs[1], list(outs[2:])


def place_kernel(places, number, aliased, scal, *refs):
    parts, (up_out, down_out) = refs[: -2 - aliased], refs[-2:]
    step = number(pl.program_id(0))
    up_rows = up_out.shape[1]

    def put(block):
        up_out[0] = block[0, :up_rows].astype(F32)
        down_out[0] = block[0, up_rows:].astype(F32)

    at = 0
    for place in places:
        core, base, count = place
        pl.when((scal[0] == core) & (step >= base) & (step < base + count))(
            functools.partial(put, parts[at])
        )
        at += 1


def place_experts(scal, pieces, held_experts, up_rows, experts, into=()):
    rows, width = pieces[0][2].shape[1:]
    run = next((i for i in range(1, len(experts)) if experts[i] != experts[0] + i), len(experts))
    skip = experts[run] - experts[run - 1] if run < len(experts) else 1
    number = lambda i: experts[0] + (i // run) * (run - 1 + skip) + i % run
    assert [number(i) for i in range(len(experts))] == list(experts)
    places = [(core, base, array.shape[0]) for core, base, array in pieces]
    arrays = [array for _, _, array in pieces]
    specs = [
        pl.BlockSpec(
            (1, rows, width),
            lambda i, scal, base=base, top=count - 1: (jnp.clip(number(i) - base, 0, top), 0, 0),
        )
        for _, base, count in places
    ]
    specs += [pl.BlockSpec(memory_space=pl.ANY) for _ in into]
    return pl.pallas_call(
        functools.partial(place_kernel, places, number, len(into)),
        name="place_experts",
        grid_spec=pltpu.PrefetchScalarGridSpec(
            num_scalar_prefetch=1,
            grid=(len(experts),),
            in_specs=specs,
            out_specs=[
                pl.BlockSpec((1, up_rows, width), lambda i, scal: (number(i), 0, 0)),
                pl.BlockSpec((1, rows - up_rows, width), lambda i, scal: (number(i), 0, 0)),
            ],
        ),
        out_shape=[
            jax.ShapeDtypeStruct((held_experts, up_rows, width), F32),
            jax.ShapeDtypeStruct((held_experts, rows - up_rows, width), F32),
        ],
        input_output_aliases={1 + len(arrays) + i: i for i in range(len(into))},
        compiler_params=params(1),
        cost_estimate=cost(0, 8 * len(experts) * rows * width),
    )(scal, *arrays, *into)


def assemble_kernel(devices, depth, scal, *refs):
    owns, others, whole, sem = refs[:devices], refs[devices : 2 * devices], refs[-2], refs[-1]
    piece = whole.shape[0] // (devices * depth)
    for home, blocks in ((1, owns), (0, others)):

        @pl.when(scal[0] == home)
        def _(blocks=blocks):
            for k in range(devices):
                for i in range(depth):
                    to = pl.multiple_of(((scal[1] ^ k) * depth + (scal[2] ^ i)) * piece, piece)
                    pltpu.make_async_copy(
                        blocks[k].at[pl.ds(i * piece, piece)], whole.at[pl.ds(to, piece)], sem
                    ).start()
            pltpu.make_async_copy(whole, whole, sem).wait()


def assemble(scal, owns, others, depth):
    devices = len(owns)
    rows, columns = owns[0].shape
    return pl.pallas_call(
        functools.partial(assemble_kernel, devices, depth),
        name="assemble",
        in_specs=[pl.BlockSpec(memory_space=pltpu.SMEM)]
        + [pl.BlockSpec(memory_space=pl.ANY)] * (2 * devices),
        out_specs=pl.BlockSpec(memory_space=pltpu.VMEM),
        out_shape=jax.ShapeDtypeStruct((rows * devices, columns), owns[0].dtype),
        scratch_shapes=[pltpu.SemaphoreType.DMA(())],
        compiler_params=params(),
        cost_estimate=cost(0, 4 * rows * devices * columns),
    )(scal, *owns, *others)


def attend_back_kernel(devices, arrived, scal, *rest):
    parts, rest = rest[:arrived], rest[arrived:]
    grad_out, middle, gain, attended, wo, q, lse, cosine, sine, x, gain_first = rest[:11]
    ks, vs, rest = rest[11 : 11 + devices], rest[11 + devices : 11 + 2 * devices], rest[11 + 2 * devices :]
    mid_out, weight_grads, gain_grad, dq_out = rest[:4]
    dkv_outs, (bias, held) = rest[4 : 4 + devices], rest[4 + devices :]
    width = middle.shape[1]
    rows = middle.shape[0]
    scale = 1.0 / math.sqrt(HD)
    step = pl.program_id(0)

    @pl.when(step == 0)
    def _():
        fill_bias(bias, scal, devices, rows)
        grad_mix = parts[0][...].astype(F32)
        for part in parts[1:]:
            grad_mix = grad_mix + part[...].astype(F32)
        mid = middle[...]
        factor = lax.rsqrt(jnp.mean(mid * mid, axis=-1, keepdims=True) + epsilon)
        scaled = grad_mix * gain[...]
        inner = jnp.mean(mid * scaled, axis=-1, keepdims=True)
        gain_grad[...] = jnp.sum(grad_mix * mid * factor, axis=0, keepdims=True)
        grad_mid = grad_out[...] + factor * scaled - mid * (factor * factor * factor * inner)
        mid_out[...] = grad_mid
        branch = grad_mid.astype(BF16)
        weight_grads[:, :width] = mm_tn(attended[...], branch).astype(BF16)
        held[...] = mm_nt(branch, wo[...]).astype(BF16)

    keys = jnp.concatenate([r[0] for r in ks], axis=0)
    values = jnp.concatenate([r[0] for r in vs], axis=0)
    block_bias = bias[...]
    both_bias = jnp.concatenate([block_bias, block_bias], axis=1)
    key_parts, value_parts = [], []
    for i in range(2):
        block = q[:, i * 128 : (i + 1) * 128]
        at = pl.multiple_of(step * 256 + i * 128, 128)
        grads = held[:, pl.ds(at, 128)]
        scores = mm_nt(doubled(keys, i), two_heads(block)) * scale + both_bias
        probs = jnp.exp(scores - lse[0, i : i + 1, :])
        grad_probs = mm_nt(doubled(values, i), two_heads(grads))
        product = probs * grad_probs
        dots = jnp.sum(product, axis=0, keepdims=True)
        grad_scores = (product - probs * dots).astype(BF16)
        key_parts.append(mm(grad_scores, two_heads_doubled(block)) * scale)
        value_parts.append(mm(probs.astype(BF16), two_heads_doubled(grads)))
        moved = mm_tn(keys, grad_scores)[i * HD : (i + 1) * HD] * scale
        pair = jnp.concatenate([moved[:, :rows], moved[:, rows:]], axis=0)
        dq_out[:, pl.ds(at, 128)] = turn(jnp.transpose(pair), cosine[...], sine[...]).astype(BF16)
    even = lane_index(key_parts[0].shape) < HD
    grad_keys = jnp.where(even, key_parts[0], key_parts[1]).astype(BF16)
    grad_values = jnp.where(even, value_parts[0], value_parts[1]).astype(BF16)
    for k in range(devices):
        dkv_outs[k][0] = grad_keys[k * rows : (k + 1) * rows]
        dkv_outs[k][1] = grad_values[k * rows : (k + 1) * rows]

    @pl.when(step == pl.num_programs(0) - 1)
    def _():
        values = x[...].astype(F32)
        factor = lax.rsqrt(jnp.mean(values * values, axis=-1, keepdims=True) + epsilon)
        normed = (values * factor * gain_first[...]).astype(BF16)
        weight_grads[:, width:] = mm_tn(normed, dq_out[...]).astype(BF16)


def attend_backward(
    scal, parts, grad_out, middle, gain, attended, shared, q, lse, cosine, sine, x, gain_first, kvs
):
    rows, width = middle.shape
    devices = len(kvs)
    keys = devices * rows
    kv_specs = [pl.BlockSpec((1, rows, 128), lambda h: (0, 0, h)) for _ in kvs] + [
        pl.BlockSpec((1, rows, 128), lambda h: (1, 0, h)) for _ in kvs
    ]
    return pl.pallas_call(
        functools.partial(attend_back_kernel, devices, len(parts)),
        name="attend_backward",
        grid=(KVH // 2,),
        in_specs=[
            pl.BlockSpec(memory_space=pltpu.SMEM),
            *[fixed((rows, width)) for _ in parts],
            fixed((rows, width)),
            fixed((rows, width)),
            fixed((1, width)),
            fixed((rows, QH * HD)),
            pl.BlockSpec((QH * HD, width), lambda h: (0, 2), pipeline_mode=pl.Buffered(1)),
            pl.BlockSpec((rows, 256), lambda h: (0, h)),
            pl.BlockSpec((1, 2, 2 * rows), lambda h: (h, 0, 0)),
            fixed((rows, 128)),
            fixed((rows, 128)),
            fixed((rows, width)),
            fixed((1, width)),
            *kv_specs,
        ],
        out_specs=[
            resident((rows, width)),
            resident((width, width + QH * HD)),
            resident((1, width)),
            resident((rows, QH * HD)),
            *[pl.BlockSpec((2, rows, 128), lambda h: (0, 0, h)) for _ in kvs],
        ],
        out_shape=[
            jax.ShapeDtypeStruct((rows, width), F32),
            jax.ShapeDtypeStruct((width, width + QH * HD), BF16),
            jax.ShapeDtypeStruct((1, width), F32),
            jax.ShapeDtypeStruct((rows, QH * HD), BF16),
            *[jax.ShapeDtypeStruct((2, rows, KW), BF16) for _ in kvs],
        ],
        scratch_shapes=[pltpu.VMEM((keys, rows), F32), pltpu.VMEM((rows, QH * HD), BF16)],
        compiler_params=params(1),
        cost_estimate=cost(
            10 * rows * keys * QH * HD * 2 + 4 * rows * width * width,
            6 * width * width + 8 * keys * width + 20 * rows * width,
            rows * keys * QH,
        ),
    )(
        scal,
        *parts,
        grad_out,
        middle,
        gain,
        attended,
        shared,
        q,
        lse,
        cosine,
        sine,
        x,
        gain_first,
        *kvs,
        *kvs,
    )


def project_back_kernel(devices, x, gain, dq, *rest):
    parts, rest = rest[:devices], rest[devices:]
    grad_mid, wq, wm, cosine, sine, small, dx_out, packed = rest
    values = x[...].astype(F32)
    width = values.shape[1]
    factor = lax.rsqrt(jnp.mean(values * values, axis=-1, keepdims=True) + epsilon)
    normed = (values * factor * gain[...]).astype(BF16)
    summed = parts[0][...].astype(F32)
    for part in parts[1:]:
        summed = summed + part[...].astype(F32)
    grad_keys = [
        turn(summed[0, :, b * 128 : (b + 1) * 128], cosine[...], sine[...]).astype(BF16)
        for b in range(KW // 128)
    ]
    grad_memory = jnp.concatenate(grad_keys + [summed[1].astype(BF16)], axis=1)
    grad_query = dq[...]
    packed[:, : 2 * KW] = mm_tn(normed, grad_memory).astype(BF16)
    grad_normed = mm_nt(grad_query, wq[...]) + mm_nt(grad_memory, wm[...])
    scaled = grad_normed * gain[...]
    inner = jnp.mean(values * scaled, axis=-1, keepdims=True)
    gain_grad = jnp.sum(grad_normed * values * factor, axis=0, keepdims=True)
    row = lax.broadcasted_iota(jnp.int32, (128, width), 0)
    packed[:, 2 * KW :] = jnp.transpose(
        jnp.where(row == EXPERTS, gain_grad, small[...])
    ).astype(BF16)
    dx_out[...] = (
        grad_mid[...] + factor * scaled - values * (factor * factor * factor * inner)
    )


def project_backward(x, gain, dq, parts, grad_mid, shared, cosine, sine, small):
    rows, width = x.shape
    columns = 2 * KW + 128
    return pl.pallas_call(
        functools.partial(project_back_kernel, len(parts)),
        name="project_backward",
        grid=(1,),
        in_specs=[
            fixed((rows, width)),
            fixed((1, width)),
            fixed((rows, QH * HD)),
            *[fixed((2, rows, KW)) for _ in parts],
            fixed((rows, width)),
            pl.BlockSpec((width, QH * HD), lambda i: (0, 0), pipeline_mode=pl.Buffered(1)),
            pl.BlockSpec((width, 2 * KW), lambda i: (0, 1), pipeline_mode=pl.Buffered(1)),
            fixed((rows, 128)),
            fixed((rows, 128)),
            fixed((128, width)),
        ],
        out_specs=[resident((rows, width)), resident((width, columns))],
        out_shape=[
            jax.ShapeDtypeStruct((rows, width), F32),
            jax.ShapeDtypeStruct((width, columns), BF16),
        ],
        compiler_params=params(1),
        cost_estimate=cost(8 * rows * width * 2048, 8 * width * 2048 + 16 * rows * width),
    )(x, gain, dq, *parts, grad_mid, shared, shared, cosine, sine, small)


def pairs_within(axis, by, sections=(0, 1)):
    count = lax.axis_size(axis)
    return [(s * count + i, s * count + (i ^ by)) for s in sections for i in range(count)]


def exchanged(value, axis, by, sections=(0, 1)):
    return lax.ppermute(value, ("section", axis), pairs_within(axis, by, sections))


def swapped(value):
    return lax.ppermute(value, "section", [(0, 1), (1, 0)])


def from_all(value, axis, sections=(0, 1)):
    count = lax.axis_size(axis)
    return [value] + [exchanged(value, axis, k, sections) for k in range(1, count)]


def after(value, other):
    return lax.optimization_barrier((value, other))[0]


def scattered_sum(blocks, axis, sections):
    total = blocks[0].astype(F32)
    for k in range(1, len(blocks)):
        total = total + exchanged(blocks[k], axis, k, sections).astype(F32)
    return total


def shards(
    tokens,
    targets,
    lengths,
    routes,
    attention_gain,
    query_weight,
    memory_weight,
    output_weight,
    mixture_gain,
    router_weight,
    gate_up_weight,
    down_weight,
):
    section = lax.axis_index("section")
    context = lax.axis_index("ctx")
    line = lax.axis_index("fsdp")
    devices = lax.axis_size("ctx")
    depth = lax.axis_size("fsdp")
    first_core = section == 0
    rows, width = tokens.shape[2:]
    layers = 2
    held_experts = gate_up_weight.shape[1]
    half_held = held_experts // 2
    capacity = rows * TOPK * 9 // (EXPERTS * 8)
    slots = -(-capacity // 16) * 16
    up_rows, down_rows = gate_up_weight.shape[2], down_weight.shape[2]
    shard_rows = up_rows + down_rows

    column = context * held_experts
    plain = (column + section * half_held, half_held, 2 * devices)
    places = [plain, plain]

    pack = jnp.concatenate(
        [
            query_weight[0],
            memory_weight[0],
            output_weight[0],
            router_weight[0],
            attention_gain[0][:, None],
            mixture_gain[0][:, None],
            jnp.zeros((query_weight.shape[1], 128 - EXPERTS - 2), BF16),
        ],
        axis=1,
    )

    def shared_of_line(layer, ahead):
        mine = pack if ahead is None else after(pack, ahead)
        return jnp.concatenate(from_all(mine, "fsdp", (layer,)), axis=0)

    def shared_of_plane(layer, block, ahead):
        mine = block if ahead is None else after(block, ahead)
        owns = from_all(mine, "ctx", (layer,))
        others = [lax.ppermute(own, "section", [(layer, 1 - layer)]) for own in owns]
        scal = jnp.stack([(section == layer).astype(jnp.int32), context, line])
        whole = assemble(scal, owns, others, depth)
        small = whole[:, 3 * width :].T
        return (
            whole,
            small[:EXPERTS],
            small[EXPERTS : EXPERTS + 1].astype(F32),
            small[EXPERTS + 1 : EXPERTS + 2].astype(F32),
        )

    my_routes = jnp.swapaxes(routes[0, :, 0], 1, 2)
    other_routes = swapped(my_routes)
    layer_routes = jnp.where(
        first_core,
        jnp.stack([my_routes, other_routes]),
        jnp.stack([other_routes, my_routes])[:, ::-1],
    )
    all_routes = jnp.stack(from_all(layer_routes, "ctx"), axis=2).reshape(
        layers, 2 * devices, TOPK, rows
    )
    source_routes = [all_routes[0], all_routes[1]]
    earlier = (
        lax.broadcasted_iota(jnp.int32, (rows, rows), 0)
        < lax.broadcasted_iota(jnp.int32, (rows, rows), 1)
    ).astype(BF16)

    def ranked(layer):
        first, local, _ = places[layer]
        ids = first + jnp.arange(local, dtype=jnp.int32)
        named = jnp.any(source_routes[layer][:, None] == ids[None, :, None, None], axis=2)
        before = jnp.dot(
            named.astype(BF16).reshape(-1, rows), earlier, preferred_element_type=F32
        ).reshape(named.shape)
        return jnp.where(named, before, -1.0)

    ranks = [ranked(layer) for layer in range(layers)]
    masks = jnp.any(
        layer_routes[:, 0, None] == jnp.arange(EXPERTS, dtype=jnp.int32)[None, :, None, None], axis=2
    ).astype(F32)

    line_blocks = [after(shared_of_line(0, None), (ranks, masks)), None]

    whole = [(0, half_held)]
    split = [(0, half_held - 1), (half_held - 1, 1)] if half_held > 1 else whole
    runs = [whole, split]
    back_runs = [split, split[::-1]]

    def gathered_experts(layer, ahead):
        parts = []
        for a, n in runs[layer]:
            rows_of = lambda half: jnp.concatenate(
                [
                    weight[0, half * half_held + a : half * half_held + a + n]
                    for weight in (gate_up_weight, down_weight)
                ],
                axis=1,
            )
            arrived = lax.ppermute(rows_of(1 - layer), "section", [(layer, 1 - layer)])
            shard = jnp.where(section == layer, rows_of(layer), arrived)
            if ahead is not None:
                shard = after(shard, ahead)
            parts.append([lax.all_gather(shard, "fsdp", axis=1, tiled=True)])
        return parts

    half = rows // 2
    within = jnp.arange(rows, dtype=jnp.int32)
    positions = jnp.where(
        within < half, context * half + within, (2 * devices - 1 - context) * half + within - half
    )
    inverse = rope_base ** (-2.0 * jnp.arange(HD // 2, dtype=F32) / HD)
    angles = positions.astype(F32)[:, None] * inverse[None, :]
    sine, cosine = jnp.sin(angles), jnp.cos(angles)
    cos_table = jnp.concatenate([cosine] * 4, axis=1)
    sin_table = jnp.concatenate([-sine, sine, -sine, sine], axis=1)
    length = lengths[section, line]
    attend_scalars = jnp.stack([context, length]).astype(jnp.int32)

    def dispatched(message):
        plane = from_all(message, "ctx")
        blocks = plane + [swapped(block) for block in plane]
        return blocks

    def returned(outs):
        own, other = outs[:devices], outs[devices : 2 * devices]
        crossed = [swapped(block) for block in other]
        near = [own[0], crossed[0]]
        for k in range(1, devices):
            chip = (own[k].astype(F32) + crossed[k].astype(F32)).astype(BF16)
            near.append(exchanged(chip, "ctx", k))
        return near

    my_targets = lax.dynamic_index_in_dim(targets[:, 0], section, 0, keepdims=False)
    layer_input = lax.dynamic_index_in_dim(tokens[:, 0], section, 0, keepdims=False)
    valid = (positions < length).astype(F32)[:, None]
    saved, hidden = [], []
    early_experts = gathered_experts(0, None)
    ahead = None
    for layer in range(layers):
        first, local, sources = places[layer]
        shared, router, gain_first, gain_second = shared_of_plane(
            layer, line_blocks[layer], ahead
        )
        q, kv = project(layer_input, gain_first, shared, cos_table, sin_table)
        if layer == 0:
            line_blocks[1] = shared_of_line(1, kv)
        kvs = from_all(kv, "ctx")
        attended, lse, middle, message = attend(
            attend_scalars, layer_input, q, kvs, shared, gain_second, router, masks[layer]
        )
        messages = dispatched(message)
        if layer == 0:
            ahead = messages
            weights = early_experts
            late_experts = gathered_experts(1, message)
        else:
            weights = late_experts
        kept, outs = [], ()
        xs, gates = dispatch(
            first.astype(jnp.int32).reshape(1), messages, ranks[layer], slots, False
        )
        for (a, n), blocks in zip(runs[layer], weights):
            order = [line ^ k for k in range(depth)] if len(blocks) > 1 else range(depth)
            scal = jnp.stack([first + a, *[jnp.asarray(o) for o in order]]).astype(jnp.int32)
            run, outs = experts_forward(
                scal,
                xs,
                ranks[layer][:, a : a + n],
                gates[:, a : a + n],
                blocks,
                depth,
                slots,
                a,
                outs,
            )
            kept.append((a, n, scal, run, blocks))
        if layer == layers - 1:
            hidden_rows, mixed, grad_output, message = finish(
                returned(outs), middle, my_targets, valid
            )
            hidden.append(hidden_rows)
        else:
            mixed = functools.reduce(lambda a, b: a + b, [t.astype(F32) for t in returned(outs)])
            hidden.append((middle + mixed).astype(BF16))
        saved.append(
            dict(
                x=layer_input,
                shared=shared,
                router=router,
                gain_first=gain_first,
                gain_second=gain_second,
                q=q,
                kvs=kvs,
                attended=attended,
                lse=lse,
                middle=middle,
                kept=kept,
                xs=xs,
                gates=gates,
                mixed=mixed,
            )
        )
        layer_input = hidden[-1]

    def home_blocks(packed, layer):
        arrived = lax.ppermute(packed, "section", [(1 - layer, layer)])
        size = packed.shape[0] // devices
        return [
            (
                lax.dynamic_slice_in_dim(packed, (context ^ k) * size, size, 0).astype(F32)
                + lax.dynamic_slice_in_dim(arrived, (context ^ k) * size, size, 0).astype(F32)
            ).astype(BF16)
            for k in range(devices)
        ]

    def home_plane(blocks, layer):
        return scattered_sum(blocks, "ctx", (layer,)).astype(BF16)

    def home_line(plane, layer):
        size = plane.shape[0] // depth
        return scattered_sum(
            [
                lax.dynamic_slice_in_dim(plane, (line ^ k) * size, size, 0)
                for k in range(depth)
            ],
            "fsdp",
            (layer,),
        )

    def placed_rows(values):
        home = jnp.where(first_core, values[0], values[1])
        arrived = swapped(jnp.where(first_core, values[1], values[0]))
        return jnp.stack(
            [jnp.where(first_core, home, arrived), jnp.where(first_core, arrived, home)]
        )

    input_grads, expert_grads = [None] * layers, [None] * layers
    shared_grads = [None] * layers
    waiting = None
    summed = {}
    for layer in reversed(range(layers)):
        held = saved[layer]
        first, local, sources = places[layer]
        if layer < layers - 1:
            message = grad_message(grad_output, held["mixed"])
        messages = dispatched(message)
        if waiting is not None:
            blocks_1 = [home_blocks(part, 1) for part in waiting]
            messages = after(messages, blocks_1)
            blocks_1 = after(blocks_1, messages)
            planes = [home_plane(blocks, 1) for blocks in blocks_1]
        own_router = lax.dynamic_slice_in_dim(held["router"], first, local, 0).astype(F32)
        small = jnp.zeros((128, width), F32)
        outs = ()
        gathered = []
        steps = back_runs[layer]
        spans = [a for a, _ in steps]
        for at, (a, n) in enumerate(steps):
            base, _, scal, run, blocks = next(
                kept for kept in held["kept"] if kept[0] <= a and a + n <= kept[0] + kept[1]
            )
            scal = jnp.concatenate([scal[:1] + (a - base), scal[1:]])
            last = None
            if at == len(steps) - 1:
                order = tuple(sorted(range(len(spans)), key=lambda i: spans[i]))
                last = (ranks[layer], [rows_of for rows_of in outs], order)
            grad_rows, inners = dispatch(
                scal[:1], messages, ranks[layer][:, a : a + n], slots, True
            )
            grads, router_grad, rows_out = experts_backward(
                scal,
                grad_rows,
                ranks[layer][:, a : a + n],
                held["gates"][:, a : a + n],
                inners,
                held["xs"],
                run,
                own_router[a : a + n, None, :],
                blocks,
                depth,
                slots,
                a,
                a - base,
                last,
            )
            outs = rows_out if last else list(outs) + rows_out
            if layer == 1 and at == 0:
                error = jnp.sum(inners[:, 1, 0])
            small = lax.dynamic_update_slice_in_dim(small, router_grad[:, 0], first + a, 0)
            gathered.append(grads)
        summed[layer] = [
            lax.psum_scatter(grads, "fsdp", scatter_dimension=1, tiled=True)
            for grads in gathered
        ]
        expert_grads[layer] = list(zip(spans, summed[layer]))
        if layer == 1:
            grad_output = after(grad_output, summed[1][0])
        else:
            grad_output = after(grad_output, summed[1][-1])
            outs = after(outs, planes)
        back = attend_backward(
            attend_scalars,
            returned(outs),
            grad_output,
            held["middle"],
            held["gain_second"],
            held["attended"],
            held["shared"],
            held["q"],
            held["lse"],
            cos_table,
            -sin_table,
            held["x"],
            held["gain_first"],
            held["kvs"],
        )
        grad_mid, weight_grads, gain_second_grad, dq = back[:4]
        dkv = back[4:]
        parts = [dkv[0]] + [exchanged(dkv[k], "ctx", k) for k in range(1, devices)]
        if layer == 0:
            outward = home_blocks(weight_grads, 0)
            grad_mid = after(grad_mid, outward)
        else:
            by = 1
            while by < depth:
                error = error + lax.ppermute(error, "fsdp", [(i, i ^ by) for i in range(depth)])
                by *= 2
            loss_value = error / jnp.sum(lengths).astype(F32)
            hidden_out = placed_rows(hidden)
            grad_mid = after(grad_mid, (loss_value, hidden_out))
        small = lax.dynamic_update_slice_in_dim(small, gain_second_grad, EXPERTS + 1, 0)
        dx, packed = project_backward(
            held["x"],
            held["gain_first"],
            dq,
            parts,
            grad_mid,
            held["shared"],
            cos_table,
            -sin_table,
            small,
        )
        input_grads[layer] = dx
        grad_output = dx.astype(BF16).astype(F32)
        if layer == 1:
            waiting = (weight_grads, packed)
        else:
            outward, planes = after((outward, planes), packed)
            shared_grads[0] = [
                home_line(home_plane(blocks, 0), 0) for blocks in (home_blocks(packed, 0), outward)
            ][::-1]
            shared_grads[1] = [home_line(part, 1) for part in planes]

    pick = lambda values: jnp.where(first_core, values[0], values[1])
    outward, inward = (pick([shared_grads[0][i], shared_grads[1][i]]) for i in range(2))
    input_out = placed_rows(input_grads)
    def pieces_of(layer, at, part):
        arrived = lax.ppermute(part, "section", [(1 - layer, layer)])
        return [
            (layer, half * half_held + at, term)
            for half, term in ((layer, part), (1 - layer, arrived))
        ]

    def placed(pieces, experts, into):
        touched = [p for p in pieces if any(0 <= e - p[1] < p[2].shape[0] for e in experts)]
        return place_experts(
            section.astype(jnp.int32).reshape(1), touched, held_experts, up_rows, experts, into
        )

    parts = [(layer, at, part) for layer in (1, 0) for at, part in expert_grads[layer]]
    pieces = [piece for part in parts[:-1] for piece in pieces_of(*part)]
    layer, at, part = parts[-1]
    last = [half * half_held + at + i for half in range(2) for i in range(part.shape[0])]
    sums = ()
    if len(last) < held_experts:
        sums = placed(pieces, [e for e in range(held_experts) if e not in last], ())
        outward, inward = after((outward, inward), sums)
        part = after(part, (outward, inward, input_out))
    up_sum, down_sum = placed(pieces + pieces_of(layer, at, part), last, sums)
    at = 2 * KW
    return (
        hidden_out[None, :, None],
        input_out[None, :, None],
        loss_value,
        inward[:, at + EXPERTS][None],
        outward[:, width:][None],
        inward[:, :at][None],
        outward[:, :width][None],
        inward[:, at + EXPERTS + 1][None],
        inward[:, at : at + EXPERTS][None],
        up_sum[None],
        down_sum[None],
    )


def solution(mesh):
    placed = (
        P(None, "fsdp", "ctx", None),
        P(None, "fsdp", "ctx", None),
        P(),
        P("section", None, "fsdp", "ctx", None),
        P("section", ("ctx", "fsdp")),
        P("section", ("ctx", "fsdp"), None),
        P("section", ("ctx", "fsdp"), None),
        P("section", ("ctx", "fsdp"), None),
        P("section", ("ctx", "fsdp")),
        P("section", ("ctx", "fsdp"), None),
        P("section", "ctx", "fsdp", None),
        P("section", "ctx", "fsdp", None),
    )
    return jax.shard_map(
        shards,
        mesh=mesh,
        in_specs=placed,
        out_specs=(
            P("section", None, "fsdp", "ctx", None),
            P("section", None, "fsdp", "ctx", None),
            P(),
            P("section", ("ctx", "fsdp")),
            P("section", ("ctx", "fsdp"), None),
            P("section", ("ctx", "fsdp"), None),
            P("section", ("ctx", "fsdp"), None),
            P("section", ("ctx", "fsdp")),
            P("section", ("ctx", "fsdp"), None),
            P("section", "ctx", "fsdp", None),
            P("section", "ctx", "fsdp", None),
        ),
        check_vma=False,
    )
```

```python
import functools
import math

import jax
import jax.numpy as jnp
from jax import lax
from jax.experimental import pallas as pl
from jax.experimental.pallas import tpu as pltpu
from jax.sharding import PartitionSpec as P

QH = 16
KVH = 8
HD = 64
EXPERTS = 32
FF_E = 512
TOPK = 8
KW = KVH * HD
EXT = 16

epsilon = 1e-06
rope_base = 10000.0
negative = -1e30
F32 = jnp.float32
BF16 = jnp.bfloat16
VMEM_LIMIT = 60 * 1024 * 1024


def params(grid_dims=0):
    return pltpu.CompilerParams(
        vmem_limit_bytes=VMEM_LIMIT,
        dimension_semantics=("arbitrary",) * grid_dims if grid_dims else None,
    )


def cost(flops, moved, exps=0, share=1.0):
    return pl.CostEstimate(
        flops=int(flops / share), bytes_accessed=int(moved), transcendentals=int(exps)
    )


def mm(a, b):
    return jnp.dot(a, b, preferred_element_type=F32)


def mm_nt(a, b):
    return lax.dot_general(a, b, (((1,), (1,)), ((), ())), preferred_element_type=F32)


def mm_tn(a, b):
    return lax.dot_general(a, b, (((0,), (0,)), ((), ())), preferred_element_type=F32)


def fixed(shape):
    return pl.BlockSpec(shape, lambda *_: (0,) * len(shape), pipeline_mode=pl.Buffered(1))


def resident(shape):
    return pl.BlockSpec(shape, lambda *_: (0,) * len(shape))


def lane_index(shape):
    return lax.broadcasted_iota(jnp.int32, shape, len(shape) - 1)


def turn(block, cosine, sine):
    low_half = lane_index(block.shape) % HD < HD // 2
    swapped = jnp.where(
        low_half, pltpu.roll(block, 128 - HD // 2, axis=1), pltpu.roll(block, HD // 2, axis=1)
    )
    return block * cosine + swapped * sine


def rolled(block):
    return pltpu.roll(block.astype(F32), HD, axis=1).astype(BF16)


def key_positions(device, half, devices, shape, dim):
    within = lax.broadcasted_iota(jnp.int32, shape, dim)
    return jnp.where(
        within < half, device * half + within, (2 * devices - 1 - device) * half + within - half
    )


def fill_bias(bias, scal, devices, rows):
    context, length = scal[0], scal[1]
    query_pos = key_positions(context, rows // 2, devices, (rows, rows), 1)
    for k in range(devices):
        key_pos = key_positions(context ^ k, rows // 2, devices, (rows, rows), 0)
        taken = (key_pos <= query_pos) & (key_pos < length)
        bias[k * rows : (k + 1) * rows, :] = jnp.where(taken, 0.0, negative)


def two_heads(block):
    even = lane_index(block.shape) < HD
    zero = jnp.zeros((), block.dtype)
    return jnp.concatenate([jnp.where(even, block, zero), jnp.where(even, zero, block)], axis=0)


def two_heads_doubled(block):
    even = lane_index(block.shape) < HD
    other = rolled(block)
    return jnp.concatenate([jnp.where(even, block, other), jnp.where(even, other, block)], axis=0)


def doubled(block, odd):
    even = lane_index(block.shape) < HD
    other = rolled(block)
    return jnp.where(even, other, block) if odd else jnp.where(even, block, other)


def one_hot(rank_row, slots):
    rows = rank_row.shape[-1]
    index = lax.broadcasted_iota(jnp.int32, (slots, rows), 0).astype(F32)
    return rank_row == index


def project_kernel(x, gain, wq, wm, cosine, sine, q_out, kv_out):
    values = x[...].astype(F32)
    factor = lax.rsqrt(jnp.mean(values * values, axis=-1, keepdims=True) + epsilon)
    normed = (values * factor * gain[...]).astype(BF16)
    cos, sin = cosine[...], sine[...]
    q0 = mm(normed, wq[...])
    for b in range(QH * HD // 128):
        at = slice(b * 128, (b + 1) * 128)
        q_out[:, at] = turn(q0[:, at], cos, sin).astype(BF16)
    kv0 = mm(normed, wm[...])
    for b in range(KW // 128):
        at = slice(b * 128, (b + 1) * 128)
        kv_out[0, :, at] = turn(kv0[:, at], cos, sin).astype(BF16)
    kv_out[1] = kv0[:, KW:].astype(BF16)


def project(x, gain, shared, cosine, sine):
    rows, width = x.shape
    return pl.pallas_call(
        project_kernel,
        name="project",
        grid=(1,),
        in_specs=[
            fixed((rows, width)),
            fixed((1, width)),
            pl.BlockSpec((width, QH * HD), lambda i: (0, 0), pipeline_mode=pl.Buffered(1)),
            pl.BlockSpec((width, 2 * KW), lambda i: (0, 1), pipeline_mode=pl.Buffered(1)),
            fixed((rows, 128)),
            fixed((rows, 128)),
        ],
        out_specs=[resident((rows, QH * HD)), resident((2, rows, KW))],
        out_shape=[
            jax.ShapeDtypeStruct((rows, QH * HD), BF16),
            jax.ShapeDtypeStruct((2, rows, KW), BF16),
        ],
        compiler_params=params(1),
        cost_estimate=cost(
            2 * rows * width * 2048, 2 * width * 2048 + 8 * rows * width, share=0.2
        ),
    )(x, gain, shared, shared, cosine, sine)


def attend_kernel(devices, scal, x, q, *rest):
    ks, vs, rest = rest[:devices], rest[devices : 2 * devices], rest[2 * devices :]
    wo, gain, router, mask, o_out, lse_out, mid_out, msg_out, bias, held = rest
    rows = x.shape[0]
    step = pl.program_id(0)

    @pl.when(step == 0)
    def _():
        fill_bias(bias, scal, devices, rows)

    keys = jnp.concatenate([r[0] for r in ks], axis=0)
    values = jnp.concatenate([r[0] for r in vs], axis=0)
    block_bias = bias[...]
    both_bias = jnp.concatenate([block_bias, block_bias], axis=1)
    for i in range(2):
        query = two_heads(q[:, i * 128 : (i + 1) * 128])
        scores = mm_nt(doubled(keys, i), query) * (1.0 / math.sqrt(HD)) + both_bias
        top = jnp.max(scores, axis=0, keepdims=True)
        raised = jnp.exp(scores - top)
        total = jnp.sum(raised, axis=0, keepdims=True)
        probs = (raised * (1.0 / total)).astype(BF16)
        lse_out[0, i : i + 1, :] = top + jnp.log(total)
        mixed = mm_tn(values, probs)[i * HD : (i + 1) * HD]
        pair = jnp.concatenate([mixed[:, :rows], mixed[:, rows:]], axis=0)
        at = pl.multiple_of(step * 256 + i * 128, 128)
        held[:, pl.ds(at, 128)] = jnp.transpose(pair).astype(BF16)

    @pl.when(step == pl.num_programs(0) - 1)
    def _():
        attended = held[...]
        o_out[...] = attended
        middle = x[...].astype(F32) + mm(attended, wo[...])
        mid_out[...] = middle
        factor = lax.rsqrt(jnp.mean(middle * middle, axis=-1, keepdims=True) + epsilon)
        normed = (middle * factor * gain[...]).astype(BF16)
        msg_out[:rows, :] = normed
        logits = mm_nt(router[...], normed)
        chosen = mask[...] > 0.5
        top = jnp.max(jnp.where(chosen, logits, negative), axis=0, keepdims=True)
        raised = jnp.where(chosen, jnp.exp(jnp.where(chosen, logits - top, 0.0)), 0.0)
        gates = raised / jnp.sum(raised, axis=0, keepdims=True)
        high = gates.astype(BF16)
        low = (gates - high.astype(F32)).astype(BF16)
        ext = [high[:EXT], high[EXT:], low[:EXT], low[EXT:]]
        if 4 * rows < x.shape[1]:
            ext.append(jnp.zeros((EXT, x.shape[1] - 4 * rows), BF16))
        msg_out[rows:, :] = jnp.concatenate(ext, axis=1)


def attend(scal, x, q, kvs, shared, gain, router, mask):
    rows, width = x.shape
    devices = len(kvs)
    keys = devices * rows
    kv_specs = [pl.BlockSpec((1, rows, 128), lambda h: (0, 0, h)) for _ in kvs] + [
        pl.BlockSpec((1, rows, 128), lambda h: (1, 0, h)) for _ in kvs
    ]
    return pl.pallas_call(
        functools.partial(attend_kernel, devices),
        name="attend",
        grid=(KVH // 2,),
        in_specs=[
            pl.BlockSpec(memory_space=pltpu.SMEM),
            fixed((rows, width)),
            pl.BlockSpec((rows, 256), lambda h: (0, h)),
            *kv_specs,
            pl.BlockSpec((QH * HD, width), lambda h: (0, 2), pipeline_mode=pl.Buffered(1)),
            fixed((1, width)),
            fixed((EXPERTS, width)),
            fixed((EXPERTS, rows)),
        ],
        out_specs=[
            resident((rows, QH * HD)),
            pl.BlockSpec((1, 2, 2 * rows), lambda h: (h, 0, 0)),
            resident((rows, width)),
            resident((rows + EXT, width)),
        ],
        out_shape=[
            jax.ShapeDtypeStruct((rows, QH * HD), BF16),
            jax.ShapeDtypeStruct((KVH // 2, 2, 2 * rows), F32),
            jax.ShapeDtypeStruct((rows, width), F32),
            jax.ShapeDtypeStruct((rows + EXT, width), BF16),
        ],
        scratch_shapes=[pltpu.VMEM((keys, rows), F32), pltpu.VMEM((rows, QH * HD), BF16)],
        compiler_params=params(1),
        cost_estimate=cost(
            4 * rows * keys * QH * HD * 2 + 2 * rows * width * width,
            2 * width * width + 4 * keys * width + 12 * rows * width,
            rows * keys * QH,
            0.17,
        ),
    )(scal, x, q, *kvs, *kvs, shared, gain, router, mask)


def hot_rows(rank, j, slots):
    local = rank.shape[1]
    return jnp.concatenate(
        [
            jnp.where(one_hot(rank[j, i : i + 1, :], slots), 1.0, 0.0).astype(BF16)
            for i in range(local)
        ],
        axis=0,
    )


def combine(rank, held, prior, outs, buffers, slots):
    held = held if isinstance(held, list) else [held]
    prior_buffer, out_buffer, prior_sems, out_sems = buffers
    width = held[0].shape[-1]
    depth = out_buffer.shape[0]
    count = len(outs)
    fetch = lambda j: pltpu.make_async_copy(
        prior[j], prior_buffer.at[j % depth], prior_sems.at[j % depth]
    )
    send = lambda j: pltpu.make_async_copy(
        out_buffer.at[j % depth], outs[j], out_sems.at[j % depth]
    )
    for j in range(min(depth - 1, count) if prior else 0):
        fetch(j).start()
    for j in range(count):
        rows = [part[:, j].reshape(part.shape[0] * slots, width) for part in held]
        rows = rows[0] if len(rows) == 1 else jnp.concatenate(rows, axis=0)
        total = mm_tn(hot_rows(rank, j, slots), rows)
        if prior:
            if j + depth - 1 < count:
                fetch(j + depth - 1).start()
            fetch(j).wait()
            total = total + prior_buffer[j % depth].astype(F32)
        if j >= depth:
            send(j - depth).wait()
        out_buffer[j % depth] = total.astype(BF16)
        send(j).start()
    for j in range(max(0, count - depth), count):
        send(j).wait()


def gate_columns(rank, values, step, sources, slots):
    columns = []
    for j in sources:
        hot = one_hot(rank[j, pl.ds(step, 1), :], slots)
        columns.append(jnp.sum(jnp.where(hot, values(j), 0.0), axis=1, keepdims=True))
    return jnp.concatenate(columns, axis=0)


def finish_kernel(count, routed, slots, *refs):
    terms, (middle, goal, valid, refs) = refs[:count], (*refs[count : count + 3], refs[count + 3 :])
    if routed:
        rank, refs = refs[0], refs[1:]
        arrived, refs = refs[:routed], refs[routed:]
    hidden, mixed_out, grad_out, message, refs = *refs[:4], refs[4:]
    rows, width = middle.shape
    mixed = terms[0][...].astype(F32)
    for term in terms[1:]:
        mixed = mixed + term[...].astype(F32)
    if routed:
        given = jnp.concatenate([ref[...].reshape(-1, width) for ref in arrived], axis=0)
        hots = [
            jnp.where(one_hot(rank[i : i + 1, :], slots), 1.0, 0.0).astype(BF16)
            for i in range(rank.shape[0])
        ]
        mixed = mixed + mm_tn(jnp.concatenate(hots, axis=0), given)
    output = middle[...] + mixed
    hidden[...] = output.astype(BF16)
    mixed_out[...] = mixed
    grad = (output - goal[...].astype(F32)) * valid[...]
    grad_out[...] = grad
    error = 0.5 * jnp.sum(jnp.sum(grad * grad, axis=1, keepdims=True), axis=0, keepdims=True)
    fill_message(message, grad, mixed, error)
    if routed:
        low = message[:rows, :]
        inner = message[rows:, :rows]
        for i, hot in enumerate(hots):
            out = refs[i // 2]
            out[i % 2, :slots, :] = mm(hot, low).astype(BF16)
            spread = jnp.where(one_hot(rank[i : i + 1, :], 128), 1.0, 0.0).astype(BF16)
            out[i % 2, slots:, :128] = mm_nt(inner, spread).astype(BF16)
            out[i % 2, slots:, 128:] = jnp.zeros((EXT, width - 128), BF16)


def finish(terms, middle, goal, valid, rank=None, arrived=(), slots=0):
    rows, width = middle.shape
    messages = len(rank) // 2 if arrived else 0
    return pl.pallas_call(
        functools.partial(finish_kernel, len(terms), len(arrived), slots),
        name="finish",
        out_shape=[
            jax.ShapeDtypeStruct((rows, width), BF16),
            jax.ShapeDtypeStruct((rows, width), F32),
            jax.ShapeDtypeStruct((rows, width), F32),
            jax.ShapeDtypeStruct((rows + EXT, width), BF16),
            *[jax.ShapeDtypeStruct((2, slots + EXT, width), BF16) for _ in range(messages)],
        ],
        compiler_params=params(),
        cost_estimate=cost(8 * rows * width, 24 * rows * width),
    )(*terms, middle, goal, valid, *([rank, *arrived] if arrived else []))


def fill_message(message, grad, mixed, error):
    rows, width = grad.shape
    message[:rows, :] = grad.astype(BF16)
    inner = jnp.transpose(
        jnp.broadcast_to(jnp.sum(grad * mixed, axis=1, keepdims=True), (rows, 128))
    )[:EXT]
    high = inner.astype(BF16)
    low = (inner - high.astype(F32)).astype(BF16)
    row = lax.broadcasted_iota(jnp.int32, (EXT, rows), 0)
    ext = jnp.where(row == 0, high.astype(F32), jnp.where(row == 1, low.astype(F32), 0.0))
    for at in range(2, 5):
        term = error.astype(BF16).astype(F32)
        ext = jnp.where(row == at, term, ext)
        error = error - term
    message[rows:, :rows] = ext.astype(BF16)
    message[rows:, rows:] = jnp.zeros((EXT, width - rows), BF16)


def message_kernel(grad, mixed, message):
    fill_message(message, grad[...], mixed[...], jnp.zeros((1, 1), F32))


def grad_message(grad, mixed):
    rows, width = grad.shape
    return pl.pallas_call(
        message_kernel,
        name="grad_message",
        out_shape=jax.ShapeDtypeStruct((rows + EXT, width), BF16),
        compiler_params=params(),
        cost_estimate=cost(4 * rows * width, 10 * rows * width),
    )(grad, mixed)


def dispatch_kernel(sources, slots, backward, scal, *rest):
    msgs, (rank, x_out, side_out, arrived, picked, in_sems, out_sems) = (
        rest[:sources],
        rest[sources:],
    )
    local, rows = rank.shape[1:]
    fetch = lambda j: pltpu.make_async_copy(msgs[j], arrived.at[j], in_sems.at[j])
    send = lambda j: pltpu.make_async_copy(picked.at[j], x_out.at[:, j], out_sems.at[j])
    for j in range(sources):
        fetch(j).start()
    pick_row = lax.broadcasted_iota(jnp.int32, (EXT, 4 * rows), 0)
    for j in range(sources):
        fetch(j).wait()
        taken = mm(hot_rows(rank, j, slots), arrived[j, :rows, :]).astype(BF16)
        for i in range(local):
            picked[j, i] = taken[i * slots : (i + 1) * slots]
        send(j).start()
        if backward:
            ext = arrived[j, rows:, :rows].astype(F32)
            side_out[j, 0:1, :] = ext[0:1, :] + ext[1:2, :]
            side_out[j, 1:2, :] = ext[2:3, :] + ext[3:4, :] + ext[4:5, :]
        else:
            ext = arrived[j, rows:, : 4 * rows].astype(F32)
            for i in range(local):
                expert = scal[0] + i
                row = jnp.sum(jnp.where(pick_row == expert % EXT, ext, 0.0), axis=0, keepdims=True)
                high = jnp.where(expert < EXT, row[:, :rows], row[:, rows : 2 * rows])
                low = jnp.where(expert < EXT, row[:, 2 * rows : 3 * rows], row[:, 3 * rows :])
                side_out[j, i : i + 1, :] = high + low
    for j in range(sources):
        send(j).wait()


def dispatch(scal, msgs, rank, slots, backward):
    sources, local, rows = rank.shape
    width = msgs[0].shape[1]
    anywhere = pl.BlockSpec(memory_space=pl.ANY)
    side = (sources, 2 if backward else local, rows)
    taken, beside = pl.pallas_call(
        functools.partial(dispatch_kernel, sources, slots, backward),
        name="dispatch",
        grid=(1,),
        in_specs=[
            pl.BlockSpec(memory_space=pltpu.SMEM),
            *[anywhere for _ in msgs],
            fixed(rank.shape),
        ],
        out_specs=[anywhere, resident(side)],
        out_shape=[
            jax.ShapeDtypeStruct((local, sources, slots, width), BF16),
            jax.ShapeDtypeStruct(side, F32),
        ],
        scratch_shapes=[
            pltpu.VMEM((sources, rows + EXT, width), BF16),
            pltpu.VMEM((sources, local, slots, width), BF16),
            pltpu.SemaphoreType.DMA((sources,)),
            pltpu.SemaphoreType.DMA((sources,)),
        ],
        compiler_params=params(1),
        cost_estimate=cost(
            2 * local * sources * slots * rows * width,
            2 * sources * width * (rows + local * slots),
            0,
            0.05 * local,
        ),
    )(scal, *msgs, rank)
    return taken.reshape(local, sources * slots, width), beside


def fill_weights(scal, blocks, w1, w2):
    up = w1.shape[0] // len(blocks)
    down = w2.shape[0] // len(blocks)
    for k, block in enumerate(blocks):
        at = scal[1 + k]
        w1[pl.ds(pl.multiple_of(at * up, up), up), :] = block[0, :up]
        w2[pl.ds(pl.multiple_of(at * down, down), down), :] = block[0, up:]


def experts_kernel(sources, depth, slots, chained, combined, scal, *rest):
    prior = ()
    if chained:
        prior, rest = rest[:sources], rest[sources:]
    rank, gates, xs, rest = *rest[:3], rest[3:]
    blocks, rest = rest[:depth], rest[depth:]
    gu_out, y_out, rest = *rest[:2], rest[2:]
    if combined:
        outs, rest = rest[:sources], rest[sources:]
        held, w1, w2 = rest[:3]
    else:
        rows_out, w1, w2 = rest
    width = w1.shape[0]
    step, part = pl.program_id(0), pl.program_id(1)
    portions = sources // (xs.shape[1] // slots)
    portion = sources // portions

    @pl.when(part == 0)
    def _():
        fill_weights(scal, blocks, w1, w2)

    gate_up = mm(xs[0], w1[...])
    gu_out[0] = gate_up
    gate, up = gate_up[:, :FF_E], gate_up[:, FF_E:]
    activated = (gate * jax.nn.sigmoid(gate) * up).astype(BF16)
    out = mm(activated, w2[...]).astype(BF16)
    y_out[0] = out
    column = gate_columns(
        rank,
        lambda j: gates[j, pl.ds(step, 1), :],
        step,
        [part * portion + n for n in range(portion)],
        slots,
    )
    given = (column * out.astype(F32)).astype(BF16).reshape(portion, slots, width)
    if combined:
        held[step, pl.ds(part * portion, portion)] = given

        @pl.when((step == pl.num_programs(0) - 1) & (part == portions - 1))
        def _():
            combine(rank, held, prior, outs, rest[3:], slots)

    else:
        rows_out[0] = given


def weight_specs(blocks, depth, base=0):
    arrays = blocks if len(blocks) == depth else blocks * depth
    rows = arrays[0].shape[1] // (depth // len(blocks))
    width = arrays[0].shape[2]
    specs = [
        pl.BlockSpec((1, rows, width), lambda e, r, f=(k if len(blocks) == 1 else 0): (e + base, f, 0))
        for k in range(depth)
    ]
    return arrays, specs


def stream_scratch(rows, width):
    return [
        pltpu.VMEM((4, rows, width), BF16),
        pltpu.VMEM((4, rows, width), BF16),
        pltpu.SemaphoreType.DMA((4,)),
        pltpu.SemaphoreType.DMA((4,)),
    ]


def experts_forward(scal, xs, rank, gates, blocks, depth, slots, first, prior=(), combined=True):
    sources, local, rows = rank.shape
    width = xs.shape[2]
    portions = max(1, sources // 8)
    count = sources * slots
    arrays, specs = weight_specs(blocks, depth)
    anywhere = pl.BlockSpec(memory_space=pl.ANY)
    each = lambda shape, base=0: pl.BlockSpec((1,) + shape, lambda e, r: (e + base, r, 0))
    outs = pl.pallas_call(
        functools.partial(experts_kernel, sources, depth, slots, bool(prior), combined),
        name="experts_forward",
        grid=(local, portions),
        in_specs=[
            pl.BlockSpec(memory_space=pltpu.SMEM),
            *[anywhere for _ in prior],
            fixed((sources, local, rows)),
            fixed((sources, local, rows)),
            each((count // portions, width), first),
            *specs,
        ],
        out_specs=[
            each((count // portions, 2 * FF_E)),
            each((count // portions, width)),
            *(
                [anywhere] * sources
                if combined
                else [
                    pl.BlockSpec((1, sources // portions, slots, width), lambda e, r: (e, r, 0, 0))
                ]
            ),
        ],
        out_shape=[
            jax.ShapeDtypeStruct((local, count, 2 * FF_E), F32),
            jax.ShapeDtypeStruct((local, count, width), BF16),
            *(
                [jax.ShapeDtypeStruct((rows, width), BF16)] * sources
                if combined
                else [jax.ShapeDtypeStruct((local, sources, slots, width), BF16)]
            ),
        ],
        scratch_shapes=[
            *([pltpu.VMEM((local, sources, slots, width), BF16)] if combined else []),
            pltpu.VMEM((width, 2 * FF_E), BF16),
            pltpu.VMEM((FF_E, width), BF16),
            *(stream_scratch(rows, width) if combined else []),
        ],
        compiler_params=params(2),
        cost_estimate=cost(
            2 * local * count * width * 3 * FF_E * 1.3,
            8 * local * count * width,
            local * count * FF_E,
            0.1 * (local + 1),
        ),
    )(scal, *prior, rank, gates, xs, *arrays)
    return outs[:2], list(outs[2:])


def experts_back_kernel(sources, depth, slots, mode, scal, *rest):
    last, order, direct = mode
    earlier = ()
    if last:
        full_rank, rest = rest[0], rest[1:]
        earlier, rest = rest[: len(order) - 1], rest[len(order) - 1 :]
    if direct:
        rank, gates, rest = *rest[:2], rest[2:]
        given_rows, rest = rest[:sources], rest[sources:]
    else:
        rank, gates, inners, grads, rest = *rest[:4], rest[4:]
    xs, gu, ys, router, rest = *rest[:4], rest[4:]
    blocks, rest = rest[:depth], rest[depth:]
    grad_out_ref, router_out, rest = *rest[:2], rest[2:]
    outs, rest = (rest[:sources], rest[sources:]) if last else (rest[:1], rest[1:])
    held, w1, w2, sum1, sum2 = rest[:5]
    width = w1.shape[0]
    step, part = pl.program_id(0), pl.program_id(1)
    portions = sources // (xs.shape[1] // slots)
    portion = sources // portions

    @pl.when(part == 0)
    def _():
        fill_weights(scal, blocks, w1, w2)

    mine = [part * portion + n for n in range(portion)]
    gate_column = gate_columns(rank, lambda j: gates[j, pl.ds(step, 1), :], step, mine, slots)
    if direct:
        blocks_of = [ref[0] if len(ref.shape) == 3 else ref[...] for ref in given_rows]
        grad_out = jnp.concatenate([block[:slots] for block in blocks_of], axis=0).astype(F32)
        inner_column = jnp.concatenate(
            [
                jnp.transpose(block[slots:, :128].astype(F32))[:slots, :2].sum(axis=1, keepdims=True)
                for block in blocks_of
            ],
            axis=0,
        )
    else:
        inner_column = gate_columns(rank, lambda j: inners[j, 0:1, :], step, mine, slots)
        grad_out = grads[0].astype(F32)
    grad_y = (gate_column * grad_out).astype(BF16)
    given = jnp.sum(grad_out * ys[0].astype(F32), axis=1, keepdims=True)
    grad_logit = gate_column * (given - inner_column)
    gate, up = gu[0, :, :FF_E], gu[0, :, FF_E:]
    sigmoid = jax.nn.sigmoid(gate)
    silu = gate * sigmoid
    activated = (silu * up).astype(BF16)
    down_part = mm_tn(activated, grad_y)
    grad_act = mm_nt(grad_y, w2[...])
    grad_gate = grad_act * up * sigmoid * (1.0 + gate * (1.0 - sigmoid))
    grad_up = grad_act * silu
    grad_gate_up = jnp.concatenate([grad_gate.astype(BF16), grad_up.astype(BF16)], axis=1)
    taken = xs[0]
    up_part = mm_tn(taken, grad_gate_up)
    router_part = jnp.sum(taken.astype(F32) * grad_logit, axis=0, keepdims=True)
    grad_rows = mm_nt(grad_gate_up, w1[...]) + grad_logit * router[0]
    if last:
        held[step, pl.ds(part * portion, portion)] = grad_rows.astype(BF16).reshape(
            portion, slots, width
        )
    else:
        outs[0][0] = grad_rows.astype(BF16)

    def write(up_total, down_total):
        up_rows, down_rows = width // depth, FF_E // depth
        for f in range(depth):
            top = f * (up_rows + down_rows)
            grad_out_ref[0, top : top + up_rows, :] = up_total[
                f * up_rows : (f + 1) * up_rows
            ].astype(BF16)
            grad_out_ref[0, top + up_rows : top + up_rows + down_rows, :] = down_total[
                f * down_rows : (f + 1) * down_rows
            ].astype(BF16)

    if sum1 is None:
        write(up_part, down_part)
        router_out[0] = router_part
    else:

        @pl.when(part == 0)
        def _():
            sum1[...] = up_part
            sum2[...] = down_part
            router_out[0] = router_part

        @pl.when(part > 0)
        def _():
            sum1[...] += up_part
            sum2[...] += down_part
            router_out[0] += router_part

        @pl.when(part == portions - 1)
        def _():
            write(sum1, sum2)

    if last:

        @pl.when((step == pl.num_programs(0) - 1) & (part == portions - 1))
        def _():
            pieces = list(earlier) + [held]
            combine(full_rank, [pieces[o] for o in order], (), outs, rest[5:], slots)


def experts_backward(
    scal, grads, rank, gates, inners, xs, kept, router, blocks, depth, slots, first, base, begin, last
):
    direct = isinstance(grads, list)
    sources, local, rows = rank.shape
    width = xs.shape[2]
    portions = max(1, sources // 8)
    count = sources * slots
    gu, ys = kept
    arrays, specs = weight_specs(blocks, depth, base)
    merged = width + FF_E
    anywhere = pl.BlockSpec(memory_space=pl.ANY)
    each = lambda shape, base=0: pl.BlockSpec((1,) + shape, lambda e, r: (e + base, r, 0))
    whole = lambda shape: pl.BlockSpec((1,) + shape, lambda e, r: (e, 0, 0))
    before = []
    if last:
        before = [last[0]] + [
            part.reshape(part.shape[0], sources, slots, width) for part in last[1]
        ]
    mode = (bool(last), last[2] if last else (), direct)
    if direct:
        given = grads
        given_specs = [
            fixed(block.shape)
            if block.ndim == 2
            else pl.BlockSpec(
                (1,) + block.shape[1:], lambda *_: (0, 0, 0), pipeline_mode=pl.Buffered(1)
            )
            for block in grads
        ]
    else:
        given = [inners, grads]
        given_specs = [fixed((sources, 2, rows)), each((count // portions, width), begin)]

    def kernel(*refs):
        refs = list(refs)
        if portions == 1:
            at = len(refs) - (4 if last else 0)
            refs[at:at] = [None, None]
        if not last:
            refs[-4:-4] = [None]
        experts_back_kernel(sources, depth, slots, mode, *refs)

    sums = [pltpu.VMEM((width, 2 * FF_E), F32), pltpu.VMEM((FF_E, width), F32)]
    outs = pl.pallas_call(
        kernel,
        name="experts_backward",
        grid=(local, portions),
        in_specs=[
            pl.BlockSpec(memory_space=pltpu.SMEM),
            *[fixed(part.shape) for part in before],
            fixed((sources, local, rows)),
            fixed((sources, local, rows)),
            *given_specs,
            each((count // portions, width), first),
            each((count // portions, 2 * FF_E), base),
            each((count // portions, width), base),
            whole((1, width)),
            *specs,
        ],
        out_specs=[
            whole((merged, width)),
            whole((1, width)),
            *([anywhere] * sources if last else [each((count // portions, width))]),
        ],
        out_shape=[
            jax.ShapeDtypeStruct((local, merged, width), BF16),
            jax.ShapeDtypeStruct((local, 1, width), F32),
            *(
                [jax.ShapeDtypeStruct((rows, width), BF16)] * sources
                if last
                else [jax.ShapeDtypeStruct((local, count, width), BF16)]
            ),
        ],
        scratch_shapes=[
            *([pltpu.VMEM((local, sources, slots, width), BF16)] if last else []),
            pltpu.VMEM((width, 2 * FF_E), BF16),
            pltpu.VMEM((FF_E, width), BF16),
            *(sums if portions > 1 else []),
            *(stream_scratch(rows, width) if last else []),
        ],
        compiler_params=params(2),
        cost_estimate=cost(
            2 * local * count * width * 3 * FF_E * 2.3,
            14 * local * count * width,
            local * count * FF_E,
            0.37,
        ),
    )(scal, *before, rank, gates, *given, xs, gu, ys, router, *arrays)
    return outs[0], outs[1], list(outs[2:])


def place_kernel(places, number, aliased, scal, *refs):
    parts, (up_out, down_out) = refs[: -2 - aliased], refs[-2:]
    step = number(pl.program_id(0))
    up_rows = up_out.shape[1]

    def put(block):
        up_out[0] = block[0, :up_rows].astype(F32)
        down_out[0] = block[0, up_rows:].astype(F32)

    at = 0
    for place in places:
        core, base, count = place
        pl.when((scal[0] == core) & (step >= base) & (step < base + count))(
            functools.partial(put, parts[at])
        )
        at += 1


def place_experts(scal, pieces, held_experts, up_rows, experts, into=()):
    rows, width = pieces[0][2].shape[1:]
    run = next((i for i in range(1, len(experts)) if experts[i] != experts[0] + i), len(experts))
    skip = experts[run] - experts[run - 1] if run < len(experts) else 1
    number = lambda i: experts[0] + (i // run) * (run - 1 + skip) + i % run
    assert [number(i) for i in range(len(experts))] == list(experts)
    places = [(core, base, array.shape[0]) for core, base, array in pieces]
    arrays = [array for _, _, array in pieces]
    specs = [
        pl.BlockSpec(
            (1, rows, width),
            lambda i, scal, base=base, top=count - 1: (jnp.clip(number(i) - base, 0, top), 0, 0),
        )
        for _, base, count in places
    ]
    specs += [pl.BlockSpec(memory_space=pl.ANY) for _ in into]
    return pl.pallas_call(
        functools.partial(place_kernel, places, number, len(into)),
        name="place_experts",
        grid_spec=pltpu.PrefetchScalarGridSpec(
            num_scalar_prefetch=1,
            grid=(len(experts),),
            in_specs=specs,
            out_specs=[
                pl.BlockSpec((1, up_rows, width), lambda i, scal: (number(i), 0, 0)),
                pl.BlockSpec((1, rows - up_rows, width), lambda i, scal: (number(i), 0, 0)),
            ],
        ),
        out_shape=[
            jax.ShapeDtypeStruct((held_experts, up_rows, width), F32),
            jax.ShapeDtypeStruct((held_experts, rows - up_rows, width), F32),
        ],
        input_output_aliases={1 + len(arrays) + i: i for i in range(len(into))},
        compiler_params=params(1),
        cost_estimate=cost(0, 8 * len(experts) * rows * width),
    )(scal, *arrays, *into)


def pack_kernel(scal, up, down, out):
    up_rows = up.shape[1]
    out[0, :up_rows, :] = up[0]
    out[0, up_rows:, :] = down[0]


def pack_experts(half, up, down):
    experts, up_rows, width = up.shape
    rows = up_rows + down.shape[1]
    local = experts // 2
    take = lambda i, scal: (scal[0] * local + i, 0, 0)
    return pl.pallas_call(
        pack_kernel,
        name="pack_experts",
        grid_spec=pltpu.PrefetchScalarGridSpec(
            num_scalar_prefetch=1,
            grid=(local,),
            in_specs=[
                pl.BlockSpec((1, up_rows, width), take),
                pl.BlockSpec((1, rows - up_rows, width), take),
            ],
            out_specs=pl.BlockSpec((1, rows, width), lambda i, scal: (i, 0, 0)),
        ),
        out_shape=jax.ShapeDtypeStruct((local, rows, width), BF16),
        compiler_params=params(1),
        cost_estimate=cost(0, 4 * local * rows * width),
    )(half.astype(jnp.int32).reshape(1), up, down)


def assemble_kernel(devices, depth, scal, *refs):
    owns, others, whole, sem = refs[:devices], refs[devices : 2 * devices], refs[-2], refs[-1]
    piece = whole.shape[0] // (devices * depth)
    for home, blocks in ((1, owns), (0, others)):

        @pl.when(scal[0] == home)
        def _(blocks=blocks):
            for k in range(devices):
                for i in range(depth):
                    to = pl.multiple_of(((scal[1] ^ k) * depth + (scal[2] ^ i)) * piece, piece)
                    pltpu.make_async_copy(
                        blocks[k].at[pl.ds(i * piece, piece)], whole.at[pl.ds(to, piece)], sem
                    ).start()
            pltpu.make_async_copy(whole, whole, sem).wait()


def assemble(scal, owns, others, depth):
    devices = len(owns)
    rows, columns = owns[0].shape
    return pl.pallas_call(
        functools.partial(assemble_kernel, devices, depth),
        name="assemble",
        in_specs=[pl.BlockSpec(memory_space=pltpu.SMEM)]
        + [pl.BlockSpec(memory_space=pl.ANY)] * (2 * devices),
        out_specs=pl.BlockSpec(memory_space=pltpu.VMEM),
        out_shape=jax.ShapeDtypeStruct((rows * devices, columns), owns[0].dtype),
        scratch_shapes=[pltpu.SemaphoreType.DMA(())],
        compiler_params=params(),
        cost_estimate=cost(0, 4 * rows * devices * columns),
    )(scal, *owns, *others)


def attend_back_kernel(devices, arrived, scal, *rest):
    parts, rest = rest[:arrived], rest[arrived:]
    grad_out, middle, gain, attended, wo, q, lse, cosine, sine, x, gain_first = rest[:11]
    ks, vs, rest = rest[11 : 11 + devices], rest[11 + devices : 11 + 2 * devices], rest[11 + 2 * devices :]
    mid_out, weight_grads, gain_grad, dq_out = rest[:4]
    dkv_outs, (bias, held) = rest[4 : 4 + devices], rest[4 + devices :]
    width = middle.shape[1]
    rows = middle.shape[0]
    scale = 1.0 / math.sqrt(HD)
    step = pl.program_id(0)

    @pl.when(step == 0)
    def _():
        fill_bias(bias, scal, devices, rows)
        grad_mix = parts[0][...].astype(F32)
        for part in parts[1:]:
            grad_mix = grad_mix + part[...].astype(F32)
        mid = middle[...]
        factor = lax.rsqrt(jnp.mean(mid * mid, axis=-1, keepdims=True) + epsilon)
        scaled = grad_mix * gain[...]
        inner = jnp.mean(mid * scaled, axis=-1, keepdims=True)
        gain_grad[...] = jnp.sum(grad_mix * mid * factor, axis=0, keepdims=True)
        grad_mid = grad_out[...] + factor * scaled - mid * (factor * factor * factor * inner)
        mid_out[...] = grad_mid
        branch = grad_mid.astype(BF16)
        weight_grads[:, :width] = mm_tn(attended[...], branch).astype(BF16)
        held[...] = mm_nt(branch, wo[...]).astype(BF16)

    keys = jnp.concatenate([r[0] for r in ks], axis=0)
    values = jnp.concatenate([r[0] for r in vs], axis=0)
    block_bias = bias[...]
    both_bias = jnp.concatenate([block_bias, block_bias], axis=1)
    key_parts, value_parts = [], []
    for i in range(2):
        block = q[:, i * 128 : (i + 1) * 128]
        at = pl.multiple_of(step * 256 + i * 128, 128)
        grads = held[:, pl.ds(at, 128)]
        scores = mm_nt(doubled(keys, i), two_heads(block)) * scale + both_bias
        probs = jnp.exp(scores - lse[0, i : i + 1, :])
        grad_probs = mm_nt(doubled(values, i), two_heads(grads))
        product = probs * grad_probs
        dots = jnp.sum(product, axis=0, keepdims=True)
        grad_scores = (product - probs * dots).astype(BF16)
        key_parts.append(mm(grad_scores, two_heads_doubled(block)) * scale)
        value_parts.append(mm(probs.astype(BF16), two_heads_doubled(grads)))
        moved = mm_tn(keys, grad_scores)[i * HD : (i + 1) * HD] * scale
        pair = jnp.concatenate([moved[:, :rows], moved[:, rows:]], axis=0)
        dq_out[:, pl.ds(at, 128)] = turn(jnp.transpose(pair), cosine[...], sine[...]).astype(BF16)
    even = lane_index(key_parts[0].shape) < HD
    grad_keys = jnp.where(even, key_parts[0], key_parts[1]).astype(BF16)
    grad_values = jnp.where(even, value_parts[0], value_parts[1]).astype(BF16)
    for k in range(devices):
        dkv_outs[k][0] = grad_keys[k * rows : (k + 1) * rows]
        dkv_outs[k][1] = grad_values[k * rows : (k + 1) * rows]

    @pl.when(step == pl.num_programs(0) - 1)
    def _():
        values = x[...].astype(F32)
        factor = lax.rsqrt(jnp.mean(values * values, axis=-1, keepdims=True) + epsilon)
        normed = (values * factor * gain_first[...]).astype(BF16)
        weight_grads[:, width:] = mm_tn(normed, dq_out[...]).astype(BF16)


def attend_backward(
    scal, parts, grad_out, middle, gain, attended, shared, q, lse, cosine, sine, x, gain_first, kvs
):
    rows, width = middle.shape
    devices = len(kvs)
    keys = devices * rows
    kv_specs = [pl.BlockSpec((1, rows, 128), lambda h: (0, 0, h)) for _ in kvs] + [
        pl.BlockSpec((1, rows, 128), lambda h: (1, 0, h)) for _ in kvs
    ]
    return pl.pallas_call(
        functools.partial(attend_back_kernel, devices, len(parts)),
        name="attend_backward",
        grid=(KVH // 2,),
        in_specs=[
            pl.BlockSpec(memory_space=pltpu.SMEM),
            *[fixed((rows, width)) for _ in parts],
            fixed((rows, width)),
            fixed((rows, width)),
            fixed((1, width)),
            fixed((rows, QH * HD)),
            pl.BlockSpec((QH * HD, width), lambda h: (0, 2), pipeline_mode=pl.Buffered(1)),
            pl.BlockSpec((rows, 256), lambda h: (0, h)),
            pl.BlockSpec((1, 2, 2 * rows), lambda h: (h, 0, 0)),
            fixed((rows, 128)),
            fixed((rows, 128)),
            fixed((rows, width)),
            fixed((1, width)),
            *kv_specs,
        ],
        out_specs=[
            resident((rows, width)),
            resident((width, width + QH * HD)),
            resident((1, width)),
            resident((rows, QH * HD)),
            *[pl.BlockSpec((2, rows, 128), lambda h: (0, 0, h)) for _ in kvs],
        ],
        out_shape=[
            jax.ShapeDtypeStruct((rows, width), F32),
            jax.ShapeDtypeStruct((width, width + QH * HD), BF16),
            jax.ShapeDtypeStruct((1, width), F32),
            jax.ShapeDtypeStruct((rows, QH * HD), BF16),
            *[jax.ShapeDtypeStruct((2, rows, KW), BF16) for _ in kvs],
        ],
        scratch_shapes=[pltpu.VMEM((keys, rows), F32), pltpu.VMEM((rows, QH * HD), BF16)],
        compiler_params=params(1),
        cost_estimate=cost(
            10 * rows * keys * QH * HD * 2 + 4 * rows * width * width,
            6 * width * width + 8 * keys * width + 20 * rows * width,
            rows * keys * QH,
            0.23,
        ),
    )(
        scal,
        *parts,
        grad_out,
        middle,
        gain,
        attended,
        shared,
        q,
        lse,
        cosine,
        sine,
        x,
        gain_first,
        *kvs,
        *kvs,
    )


def project_back_kernel(devices, x, gain, dq, *rest):
    parts, rest = rest[:devices], rest[devices:]
    grad_mid, wq, wm, cosine, sine, small, dx_out, packed = rest
    values = x[...].astype(F32)
    width = values.shape[1]
    factor = lax.rsqrt(jnp.mean(values * values, axis=-1, keepdims=True) + epsilon)
    normed = (values * factor * gain[...]).astype(BF16)
    summed = parts[0][...].astype(F32)
    for part in parts[1:]:
        summed = summed + part[...].astype(F32)
    grad_keys = [
        turn(summed[0, :, b * 128 : (b + 1) * 128], cosine[...], sine[...]).astype(BF16)
        for b in range(KW // 128)
    ]
    grad_memory = jnp.concatenate(grad_keys + [summed[1].astype(BF16)], axis=1)
    grad_query = dq[...]
    packed[:, : 2 * KW] = mm_tn(normed, grad_memory).astype(BF16)
    grad_normed = mm_nt(grad_query, wq[...]) + mm_nt(grad_memory, wm[...])
    scaled = grad_normed * gain[...]
    inner = jnp.mean(values * scaled, axis=-1, keepdims=True)
    gain_grad = jnp.sum(grad_normed * values * factor, axis=0, keepdims=True)
    row = lax.broadcasted_iota(jnp.int32, (128, width), 0)
    packed[:, 2 * KW :] = jnp.transpose(
        jnp.where(row == EXPERTS, gain_grad, small[...])
    ).astype(BF16)
    dx_out[...] = (
        grad_mid[...] + factor * scaled - values * (factor * factor * factor * inner)
    )


def project_backward(x, gain, dq, parts, grad_mid, shared, cosine, sine, small):
    rows, width = x.shape
    columns = 2 * KW + 128
    return pl.pallas_call(
        functools.partial(project_back_kernel, len(parts)),
        name="project_backward",
        grid=(1,),
        in_specs=[
            fixed((rows, width)),
            fixed((1, width)),
            fixed((rows, QH * HD)),
            *[fixed((2, rows, KW)) for _ in parts],
            fixed((rows, width)),
            pl.BlockSpec((width, QH * HD), lambda i: (0, 0), pipeline_mode=pl.Buffered(1)),
            pl.BlockSpec((width, 2 * KW), lambda i: (0, 1), pipeline_mode=pl.Buffered(1)),
            fixed((rows, 128)),
            fixed((rows, 128)),
            fixed((128, width)),
        ],
        out_specs=[resident((rows, width)), resident((width, columns))],
        out_shape=[
            jax.ShapeDtypeStruct((rows, width), F32),
            jax.ShapeDtypeStruct((width, columns), BF16),
        ],
        compiler_params=params(1),
        cost_estimate=cost(
            6 * rows * width * 2048, 8 * width * 2048 + 16 * rows * width, share=0.35
        ),
    )(x, gain, dq, *parts, grad_mid, shared, shared, cosine, sine, small)


def pairs_within(axis, by, sections=(0, 1)):
    count = lax.axis_size(axis)
    return [(s * count + i, s * count + (i ^ by)) for s in sections for i in range(count)]


def exchanged(value, axis, by, sections=(0, 1)):
    return lax.ppermute(value, ("section", axis), pairs_within(axis, by, sections))


def swapped(value):
    return lax.ppermute(value, "section", [(0, 1), (1, 0)])


def from_all(value, axis, sections=(0, 1)):
    count = lax.axis_size(axis)
    return [value] + [exchanged(value, axis, k, sections) for k in range(1, count)]


def after(value, other):
    return lax.optimization_barrier((value, other))[0]


def scattered(blocks, axis, sections):
    return [blocks[0]] + [
        exchanged(blocks[k], axis, k, sections) for k in range(1, len(blocks))
    ]


def added(terms):
    return functools.reduce(lambda a, b: a + b, [term.astype(F32) for term in terms])


def shards(
    tokens,
    targets,
    lengths,
    routes,
    attention_gain,
    query_weight,
    memory_weight,
    output_weight,
    mixture_gain,
    router_weight,
    gate_up_weight,
    down_weight,
):
    section = lax.axis_index("section")
    context = lax.axis_index("ctx")
    line = lax.axis_index("fsdp")
    devices = lax.axis_size("ctx")
    depth = lax.axis_size("fsdp")
    first_core = section == 0
    rows, width = tokens.shape[2:]
    layers = 2
    held_experts = gate_up_weight.shape[1]
    half_held = held_experts // 2
    capacity = rows * TOPK * 9 // (EXPERTS * 8)
    slots = -(-capacity // 16) * 16
    up_rows, down_rows = gate_up_weight.shape[2], down_weight.shape[2]
    shard_rows = up_rows + down_rows

    column = context * held_experts
    plain = (column + section * half_held, half_held, 2 * devices)
    places = [plain, plain]

    pack = jnp.concatenate(
        [
            query_weight[0],
            memory_weight[0],
            output_weight[0],
            router_weight[0],
            attention_gain[0][:, None],
            mixture_gain[0][:, None],
            jnp.zeros((query_weight.shape[1], 128 - EXPERTS - 2), BF16),
        ],
        axis=1,
    )

    def shared_of_line(layer, ahead):
        mine = pack if ahead is None else after(pack, ahead)
        return jnp.concatenate(from_all(mine, "fsdp", (layer,)), axis=0)

    def shared_of_plane(layer, block, ahead):
        mine = block if ahead is None else after(block, ahead)
        owns = from_all(mine, "ctx", (layer,))
        others = [lax.ppermute(own, "section", [(layer, 1 - layer)]) for own in owns]
        scal = jnp.stack([(section == layer).astype(jnp.int32), context, line])
        whole = assemble(scal, owns, others, depth)
        small = whole[:, 3 * width :].T
        return (
            whole,
            small[:EXPERTS],
            small[EXPERTS : EXPERTS + 1].astype(F32),
            small[EXPERTS + 1 : EXPERTS + 2].astype(F32),
        )

    my_routes = jnp.swapaxes(routes[0, :, 0], 1, 2)
    other_routes = swapped(my_routes)
    layer_routes = jnp.where(
        first_core,
        jnp.stack([my_routes, other_routes]),
        jnp.stack([other_routes, my_routes])[:, ::-1],
    )
    all_routes = jnp.stack(from_all(layer_routes, "ctx"), axis=2).reshape(
        layers, 2 * devices, TOPK, rows
    )
    source_routes = [all_routes[0], all_routes[1]]
    earlier = (
        lax.broadcasted_iota(jnp.int32, (rows, rows), 0)
        < lax.broadcasted_iota(jnp.int32, (rows, rows), 1)
    ).astype(BF16)

    def ranked(layer):
        first, local, _ = places[layer]
        ids = first + jnp.arange(local, dtype=jnp.int32)
        named = jnp.any(source_routes[layer][:, None] == ids[None, :, None, None], axis=2)
        before = jnp.dot(
            named.astype(BF16).reshape(-1, rows), earlier, preferred_element_type=F32
        ).reshape(named.shape)
        return jnp.where(named, before, -1.0)

    ranks = [ranked(layer) for layer in range(layers)]
    masks = jnp.any(
        layer_routes[:, 0, None] == jnp.arange(EXPERTS, dtype=jnp.int32)[None, :, None, None], axis=2
    ).astype(F32)

    own_ranks = jnp.where(
        masks[1] > 0.5,
        jnp.dot(masks[1].astype(BF16), earlier, preferred_element_type=F32),
        -1.0,
    )
    last_rank = jnp.take(
        own_ranks,
        jnp.stack(
            [
                (context ^ k) * held_experts + (section ^ m) * half_held + half_held - 1
                for k in range(devices)
                for m in range(2)
            ]
        ),
        axis=0,
    )

    line_blocks = [after(shared_of_line(0, None), (ranks, masks, last_rank)), None]

    whole = [(0, half_held)]
    split = [(0, half_held - 1), (half_held - 1, 1)] if half_held > 1 else whole
    runs = [whole, split]
    back_runs = [split, split[::-1]]
    if half_held > 2:
        back_runs[1] = [(half_held - 1, 1), (half_held - 2, 1), (0, half_held - 2)]

    arrived = swapped(pack_experts(1 - section, gate_up_weight[0], down_weight[0]))
    mine = pack_experts(section, gate_up_weight[0], down_weight[0])

    def gathered_experts(layer, ahead):
        own, other = (mine, arrived) if ahead is None else after((mine, arrived), ahead)
        parts = []
        for a, n in runs[layer]:
            shard = jnp.where(section == layer, own[a : a + n], other[a : a + n])
            parts.append([lax.all_gather(shard, "fsdp", axis=1, tiled=True)])
        return parts

    half = rows // 2
    within = jnp.arange(rows, dtype=jnp.int32)
    positions = jnp.where(
        within < half, context * half + within, (2 * devices - 1 - context) * half + within - half
    )
    inverse = rope_base ** (-2.0 * jnp.arange(HD // 2, dtype=F32) / HD)
    angles = positions.astype(F32)[:, None] * inverse[None, :]
    sine, cosine = jnp.sin(angles), jnp.cos(angles)
    cos_table = jnp.concatenate([cosine] * 4, axis=1)
    sin_table = jnp.concatenate([-sine, sine, -sine, sine], axis=1)
    length = lengths[section, line]
    attend_scalars = jnp.stack([context, length]).astype(jnp.int32)

    def dispatched(message):
        plane = from_all(message, "ctx")
        blocks = plane + [swapped(block) for block in plane]
        return blocks

    def returned(outs):
        own, other = outs[:devices], outs[devices : 2 * devices]
        crossed = [swapped(block) for block in other]
        near = [own[0], crossed[0]]
        for k in range(1, devices):
            chip = (own[k].astype(F32) + crossed[k].astype(F32)).astype(BF16)
            near.append(exchanged(chip, "ctx", k))
        return near

    my_targets = lax.dynamic_index_in_dim(targets[:, 0], section, 0, keepdims=False)
    layer_input = lax.dynamic_index_in_dim(tokens[:, 0], section, 0, keepdims=False)
    valid = (positions < length).astype(F32)[:, None]
    saved, hidden = [], []
    early_experts = gathered_experts(0, None)
    ahead = None
    for layer in range(layers):
        first, local, sources = places[layer]
        shared, router, gain_first, gain_second = shared_of_plane(
            layer, line_blocks[layer], ahead
        )
        q, kv = project(layer_input, gain_first, shared, cos_table, sin_table)
        if layer == 0:
            line_blocks[1] = shared_of_line(1, kv)
        kvs = from_all(kv, "ctx")
        attended, lse, middle, message = attend(
            attend_scalars, layer_input, q, kvs, shared, gain_second, router, masks[layer]
        )
        messages = dispatched(message)
        if layer == 0:
            ahead = messages
            weights = early_experts
            late_experts = gathered_experts(1, message)
        else:
            weights = late_experts
        kept, outs = [], ()
        xs, gates = dispatch(
            first.astype(jnp.int32).reshape(1), messages, ranks[layer], slots, False
        )
        sparse = layer == 1 and len(runs[layer]) > 1
        for at, ((a, n), blocks) in enumerate(zip(runs[layer], weights)):
            scal = jnp.stack([first + a, *[jnp.asarray(k) for k in range(depth)]]).astype(jnp.int32)
            by_rows = sparse and at == len(runs[layer]) - 1
            if by_rows:
                scal = after(scal, terms)
            run, outs = experts_forward(
                scal,
                xs,
                ranks[layer][:, a : a + n],
                gates[:, a : a + n],
                blocks,
                depth,
                slots,
                a,
                () if by_rows else outs,
                not by_rows,
            )
            kept.append((a, n, scal, run, blocks))
            if not by_rows:
                terms = returned(outs)
        if layer == layers - 1:
            routed = [last_rank, [], slots] if sparse else []
            if sparse:
                near, far = outs[0][0, :devices], swapped(outs[0][0, devices:])
                routed[1] = [near[0], far[0]] + [
                    exchanged(jnp.stack([near[k], far[k]]), "ctx", k) for k in range(1, devices)
                ]
            hidden_rows, mixed, grad_output, message, *row_messages = finish(
                terms, middle, my_targets, valid, *routed
            )
            hidden.append(hidden_rows)
        else:
            mixed = functools.reduce(lambda a, b: a + b, [t.astype(F32) for t in terms])
            hidden.append((middle + mixed).astype(BF16))
        saved.append(
            dict(
                x=layer_input,
                shared=shared,
                router=router,
                gain_first=gain_first,
                gain_second=gain_second,
                q=q,
                kvs=kvs,
                attended=attended,
                lse=lse,
                middle=middle,
                kept=kept,
                xs=xs,
                gates=gates,
                mixed=mixed,
            )
        )
        layer_input = hidden[-1]

    def home_blocks(packed, layer):
        arrived = lax.ppermute(packed, "section", [(1 - layer, layer)])
        size = packed.shape[0] // devices
        return [
            (
                lax.dynamic_slice_in_dim(packed, (context ^ k) * size, size, 0).astype(F32)
                + lax.dynamic_slice_in_dim(arrived, (context ^ k) * size, size, 0).astype(F32)
            ).astype(BF16)
            for k in range(devices)
        ]

    def home_plane(blocks, layer):
        return added(scattered(blocks, "ctx", (layer,))).astype(BF16)

    def home_line(plane, layer, ahead=None):
        size = plane.shape[0] // depth
        blocks = [
            lax.dynamic_slice_in_dim(plane, (line ^ k) * size, size, 0) for k in range(depth)
        ]
        if ahead is not None:
            blocks[-1] = after(blocks[-1], ahead)
        return scattered(blocks, "fsdp", (layer,))

    def placed_rows(values):
        home = jnp.where(first_core, values[0], values[1])
        arrived = swapped(jnp.where(first_core, values[1], values[0]))
        return jnp.stack(
            [jnp.where(first_core, home, arrived), jnp.where(first_core, arrived, home)]
        )

    input_grads, expert_grads = [None] * layers, [None] * layers
    waiting = None
    summed = {}
    for layer in reversed(range(layers)):
        held = saved[layer]
        first, local, sources = places[layer]
        if layer < layers - 1:
            message = grad_message(grad_output, held["mixed"])
        sparse = layer == 1 and len(back_runs[layer]) > 1
        if sparse:
            plane = [row_messages[0]] + [
                exchanged(row_messages[k], "ctx", k) for k in range(1, devices)
            ]
            row_blocks = plane + [swapped(block[1]) for block in plane]
            message = after(message, plane[1])
        messages = dispatched(message)
        if waiting is not None:
            blocks_1 = [home_blocks(part, 1) for part in waiting]
            messages = after(messages, blocks_1)
            blocks_1 = after(blocks_1, messages)
            planes = [home_plane(blocks, 1) for blocks in blocks_1]
        own_router = lax.dynamic_slice_in_dim(held["router"], first, local, 0).astype(F32)
        small = jnp.zeros((128, width), F32)
        outs = ()
        gathered = []
        steps = back_runs[layer]
        spans = [a for a, _ in steps]
        for at, (a, n) in enumerate(steps):
            base, _, scal, run, blocks = next(
                kept for kept in held["kept"] if kept[0] <= a and a + n <= kept[0] + kept[1]
            )
            scal = jnp.concatenate([scal[:1] + (a - base), scal[1:]])
            last = None
            if at == len(steps) - 1:
                order = tuple(sorted(range(len(spans)), key=lambda i: spans[i]))
                last = (ranks[layer], [rows_of for rows_of in outs], order)
            if sparse and at == 0:
                grad_rows, inners, start = row_blocks, None, a
            elif not sparse:
                grad_rows, inners = dispatch(
                    scal[:1], messages, ranks[layer][:, a : a + n], slots, True
                )
                start = a
            elif at == 1:
                start = 0
                grad_rows, inners = dispatch(
                    scal[:1], messages, ranks[layer][:, : half_held - 1], slots, True
                )
            grads, router_grad, rows_out = experts_backward(
                scal,
                grad_rows,
                ranks[layer][:, a : a + n],
                held["gates"][:, a : a + n],
                inners,
                held["xs"],
                run,
                own_router[a : a + n, None, :],
                blocks,
                depth,
                slots,
                a,
                a - base,
                a - start,
                last,
            )
            outs = rows_out if last else list(outs) + rows_out
            if layer == 1 and inners is not None:
                error = jnp.sum(inners[:, 1, 0])
            small = lax.dynamic_update_slice_in_dim(small, router_grad[:, 0], first + a, 0)
            gathered.append(grads)
        over_line = lambda grads: lax.psum_scatter(
            grads, "fsdp", scatter_dimension=1, tiled=True
        )
        at_once = gathered if layer == 1 or len(gathered) == 1 else gathered[:-1]
        summed[layer] = [over_line(grads) for grads in at_once]
        if layer == 1:
            grad_output = after(grad_output, summed[1][0])
        else:
            grad_output = after(grad_output, summed[1][-1])
            outs = after(outs, planes)
        back = attend_backward(
            attend_scalars,
            returned(outs),
            grad_output,
            held["middle"],
            held["gain_second"],
            held["attended"],
            held["shared"],
            held["q"],
            held["lse"],
            cos_table,
            -sin_table,
            held["x"],
            held["gain_first"],
            held["kvs"],
        )
        grad_mid, weight_grads, gain_second_grad, dq = back[:4]
        dkv = back[4:]
        parts = [dkv[0]] + [exchanged(dkv[k], "ctx", k) for k in range(1, devices)]
        if layer == 0:
            outward = home_blocks(weight_grads, 0)
            grad_mid = after(grad_mid, outward)
        else:
            by = 1
            while by < depth:
                error = error + lax.ppermute(error, "fsdp", [(i, i ^ by) for i in range(depth)])
                by *= 2
            loss_value = error / jnp.sum(lengths).astype(F32)
            hidden_out = placed_rows(hidden)
            grad_mid = after(grad_mid, (loss_value, hidden_out, summed[1][: len(steps) - 1]))
        small = lax.dynamic_update_slice_in_dim(small, gain_second_grad, EXPERTS + 1, 0)
        dx, packed = project_backward(
            held["x"],
            held["gain_first"],
            dq,
            parts,
            grad_mid,
            held["shared"],
            cos_table,
            -sin_table,
            small,
        )
        expert_grads[layer] = (spans, summed[layer])
        input_grads[layer] = dx
        grad_output = dx.astype(BF16).astype(F32)
        if layer == 1:
            waiting = (weight_grads, packed)
        else:
            outward, planes = after((outward, planes), packed)
            summed[0] += [over_line(after(grads, packed)) for grads in gathered[len(at_once) :]]
            inward_plane = home_plane(home_blocks(packed, 0), 0)
            outward_plane = home_plane(outward, 0)

    def pieces_of(layer, at, part):
        arrived = lax.ppermute(part, "section", [(1 - layer, layer)])
        return [
            (layer, half * half_held + at, term)
            for half, term in ((layer, part), (1 - layer, arrived))
        ]

    def placed(pieces, experts, into):
        touched = [p for p in pieces if any(0 <= e - p[1] < p[2].shape[0] for e in experts)]
        return place_experts(
            section.astype(jnp.int32).reshape(1), touched, held_experts, up_rows, experts, into
        )

    parts = [(layer, at, part) for layer in (1, 0) for at, part in zip(*expert_grads[layer])]
    pieces = [piece for part in parts[:-1] for piece in pieces_of(*part)]
    layer, at, part = parts[-1]
    last = [half * half_held + at + i for half in range(2) for i in range(part.shape[0])]
    sums = ()
    if len(last) < held_experts:
        sums = placed(pieces, [e for e in range(held_experts) if e not in last], ())
    first_terms = home_line(
        jnp.concatenate([outward_plane, inward_plane], axis=1), 0, sums if sums else None
    )
    second_terms = home_line(jnp.concatenate(planes, axis=1), 1)
    shared_grads = jnp.where(first_core, added(first_terms), added(second_terms))
    outward, inward = shared_grads[:, : 2 * width], shared_grads[:, 2 * width :]
    input_out = placed_rows(input_grads)
    if sums:
        part = after(part, (first_terms, second_terms))
    up_sum, down_sum = placed(pieces + pieces_of(layer, at, part), last, sums)
    at = 2 * KW
    return (
        hidden_out[None, :, None],
        input_out[None, :, None],
        loss_value,
        inward[:, at + EXPERTS][None],
        outward[:, width:][None],
        inward[:, :at][None],
        outward[:, :width][None],
        inward[:, at + EXPERTS + 1][None],
        inward[:, at : at + EXPERTS][None],
        up_sum[None],
        down_sum[None],
    )


def solution(mesh):
    placed = (
        P(None, "fsdp", "ctx", None),
        P(None, "fsdp", "ctx", None),
        P(),
        P("section", None, "fsdp", "ctx", None),
        P("section", ("ctx", "fsdp")),
        P("section", ("ctx", "fsdp"), None),
        P("section", ("ctx", "fsdp"), None),
        P("section", ("ctx", "fsdp"), None),
        P("section", ("ctx", "fsdp")),
        P("section", ("ctx", "fsdp"), None),
        P("section", "ctx", "fsdp", None),
        P("section", "ctx", "fsdp", None),
    )
    return jax.shard_map(
        shards,
        mesh=mesh,
        in_specs=placed,
        out_specs=(
            P("section", None, "fsdp", "ctx", None),
            P("section", None, "fsdp", "ctx", None),
            P(),
            P("section", ("ctx", "fsdp")),
            P("section", ("ctx", "fsdp"), None),
            P("section", ("ctx", "fsdp"), None),
            P("section", ("ctx", "fsdp"), None),
            P("section", ("ctx", "fsdp")),
            P("section", ("ctx", "fsdp"), None),
            P("section", "ctx", "fsdp", None),
            P("section", "ctx", "fsdp", None),
        ),
        check_vma=False,
    )
```

```python
import functools
import math

import jax
import jax.numpy as jnp
from jax import lax
from jax.experimental import pallas as pl
from jax.experimental.pallas import tpu as pltpu
from jax.sharding import PartitionSpec as P

QH = 16
KVH = 8
HD = 64
EXPERTS = 32
FF_E = 512
TOPK = 8
KW = KVH * HD
EXT = 16

epsilon = 1e-06
rope_base = 10000.0
negative = -1e30
F32 = jnp.float32
BF16 = jnp.bfloat16
VMEM_LIMIT = 60 * 1024 * 1024


def params(grid_dims=0):
    return pltpu.CompilerParams(
        vmem_limit_bytes=VMEM_LIMIT,
        dimension_semantics=("arbitrary",) * grid_dims if grid_dims else None,
    )


def cost(flops, moved, exps=0, share=1.0):
    return pl.CostEstimate(
        flops=int(flops / share), bytes_accessed=int(moved), transcendentals=int(exps)
    )


def mm(a, b):
    return jnp.dot(a, b, preferred_element_type=F32)


def mm_nt(a, b):
    return lax.dot_general(a, b, (((1,), (1,)), ((), ())), preferred_element_type=F32)


def mm_tn(a, b):
    return lax.dot_general(a, b, (((0,), (0,)), ((), ())), preferred_element_type=F32)


def fixed(shape):
    return pl.BlockSpec(shape, lambda *_: (0,) * len(shape), pipeline_mode=pl.Buffered(1))


def resident(shape):
    return pl.BlockSpec(shape, lambda *_: (0,) * len(shape))


def lane_index(shape):
    return lax.broadcasted_iota(jnp.int32, shape, len(shape) - 1)


def turn(block, cosine, sine):
    low_half = lane_index(block.shape) % HD < HD // 2
    swapped = jnp.where(
        low_half, pltpu.roll(block, 128 - HD // 2, axis=1), pltpu.roll(block, HD // 2, axis=1)
    )
    return block * cosine + swapped * sine


def rolled(block):
    return pltpu.roll(block.astype(F32), HD, axis=1).astype(BF16)


def key_positions(device, half, devices, shape, dim):
    within = lax.broadcasted_iota(jnp.int32, shape, dim)
    return jnp.where(
        within < half, device * half + within, (2 * devices - 1 - device) * half + within - half
    )


def fill_bias(bias, scal, devices, rows):
    context, length = scal[0], scal[1]
    query_pos = key_positions(context, rows // 2, devices, (rows, rows), 1)
    for k in range(devices):
        key_pos = key_positions(context ^ k, rows // 2, devices, (rows, rows), 0)
        taken = (key_pos <= query_pos) & (key_pos < length)
        bias[k * rows : (k + 1) * rows, :] = jnp.where(taken, 0.0, negative)


def two_heads(block):
    even = lane_index(block.shape) < HD
    zero = jnp.zeros((), block.dtype)
    return jnp.concatenate([jnp.where(even, block, zero), jnp.where(even, zero, block)], axis=0)


def two_heads_doubled(block):
    even = lane_index(block.shape) < HD
    other = rolled(block)
    return jnp.concatenate([jnp.where(even, block, other), jnp.where(even, other, block)], axis=0)


def doubled(block, odd):
    even = lane_index(block.shape) < HD
    other = rolled(block)
    return jnp.where(even, other, block) if odd else jnp.where(even, block, other)


def one_hot(rank_row, slots):
    rows = rank_row.shape[-1]
    index = lax.broadcasted_iota(jnp.int32, (slots, rows), 0).astype(F32)
    return rank_row == index


def project_kernel(x, gain, wq, wm, cosine, sine, q_out, kv_out):
    values = x[...].astype(F32)
    factor = lax.rsqrt(jnp.mean(values * values, axis=-1, keepdims=True) + epsilon)
    normed = (values * factor * gain[...]).astype(BF16)
    cos, sin = cosine[...], sine[...]
    q0 = mm(normed, wq[...])
    for b in range(QH * HD // 128):
        at = slice(b * 128, (b + 1) * 128)
        q_out[:, at] = turn(q0[:, at], cos, sin).astype(BF16)
    kv0 = mm(normed, wm[...])
    for b in range(KW // 128):
        at = slice(b * 128, (b + 1) * 128)
        kv_out[0, :, at] = turn(kv0[:, at], cos, sin).astype(BF16)
    kv_out[1] = kv0[:, KW:].astype(BF16)


def project(x, gain, shared, cosine, sine):
    rows, width = x.shape
    return pl.pallas_call(
        project_kernel,
        name="project",
        grid=(1,),
        in_specs=[
            fixed((rows, width)),
            fixed((1, width)),
            pl.BlockSpec((width, QH * HD), lambda i: (0, 0), pipeline_mode=pl.Buffered(1)),
            pl.BlockSpec((width, 2 * KW), lambda i: (0, 1), pipeline_mode=pl.Buffered(1)),
            fixed((rows, 128)),
            fixed((rows, 128)),
        ],
        out_specs=[resident((rows, QH * HD)), resident((2, rows, KW))],
        out_shape=[
            jax.ShapeDtypeStruct((rows, QH * HD), BF16),
            jax.ShapeDtypeStruct((2, rows, KW), BF16),
        ],
        compiler_params=params(1),
        cost_estimate=cost(
            2 * rows * width * 2048, 2 * width * 2048 + 8 * rows * width, share=0.2
        ),
    )(x, gain, shared, shared, cosine, sine)


def attend_kernel(devices, scal, x, q, *rest):
    ks, vs, rest = rest[:devices], rest[devices : 2 * devices], rest[2 * devices :]
    wo, gain, router, mask, o_out, lse_out, mid_out, msg_out, bias, held = rest
    rows = x.shape[0]
    step = pl.program_id(0)

    @pl.when(step == 0)
    def _():
        fill_bias(bias, scal, devices, rows)

    keys = jnp.concatenate([r[0] for r in ks], axis=0)
    values = jnp.concatenate([r[0] for r in vs], axis=0)
    block_bias = bias[...]
    both_bias = jnp.concatenate([block_bias, block_bias], axis=1)
    for i in range(2):
        query = two_heads(q[:, i * 128 : (i + 1) * 128])
        scores = mm_nt(doubled(keys, i), query) * (1.0 / math.sqrt(HD)) + both_bias
        top = jnp.max(scores, axis=0, keepdims=True)
        raised = jnp.exp(scores - top)
        total = jnp.sum(raised, axis=0, keepdims=True)
        probs = (raised * (1.0 / total)).astype(BF16)
        lse_out[0, i : i + 1, :] = top + jnp.log(total)
        mixed = mm_tn(values, probs)[i * HD : (i + 1) * HD]
        pair = jnp.concatenate([mixed[:, :rows], mixed[:, rows:]], axis=0)
        at = pl.multiple_of(step * 256 + i * 128, 128)
        held[:, pl.ds(at, 128)] = jnp.transpose(pair).astype(BF16)

    @pl.when(step == pl.num_programs(0) - 1)
    def _():
        attended = held[...]
        o_out[...] = attended
        middle = x[...].astype(F32) + mm(attended, wo[...])
        mid_out[...] = middle
        factor = lax.rsqrt(jnp.mean(middle * middle, axis=-1, keepdims=True) + epsilon)
        normed = (middle * factor * gain[...]).astype(BF16)
        msg_out[:rows, :] = normed
        logits = mm_nt(router[...], normed)
        chosen = mask[...] > 0.5
        top = jnp.max(jnp.where(chosen, logits, negative), axis=0, keepdims=True)
        raised = jnp.where(chosen, jnp.exp(jnp.where(chosen, logits - top, 0.0)), 0.0)
        gates = raised / jnp.sum(raised, axis=0, keepdims=True)
        high = gates.astype(BF16)
        low = (gates - high.astype(F32)).astype(BF16)
        ext = [high[:EXT], high[EXT:], low[:EXT], low[EXT:]]
        if 4 * rows < x.shape[1]:
            ext.append(jnp.zeros((EXT, x.shape[1] - 4 * rows), BF16))
        msg_out[rows:, :] = jnp.concatenate(ext, axis=1)


def attend(scal, x, q, kvs, shared, gain, router, mask):
    rows, width = x.shape
    devices = len(kvs)
    keys = devices * rows
    kv_specs = [pl.BlockSpec((1, rows, 128), lambda h: (0, 0, h)) for _ in kvs] + [
        pl.BlockSpec((1, rows, 128), lambda h: (1, 0, h)) for _ in kvs
    ]
    return pl.pallas_call(
        functools.partial(attend_kernel, devices),
        name="attend",
        grid=(KVH // 2,),
        in_specs=[
            pl.BlockSpec(memory_space=pltpu.SMEM),
            fixed((rows, width)),
            pl.BlockSpec((rows, 256), lambda h: (0, h)),
            *kv_specs,
            pl.BlockSpec((QH * HD, width), lambda h: (0, 2), pipeline_mode=pl.Buffered(1)),
            fixed((1, width)),
            fixed((EXPERTS, width)),
            fixed((EXPERTS, rows)),
        ],
        out_specs=[
            resident((rows, QH * HD)),
            pl.BlockSpec((1, 2, 2 * rows), lambda h: (h, 0, 0)),
            resident((rows, width)),
            resident((rows + EXT, width)),
        ],
        out_shape=[
            jax.ShapeDtypeStruct((rows, QH * HD), BF16),
            jax.ShapeDtypeStruct((KVH // 2, 2, 2 * rows), F32),
            jax.ShapeDtypeStruct((rows, width), F32),
            jax.ShapeDtypeStruct((rows + EXT, width), BF16),
        ],
        scratch_shapes=[pltpu.VMEM((keys, rows), F32), pltpu.VMEM((rows, QH * HD), BF16)],
        compiler_params=params(1),
        cost_estimate=cost(
            4 * rows * keys * QH * HD * 2 + 2 * rows * width * width,
            2 * width * width + 4 * keys * width + 12 * rows * width,
            rows * keys * QH,
            0.17,
        ),
    )(scal, x, q, *kvs, *kvs, shared, gain, router, mask)


def hot_rows(rank, j, slots):
    local = rank.shape[1]
    return jnp.concatenate(
        [
            jnp.where(one_hot(rank[j, i : i + 1, :], slots), 1.0, 0.0).astype(BF16)
            for i in range(local)
        ],
        axis=0,
    )


def combine(rank, held, prior, outs, buffers, slots):
    held = held if isinstance(held, list) else [held]
    prior_buffer, out_buffer, prior_sems, out_sems = buffers
    width = held[0].shape[-1]
    depth = out_buffer.shape[0]
    count = len(outs)
    fetch = lambda j: pltpu.make_async_copy(
        prior[j], prior_buffer.at[j % depth], prior_sems.at[j % depth]
    )
    send = lambda j: pltpu.make_async_copy(
        out_buffer.at[j % depth], outs[j], out_sems.at[j % depth]
    )
    for j in range(min(depth - 1, count) if prior else 0):
        fetch(j).start()
    for j in range(count):
        rows = [part[:, j].reshape(part.shape[0] * slots, width) for part in held]
        rows = rows[0] if len(rows) == 1 else jnp.concatenate(rows, axis=0)
        total = mm_tn(hot_rows(rank, j, slots), rows)
        if prior:
            if j + depth - 1 < count:
                fetch(j + depth - 1).start()
            fetch(j).wait()
            total = total + prior_buffer[j % depth].astype(F32)
        if j >= depth:
            send(j - depth).wait()
        out_buffer[j % depth] = total.astype(BF16)
        send(j).start()
    for j in range(max(0, count - depth), count):
        send(j).wait()


def gate_columns(rank, values, step, sources, slots):
    columns = []
    for j in sources:
        hot = one_hot(rank[j, pl.ds(step, 1), :], slots)
        columns.append(jnp.sum(jnp.where(hot, values(j), 0.0), axis=1, keepdims=True))
    return jnp.concatenate(columns, axis=0)


def finish_kernel(count, routed, slots, *refs):
    terms, (middle, goal, valid, refs) = refs[:count], (*refs[count : count + 3], refs[count + 3 :])
    if routed:
        rank, refs = refs[0], refs[1:]
        arrived, refs = refs[:routed], refs[routed:]
    hidden, mixed_out, grad_out, message, refs = *refs[:4], refs[4:]
    rows, width = middle.shape
    mixed = terms[0][...].astype(F32)
    for term in terms[1:]:
        mixed = mixed + term[...].astype(F32)
    if routed:
        given = jnp.concatenate([ref[...].reshape(-1, width) for ref in arrived], axis=0)
        hots = [
            jnp.where(one_hot(rank[i : i + 1, :], slots), 1.0, 0.0).astype(BF16)
            for i in range(rank.shape[0])
        ]
        mixed = mixed + mm_tn(jnp.concatenate(hots, axis=0), given)
    output = middle[...] + mixed
    hidden[...] = output.astype(BF16)
    mixed_out[...] = mixed
    grad = (output - goal[...].astype(F32)) * valid[...]
    grad_out[...] = grad
    error = 0.5 * jnp.sum(jnp.sum(grad * grad, axis=1, keepdims=True), axis=0, keepdims=True)
    fill_message(message, grad, mixed, error)
    if routed:
        low = message[:rows, :]
        inner = message[rows:, :rows]
        for i, hot in enumerate(hots):
            spread = jnp.where(one_hot(rank[i : i + 1, :], 128), 1.0, 0.0).astype(BF16)
            below = jnp.concatenate(
                [mm_nt(inner, spread)[:8], jnp.zeros((8, width - 128), F32)], axis=1
            )
            refs[i // 2][i % 2] = jnp.concatenate(
                [mm(hot, low)[: slots - 8], below], axis=0
            ).astype(BF16)


def finish(terms, middle, goal, valid, rank=None, arrived=(), slots=0):
    rows, width = middle.shape
    messages = len(rank) // 2 if arrived else 0
    return pl.pallas_call(
        functools.partial(finish_kernel, len(terms), len(arrived), slots),
        name="finish",
        out_shape=[
            jax.ShapeDtypeStruct((rows, width), BF16),
            jax.ShapeDtypeStruct((rows, width), F32),
            jax.ShapeDtypeStruct((rows, width), F32),
            jax.ShapeDtypeStruct((rows + EXT, width), BF16),
            *[jax.ShapeDtypeStruct((2, slots, width), BF16) for _ in range(messages)],
        ],
        compiler_params=params(),
        cost_estimate=cost(8 * rows * width, 24 * rows * width),
    )(*terms, middle, goal, valid, *([rank, *arrived] if arrived else []))


def fill_message(message, grad, mixed, error):
    rows, width = grad.shape
    message[:rows, :] = grad.astype(BF16)
    inner = jnp.transpose(
        jnp.broadcast_to(jnp.sum(grad * mixed, axis=1, keepdims=True), (rows, 128))
    )[:EXT]
    high = inner.astype(BF16)
    low = (inner - high.astype(F32)).astype(BF16)
    row = lax.broadcasted_iota(jnp.int32, (EXT, rows), 0)
    ext = jnp.where(row == 0, high.astype(F32), jnp.where(row == 1, low.astype(F32), 0.0))
    for at in range(2, 5):
        term = error.astype(BF16).astype(F32)
        ext = jnp.where(row == at, term, ext)
        error = error - term
    message[rows:, :rows] = ext.astype(BF16)
    message[rows:, rows:] = jnp.zeros((EXT, width - rows), BF16)


def message_kernel(grad, mixed, message):
    fill_message(message, grad[...], mixed[...], jnp.zeros((1, 1), F32))


def grad_message(grad, mixed):
    rows, width = grad.shape
    return pl.pallas_call(
        message_kernel,
        name="grad_message",
        out_shape=jax.ShapeDtypeStruct((rows + EXT, width), BF16),
        compiler_params=params(),
        cost_estimate=cost(4 * rows * width, 10 * rows * width),
    )(grad, mixed)


def dispatch_kernel(sources, slots, backward, scal, *rest):
    msgs, (rank, x_out, side_out, arrived, picked, in_sems, out_sems) = (
        rest[:sources],
        rest[sources:],
    )
    local, rows = rank.shape[1:]
    fetch = lambda j: pltpu.make_async_copy(msgs[j], arrived.at[j], in_sems.at[j])
    send = lambda j: pltpu.make_async_copy(picked.at[j], x_out.at[:, j], out_sems.at[j])
    for j in range(sources):
        fetch(j).start()
    pick_row = lax.broadcasted_iota(jnp.int32, (EXT, 4 * rows), 0)
    for j in range(sources):
        fetch(j).wait()
        taken = mm(hot_rows(rank, j, slots), arrived[j, :rows, :]).astype(BF16)
        for i in range(local):
            picked[j, i] = taken[i * slots : (i + 1) * slots]
        send(j).start()
        if backward:
            ext = arrived[j, rows:, :rows].astype(F32)
            side_out[j, 0:1, :] = ext[0:1, :] + ext[1:2, :]
            side_out[j, 1:2, :] = ext[2:3, :] + ext[3:4, :] + ext[4:5, :]
        else:
            ext = arrived[j, rows:, : 4 * rows].astype(F32)
            for i in range(local):
                expert = scal[0] + i
                row = jnp.sum(jnp.where(pick_row == expert % EXT, ext, 0.0), axis=0, keepdims=True)
                high = jnp.where(expert < EXT, row[:, :rows], row[:, rows : 2 * rows])
                low = jnp.where(expert < EXT, row[:, 2 * rows : 3 * rows], row[:, 3 * rows :])
                side_out[j, i : i + 1, :] = high + low
    for j in range(sources):
        send(j).wait()


def dispatch(scal, msgs, rank, slots, backward):
    sources, local, rows = rank.shape
    width = msgs[0].shape[1]
    anywhere = pl.BlockSpec(memory_space=pl.ANY)
    side = (sources, 2 if backward else local, rows)
    taken, beside = pl.pallas_call(
        functools.partial(dispatch_kernel, sources, slots, backward),
        name="dispatch",
        grid=(1,),
        in_specs=[
            pl.BlockSpec(memory_space=pltpu.SMEM),
            *[anywhere for _ in msgs],
            fixed(rank.shape),
        ],
        out_specs=[anywhere, resident(side)],
        out_shape=[
            jax.ShapeDtypeStruct((local, sources, slots, width), BF16),
            jax.ShapeDtypeStruct(side, F32),
        ],
        scratch_shapes=[
            pltpu.VMEM((sources, rows + EXT, width), BF16),
            pltpu.VMEM((sources, local, slots, width), BF16),
            pltpu.SemaphoreType.DMA((sources,)),
            pltpu.SemaphoreType.DMA((sources,)),
        ],
        compiler_params=params(1),
        cost_estimate=cost(
            2 * local * sources * slots * rows * width,
            2 * sources * width * (rows + local * slots),
            0,
            0.05 * local,
        ),
    )(scal, *msgs, rank)
    return taken.reshape(local, sources * slots, width), beside


def fill_weights(scal, blocks, w1, w2):
    up = w1.shape[0] // len(blocks)
    down = w2.shape[0] // len(blocks)
    for k, block in enumerate(blocks):
        at = scal[1 + k]
        w1[pl.ds(pl.multiple_of(at * up, up), up), :] = block[0, :up]
        w2[pl.ds(pl.multiple_of(at * down, down), down), :] = block[0, up:]


def experts_kernel(sources, depth, slots, chained, combined, scal, *rest):
    prior = ()
    if chained:
        prior, rest = rest[:sources], rest[sources:]
    rank, gates, xs, rest = *rest[:3], rest[3:]
    blocks, rest = rest[:depth], rest[depth:]
    gu_out, y_out, rest = *rest[:2], rest[2:]
    if combined:
        outs, rest = rest[:sources], rest[sources:]
        held, w1, w2 = rest[:3]
    else:
        rows_out, w1, w2 = rest
    width = w1.shape[0]
    step, part = pl.program_id(0), pl.program_id(1)
    portions = sources // (xs.shape[1] // slots)
    portion = sources // portions

    @pl.when(part == 0)
    def _():
        fill_weights(scal, blocks, w1, w2)

    gate_up = mm(xs[0], w1[...])
    gu_out[0] = gate_up
    gate, up = gate_up[:, :FF_E], gate_up[:, FF_E:]
    activated = (gate * jax.nn.sigmoid(gate) * up).astype(BF16)
    out = mm(activated, w2[...]).astype(BF16)
    y_out[0] = out
    column = gate_columns(
        rank,
        lambda j: gates[j, pl.ds(step, 1), :],
        step,
        [part * portion + n for n in range(portion)],
        slots,
    )
    given = (column * out.astype(F32)).astype(BF16).reshape(portion, slots, width)
    if combined:
        held[step, pl.ds(part * portion, portion)] = given

        @pl.when((step == pl.num_programs(0) - 1) & (part == portions - 1))
        def _():
            combine(rank, held, prior, outs, rest[3:], slots)

    else:
        rows_out[0] = given


def weight_specs(blocks, depth, base=0):
    arrays = blocks if len(blocks) == depth else blocks * depth
    rows = arrays[0].shape[1] // (depth // len(blocks))
    width = arrays[0].shape[2]
    specs = [
        pl.BlockSpec((1, rows, width), lambda e, r, f=(k if len(blocks) == 1 else 0): (e + base, f, 0))
        for k in range(depth)
    ]
    return arrays, specs


def combine_kernel(order, rank, *refs):
    parts, rest = refs[: len(order)], refs[len(order) :]
    outs, buffers = rest[:-4], rest[-4:]
    slots = parts[0].shape[2]
    combine(rank, [parts[o] for o in order], (), outs, buffers, slots)


def combine_rows(rank, parts, order, slots):
    sources, _, rows = rank.shape
    width = parts[0].shape[-1]
    parts = [part.reshape(part.shape[0], sources, slots, width) for part in parts]
    return list(
        pl.pallas_call(
            functools.partial(combine_kernel, order),
            name="combine_rows",
            grid=(1,),
            in_specs=[fixed(rank.shape), *[fixed(part.shape) for part in parts]],
            out_specs=[pl.BlockSpec(memory_space=pl.ANY)] * sources,
            out_shape=[jax.ShapeDtypeStruct((rows, width), BF16)] * sources,
            scratch_shapes=stream_scratch(rows, width),
            compiler_params=params(1),
            cost_estimate=cost(
                2 * sources * rows * width * rank.shape[1] * slots,
                4 * sources * width * rank.shape[1] * slots,
                share=0.2,
            ),
        )(rank, *parts)
    )


def stream_scratch(rows, width):
    return [
        pltpu.VMEM((4, rows, width), BF16),
        pltpu.VMEM((4, rows, width), BF16),
        pltpu.SemaphoreType.DMA((4,)),
        pltpu.SemaphoreType.DMA((4,)),
    ]


def experts_forward(scal, xs, rank, gates, blocks, depth, slots, first, prior=(), combined=True):
    sources, local, rows = rank.shape
    width = xs.shape[2]
    portions = max(1, sources // 8)
    count = sources * slots
    arrays, specs = weight_specs(blocks, depth)
    anywhere = pl.BlockSpec(memory_space=pl.ANY)
    each = lambda shape, base=0: pl.BlockSpec((1,) + shape, lambda e, r: (e + base, r, 0))
    outs = pl.pallas_call(
        functools.partial(experts_kernel, sources, depth, slots, bool(prior), combined),
        name="experts_forward",
        grid=(local, portions),
        in_specs=[
            pl.BlockSpec(memory_space=pltpu.SMEM),
            *[anywhere for _ in prior],
            fixed((sources, local, rows)),
            fixed((sources, local, rows)),
            each((count // portions, width), first),
            *specs,
        ],
        out_specs=[
            each((count // portions, 2 * FF_E)),
            each((count // portions, width)),
            *(
                [anywhere] * sources
                if combined
                else [
                    pl.BlockSpec((1, sources // portions, slots, width), lambda e, r: (e, r, 0, 0))
                ]
            ),
        ],
        out_shape=[
            jax.ShapeDtypeStruct((local, count, 2 * FF_E), F32),
            jax.ShapeDtypeStruct((local, count, width), BF16),
            *(
                [jax.ShapeDtypeStruct((rows, width), BF16)] * sources
                if combined
                else [jax.ShapeDtypeStruct((local, sources, slots, width), BF16)]
            ),
        ],
        scratch_shapes=[
            *([pltpu.VMEM((local, sources, slots, width), BF16)] if combined else []),
            pltpu.VMEM((width, 2 * FF_E), BF16),
            pltpu.VMEM((FF_E, width), BF16),
            *(stream_scratch(rows, width) if combined else []),
        ],
        compiler_params=params(2),
        cost_estimate=cost(
            2 * local * count * width * 3 * FF_E * 1.3,
            8 * local * count * width,
            local * count * FF_E,
            0.1 * (local + 1),
        ),
    )(scal, *prior, rank, gates, xs, *arrays)
    return outs[:2], list(outs[2:])


def experts_back_kernel(sources, depth, slots, mode, scal, *rest):
    last, order, direct = mode
    earlier = ()
    if last:
        full_rank, rest = rest[0], rest[1:]
        earlier, rest = rest[: len(order) - 1], rest[len(order) - 1 :]
    if direct:
        rank, gates, rest = *rest[:2], rest[2:]
        given_rows, rest = rest[:sources], rest[sources:]
    else:
        rank, gates, inners, grads, rest = *rest[:4], rest[4:]
    xs, gu, ys, router, rest = *rest[:4], rest[4:]
    blocks, rest = rest[:depth], rest[depth:]
    grad_out_ref, router_out, rest = *rest[:2], rest[2:]
    outs, rest = (rest[:sources], rest[sources:]) if last else (rest[:1], rest[1:])
    held, w1, w2, sum1, sum2 = rest[:5]
    width = w1.shape[0]
    step, part = pl.program_id(0), pl.program_id(1)
    portions = sources // (xs.shape[1] // slots)
    portion = sources // portions

    @pl.when(part == 0)
    def _():
        fill_weights(scal, blocks, w1, w2)

    mine = [part * portion + n for n in range(portion)]
    gate_column = gate_columns(rank, lambda j: gates[j, pl.ds(step, 1), :], step, mine, slots)
    if direct:
        blocks_of = [ref[0] if len(ref.shape) == 3 else ref[...] for ref in given_rows]
        blocks_of = [block.astype(F32) for block in blocks_of]
        grad_out = jnp.concatenate(blocks_of, axis=0)
        inner_column = jnp.concatenate(
            [
                jnp.transpose(block[slots - 8 :, :128])[:slots, :2].sum(axis=1, keepdims=True)
                for block in blocks_of
            ],
            axis=0,
        )
    else:
        inner_column = gate_columns(rank, lambda j: inners[j, 0:1, :], step, mine, slots)
        grad_out = grads[0].astype(F32)
    grad_y = (gate_column * grad_out).astype(BF16)
    given = jnp.sum(grad_out * ys[0].astype(F32), axis=1, keepdims=True)
    grad_logit = gate_column * (given - inner_column)
    gate, up = gu[0, :, :FF_E], gu[0, :, FF_E:]
    sigmoid = jax.nn.sigmoid(gate)
    silu = gate * sigmoid
    activated = (silu * up).astype(BF16)
    down_part = mm_tn(activated, grad_y)
    grad_act = mm_nt(grad_y, w2[...])
    grad_gate = grad_act * up * sigmoid * (1.0 + gate * (1.0 - sigmoid))
    grad_up = grad_act * silu
    grad_gate_up = jnp.concatenate([grad_gate.astype(BF16), grad_up.astype(BF16)], axis=1)
    taken = xs[0]
    up_part = mm_tn(taken, grad_gate_up)
    router_part = jnp.sum(taken.astype(F32) * grad_logit, axis=0, keepdims=True)
    grad_rows = mm_nt(grad_gate_up, w1[...]) + grad_logit * router[0]
    if last:
        held[step, pl.ds(part * portion, portion)] = grad_rows.astype(BF16).reshape(
            portion, slots, width
        )
    else:
        outs[0][0] = grad_rows.astype(BF16)

    def write(up_total, down_total):
        up_rows, down_rows = width // depth, FF_E // depth
        for f in range(depth):
            top = f * (up_rows + down_rows)
            grad_out_ref[0, top : top + up_rows, :] = up_total[
                f * up_rows : (f + 1) * up_rows
            ].astype(BF16)
            grad_out_ref[0, top + up_rows : top + up_rows + down_rows, :] = down_total[
                f * down_rows : (f + 1) * down_rows
            ].astype(BF16)

    if sum1 is None:
        write(up_part, down_part)
        router_out[0] = router_part
    else:

        @pl.when(part == 0)
        def _():
            sum1[...] = up_part
            sum2[...] = down_part
            router_out[0] = router_part

        @pl.when(part > 0)
        def _():
            sum1[...] += up_part
            sum2[...] += down_part
            router_out[0] += router_part

        @pl.when(part == portions - 1)
        def _():
            write(sum1, sum2)

    if last:

        @pl.when((step == pl.num_programs(0) - 1) & (part == portions - 1))
        def _():
            pieces = list(earlier) + [held]
            combine(full_rank, [pieces[o] for o in order], (), outs, rest[5:], slots)


def experts_backward(
    scal, grads, rank, gates, inners, xs, kept, router, blocks, depth, slots, first, base, begin, last
):
    direct = isinstance(grads, list)
    sources, local, rows = rank.shape
    width = xs.shape[2]
    portions = max(1, sources // 8)
    count = sources * slots
    gu, ys = kept
    arrays, specs = weight_specs(blocks, depth, base)
    merged = width + FF_E
    anywhere = pl.BlockSpec(memory_space=pl.ANY)
    each = lambda shape, base=0: pl.BlockSpec((1,) + shape, lambda e, r: (e + base, r, 0))
    whole = lambda shape: pl.BlockSpec((1,) + shape, lambda e, r: (e, 0, 0))
    before = []
    if last:
        before = [last[0]] + [
            part.reshape(part.shape[0], sources, slots, width) for part in last[1]
        ]
    mode = (bool(last), last[2] if last else (), direct)
    if direct:
        given = grads
        given_specs = [
            fixed(block.shape)
            if block.ndim == 2
            else pl.BlockSpec(
                (1,) + block.shape[1:], lambda *_: (0, 0, 0), pipeline_mode=pl.Buffered(1)
            )
            for block in grads
        ]
    else:
        given = [inners, grads]
        given_specs = [fixed((sources, 2, rows)), each((count // portions, width), begin)]

    def kernel(*refs):
        refs = list(refs)
        if portions == 1:
            at = len(refs) - (4 if last else 0)
            refs[at:at] = [None, None]
        if not last:
            refs[-4:-4] = [None]
        experts_back_kernel(sources, depth, slots, mode, *refs)

    sums = [pltpu.VMEM((width, 2 * FF_E), F32), pltpu.VMEM((FF_E, width), F32)]
    outs = pl.pallas_call(
        kernel,
        name="experts_backward",
        grid=(local, portions),
        in_specs=[
            pl.BlockSpec(memory_space=pltpu.SMEM),
            *[fixed(part.shape) for part in before],
            fixed((sources, local, rows)),
            fixed((sources, local, rows)),
            *given_specs,
            each((count // portions, width), first),
            each((count // portions, 2 * FF_E), base),
            each((count // portions, width), base),
            whole((1, width)),
            *specs,
        ],
        out_specs=[
            whole((merged, width)),
            whole((1, width)),
            *([anywhere] * sources if last else [each((count // portions, width))]),
        ],
        out_shape=[
            jax.ShapeDtypeStruct((local, merged, width), BF16),
            jax.ShapeDtypeStruct((local, 1, width), F32),
            *(
                [jax.ShapeDtypeStruct((rows, width), BF16)] * sources
                if last
                else [jax.ShapeDtypeStruct((local, count, width), BF16)]
            ),
        ],
        scratch_shapes=[
            *([pltpu.VMEM((local, sources, slots, width), BF16)] if last else []),
            pltpu.VMEM((width, 2 * FF_E), BF16),
            pltpu.VMEM((FF_E, width), BF16),
            *(sums if portions > 1 else []),
            *(stream_scratch(rows, width) if last else []),
        ],
        compiler_params=params(2),
        cost_estimate=cost(
            2 * local * count * width * 3 * FF_E * 2.3,
            14 * local * count * width,
            local * count * FF_E,
            0.37,
        ),
    )(scal, *before, rank, gates, *given, xs, gu, ys, router, *arrays)
    return outs[0], outs[1], list(outs[2:])


def place_kernel(places, number, aliased, scal, *refs):
    parts, (up_out, down_out) = refs[: -2 - aliased], refs[-2:]
    step = number(pl.program_id(0))
    up_rows = up_out.shape[1]

    def put(block):
        up_out[0] = block[0, :up_rows].astype(F32)
        down_out[0] = block[0, up_rows:].astype(F32)

    at = 0
    for place in places:
        core, base, count = place
        pl.when((scal[0] == core) & (step >= base) & (step < base + count))(
            functools.partial(put, parts[at])
        )
        at += 1


def place_experts(scal, pieces, held_experts, up_rows, experts, into=()):
    rows, width = pieces[0][2].shape[1:]
    run = next((i for i in range(1, len(experts)) if experts[i] != experts[0] + i), len(experts))
    skip = experts[run] - experts[run - 1] if run < len(experts) else 1
    number = lambda i: experts[0] + (i // run) * (run - 1 + skip) + i % run
    assert [number(i) for i in range(len(experts))] == list(experts)
    places = [(core, base, array.shape[0]) for core, base, array in pieces]
    arrays = [array for _, _, array in pieces]
    specs = [
        pl.BlockSpec(
            (1, rows, width),
            lambda i, scal, base=base, top=count - 1: (jnp.clip(number(i) - base, 0, top), 0, 0),
        )
        for _, base, count in places
    ]
    specs += [pl.BlockSpec(memory_space=pl.ANY) for _ in into]
    return pl.pallas_call(
        functools.partial(place_kernel, places, number, len(into)),
        name="place_experts",
        grid_spec=pltpu.PrefetchScalarGridSpec(
            num_scalar_prefetch=1,
            grid=(len(experts),),
            in_specs=specs,
            out_specs=[
                pl.BlockSpec((1, up_rows, width), lambda i, scal: (number(i), 0, 0)),
                pl.BlockSpec((1, rows - up_rows, width), lambda i, scal: (number(i), 0, 0)),
            ],
        ),
        out_shape=[
            jax.ShapeDtypeStruct((held_experts, up_rows, width), F32),
            jax.ShapeDtypeStruct((held_experts, rows - up_rows, width), F32),
        ],
        input_output_aliases={1 + len(arrays) + i: i for i in range(len(into))},
        compiler_params=params(1),
        cost_estimate=cost(0, 8 * len(experts) * rows * width),
    )(scal, *arrays, *into)


def pack_kernel(scal, up, down, out):
    up_rows = up.shape[1]
    out[0, :up_rows, :] = up[0]
    out[0, up_rows:, :] = down[0]


def pack_experts(half, up, down):
    experts, up_rows, width = up.shape
    rows = up_rows + down.shape[1]
    local = experts // 2
    take = lambda i, scal: (scal[0] * local + i, 0, 0)
    return pl.pallas_call(
        pack_kernel,
        name="pack_experts",
        grid_spec=pltpu.PrefetchScalarGridSpec(
            num_scalar_prefetch=1,
            grid=(local,),
            in_specs=[
                pl.BlockSpec((1, up_rows, width), take),
                pl.BlockSpec((1, rows - up_rows, width), take),
            ],
            out_specs=pl.BlockSpec((1, rows, width), lambda i, scal: (i, 0, 0)),
        ),
        out_shape=jax.ShapeDtypeStruct((local, rows, width), BF16),
        compiler_params=params(1),
        cost_estimate=cost(0, 4 * local * rows * width),
    )(half.astype(jnp.int32).reshape(1), up, down)


def assemble_kernel(devices, depth, scal, *refs):
    owns, others, whole, sem = refs[:devices], refs[devices : 2 * devices], refs[-2], refs[-1]
    piece = whole.shape[0] // (devices * depth)
    for home, blocks in ((1, owns), (0, others)):

        @pl.when(scal[0] == home)
        def _(blocks=blocks):
            for k in range(devices):
                for i in range(depth):
                    to = pl.multiple_of(((scal[1] ^ k) * depth + (scal[2] ^ i)) * piece, piece)
                    pltpu.make_async_copy(
                        blocks[k].at[pl.ds(i * piece, piece)], whole.at[pl.ds(to, piece)], sem
                    ).start()
            pltpu.make_async_copy(whole, whole, sem).wait()


def assemble(scal, owns, others, depth):
    devices = len(owns)
    rows, columns = owns[0].shape
    return pl.pallas_call(
        functools.partial(assemble_kernel, devices, depth),
        name="assemble",
        in_specs=[pl.BlockSpec(memory_space=pltpu.SMEM)]
        + [pl.BlockSpec(memory_space=pl.ANY)] * (2 * devices),
        out_specs=pl.BlockSpec(memory_space=pltpu.VMEM),
        out_shape=jax.ShapeDtypeStruct((rows * devices, columns), owns[0].dtype),
        scratch_shapes=[pltpu.SemaphoreType.DMA(())],
        compiler_params=params(),
        cost_estimate=cost(0, 4 * rows * devices * columns),
    )(scal, *owns, *others)


def attend_back_kernel(devices, arrived, scal, *rest):
    parts, rest = rest[:arrived], rest[arrived:]
    grad_out, middle, gain, attended, wo, q, lse, cosine, sine, x, gain_first = rest[:11]
    ks, vs, rest = rest[11 : 11 + devices], rest[11 + devices : 11 + 2 * devices], rest[11 + 2 * devices :]
    mid_out, weight_grads, gain_grad, dq_out = rest[:4]
    dkv_outs, (bias, held) = rest[4 : 4 + devices], rest[4 + devices :]
    width = middle.shape[1]
    rows = middle.shape[0]
    scale = 1.0 / math.sqrt(HD)
    step = pl.program_id(0)

    @pl.when(step == 0)
    def _():
        fill_bias(bias, scal, devices, rows)
        grad_mix = parts[0][...].astype(F32)
        for part in parts[1:]:
            grad_mix = grad_mix + part[...].astype(F32)
        mid = middle[...]
        factor = lax.rsqrt(jnp.mean(mid * mid, axis=-1, keepdims=True) + epsilon)
        scaled = grad_mix * gain[...]
        inner = jnp.mean(mid * scaled, axis=-1, keepdims=True)
        gain_grad[...] = jnp.sum(grad_mix * mid * factor, axis=0, keepdims=True)
        grad_mid = grad_out[...] + factor * scaled - mid * (factor * factor * factor * inner)
        mid_out[...] = grad_mid
        branch = grad_mid.astype(BF16)
        weight_grads[:, :width] = mm_tn(attended[...], branch).astype(BF16)
        held[...] = mm_nt(branch, wo[...]).astype(BF16)

    keys = jnp.concatenate([r[0] for r in ks], axis=0)
    values = jnp.concatenate([r[0] for r in vs], axis=0)
    block_bias = bias[...]
    both_bias = jnp.concatenate([block_bias, block_bias], axis=1)
    key_parts, value_parts = [], []
    for i in range(2):
        block = q[:, i * 128 : (i + 1) * 128]
        at = pl.multiple_of(step * 256 + i * 128, 128)
        grads = held[:, pl.ds(at, 128)]
        scores = mm_nt(doubled(keys, i), two_heads(block)) * scale + both_bias
        probs = jnp.exp(scores - lse[0, i : i + 1, :])
        grad_probs = mm_nt(doubled(values, i), two_heads(grads))
        product = probs * grad_probs
        dots = jnp.sum(product, axis=0, keepdims=True)
        grad_scores = (product - probs * dots).astype(BF16)
        key_parts.append(mm(grad_scores, two_heads_doubled(block)) * scale)
        value_parts.append(mm(probs.astype(BF16), two_heads_doubled(grads)))
        moved = mm_tn(keys, grad_scores)[i * HD : (i + 1) * HD] * scale
        pair = jnp.concatenate([moved[:, :rows], moved[:, rows:]], axis=0)
        dq_out[:, pl.ds(at, 128)] = turn(jnp.transpose(pair), cosine[...], sine[...]).astype(BF16)
    even = lane_index(key_parts[0].shape) < HD
    grad_keys = jnp.where(even, key_parts[0], key_parts[1]).astype(BF16)
    grad_values = jnp.where(even, value_parts[0], value_parts[1]).astype(BF16)
    for k in range(devices):
        dkv_outs[k][0] = grad_keys[k * rows : (k + 1) * rows]
        dkv_outs[k][1] = grad_values[k * rows : (k + 1) * rows]

    @pl.when(step == pl.num_programs(0) - 1)
    def _():
        values = x[...].astype(F32)
        factor = lax.rsqrt(jnp.mean(values * values, axis=-1, keepdims=True) + epsilon)
        normed = (values * factor * gain_first[...]).astype(BF16)
        weight_grads[:, width:] = mm_tn(normed, dq_out[...]).astype(BF16)


def attend_backward(
    scal, parts, grad_out, middle, gain, attended, shared, q, lse, cosine, sine, x, gain_first, kvs
):
    rows, width = middle.shape
    devices = len(kvs)
    keys = devices * rows
    kv_specs = [pl.BlockSpec((1, rows, 128), lambda h: (0, 0, h)) for _ in kvs] + [
        pl.BlockSpec((1, rows, 128), lambda h: (1, 0, h)) for _ in kvs
    ]
    return pl.pallas_call(
        functools.partial(attend_back_kernel, devices, len(parts)),
        name="attend_backward",
        grid=(KVH // 2,),
        in_specs=[
            pl.BlockSpec(memory_space=pltpu.SMEM),
            *[fixed((rows, width)) for _ in parts],
            fixed((rows, width)),
            fixed((rows, width)),
            fixed((1, width)),
            fixed((rows, QH * HD)),
            pl.BlockSpec((QH * HD, width), lambda h: (0, 2), pipeline_mode=pl.Buffered(1)),
            pl.BlockSpec((rows, 256), lambda h: (0, h)),
            pl.BlockSpec((1, 2, 2 * rows), lambda h: (h, 0, 0)),
            fixed((rows, 128)),
            fixed((rows, 128)),
            fixed((rows, width)),
            fixed((1, width)),
            *kv_specs,
        ],
        out_specs=[
            resident((rows, width)),
            resident((width, width + QH * HD)),
            resident((1, width)),
            resident((rows, QH * HD)),
            *[pl.BlockSpec((2, rows, 128), lambda h: (0, 0, h)) for _ in kvs],
        ],
        out_shape=[
            jax.ShapeDtypeStruct((rows, width), F32),
            jax.ShapeDtypeStruct((width, width + QH * HD), BF16),
            jax.ShapeDtypeStruct((1, width), F32),
            jax.ShapeDtypeStruct((rows, QH * HD), BF16),
            *[jax.ShapeDtypeStruct((2, rows, KW), BF16) for _ in kvs],
        ],
        scratch_shapes=[pltpu.VMEM((keys, rows), F32), pltpu.VMEM((rows, QH * HD), BF16)],
        compiler_params=params(1),
        cost_estimate=cost(
            10 * rows * keys * QH * HD * 2 + 4 * rows * width * width,
            6 * width * width + 8 * keys * width + 20 * rows * width,
            rows * keys * QH,
            0.23,
        ),
    )(
        scal,
        *parts,
        grad_out,
        middle,
        gain,
        attended,
        shared,
        q,
        lse,
        cosine,
        sine,
        x,
        gain_first,
        *kvs,
        *kvs,
    )


def project_back_kernel(devices, x, gain, dq, *rest):
    parts, rest = rest[:devices], rest[devices:]
    grad_mid, wq, wm, cosine, sine, small, dx_out, packed = rest
    values = x[...].astype(F32)
    width = values.shape[1]
    factor = lax.rsqrt(jnp.mean(values * values, axis=-1, keepdims=True) + epsilon)
    normed = (values * factor * gain[...]).astype(BF16)
    summed = parts[0][...].astype(F32)
    for part in parts[1:]:
        summed = summed + part[...].astype(F32)
    grad_keys = [
        turn(summed[0, :, b * 128 : (b + 1) * 128], cosine[...], sine[...]).astype(BF16)
        for b in range(KW // 128)
    ]
    grad_memory = jnp.concatenate(grad_keys + [summed[1].astype(BF16)], axis=1)
    grad_query = dq[...]
    packed[:, : 2 * KW] = mm_tn(normed, grad_memory).astype(BF16)
    grad_normed = mm_nt(grad_query, wq[...]) + mm_nt(grad_memory, wm[...])
    scaled = grad_normed * gain[...]
    inner = jnp.mean(values * scaled, axis=-1, keepdims=True)
    gain_grad = jnp.sum(grad_normed * values * factor, axis=0, keepdims=True)
    row = lax.broadcasted_iota(jnp.int32, (128, width), 0)
    packed[:, 2 * KW :] = jnp.transpose(
        jnp.where(row == EXPERTS, gain_grad, small[...])
    ).astype(BF16)
    dx_out[...] = (
        grad_mid[...] + factor * scaled - values * (factor * factor * factor * inner)
    )


def project_backward(x, gain, dq, parts, grad_mid, shared, cosine, sine, small):
    rows, width = x.shape
    columns = 2 * KW + 128
    return pl.pallas_call(
        functools.partial(project_back_kernel, len(parts)),
        name="project_backward",
        grid=(1,),
        in_specs=[
            fixed((rows, width)),
            fixed((1, width)),
            fixed((rows, QH * HD)),
            *[fixed((2, rows, KW)) for _ in parts],
            fixed((rows, width)),
            pl.BlockSpec((width, QH * HD), lambda i: (0, 0), pipeline_mode=pl.Buffered(1)),
            pl.BlockSpec((width, 2 * KW), lambda i: (0, 1), pipeline_mode=pl.Buffered(1)),
            fixed((rows, 128)),
            fixed((rows, 128)),
            fixed((128, width)),
        ],
        out_specs=[resident((rows, width)), resident((width, columns))],
        out_shape=[
            jax.ShapeDtypeStruct((rows, width), F32),
            jax.ShapeDtypeStruct((width, columns), BF16),
        ],
        compiler_params=params(1),
        cost_estimate=cost(
            6 * rows * width * 2048, 8 * width * 2048 + 16 * rows * width, share=0.35
        ),
    )(x, gain, dq, *parts, grad_mid, shared, shared, cosine, sine, small)


def pairs_within(axis, by, sections=(0, 1)):
    count = lax.axis_size(axis)
    return [(s * count + i, s * count + (i ^ by)) for s in sections for i in range(count)]


def exchanged(value, axis, by, sections=(0, 1)):
    return lax.ppermute(value, ("section", axis), pairs_within(axis, by, sections))


def swapped(value):
    return lax.ppermute(value, "section", [(0, 1), (1, 0)])


def from_all(value, axis, sections=(0, 1)):
    count = lax.axis_size(axis)
    return [value] + [exchanged(value, axis, k, sections) for k in range(1, count)]


def after(value, other):
    return lax.optimization_barrier((value, other))[0]


def scattered(blocks, axis, sections):
    return [blocks[0]] + [
        exchanged(blocks[k], axis, k, sections) for k in range(1, len(blocks))
    ]


def added(terms):
    return functools.reduce(lambda a, b: a + b, [term.astype(F32) for term in terms])


def shards(
    tokens,
    targets,
    lengths,
    routes,
    attention_gain,
    query_weight,
    memory_weight,
    output_weight,
    mixture_gain,
    router_weight,
    gate_up_weight,
    down_weight,
):
    section = lax.axis_index("section")
    context = lax.axis_index("ctx")
    line = lax.axis_index("fsdp")
    devices = lax.axis_size("ctx")
    depth = lax.axis_size("fsdp")
    first_core = section == 0
    rows, width = tokens.shape[2:]
    layers = 2
    held_experts = gate_up_weight.shape[1]
    half_held = held_experts // 2
    capacity = rows * TOPK * 9 // (EXPERTS * 8)
    slots = -(-capacity // 16) * 16
    up_rows, down_rows = gate_up_weight.shape[2], down_weight.shape[2]
    shard_rows = up_rows + down_rows

    column = context * held_experts
    plain = (column + section * half_held, half_held, 2 * devices)
    places = [plain, plain]

    pack = jnp.concatenate(
        [
            query_weight[0],
            memory_weight[0],
            output_weight[0],
            router_weight[0],
            attention_gain[0][:, None],
            mixture_gain[0][:, None],
            jnp.zeros((query_weight.shape[1], 128 - EXPERTS - 2), BF16),
        ],
        axis=1,
    )

    def shared_of_line(layer, ahead):
        mine = pack if ahead is None else after(pack, ahead)
        return jnp.concatenate(from_all(mine, "fsdp", (layer,)), axis=0)

    def shared_of_plane(layer, block, ahead):
        mine = block if ahead is None else after(block, ahead)
        owns = from_all(mine, "ctx", (layer,))
        others = [lax.ppermute(own, "section", [(layer, 1 - layer)]) for own in owns]
        scal = jnp.stack([(section == layer).astype(jnp.int32), context, line])
        whole = assemble(scal, owns, others, depth)
        small = whole[:, 3 * width :].T
        return (
            whole,
            small[:EXPERTS],
            small[EXPERTS : EXPERTS + 1].astype(F32),
            small[EXPERTS + 1 : EXPERTS + 2].astype(F32),
        )

    my_routes = jnp.swapaxes(routes[0, :, 0], 1, 2)
    other_routes = swapped(my_routes)
    layer_routes = jnp.where(
        first_core,
        jnp.stack([my_routes, other_routes]),
        jnp.stack([other_routes, my_routes])[:, ::-1],
    )
    all_routes = jnp.stack(from_all(layer_routes, "ctx"), axis=2).reshape(
        layers, 2 * devices, TOPK, rows
    )
    source_routes = [all_routes[0], all_routes[1]]
    earlier = (
        lax.broadcasted_iota(jnp.int32, (rows, rows), 0)
        < lax.broadcasted_iota(jnp.int32, (rows, rows), 1)
    ).astype(BF16)

    def ranked(layer):
        first, local, _ = places[layer]
        ids = first + jnp.arange(local, dtype=jnp.int32)
        named = jnp.any(source_routes[layer][:, None] == ids[None, :, None, None], axis=2)
        before = jnp.dot(
            named.astype(BF16).reshape(-1, rows), earlier, preferred_element_type=F32
        ).reshape(named.shape)
        return jnp.where(named, before, -1.0)

    ranks = [ranked(layer) for layer in range(layers)]
    masks = jnp.any(
        layer_routes[:, 0, None] == jnp.arange(EXPERTS, dtype=jnp.int32)[None, :, None, None], axis=2
    ).astype(F32)

    own_ranks = jnp.where(
        masks[1] > 0.5,
        jnp.dot(masks[1].astype(BF16), earlier, preferred_element_type=F32),
        -1.0,
    )
    last_rank = jnp.take(
        own_ranks,
        jnp.stack(
            [
                (context ^ k) * held_experts + (section ^ m) * half_held + half_held - 1
                for k in range(devices)
                for m in range(2)
            ]
        ),
        axis=0,
    )

    line_blocks = [after(shared_of_line(0, None), (ranks, masks, last_rank)), None]

    whole = [(0, half_held)]
    split = [(0, half_held - 1), (half_held - 1, 1)] if half_held > 1 else whole
    runs = [whole, split]
    back_runs = [split, split[::-1]]
    by_rows_fits = half_held > 1 and slots - capacity >= 8 and slots % 16 == 0

    arrived = swapped(pack_experts(1 - section, gate_up_weight[0], down_weight[0]))
    mine = pack_experts(section, gate_up_weight[0], down_weight[0])

    def gathered_experts(layer, ahead):
        own, other = (mine, arrived) if ahead is None else after((mine, arrived), ahead)
        parts = []
        for a, n in runs[layer]:
            shard = jnp.where(section == layer, own[a : a + n], other[a : a + n])
            parts.append([lax.all_gather(shard, "fsdp", axis=1, tiled=True)])
        return parts

    half = rows // 2
    within = jnp.arange(rows, dtype=jnp.int32)
    positions = jnp.where(
        within < half, context * half + within, (2 * devices - 1 - context) * half + within - half
    )
    inverse = rope_base ** (-2.0 * jnp.arange(HD // 2, dtype=F32) / HD)
    angles = positions.astype(F32)[:, None] * inverse[None, :]
    sine, cosine = jnp.sin(angles), jnp.cos(angles)
    cos_table = jnp.concatenate([cosine] * 4, axis=1)
    sin_table = jnp.concatenate([-sine, sine, -sine, sine], axis=1)
    length = lengths[section, line]
    attend_scalars = jnp.stack([context, length]).astype(jnp.int32)

    def dispatched(message):
        plane = from_all(message, "ctx")
        blocks = plane + [swapped(block) for block in plane]
        return blocks

    def returned(outs):
        own, other = outs[:devices], outs[devices : 2 * devices]
        crossed = [swapped(block) for block in other]
        near = [own[0], crossed[0]]
        for k in range(1, devices):
            chip = (own[k].astype(F32) + crossed[k].astype(F32)).astype(BF16)
            near.append(exchanged(chip, "ctx", k))
        return near

    my_targets = lax.dynamic_index_in_dim(targets[:, 0], section, 0, keepdims=False)
    layer_input = lax.dynamic_index_in_dim(tokens[:, 0], section, 0, keepdims=False)
    valid = (positions < length).astype(F32)[:, None]
    saved, hidden = [], []
    early_experts = gathered_experts(0, None)
    ahead = None
    for layer in range(layers):
        first, local, sources = places[layer]
        shared, router, gain_first, gain_second = shared_of_plane(
            layer, line_blocks[layer], ahead
        )
        q, kv = project(layer_input, gain_first, shared, cos_table, sin_table)
        if layer == 0:
            line_blocks[1] = shared_of_line(1, kv)
        kvs = from_all(kv, "ctx")
        attended, lse, middle, message = attend(
            attend_scalars, layer_input, q, kvs, shared, gain_second, router, masks[layer]
        )
        messages = dispatched(message)
        if layer == 0:
            ahead = messages
            weights = early_experts
            late_experts = gathered_experts(1, message)
        else:
            weights = late_experts
        kept, outs = [], ()
        xs, gates = dispatch(
            first.astype(jnp.int32).reshape(1), messages, ranks[layer], slots, False
        )
        sparse = layer == 1 and by_rows_fits
        for at, ((a, n), blocks) in enumerate(zip(runs[layer], weights)):
            scal = jnp.stack([first + a, *[jnp.asarray(k) for k in range(depth)]]).astype(jnp.int32)
            by_rows = sparse and at == len(runs[layer]) - 1
            if by_rows:
                scal = after(scal, terms)
            run, outs = experts_forward(
                scal,
                xs,
                ranks[layer][:, a : a + n],
                gates[:, a : a + n],
                blocks,
                depth,
                slots,
                a,
                () if by_rows else outs,
                not by_rows,
            )
            kept.append((a, n, scal, run, blocks))
            if not by_rows:
                terms = returned(outs)
        if layer == layers - 1:
            routed = [last_rank, [], slots] if sparse else []
            if sparse:
                near, far = outs[0][0, :devices], swapped(outs[0][0, devices:])
                routed[1] = [near[0], far[0]] + [
                    exchanged(jnp.stack([near[k], far[k]]), "ctx", k) for k in range(1, devices)
                ]
            hidden_rows, mixed, grad_output, message, *row_messages = finish(
                terms, middle, my_targets, valid, *routed
            )
            hidden.append(hidden_rows)
        else:
            mixed = functools.reduce(lambda a, b: a + b, [t.astype(F32) for t in terms])
            hidden.append((middle + mixed).astype(BF16))
        saved.append(
            dict(
                x=layer_input,
                shared=shared,
                router=router,
                gain_first=gain_first,
                gain_second=gain_second,
                q=q,
                kvs=kvs,
                attended=attended,
                lse=lse,
                middle=middle,
                kept=kept,
                xs=xs,
                gates=gates,
                mixed=mixed,
            )
        )
        layer_input = hidden[-1]

    def home_blocks(packed, layer):
        arrived = lax.ppermute(packed, "section", [(1 - layer, layer)])
        size = packed.shape[0] // devices
        return [
            (
                lax.dynamic_slice_in_dim(packed, (context ^ k) * size, size, 0).astype(F32)
                + lax.dynamic_slice_in_dim(arrived, (context ^ k) * size, size, 0).astype(F32)
            ).astype(BF16)
            for k in range(devices)
        ]

    def home_plane(blocks, layer):
        return added(scattered(blocks, "ctx", (layer,))).astype(BF16)

    def home_line(plane, layer, ahead=None):
        size = plane.shape[0] // depth
        blocks = [
            lax.dynamic_slice_in_dim(plane, (line ^ k) * size, size, 0) for k in range(depth)
        ]
        if ahead is not None:
            blocks[-1] = after(blocks[-1], ahead)
        return scattered(blocks, "fsdp", (layer,))

    def placed_rows(values):
        home = jnp.where(first_core, values[0], values[1])
        arrived = swapped(jnp.where(first_core, values[1], values[0]))
        return jnp.stack(
            [jnp.where(first_core, home, arrived), jnp.where(first_core, arrived, home)]
        )

    input_grads, expert_grads = [None] * layers, [None] * layers
    waiting = None
    summed = {}
    for layer in reversed(range(layers)):
        held = saved[layer]
        first, local, sources = places[layer]
        if layer < layers - 1:
            message = grad_message(grad_output, held["mixed"])
        sparse = layer == 1 and by_rows_fits
        if sparse:
            plane = [row_messages[0]] + [
                exchanged(row_messages[k], "ctx", k) for k in range(1, devices)
            ]
            row_blocks = plane + [swapped(block[1]) for block in plane]
            message = after(message, plane[1])
        messages = dispatched(message)
        if waiting is not None:
            by = 1
            while by < depth:
                error = error + lax.ppermute(error, "fsdp", [(i, i ^ by) for i in range(depth)])
                by *= 2
            loss_value = error / jnp.sum(lengths).astype(F32)
            hidden_out = placed_rows(hidden)
            blocks_1 = [waiting[0], home_blocks(waiting[1], 1)]
            messages = after(messages, (blocks_1, loss_value, hidden_out))
            planes = [home_plane(blocks, 1) for blocks in after(blocks_1, messages)]
        own_router = lax.dynamic_slice_in_dim(held["router"], first, local, 0).astype(F32)
        small = jnp.zeros((128, width), F32)
        outs = ()
        gathered = []
        steps = back_runs[layer]
        spans = [a for a, _ in steps]
        for at, (a, n) in enumerate(steps):
            base, _, scal, run, blocks = next(
                kept for kept in held["kept"] if kept[0] <= a and a + n <= kept[0] + kept[1]
            )
            scal = jnp.concatenate([scal[:1] + (a - base), scal[1:]])
            last = None
            if at == len(steps) - 1 and not sparse:
                order = tuple(sorted(range(len(spans)), key=lambda i: spans[i]))
                last = (ranks[layer], [rows_of for rows_of in outs], order)
            if sparse and at == 0:
                grad_rows, inners, start = row_blocks, None, a
            elif not sparse:
                grad_rows, inners = dispatch(
                    scal[:1], messages, ranks[layer][:, a : a + n], slots, True
                )
                start = a
            elif at == 1:
                start = 0
                grad_rows, inners = dispatch(
                    scal[:1], messages, ranks[layer][:, : half_held - 1], slots, True
                )
            grads, router_grad, rows_out = experts_backward(
                scal,
                grad_rows,
                ranks[layer][:, a : a + n],
                held["gates"][:, a : a + n],
                inners,
                held["xs"],
                run,
                own_router[a : a + n, None, :],
                blocks,
                depth,
                slots,
                a,
                a - base,
                a - start,
                last,
            )
            outs = rows_out if last else list(outs) + rows_out
            if layer == 1 and inners is not None:
                error = jnp.sum(inners[:, 1, 0])
            small = lax.dynamic_update_slice_in_dim(small, router_grad[:, 0], first + a, 0)
            gathered.append(grads)
        if sparse:
            order = tuple(sorted(range(len(spans)), key=lambda i: spans[i]))
            outs = combine_rows(ranks[layer], outs, order, slots)
        over_line = lambda grads: lax.psum_scatter(
            grads, "fsdp", scatter_dimension=1, tiled=True
        )
        at_once = gathered if layer == 1 or len(gathered) == 1 else gathered[:-1]
        summed[layer] = [over_line(grads) for grads in at_once]
        if layer == 1:
            grad_output = after(grad_output, summed[1][0])
        else:
            grad_output = after(grad_output, summed[1][-1])
            outs = after(outs, planes)
        back = attend_backward(
            attend_scalars,
            returned(outs),
            grad_output,
            held["middle"],
            held["gain_second"],
            held["attended"],
            held["shared"],
            held["q"],
            held["lse"],
            cos_table,
            -sin_table,
            held["x"],
            held["gain_first"],
            held["kvs"],
        )
        grad_mid, weight_grads, gain_second_grad, dq = back[:4]
        dkv = back[4:]
        parts = [dkv[0]] + [exchanged(dkv[k], "ctx", k) for k in range(1, devices)]
        outward = home_blocks(weight_grads, layer)
        grad_mid = after(grad_mid, outward)
        small = lax.dynamic_update_slice_in_dim(small, gain_second_grad, EXPERTS + 1, 0)
        dx, packed = project_backward(
            held["x"],
            held["gain_first"],
            dq,
            parts,
            grad_mid,
            held["shared"],
            cos_table,
            -sin_table,
            small,
        )
        expert_grads[layer] = (spans, summed[layer])
        input_grads[layer] = dx
        grad_output = dx.astype(BF16).astype(F32)
        if layer == 1:
            waiting = (outward, packed)
        else:
            outward = after(outward, packed)
            summed[0] += [over_line(after(grads, packed)) for grads in gathered[len(at_once) :]]
            inward_plane = home_plane(home_blocks(packed, 0), 0)
            outward_plane = home_plane(outward, 0)

    def pieces_of(layer, at, part):
        arrived = lax.ppermute(part, "section", [(1 - layer, layer)])
        return [
            (layer, half * half_held + at, term)
            for half, term in ((layer, part), (1 - layer, arrived))
        ]

    def placed(pieces, experts, into):
        touched = [p for p in pieces if any(0 <= e - p[1] < p[2].shape[0] for e in experts)]
        return place_experts(
            section.astype(jnp.int32).reshape(1), touched, held_experts, up_rows, experts, into
        )

    parts = [(layer, at, part) for layer in (1, 0) for at, part in zip(*expert_grads[layer])]
    pieces = [piece for part in parts[:-1] for piece in pieces_of(*part)]
    layer, at, part = parts[-1]
    last = [half * half_held + at + i for half in range(2) for i in range(part.shape[0])]
    sums = ()
    if len(last) < held_experts:
        sums = placed(pieces, [e for e in range(held_experts) if e not in last], ())
    first_terms = home_line(
        jnp.concatenate([outward_plane, inward_plane], axis=1), 0, sums if sums else None
    )
    second_terms = home_line(jnp.concatenate(planes, axis=1), 1)
    shared_grads = jnp.where(first_core, added(first_terms), added(second_terms))
    outward, inward = shared_grads[:, : 2 * width], shared_grads[:, 2 * width :]
    input_out = placed_rows(after(input_grads, inward_plane))
    if sums:
        part = after(part, (first_terms, second_terms))
    up_sum, down_sum = placed(pieces + pieces_of(layer, at, part), last, sums)
    at = 2 * KW
    return (
        hidden_out[None, :, None],
        input_out[None, :, None],
        loss_value,
        inward[:, at + EXPERTS][None],
        outward[:, width:][None],
        inward[:, :at][None],
        outward[:, :width][None],
        inward[:, at + EXPERTS + 1][None],
        inward[:, at : at + EXPERTS][None],
        up_sum[None],
        down_sum[None],
    )


def solution(mesh):
    placed = (
        P(None, "fsdp", "ctx", None),
        P(None, "fsdp", "ctx", None),
        P(),
        P("section", None, "fsdp", "ctx", None),
        P("section", ("ctx", "fsdp")),
        P("section", ("ctx", "fsdp"), None),
        P("section", ("ctx", "fsdp"), None),
        P("section", ("ctx", "fsdp"), None),
        P("section", ("ctx", "fsdp")),
        P("section", ("ctx", "fsdp"), None),
        P("section", "ctx", "fsdp", None),
        P("section", "ctx", "fsdp", None),
    )
    return jax.shard_map(
        shards,
        mesh=mesh,
        in_specs=placed,
        out_specs=(
            P("section", None, "fsdp", "ctx", None),
            P("section", None, "fsdp", "ctx", None),
            P(),
            P("section", ("ctx", "fsdp")),
            P("section", ("ctx", "fsdp"), None),
            P("section", ("ctx", "fsdp"), None),
            P("section", ("ctx", "fsdp"), None),
            P("section", ("ctx", "fsdp")),
            P("section", ("ctx", "fsdp"), None),
            P("section", "ctx", "fsdp", None),
            P("section", "ctx", "fsdp", None),
        ),
        check_vma=False,
    )
```

```python
import functools
import math

import jax
import jax.numpy as jnp
from jax import lax
from jax.experimental import pallas as pl
from jax.experimental.pallas import tpu as pltpu
from jax.sharding import PartitionSpec as P

QH = 16
KVH = 8
HD = 64
EXPERTS = 32
FF_E = 512
TOPK = 8
KW = KVH * HD
EXT = 16

epsilon = 1e-06
rope_base = 10000.0
negative = -1e30
F32 = jnp.float32
BF16 = jnp.bfloat16
VMEM_LIMIT = 60 * 1024 * 1024


def params(grid_dims=0):
    return pltpu.CompilerParams(
        vmem_limit_bytes=VMEM_LIMIT,
        dimension_semantics=("arbitrary",) * grid_dims if grid_dims else None,
    )


def cost(flops, moved, exps=0, share=1.0):
    return pl.CostEstimate(
        flops=int(flops / share), bytes_accessed=int(moved), transcendentals=int(exps)
    )


def mm(a, b):
    return jnp.dot(a, b, preferred_element_type=F32)


def mm_nt(a, b):
    return lax.dot_general(a, b, (((1,), (1,)), ((), ())), preferred_element_type=F32)


def mm_tn(a, b):
    return lax.dot_general(a, b, (((0,), (0,)), ((), ())), preferred_element_type=F32)


def fixed(shape):
    return pl.BlockSpec(shape, lambda *_: (0,) * len(shape), pipeline_mode=pl.Buffered(1))


def resident(shape):
    return pl.BlockSpec(shape, lambda *_: (0,) * len(shape))


def lane_index(shape):
    return lax.broadcasted_iota(jnp.int32, shape, len(shape) - 1)


def turn(block, cosine, sine):
    low_half = lane_index(block.shape) % HD < HD // 2
    swapped = jnp.where(
        low_half, pltpu.roll(block, 128 - HD // 2, axis=1), pltpu.roll(block, HD // 2, axis=1)
    )
    return block * cosine + swapped * sine


def rolled(block):
    return pltpu.roll(block.astype(F32), HD, axis=1).astype(BF16)


def key_positions(device, half, devices, shape, dim):
    within = lax.broadcasted_iota(jnp.int32, shape, dim)
    return jnp.where(
        within < half, device * half + within, (2 * devices - 1 - device) * half + within - half
    )


def fill_bias(bias, scal, devices, rows):
    context, length = scal[0], scal[1]
    query_pos = key_positions(context, rows // 2, devices, (rows, rows), 1)
    for k in range(devices):
        key_pos = key_positions(context ^ k, rows // 2, devices, (rows, rows), 0)
        taken = (key_pos <= query_pos) & (key_pos < length)
        bias[k * rows : (k + 1) * rows, :] = jnp.where(taken, 0.0, negative)


def two_heads(block):
    even = lane_index(block.shape) < HD
    zero = jnp.zeros((), block.dtype)
    return jnp.concatenate([jnp.where(even, block, zero), jnp.where(even, zero, block)], axis=0)


def two_heads_doubled(block):
    even = lane_index(block.shape) < HD
    other = rolled(block)
    return jnp.concatenate([jnp.where(even, block, other), jnp.where(even, other, block)], axis=0)


def doubled(block, odd):
    even = lane_index(block.shape) < HD
    other = rolled(block)
    return jnp.where(even, other, block) if odd else jnp.where(even, block, other)


def one_hot(rank_row, slots):
    rows = rank_row.shape[-1]
    index = lax.broadcasted_iota(jnp.int32, (slots, rows), 0).astype(F32)
    return rank_row == index


def project_kernel(x, gain, wq, wm, cosine, sine, q_out, kv_out):
    values = x[...].astype(F32)
    factor = lax.rsqrt(jnp.mean(values * values, axis=-1, keepdims=True) + epsilon)
    normed = (values * factor * gain[...]).astype(BF16)
    cos, sin = cosine[...], sine[...]
    q0 = mm(normed, wq[...])
    for b in range(QH * HD // 128):
        at = slice(b * 128, (b + 1) * 128)
        q_out[:, at] = turn(q0[:, at], cos, sin).astype(BF16)
    kv0 = mm(normed, wm[...])
    for b in range(KW // 128):
        at = slice(b * 128, (b + 1) * 128)
        kv_out[0, :, at] = turn(kv0[:, at], cos, sin).astype(BF16)
    kv_out[1] = kv0[:, KW:].astype(BF16)


def project(x, gain, shared, cosine, sine):
    rows, width = x.shape
    return pl.pallas_call(
        project_kernel,
        name="project",
        grid=(1,),
        in_specs=[
            fixed((rows, width)),
            fixed((1, width)),
            pl.BlockSpec((width, QH * HD), lambda i: (0, 0), pipeline_mode=pl.Buffered(1)),
            pl.BlockSpec((width, 2 * KW), lambda i: (0, 1), pipeline_mode=pl.Buffered(1)),
            fixed((rows, 128)),
            fixed((rows, 128)),
        ],
        out_specs=[resident((rows, QH * HD)), resident((2, rows, KW))],
        out_shape=[
            jax.ShapeDtypeStruct((rows, QH * HD), BF16),
            jax.ShapeDtypeStruct((2, rows, KW), BF16),
        ],
        compiler_params=params(1),
        cost_estimate=cost(
            2 * rows * width * 2048, 2 * width * 2048 + 8 * rows * width, share=0.2
        ),
    )(x, gain, shared, shared, cosine, sine)


def attend_kernel(devices, scal, x, q, *rest):
    ks, vs, rest = rest[:devices], rest[devices : 2 * devices], rest[2 * devices :]
    wo, gain, router, mask, o_out, lse_out, mid_out, msg_out, bias, held = rest
    rows = x.shape[0]
    step = pl.program_id(0)

    @pl.when(step == 0)
    def _():
        fill_bias(bias, scal, devices, rows)

    keys = jnp.concatenate([r[0] for r in ks], axis=0)
    values = jnp.concatenate([r[0] for r in vs], axis=0)
    block_bias = bias[...]
    both_bias = jnp.concatenate([block_bias, block_bias], axis=1)
    for i in range(2):
        query = two_heads(q[:, i * 128 : (i + 1) * 128])
        scores = mm_nt(doubled(keys, i), query) * (1.0 / math.sqrt(HD)) + both_bias
        top = jnp.max(scores, axis=0, keepdims=True)
        raised = jnp.exp(scores - top)
        total = jnp.sum(raised, axis=0, keepdims=True)
        probs = (raised * (1.0 / total)).astype(BF16)
        lse_out[0, i : i + 1, :] = top + jnp.log(total)
        mixed = mm_tn(values, probs)[i * HD : (i + 1) * HD]
        pair = jnp.concatenate([mixed[:, :rows], mixed[:, rows:]], axis=0)
        at = pl.multiple_of(step * 256 + i * 128, 128)
        held[:, pl.ds(at, 128)] = jnp.transpose(pair).astype(BF16)

    @pl.when(step == pl.num_programs(0) - 1)
    def _():
        attended = held[...]
        o_out[...] = attended
        middle = x[...].astype(F32) + mm(attended, wo[...])
        mid_out[...] = middle
        factor = lax.rsqrt(jnp.mean(middle * middle, axis=-1, keepdims=True) + epsilon)
        normed = (middle * factor * gain[...]).astype(BF16)
        msg_out[:rows, :] = normed
        logits = mm_nt(router[...], normed)
        chosen = mask[...] > 0.5
        top = jnp.max(jnp.where(chosen, logits, negative), axis=0, keepdims=True)
        raised = jnp.where(chosen, jnp.exp(jnp.where(chosen, logits - top, 0.0)), 0.0)
        gates = raised / jnp.sum(raised, axis=0, keepdims=True)
        high = gates.astype(BF16)
        low = (gates - high.astype(F32)).astype(BF16)
        ext = [high[:EXT], high[EXT:], low[:EXT], low[EXT:]]
        if 4 * rows < x.shape[1]:
            ext.append(jnp.zeros((EXT, x.shape[1] - 4 * rows), BF16))
        msg_out[rows:, :] = jnp.concatenate(ext, axis=1)


def attend(scal, x, q, kvs, shared, gain, router, mask):
    rows, width = x.shape
    devices = len(kvs)
    keys = devices * rows
    kv_specs = [pl.BlockSpec((1, rows, 128), lambda h: (0, 0, h)) for _ in kvs] + [
        pl.BlockSpec((1, rows, 128), lambda h: (1, 0, h)) for _ in kvs
    ]
    return pl.pallas_call(
        functools.partial(attend_kernel, devices),
        name="attend",
        grid=(KVH // 2,),
        in_specs=[
            pl.BlockSpec(memory_space=pltpu.SMEM),
            fixed((rows, width)),
            pl.BlockSpec((rows, 256), lambda h: (0, h)),
            *kv_specs,
            pl.BlockSpec((QH * HD, width), lambda h: (0, 2), pipeline_mode=pl.Buffered(1)),
            fixed((1, width)),
            fixed((EXPERTS, width)),
            fixed((EXPERTS, rows)),
        ],
        out_specs=[
            resident((rows, QH * HD)),
            pl.BlockSpec((1, 2, 2 * rows), lambda h: (h, 0, 0)),
            resident((rows, width)),
            resident((rows + EXT, width)),
        ],
        out_shape=[
            jax.ShapeDtypeStruct((rows, QH * HD), BF16),
            jax.ShapeDtypeStruct((KVH // 2, 2, 2 * rows), F32),
            jax.ShapeDtypeStruct((rows, width), F32),
            jax.ShapeDtypeStruct((rows + EXT, width), BF16),
        ],
        scratch_shapes=[pltpu.VMEM((keys, rows), F32), pltpu.VMEM((rows, QH * HD), BF16)],
        compiler_params=params(1),
        cost_estimate=cost(
            4 * rows * keys * QH * HD * 2 + 2 * rows * width * width,
            2 * width * width + 4 * keys * width + 12 * rows * width,
            rows * keys * QH,
            0.17,
        ),
    )(scal, x, q, *kvs, *kvs, shared, gain, router, mask)


def hot_rows(rank, j, slots):
    local = rank.shape[1]
    return jnp.concatenate(
        [
            jnp.where(one_hot(rank[j, i : i + 1, :], slots), 1.0, 0.0).astype(BF16)
            for i in range(local)
        ],
        axis=0,
    )


def combine(rank, held, prior, outs, buffers, slots):
    held = held if isinstance(held, list) else [held]
    prior_buffer, out_buffer, prior_sems, out_sems = buffers
    width = held[0].shape[-1]
    depth = out_buffer.shape[0]
    count = len(outs)
    fetch = lambda j: pltpu.make_async_copy(
        prior[j], prior_buffer.at[j % depth], prior_sems.at[j % depth]
    )
    send = lambda j: pltpu.make_async_copy(
        out_buffer.at[j % depth], outs[j], out_sems.at[j % depth]
    )
    for j in range(min(depth - 1, count) if prior else 0):
        fetch(j).start()
    for j in range(count):
        rows = [part[:, j].reshape(part.shape[0] * slots, width) for part in held]
        rows = rows[0] if len(rows) == 1 else jnp.concatenate(rows, axis=0)
        total = mm_tn(hot_rows(rank, j, slots), rows)
        if prior:
            if j + depth - 1 < count:
                fetch(j + depth - 1).start()
            fetch(j).wait()
            total = total + prior_buffer[j % depth].astype(F32)
        if j >= depth:
            send(j - depth).wait()
        out_buffer[j % depth] = total.astype(BF16)
        send(j).start()
    for j in range(max(0, count - depth), count):
        send(j).wait()


def gate_columns(rank, values, step, sources, slots):
    columns = []
    for j in sources:
        hot = one_hot(rank[j, pl.ds(step, 1), :], slots)
        columns.append(jnp.sum(jnp.where(hot, values(j), 0.0), axis=1, keepdims=True))
    return jnp.concatenate(columns, axis=0)


def finish_kernel(count, routed, slots, *refs):
    terms, (middle, goal, valid, refs) = refs[:count], (*refs[count : count + 3], refs[count + 3 :])
    if routed:
        rank, refs = refs[0], refs[1:]
        arrived, refs = refs[:routed], refs[routed:]
    hidden, grad_out, message, refs = *refs[:3], refs[3:]
    rows, width = middle.shape
    mixed = terms[0][...].astype(F32)
    for term in terms[1:]:
        mixed = mixed + term[...].astype(F32)
    if routed:
        given = jnp.concatenate([ref[...].reshape(-1, width) for ref in arrived], axis=0)
        hots = [
            jnp.where(one_hot(rank[i : i + 1, :], slots), 1.0, 0.0).astype(BF16)
            for i in range(rank.shape[0])
        ]
        mixed = mixed + mm_tn(jnp.concatenate(hots, axis=0), given)
    output = middle[...] + mixed
    hidden[...] = output.astype(BF16)
    grad = (output - goal[...].astype(F32)) * valid[...]
    grad_out[...] = grad
    error = 0.5 * jnp.sum(jnp.sum(grad * grad, axis=1, keepdims=True), axis=0, keepdims=True)
    fill_message(message, grad, mixed, error)
    if routed:
        low = message[:rows, :]
        inner = message[rows:, :rows]
        for i, hot in enumerate(hots):
            spread = jnp.where(one_hot(rank[i : i + 1, :], 128), 1.0, 0.0).astype(BF16)
            below = jnp.concatenate(
                [mm_nt(inner, spread)[:8], jnp.zeros((8, width - 128), F32)], axis=1
            )
            refs[i // 2][i % 2] = jnp.concatenate(
                [mm(hot, low)[: slots - 8], below], axis=0
            ).astype(BF16)


def finish(terms, middle, goal, valid, rank=None, arrived=(), slots=0):
    rows, width = middle.shape
    messages = len(rank) // 2 if arrived else 0
    return pl.pallas_call(
        functools.partial(finish_kernel, len(terms), len(arrived), slots),
        name="finish",
        out_shape=[
            jax.ShapeDtypeStruct((rows, width), BF16),
            jax.ShapeDtypeStruct((rows, width), F32),
            jax.ShapeDtypeStruct((rows + EXT, width), BF16),
            *[jax.ShapeDtypeStruct((2, slots, width), BF16) for _ in range(messages)],
        ],
        compiler_params=params(),
        cost_estimate=cost(8 * rows * width, 24 * rows * width),
    )(*terms, middle, goal, valid, *([rank, *arrived] if arrived else []))


def fill_message(message, grad, mixed, error):
    rows, width = grad.shape
    message[:rows, :] = grad.astype(BF16)
    inner = jnp.transpose(
        jnp.broadcast_to(jnp.sum(grad * mixed, axis=1, keepdims=True), (rows, 128))
    )[:EXT]
    high = inner.astype(BF16)
    low = (inner - high.astype(F32)).astype(BF16)
    row = lax.broadcasted_iota(jnp.int32, (EXT, rows), 0)
    ext = jnp.where(row == 0, high.astype(F32), jnp.where(row == 1, low.astype(F32), 0.0))
    for at in range(2, 5):
        term = error.astype(BF16).astype(F32)
        ext = jnp.where(row == at, term, ext)
        error = error - term
    message[rows:, :rows] = ext.astype(BF16)
    message[rows:, rows:] = jnp.zeros((EXT, width - rows), BF16)


def message_kernel(grad, mixed, message):
    fill_message(message, grad[...], mixed[...], jnp.zeros((1, 1), F32))


def grad_message(grad, mixed):
    rows, width = grad.shape
    return pl.pallas_call(
        message_kernel,
        name="grad_message",
        out_shape=jax.ShapeDtypeStruct((rows + EXT, width), BF16),
        compiler_params=params(),
        cost_estimate=cost(4 * rows * width, 10 * rows * width),
    )(grad, mixed)


def dispatch_kernel(sources, slots, backward, scal, *rest):
    msgs, (rank, x_out, side_out, arrived, picked, in_sems, out_sems) = (
        rest[:sources],
        rest[sources:],
    )
    local, rows = rank.shape[1:]
    fetch = lambda j: pltpu.make_async_copy(msgs[j], arrived.at[j], in_sems.at[j])
    send = lambda j: pltpu.make_async_copy(picked.at[j], x_out.at[:, j], out_sems.at[j])
    for j in range(sources):
        fetch(j).start()
    pick_row = lax.broadcasted_iota(jnp.int32, (EXT, 4 * rows), 0)
    for j in range(sources):
        fetch(j).wait()
        taken = mm(hot_rows(rank, j, slots), arrived[j, :rows, :]).astype(BF16)
        for i in range(local):
            picked[j, i] = taken[i * slots : (i + 1) * slots]
        send(j).start()
        if backward:
            ext = arrived[j, rows:, :rows].astype(F32)
            side_out[j, 0:1, :] = ext[0:1, :] + ext[1:2, :]
            side_out[j, 1:2, :] = ext[2:3, :] + ext[3:4, :] + ext[4:5, :]
        else:
            ext = arrived[j, rows:, : 4 * rows].astype(F32)
            for i in range(local):
                expert = scal[0] + i
                row = jnp.sum(jnp.where(pick_row == expert % EXT, ext, 0.0), axis=0, keepdims=True)
                high = jnp.where(expert < EXT, row[:, :rows], row[:, rows : 2 * rows])
                low = jnp.where(expert < EXT, row[:, 2 * rows : 3 * rows], row[:, 3 * rows :])
                side_out[j, i : i + 1, :] = high + low
    for j in range(sources):
        send(j).wait()


def dispatch(scal, msgs, rank, slots, backward):
    sources, local, rows = rank.shape
    width = msgs[0].shape[1]
    anywhere = pl.BlockSpec(memory_space=pl.ANY)
    side = (sources, 2 if backward else local, rows)
    taken, beside = pl.pallas_call(
        functools.partial(dispatch_kernel, sources, slots, backward),
        name="dispatch",
        grid=(1,),
        in_specs=[
            pl.BlockSpec(memory_space=pltpu.SMEM),
            *[anywhere for _ in msgs],
            fixed(rank.shape),
        ],
        out_specs=[anywhere, resident(side)],
        out_shape=[
            jax.ShapeDtypeStruct((local, sources, slots, width), BF16),
            jax.ShapeDtypeStruct(side, F32),
        ],
        scratch_shapes=[
            pltpu.VMEM((sources, rows + EXT, width), BF16),
            pltpu.VMEM((sources, local, slots, width), BF16),
            pltpu.SemaphoreType.DMA((sources,)),
            pltpu.SemaphoreType.DMA((sources,)),
        ],
        compiler_params=params(1),
        cost_estimate=cost(
            2 * local * sources * slots * rows * width,
            2 * sources * width * (rows + local * slots),
            0,
            0.05 * local,
        ),
    )(scal, *msgs, rank)
    return taken.reshape(local, sources * slots, width), beside


def fill_weights(scal, blocks, w1, w2):
    up = w1.shape[0] // len(blocks)
    down = w2.shape[0] // len(blocks)
    for k, block in enumerate(blocks):
        at = scal[1 + k]
        w1[pl.ds(pl.multiple_of(at * up, up), up), :] = block[0, :up]
        w2[pl.ds(pl.multiple_of(at * down, down), down), :] = block[0, up:]


def experts_kernel(sources, depth, slots, chained, combined, scal, *rest):
    prior = ()
    if chained:
        prior, rest = rest[:sources], rest[sources:]
    rank, gates, xs, rest = *rest[:3], rest[3:]
    blocks, rest = rest[:depth], rest[depth:]
    gu_out, y_out, rest = *rest[:2], rest[2:]
    if combined:
        outs, rest = rest[:sources], rest[sources:]
        held, w1, w2 = rest[:3]
    else:
        outs, (w1, w2) = rest[:sources], rest[sources:]
    width = w1.shape[0]
    step, part = pl.program_id(0), pl.program_id(1)
    portions = sources // (xs.shape[1] // slots)
    portion = sources // portions

    @pl.when(part == 0)
    def _():
        fill_weights(scal, blocks, w1, w2)

    gate_up = mm(xs[0], w1[...])
    gu_out[0] = gate_up
    gate, up = gate_up[:, :FF_E], gate_up[:, FF_E:]
    activated = (gate * jax.nn.sigmoid(gate) * up).astype(BF16)
    out = mm(activated, w2[...]).astype(BF16)
    y_out[0] = out
    column = gate_columns(
        rank,
        lambda j: gates[j, pl.ds(step, 1), :],
        step,
        [part * portion + n for n in range(portion)],
        slots,
    )
    given = (column * out.astype(F32)).astype(BF16).reshape(portion, slots, width)
    if combined:
        held[step, pl.ds(part * portion, portion)] = given

        @pl.when((step == pl.num_programs(0) - 1) & (part == portions - 1))
        def _():
            combine(rank, held, prior, outs, rest[3:], slots)

    else:
        for j in range(sources):
            outs[j][...] = given[j]


def weight_specs(blocks, depth, base=0):
    arrays = blocks if len(blocks) == depth else blocks * depth
    rows = arrays[0].shape[1] // (depth // len(blocks))
    width = arrays[0].shape[2]
    specs = [
        pl.BlockSpec((1, rows, width), lambda e, r, f=(k if len(blocks) == 1 else 0): (e + base, f, 0))
        for k in range(depth)
    ]
    return arrays, specs


def combine_kernel(order, rank, *refs):
    parts, rest = refs[: len(order)], refs[len(order) :]
    outs, buffers = rest[:-4], rest[-4:]
    slots = parts[0].shape[2]
    combine(rank, [parts[o] for o in order], (), outs, buffers, slots)


def combine_rows(rank, parts, order, slots):
    sources, _, rows = rank.shape
    width = parts[0].shape[-1]
    parts = [part.reshape(part.shape[0], sources, slots, width) for part in parts]
    return list(
        pl.pallas_call(
            functools.partial(combine_kernel, order),
            name="combine_rows",
            grid=(1,),
            in_specs=[fixed(rank.shape), *[fixed(part.shape) for part in parts]],
            out_specs=[pl.BlockSpec(memory_space=pl.ANY)] * sources,
            out_shape=[jax.ShapeDtypeStruct((rows, width), BF16)] * sources,
            scratch_shapes=stream_scratch(rows, width),
            compiler_params=params(1),
            cost_estimate=cost(
                2 * sources * rows * width * rank.shape[1] * slots,
                4 * sources * width * rank.shape[1] * slots,
                share=0.2,
            ),
        )(rank, *parts)
    )


def stream_scratch(rows, width):
    return [
        pltpu.VMEM((4, rows, width), BF16),
        pltpu.VMEM((4, rows, width), BF16),
        pltpu.SemaphoreType.DMA((4,)),
        pltpu.SemaphoreType.DMA((4,)),
    ]


def experts_forward(scal, xs, rank, gates, blocks, depth, slots, first, prior=(), combined=True):
    sources, local, rows = rank.shape
    width = xs.shape[2]
    portions = max(1, sources // 8) if combined else 1
    count = sources * slots
    arrays, specs = weight_specs(blocks, depth)
    anywhere = pl.BlockSpec(memory_space=pl.ANY)
    each = lambda shape, base=0: pl.BlockSpec((1,) + shape, lambda e, r: (e + base, r, 0))
    outs = pl.pallas_call(
        functools.partial(experts_kernel, sources, depth, slots, bool(prior), combined),
        name="experts_forward",
        grid=(local, portions),
        in_specs=[
            pl.BlockSpec(memory_space=pltpu.SMEM),
            *[anywhere for _ in prior],
            fixed((sources, local, rows)),
            fixed((sources, local, rows)),
            each((count // portions, width), first),
            *specs,
        ],
        out_specs=[
            each((count // portions, 2 * FF_E)),
            each((count // portions, width)),
            *(
                [anywhere] * sources
                if combined
                else [resident((slots, width))] * sources
            ),
        ],
        out_shape=[
            jax.ShapeDtypeStruct((local, count, 2 * FF_E), F32),
            jax.ShapeDtypeStruct((local, count, width), BF16),
            *(
                [jax.ShapeDtypeStruct((rows, width), BF16)] * sources
                if combined
                else [jax.ShapeDtypeStruct((slots, width), BF16)] * sources
            ),
        ],
        scratch_shapes=[
            *([pltpu.VMEM((local, sources, slots, width), BF16)] if combined else []),
            pltpu.VMEM((width, 2 * FF_E), BF16),
            pltpu.VMEM((FF_E, width), BF16),
            *(stream_scratch(rows, width) if combined else []),
        ],
        compiler_params=params(2),
        cost_estimate=cost(
            2 * local * count * width * 3 * FF_E * 1.3,
            8 * local * count * width,
            local * count * FF_E,
            0.1 * (local + 1),
        ),
    )(scal, *prior, rank, gates, xs, *arrays)
    return outs[:2], list(outs[2:])


def experts_back_kernel(sources, depth, slots, mode, scal, *rest):
    last, order, direct = mode
    earlier = ()
    if last:
        full_rank, rest = rest[0], rest[1:]
        earlier, rest = rest[: len(order) - 1], rest[len(order) - 1 :]
    if direct:
        rank, gates, rest = *rest[:2], rest[2:]
        given_rows, rest = rest[:sources], rest[sources:]
    else:
        rank, gates, inners, grads, rest = *rest[:4], rest[4:]
    xs, gu, ys, router, rest = *rest[:4], rest[4:]
    blocks, rest = rest[:depth], rest[depth:]
    grad_out_ref, router_out, rest = *rest[:2], rest[2:]
    outs, rest = (rest[:sources], rest[sources:]) if last else (rest[:1], rest[1:])
    held, w1, w2, sum1, sum2 = rest[:5]
    width = w1.shape[0]
    step, part = pl.program_id(0), pl.program_id(1)
    portions = sources // (xs.shape[1] // slots)
    portion = sources // portions

    @pl.when(part == 0)
    def _():
        fill_weights(scal, blocks, w1, w2)

    mine = [part * portion + n for n in range(portion)]
    gate_column = gate_columns(rank, lambda j: gates[j, pl.ds(step, 1), :], step, mine, slots)
    if direct:
        blocks_of = [ref[0] if len(ref.shape) == 3 else ref[...] for ref in given_rows]
        blocks_of = [block.astype(F32) for block in blocks_of]
        grad_out = jnp.concatenate(blocks_of, axis=0)
        inner_column = jnp.concatenate(
            [
                jnp.transpose(block[slots - 8 :, :128])[:slots, :2].sum(axis=1, keepdims=True)
                for block in blocks_of
            ],
            axis=0,
        )
    else:
        inner_column = gate_columns(rank, lambda j: inners[j, 0:1, :], step, mine, slots)
        grad_out = grads[0].astype(F32)
    grad_y = (gate_column * grad_out).astype(BF16)
    given = jnp.sum(grad_out * ys[0].astype(F32), axis=1, keepdims=True)
    grad_logit = gate_column * (given - inner_column)
    gate, up = gu[0, :, :FF_E], gu[0, :, FF_E:]
    sigmoid = jax.nn.sigmoid(gate)
    silu = gate * sigmoid
    activated = (silu * up).astype(BF16)
    down_part = mm_tn(activated, grad_y)
    grad_act = mm_nt(grad_y, w2[...])
    grad_gate = grad_act * up * sigmoid * (1.0 + gate * (1.0 - sigmoid))
    grad_up = grad_act * silu
    grad_gate_up = jnp.concatenate([grad_gate.astype(BF16), grad_up.astype(BF16)], axis=1)
    taken = xs[0]
    up_part = mm_tn(taken, grad_gate_up)
    router_part = jnp.sum(taken.astype(F32) * grad_logit, axis=0, keepdims=True)
    grad_rows = mm_nt(grad_gate_up, w1[...]) + grad_logit * router[0]
    if last:
        held[step, pl.ds(part * portion, portion)] = grad_rows.astype(BF16).reshape(
            portion, slots, width
        )
    else:
        outs[0][0] = grad_rows.astype(BF16)

    def write(up_total, down_total):
        up_rows, down_rows = width // depth, FF_E // depth
        for f in range(depth):
            top = f * (up_rows + down_rows)
            grad_out_ref[0, top : top + up_rows, :] = up_total[
                f * up_rows : (f + 1) * up_rows
            ].astype(BF16)
            grad_out_ref[0, top + up_rows : top + up_rows + down_rows, :] = down_total[
                f * down_rows : (f + 1) * down_rows
            ].astype(BF16)

    if sum1 is None:
        write(up_part, down_part)
        router_out[0] = router_part
    else:

        @pl.when(part == 0)
        def _():
            sum1[...] = up_part
            sum2[...] = down_part
            router_out[0] = router_part

        @pl.when(part > 0)
        def _():
            sum1[...] += up_part
            sum2[...] += down_part
            router_out[0] += router_part

        @pl.when(part == portions - 1)
        def _():
            write(sum1, sum2)

    if last:

        @pl.when((step == pl.num_programs(0) - 1) & (part == portions - 1))
        def _():
            pieces = list(earlier) + [held]
            combine(full_rank, [pieces[o] for o in order], (), outs, rest[5:], slots)


def experts_backward(
    scal, grads, rank, gates, inners, xs, kept, router, blocks, depth, slots, first, base, begin, last
):
    direct = isinstance(grads, list)
    sources, local, rows = rank.shape
    width = xs.shape[2]
    portions = max(1, sources // 8)
    count = sources * slots
    gu, ys = kept
    arrays, specs = weight_specs(blocks, depth, base)
    merged = width + FF_E
    anywhere = pl.BlockSpec(memory_space=pl.ANY)
    each = lambda shape, base=0: pl.BlockSpec((1,) + shape, lambda e, r: (e + base, r, 0))
    whole = lambda shape: pl.BlockSpec((1,) + shape, lambda e, r: (e, 0, 0))
    before = []
    if last:
        before = [last[0]] + [
            part.reshape(part.shape[0], sources, slots, width) for part in last[1]
        ]
    mode = (bool(last), last[2] if last else (), direct)
    if direct:
        given = grads
        given_specs = [
            fixed(block.shape)
            if block.ndim == 2
            else pl.BlockSpec(
                (1,) + block.shape[1:], lambda *_: (0, 0, 0), pipeline_mode=pl.Buffered(1)
            )
            for block in grads
        ]
    else:
        given = [inners, grads]
        given_specs = [fixed((sources, 2, rows)), each((count // portions, width), begin)]

    def kernel(*refs):
        refs = list(refs)
        if portions == 1:
            at = len(refs) - (4 if last else 0)
            refs[at:at] = [None, None]
        if not last:
            refs[-4:-4] = [None]
        experts_back_kernel(sources, depth, slots, mode, *refs)

    sums = [pltpu.VMEM((width, 2 * FF_E), F32), pltpu.VMEM((FF_E, width), F32)]
    outs = pl.pallas_call(
        kernel,
        name="experts_backward",
        grid=(local, portions),
        in_specs=[
            pl.BlockSpec(memory_space=pltpu.SMEM),
            *[fixed(part.shape) for part in before],
            fixed((sources, local, rows)),
            fixed((sources, local, rows)),
            *given_specs,
            each((count // portions, width), first),
            each((count // portions, 2 * FF_E), base),
            each((count // portions, width), base),
            whole((1, width)),
            *specs,
        ],
        out_specs=[
            whole((merged, width)),
            whole((1, width)),
            *([anywhere] * sources if last else [each((count // portions, width))]),
        ],
        out_shape=[
            jax.ShapeDtypeStruct((local, merged, width), BF16),
            jax.ShapeDtypeStruct((local, 1, width), F32),
            *(
                [jax.ShapeDtypeStruct((rows, width), BF16)] * sources
                if last
                else [jax.ShapeDtypeStruct((local, count, width), BF16)]
            ),
        ],
        scratch_shapes=[
            *([pltpu.VMEM((local, sources, slots, width), BF16)] if last else []),
            pltpu.VMEM((width, 2 * FF_E), BF16),
            pltpu.VMEM((FF_E, width), BF16),
            *(sums if portions > 1 else []),
            *(stream_scratch(rows, width) if last else []),
        ],
        compiler_params=params(2),
        cost_estimate=cost(
            2 * local * count * width * 3 * FF_E * 2.3,
            14 * local * count * width,
            local * count * FF_E,
            0.37,
        ),
    )(scal, *before, rank, gates, *given, xs, gu, ys, router, *arrays)
    return outs[0], outs[1], list(outs[2:])


def place_kernel(places, number, aliased, scal, *refs):
    parts, (up_out, down_out) = refs[: -2 - aliased], refs[-2:]
    step = number(pl.program_id(0))
    up_rows = up_out.shape[1]

    def put(block):
        up_out[0] = block[0, :up_rows].astype(F32)
        down_out[0] = block[0, up_rows:].astype(F32)

    at = 0
    for place in places:
        core, base, count = place
        pl.when((scal[0] == core) & (step >= base) & (step < base + count))(
            functools.partial(put, parts[at])
        )
        at += 1


def place_experts(scal, pieces, held_experts, up_rows, experts, into=()):
    rows, width = pieces[0][2].shape[1:]
    run = next((i for i in range(1, len(experts)) if experts[i] != experts[0] + i), len(experts))
    skip = experts[run] - experts[run - 1] if run < len(experts) else 1
    number = lambda i: experts[0] + (i // run) * (run - 1 + skip) + i % run
    assert [number(i) for i in range(len(experts))] == list(experts)
    places = [(core, base, array.shape[0]) for core, base, array in pieces]
    arrays = [array for _, _, array in pieces]
    specs = [
        pl.BlockSpec(
            (1, rows, width),
            lambda i, scal, base=base, top=count - 1: (jnp.clip(number(i) - base, 0, top), 0, 0),
        )
        for _, base, count in places
    ]
    specs += [pl.BlockSpec(memory_space=pl.ANY) for _ in into]
    return pl.pallas_call(
        functools.partial(place_kernel, places, number, len(into)),
        name="place_experts",
        grid_spec=pltpu.PrefetchScalarGridSpec(
            num_scalar_prefetch=1,
            grid=(len(experts),),
            in_specs=specs,
            out_specs=[
                pl.BlockSpec((1, up_rows, width), lambda i, scal: (number(i), 0, 0)),
                pl.BlockSpec((1, rows - up_rows, width), lambda i, scal: (number(i), 0, 0)),
            ],
        ),
        out_shape=[
            jax.ShapeDtypeStruct((held_experts, up_rows, width), F32),
            jax.ShapeDtypeStruct((held_experts, rows - up_rows, width), F32),
        ],
        input_output_aliases={1 + len(arrays) + i: i for i in range(len(into))},
        compiler_params=params(1),
        cost_estimate=cost(0, 8 * len(experts) * rows * width),
    )(scal, *arrays, *into)


def pack_kernel(scal, up, down, out):
    up_rows = up.shape[1]
    out[0, :up_rows, :] = up[0]
    out[0, up_rows:, :] = down[0]


def pack_experts(half, up, down):
    experts, up_rows, width = up.shape
    rows = up_rows + down.shape[1]
    local = experts // 2
    take = lambda i, scal: (scal[0] * local + i, 0, 0)
    return pl.pallas_call(
        pack_kernel,
        name="pack_experts",
        grid_spec=pltpu.PrefetchScalarGridSpec(
            num_scalar_prefetch=1,
            grid=(local,),
            in_specs=[
                pl.BlockSpec((1, up_rows, width), take),
                pl.BlockSpec((1, rows - up_rows, width), take),
            ],
            out_specs=pl.BlockSpec((1, rows, width), lambda i, scal: (i, 0, 0)),
        ),
        out_shape=jax.ShapeDtypeStruct((local, rows, width), BF16),
        compiler_params=params(1),
        cost_estimate=cost(0, 4 * local * rows * width),
    )(half.astype(jnp.int32).reshape(1), up, down)


def assemble_kernel(devices, depth, scal, *refs):
    owns, others, whole, sem = refs[:devices], refs[devices : 2 * devices], refs[-2], refs[-1]
    piece = whole.shape[0] // (devices * depth)
    for home, blocks in ((1, owns), (0, others)):

        @pl.when(scal[0] == home)
        def _(blocks=blocks):
            for k in range(devices):
                for i in range(depth):
                    to = pl.multiple_of(((scal[1] ^ k) * depth + (scal[2] ^ i)) * piece, piece)
                    pltpu.make_async_copy(
                        blocks[k].at[pl.ds(i * piece, piece)], whole.at[pl.ds(to, piece)], sem
                    ).start()
            pltpu.make_async_copy(whole, whole, sem).wait()


def assemble(scal, owns, others, depth):
    devices = len(owns)
    rows, columns = owns[0].shape
    return pl.pallas_call(
        functools.partial(assemble_kernel, devices, depth),
        name="assemble",
        in_specs=[pl.BlockSpec(memory_space=pltpu.SMEM)]
        + [pl.BlockSpec(memory_space=pl.ANY)] * (2 * devices),
        out_specs=pl.BlockSpec(memory_space=pltpu.VMEM),
        out_shape=jax.ShapeDtypeStruct((rows * devices, columns), owns[0].dtype),
        scratch_shapes=[pltpu.SemaphoreType.DMA(())],
        compiler_params=params(),
        cost_estimate=cost(0, 4 * rows * devices * columns),
    )(scal, *owns, *others)


def attend_back_kernel(devices, arrived, scal, *rest):
    parts, rest = rest[:arrived], rest[arrived:]
    grad_out, middle, gain, attended, wo, q, lse, cosine, sine, x, gain_first = rest[:11]
    ks, vs, rest = rest[11 : 11 + devices], rest[11 + devices : 11 + 2 * devices], rest[11 + 2 * devices :]
    mid_out, weight_grads, gain_grad, dq_out = rest[:4]
    dkv_outs, (bias, held) = rest[4 : 4 + devices], rest[4 + devices :]
    width = middle.shape[1]
    rows = middle.shape[0]
    scale = 1.0 / math.sqrt(HD)
    step = pl.program_id(0)

    @pl.when(step == 0)
    def _():
        fill_bias(bias, scal, devices, rows)
        grad_mix = parts[0][...].astype(F32)
        for part in parts[1:]:
            grad_mix = grad_mix + part[...].astype(F32)
        mid = middle[...]
        factor = lax.rsqrt(jnp.mean(mid * mid, axis=-1, keepdims=True) + epsilon)
        scaled = grad_mix * gain[...]
        inner = jnp.mean(mid * scaled, axis=-1, keepdims=True)
        gain_grad[...] = jnp.sum(grad_mix * mid * factor, axis=0, keepdims=True)
        grad_mid = grad_out[...] + factor * scaled - mid * (factor * factor * factor * inner)
        mid_out[...] = grad_mid
        branch = grad_mid.astype(BF16)
        weight_grads[:, :width] = mm_tn(attended[...], branch).astype(BF16)
        held[...] = mm_nt(branch, wo[...]).astype(BF16)

    keys = jnp.concatenate([r[0] for r in ks], axis=0)
    values = jnp.concatenate([r[0] for r in vs], axis=0)
    block_bias = bias[...]
    both_bias = jnp.concatenate([block_bias, block_bias], axis=1)
    key_parts, value_parts = [], []
    for i in range(2):
        block = q[:, i * 128 : (i + 1) * 128]
        at = pl.multiple_of(step * 256 + i * 128, 128)
        grads = held[:, pl.ds(at, 128)]
        scores = mm_nt(doubled(keys, i), two_heads(block)) * scale + both_bias
        probs = jnp.exp(scores - lse[0, i : i + 1, :])
        grad_probs = mm_nt(doubled(values, i), two_heads(grads))
        product = probs * grad_probs
        dots = jnp.sum(product, axis=0, keepdims=True)
        grad_scores = (product - probs * dots).astype(BF16)
        key_parts.append(mm(grad_scores, two_heads_doubled(block)) * scale)
        value_parts.append(mm(probs.astype(BF16), two_heads_doubled(grads)))
        moved = mm_tn(keys, grad_scores)[i * HD : (i + 1) * HD] * scale
        pair = jnp.concatenate([moved[:, :rows], moved[:, rows:]], axis=0)
        dq_out[:, pl.ds(at, 128)] = turn(jnp.transpose(pair), cosine[...], sine[...]).astype(BF16)
    even = lane_index(key_parts[0].shape) < HD
    grad_keys = jnp.where(even, key_parts[0], key_parts[1]).astype(BF16)
    grad_values = jnp.where(even, value_parts[0], value_parts[1]).astype(BF16)
    for k in range(devices):
        dkv_outs[k][0] = grad_keys[k * rows : (k + 1) * rows]
        dkv_outs[k][1] = grad_values[k * rows : (k + 1) * rows]

    @pl.when(step == pl.num_programs(0) - 1)
    def _():
        values = x[...].astype(F32)
        factor = lax.rsqrt(jnp.mean(values * values, axis=-1, keepdims=True) + epsilon)
        normed = (values * factor * gain_first[...]).astype(BF16)
        weight_grads[:, width:] = mm_tn(normed, dq_out[...]).astype(BF16)


def attend_backward(
    scal, parts, grad_out, middle, gain, attended, shared, q, lse, cosine, sine, x, gain_first, kvs
):
    rows, width = middle.shape
    devices = len(kvs)
    keys = devices * rows
    kv_specs = [pl.BlockSpec((1, rows, 128), lambda h: (0, 0, h)) for _ in kvs] + [
        pl.BlockSpec((1, rows, 128), lambda h: (1, 0, h)) for _ in kvs
    ]
    return pl.pallas_call(
        functools.partial(attend_back_kernel, devices, len(parts)),
        name="attend_backward",
        grid=(KVH // 2,),
        in_specs=[
            pl.BlockSpec(memory_space=pltpu.SMEM),
            *[fixed((rows, width)) for _ in parts],
            fixed((rows, width)),
            fixed((rows, width)),
            fixed((1, width)),
            fixed((rows, QH * HD)),
            pl.BlockSpec((QH * HD, width), lambda h: (0, 2), pipeline_mode=pl.Buffered(1)),
            pl.BlockSpec((rows, 256), lambda h: (0, h)),
            pl.BlockSpec((1, 2, 2 * rows), lambda h: (h, 0, 0)),
            fixed((rows, 128)),
            fixed((rows, 128)),
            fixed((rows, width)),
            fixed((1, width)),
            *kv_specs,
        ],
        out_specs=[
            resident((rows, width)),
            resident((width, width + QH * HD)),
            resident((1, width)),
            resident((rows, QH * HD)),
            *[pl.BlockSpec((2, rows, 128), lambda h: (0, 0, h)) for _ in kvs],
        ],
        out_shape=[
            jax.ShapeDtypeStruct((rows, width), F32),
            jax.ShapeDtypeStruct((width, width + QH * HD), BF16),
            jax.ShapeDtypeStruct((1, width), F32),
            jax.ShapeDtypeStruct((rows, QH * HD), BF16),
            *[jax.ShapeDtypeStruct((2, rows, KW), BF16) for _ in kvs],
        ],
        scratch_shapes=[pltpu.VMEM((keys, rows), F32), pltpu.VMEM((rows, QH * HD), BF16)],
        compiler_params=params(1),
        cost_estimate=cost(
            10 * rows * keys * QH * HD * 2 + 4 * rows * width * width,
            6 * width * width + 8 * keys * width + 20 * rows * width,
            rows * keys * QH,
            0.23,
        ),
    )(
        scal,
        *parts,
        grad_out,
        middle,
        gain,
        attended,
        shared,
        q,
        lse,
        cosine,
        sine,
        x,
        gain_first,
        *kvs,
        *kvs,
    )


def project_back_kernel(devices, x, gain, dq, *rest):
    parts, rest = rest[:devices], rest[devices:]
    grad_mid, wq, wm, cosine, sine, small, dx_out, packed = rest
    values = x[...].astype(F32)
    width = values.shape[1]
    factor = lax.rsqrt(jnp.mean(values * values, axis=-1, keepdims=True) + epsilon)
    normed = (values * factor * gain[...]).astype(BF16)
    summed = parts[0][...].astype(F32)
    for part in parts[1:]:
        summed = summed + part[...].astype(F32)
    grad_keys = [
        turn(summed[0, :, b * 128 : (b + 1) * 128], cosine[...], sine[...]).astype(BF16)
        for b in range(KW // 128)
    ]
    grad_memory = jnp.concatenate(grad_keys + [summed[1].astype(BF16)], axis=1)
    grad_query = dq[...]
    packed[:, : 2 * KW] = mm_tn(normed, grad_memory).astype(BF16)
    grad_normed = mm_nt(grad_query, wq[...]) + mm_nt(grad_memory, wm[...])
    scaled = grad_normed * gain[...]
    inner = jnp.mean(values * scaled, axis=-1, keepdims=True)
    gain_grad = jnp.sum(grad_normed * values * factor, axis=0, keepdims=True)
    row = lax.broadcasted_iota(jnp.int32, (128, width), 0)
    packed[:, 2 * KW :] = jnp.transpose(
        jnp.where(row == EXPERTS, gain_grad, small[...])
    ).astype(BF16)
    dx_out[...] = (
        grad_mid[...] + factor * scaled - values * (factor * factor * factor * inner)
    )


def project_backward(x, gain, dq, parts, grad_mid, shared, cosine, sine, small):
    rows, width = x.shape
    columns = 2 * KW + 128
    return pl.pallas_call(
        functools.partial(project_back_kernel, len(parts)),
        name="project_backward",
        grid=(1,),
        in_specs=[
            fixed((rows, width)),
            fixed((1, width)),
            fixed((rows, QH * HD)),
            *[fixed((2, rows, KW)) for _ in parts],
            fixed((rows, width)),
            pl.BlockSpec((width, QH * HD), lambda i: (0, 0), pipeline_mode=pl.Buffered(1)),
            pl.BlockSpec((width, 2 * KW), lambda i: (0, 1), pipeline_mode=pl.Buffered(1)),
            fixed((rows, 128)),
            fixed((rows, 128)),
            fixed((128, width)),
        ],
        out_specs=[resident((rows, width)), resident((width, columns))],
        out_shape=[
            jax.ShapeDtypeStruct((rows, width), F32),
            jax.ShapeDtypeStruct((width, columns), BF16),
        ],
        compiler_params=params(1),
        cost_estimate=cost(
            6 * rows * width * 2048, 8 * width * 2048 + 16 * rows * width, share=0.35
        ),
    )(x, gain, dq, *parts, grad_mid, shared, shared, cosine, sine, small)


def pairs_within(axis, by, sections=(0, 1)):
    count = lax.axis_size(axis)
    return [(s * count + i, s * count + (i ^ by)) for s in sections for i in range(count)]


def exchanged(value, axis, by, sections=(0, 1)):
    return lax.ppermute(value, ("section", axis), pairs_within(axis, by, sections))


def swapped(value):
    return lax.ppermute(value, "section", [(0, 1), (1, 0)])


def from_all(value, axis, sections=(0, 1)):
    count = lax.axis_size(axis)
    return [value] + [exchanged(value, axis, k, sections) for k in range(1, count)]


def after(value, other):
    return lax.optimization_barrier((value, other))[0]


def scattered(blocks, axis, sections):
    return [blocks[0]] + [
        exchanged(blocks[k], axis, k, sections) for k in range(1, len(blocks))
    ]


def added(terms):
    return functools.reduce(lambda a, b: a + b, [term.astype(F32) for term in terms])


def shards(
    tokens,
    targets,
    lengths,
    routes,
    attention_gain,
    query_weight,
    memory_weight,
    output_weight,
    mixture_gain,
    router_weight,
    gate_up_weight,
    down_weight,
):
    section = lax.axis_index("section")
    context = lax.axis_index("ctx")
    line = lax.axis_index("fsdp")
    devices = lax.axis_size("ctx")
    depth = lax.axis_size("fsdp")
    first_core = section == 0
    rows, width = tokens.shape[2:]
    layers = 2
    held_experts = gate_up_weight.shape[1]
    half_held = held_experts // 2
    capacity = rows * TOPK * 9 // (EXPERTS * 8)
    slots = -(-capacity // 16) * 16
    up_rows, down_rows = gate_up_weight.shape[2], down_weight.shape[2]
    shard_rows = up_rows + down_rows

    column = context * held_experts
    plain = (column + section * half_held, half_held, 2 * devices)
    places = [plain, plain]

    pack = jnp.concatenate(
        [
            query_weight[0],
            memory_weight[0],
            output_weight[0],
            router_weight[0],
            attention_gain[0][:, None],
            mixture_gain[0][:, None],
            jnp.zeros((query_weight.shape[1], 128 - EXPERTS - 2), BF16),
        ],
        axis=1,
    )

    def shared_of_line(layer, ahead):
        mine = pack if ahead is None else after(pack, ahead)
        return jnp.concatenate(from_all(mine, "fsdp", (layer,)), axis=0)

    def shared_of_plane(layer, block, ahead):
        mine = block if ahead is None else after(block, ahead)
        owns = from_all(mine, "ctx", (layer,))
        others = [lax.ppermute(own, "section", [(layer, 1 - layer)]) for own in owns]
        scal = jnp.stack([(section == layer).astype(jnp.int32), context, line])
        whole = assemble(scal, owns, others, depth)
        small = whole[:, 3 * width :].T
        return (
            whole,
            small[:EXPERTS],
            small[EXPERTS : EXPERTS + 1].astype(F32),
            small[EXPERTS + 1 : EXPERTS + 2].astype(F32),
        )

    my_routes = jnp.swapaxes(routes[0, :, 0], 1, 2)
    other_routes = swapped(my_routes)
    layer_routes = jnp.where(
        first_core,
        jnp.stack([my_routes, other_routes]),
        jnp.stack([other_routes, my_routes])[:, ::-1],
    )
    all_routes = jnp.stack(from_all(layer_routes, "ctx"), axis=2).reshape(
        layers, 2 * devices, TOPK, rows
    )
    source_routes = [all_routes[0], all_routes[1]]
    earlier = (
        lax.broadcasted_iota(jnp.int32, (rows, rows), 0)
        < lax.broadcasted_iota(jnp.int32, (rows, rows), 1)
    ).astype(BF16)

    def ranked(layer):
        first, local, _ = places[layer]
        ids = first + jnp.arange(local, dtype=jnp.int32)
        named = jnp.any(source_routes[layer][:, None] == ids[None, :, None, None], axis=2)
        before = jnp.dot(
            named.astype(BF16).reshape(-1, rows), earlier, preferred_element_type=F32
        ).reshape(named.shape)
        return jnp.where(named, before, -1.0)

    ranks = [ranked(layer) for layer in range(layers)]
    masks = jnp.any(
        layer_routes[:, 0, None] == jnp.arange(EXPERTS, dtype=jnp.int32)[None, :, None, None], axis=2
    ).astype(F32)

    own_ranks = jnp.where(
        masks[1] > 0.5,
        jnp.dot(masks[1].astype(BF16), earlier, preferred_element_type=F32),
        -1.0,
    )
    last_rank = jnp.take(
        own_ranks,
        jnp.stack(
            [
                (context ^ k) * held_experts + (section ^ m) * half_held + half_held - 1
                for k in range(devices)
                for m in range(2)
            ]
        ),
        axis=0,
    )

    line_blocks = [after(shared_of_line(0, None), (ranks, masks, last_rank)), None]

    whole = [(0, half_held)]
    split = [(0, half_held - 1), (half_held - 1, 1)] if half_held > 1 else whole
    runs = [whole, split]
    back_runs = [split, split[::-1]]
    by_rows_fits = half_held > 1 and slots - capacity >= 8 and slots % 16 == 0

    arrived = swapped(pack_experts(1 - section, gate_up_weight[0], down_weight[0]))
    mine = pack_experts(section, gate_up_weight[0], down_weight[0])

    def gathered_experts(layer, ahead):
        own, other = (mine, arrived) if ahead is None else after((mine, arrived), ahead)
        parts = []
        for a, n in runs[layer]:
            shard = jnp.where(section == layer, own[a : a + n], other[a : a + n])
            parts.append([lax.all_gather(shard, "fsdp", axis=1, tiled=True)])
        return parts

    half = rows // 2
    within = jnp.arange(rows, dtype=jnp.int32)
    positions = jnp.where(
        within < half, context * half + within, (2 * devices - 1 - context) * half + within - half
    )
    inverse = rope_base ** (-2.0 * jnp.arange(HD // 2, dtype=F32) / HD)
    angles = positions.astype(F32)[:, None] * inverse[None, :]
    sine, cosine = jnp.sin(angles), jnp.cos(angles)
    cos_table = jnp.concatenate([cosine] * 4, axis=1)
    sin_table = jnp.concatenate([-sine, sine, -sine, sine], axis=1)
    length = lengths[section, line]
    attend_scalars = jnp.stack([context, length]).astype(jnp.int32)

    def dispatched(message):
        plane = from_all(message, "ctx")
        blocks = plane + [swapped(block) for block in plane]
        return blocks

    def returned(outs):
        own, other = outs[:devices], outs[devices : 2 * devices]
        crossed = [swapped(block) for block in other]
        near = [own[0], crossed[0]]
        for k in range(1, devices):
            chip = (own[k].astype(F32) + crossed[k].astype(F32)).astype(BF16)
            near.append(exchanged(chip, "ctx", k))
        return near

    my_targets = lax.dynamic_index_in_dim(targets[:, 0], section, 0, keepdims=False)
    layer_input = lax.dynamic_index_in_dim(tokens[:, 0], section, 0, keepdims=False)
    valid = (positions < length).astype(F32)[:, None]
    saved, hidden = [], []
    early_experts = gathered_experts(0, None)
    ahead = None
    for layer in range(layers):
        first, local, sources = places[layer]
        shared, router, gain_first, gain_second = shared_of_plane(
            layer, line_blocks[layer], ahead
        )
        q, kv = project(layer_input, gain_first, shared, cos_table, sin_table)
        if layer == 0:
            line_blocks[1] = shared_of_line(1, kv)
        kvs = from_all(kv, "ctx")
        attended, lse, middle, message = attend(
            attend_scalars, layer_input, q, kvs, shared, gain_second, router, masks[layer]
        )
        messages = dispatched(message)
        if layer == 0:
            ahead = messages
            weights = early_experts
            late_experts = gathered_experts(1, message)
        else:
            weights = late_experts
        kept, outs = [], ()
        xs, gates = dispatch(
            first.astype(jnp.int32).reshape(1), messages, ranks[layer], slots, False
        )
        sparse = layer == 1 and by_rows_fits
        for at, ((a, n), blocks) in enumerate(zip(runs[layer], weights)):
            scal = jnp.stack([first + a, *[jnp.asarray(k) for k in range(depth)]]).astype(jnp.int32)
            by_rows = sparse and at == len(runs[layer]) - 1
            if by_rows:
                terms = [added(terms)]
                scal = after(scal, terms)
            run, outs = experts_forward(
                scal,
                xs,
                ranks[layer][:, a : a + n],
                gates[:, a : a + n],
                blocks,
                depth,
                slots,
                a,
                () if by_rows else outs,
                not by_rows,
            )
            kept.append((a, n, scal, run, blocks))
            if not by_rows:
                terms = returned(outs)
        if layer == layers - 1:
            routed = [last_rank, [], slots] if sparse else []
            if sparse:
                near = outs[:devices]
                near = near[:1] + [exchanged(near[k], "ctx", k) for k in range(1, devices)]
                far = [swapped(block) for block in outs[devices:]]
                far = far[:1] + [exchanged(far[k], "ctx", k) for k in range(1, devices)]
                routed[1] = [block for pair in zip(near, far) for block in pair]
            mixed = None
            hidden_rows, grad_output, message, *row_messages = finish(
                terms, middle, my_targets, valid, *routed
            )
            hidden.append(hidden_rows)
        else:
            mixed = functools.reduce(lambda a, b: a + b, [t.astype(F32) for t in terms])
            hidden.append((middle + mixed).astype(BF16))
        saved.append(
            dict(
                x=layer_input,
                shared=shared,
                router=router,
                gain_first=gain_first,
                gain_second=gain_second,
                q=q,
                kvs=kvs,
                attended=attended,
                lse=lse,
                middle=middle,
                kept=kept,
                xs=xs,
                gates=gates,
                mixed=mixed,
            )
        )
        layer_input = hidden[-1]

    def home_blocks(packed, layer):
        arrived = lax.ppermute(packed, "section", [(1 - layer, layer)])
        size = packed.shape[0] // devices
        return [
            (
                lax.dynamic_slice_in_dim(packed, (context ^ k) * size, size, 0).astype(F32)
                + lax.dynamic_slice_in_dim(arrived, (context ^ k) * size, size, 0).astype(F32)
            ).astype(BF16)
            for k in range(devices)
        ]

    def home_plane(blocks, layer):
        return added(scattered(blocks, "ctx", (layer,))).astype(BF16)

    def home_line(plane, layer, ahead=None):
        size = plane.shape[0] // depth
        blocks = [
            lax.dynamic_slice_in_dim(plane, (line ^ k) * size, size, 0) for k in range(depth)
        ]
        if ahead is not None:
            blocks[-1] = after(blocks[-1], ahead)
        return scattered(blocks, "fsdp", (layer,))

    def placed_rows(values):
        home = jnp.where(first_core, values[0], values[1])
        arrived = swapped(jnp.where(first_core, values[1], values[0]))
        return jnp.stack(
            [jnp.where(first_core, home, arrived), jnp.where(first_core, arrived, home)]
        )

    input_grads, expert_grads = [None] * layers, [None] * layers
    waiting = None
    summed = {}
    for layer in reversed(range(layers)):
        held = saved[layer]
        first, local, sources = places[layer]
        if layer < layers - 1:
            message = grad_message(grad_output, held["mixed"])
        sparse = layer == 1 and by_rows_fits
        if sparse:
            plane = [row_messages[0]] + [
                exchanged(row_messages[k], "ctx", k) for k in range(1, devices)
            ]
            row_blocks = plane + [swapped(block[1]) for block in plane]
            message = after(message, plane[1])
        messages = dispatched(message)
        if waiting is not None:
            by = 1
            while by < depth:
                error = error + lax.ppermute(error, "fsdp", [(i, i ^ by) for i in range(depth)])
                by *= 2
            loss_value = error / jnp.sum(lengths).astype(F32)
            hidden_out = placed_rows(hidden)
            blocks_1 = [waiting[0], home_blocks(waiting[1], 1)]
            messages = after(messages, (blocks_1, loss_value, hidden_out))
            planes = [home_plane(blocks, 1) for blocks in after(blocks_1, messages)]
        own_router = lax.dynamic_slice_in_dim(held["router"], first, local, 0).astype(F32)
        small = jnp.zeros((128, width), F32)
        outs = ()
        gathered = []
        steps = back_runs[layer]
        spans = [a for a, _ in steps]
        for at, (a, n) in enumerate(steps):
            base, _, scal, run, blocks = next(
                kept for kept in held["kept"] if kept[0] <= a and a + n <= kept[0] + kept[1]
            )
            scal = jnp.concatenate([scal[:1] + (a - base), scal[1:]])
            last = None
            if at == len(steps) - 1 and not sparse:
                order = tuple(sorted(range(len(spans)), key=lambda i: spans[i]))
                last = (ranks[layer], [rows_of for rows_of in outs], order)
            if sparse and at == 0:
                grad_rows, inners, start = row_blocks, None, a
            elif not sparse:
                grad_rows, inners = dispatch(
                    scal[:1], messages, ranks[layer][:, a : a + n], slots, True
                )
                start = a
            elif at == 1:
                start = 0
                grad_rows, inners = dispatch(
                    scal[:1], messages, ranks[layer][:, : half_held - 1], slots, True
                )
            grads, router_grad, rows_out = experts_backward(
                scal,
                grad_rows,
                ranks[layer][:, a : a + n],
                held["gates"][:, a : a + n],
                inners,
                held["xs"],
                run,
                own_router[a : a + n, None, :],
                blocks,
                depth,
                slots,
                a,
                a - base,
                a - start,
                last,
            )
            outs = rows_out if last else list(outs) + rows_out
            if layer == 1 and inners is not None:
                error = jnp.sum(inners[:, 1, 0])
            small = lax.dynamic_update_slice_in_dim(small, router_grad[:, 0], first + a, 0)
            gathered.append(grads)
        if sparse:
            order = tuple(sorted(range(len(spans)), key=lambda i: spans[i]))
            outs = combine_rows(ranks[layer], outs, order, slots)
        over_line = lambda grads: lax.psum_scatter(
            grads, "fsdp", scatter_dimension=1, tiled=True
        )
        at_once = gathered if layer == 1 or len(gathered) == 1 else gathered[:-1]
        summed[layer] = [over_line(grads) for grads in at_once]
        if layer == 1:
            grad_output = after(grad_output, summed[1][0])
        else:
            grad_output = after(grad_output, summed[1][-1])
            outs = after(outs, planes)
        back = attend_backward(
            attend_scalars,
            returned(outs),
            grad_output,
            held["middle"],
            held["gain_second"],
            held["attended"],
            held["shared"],
            held["q"],
            held["lse"],
            cos_table,
            -sin_table,
            held["x"],
            held["gain_first"],
            held["kvs"],
        )
        grad_mid, weight_grads, gain_second_grad, dq = back[:4]
        dkv = back[4:]
        parts = [dkv[0]] + [exchanged(dkv[k], "ctx", k) for k in range(1, devices)]
        outward = home_blocks(weight_grads, layer)
        grad_mid = after(grad_mid, outward)
        small = lax.dynamic_update_slice_in_dim(small, gain_second_grad, EXPERTS + 1, 0)
        dx, packed = project_backward(
            held["x"],
            held["gain_first"],
            dq,
            parts,
            grad_mid,
            held["shared"],
            cos_table,
            -sin_table,
            small,
        )
        expert_grads[layer] = (spans, summed[layer])
        input_grads[layer] = dx
        grad_output = dx.astype(BF16).astype(F32)
        if layer == 1:
            waiting = (outward, packed)
        else:
            outward = after(outward, packed)
            summed[0] += [over_line(after(grads, packed)) for grads in gathered[len(at_once) :]]
            inward_plane = home_plane(home_blocks(packed, 0), 0)
            outward_plane = home_plane(outward, 0)

    def pieces_of(layer, at, part):
        arrived = lax.ppermute(part, "section", [(1 - layer, layer)])
        return [
            (layer, half * half_held + at, term)
            for half, term in ((layer, part), (1 - layer, arrived))
        ]

    def placed(pieces, experts, into):
        touched = [p for p in pieces if any(0 <= e - p[1] < p[2].shape[0] for e in experts)]
        return place_experts(
            section.astype(jnp.int32).reshape(1), touched, held_experts, up_rows, experts, into
        )

    parts = [(layer, at, part) for layer in (1, 0) for at, part in zip(*expert_grads[layer])]
    pieces = [piece for part in parts[:-1] for piece in pieces_of(*part)]
    layer, at, part = parts[-1]
    last = [half * half_held + at + i for half in range(2) for i in range(part.shape[0])]
    sums = ()
    if len(last) < held_experts:
        sums = placed(pieces, [e for e in range(held_experts) if e not in last], ())
    first_terms = home_line(
        jnp.concatenate([outward_plane, inward_plane], axis=1), 0, sums if sums else None
    )
    second_terms = home_line(jnp.concatenate(planes, axis=1), 1)
    input_out = placed_rows(after(input_grads, inward_plane))[None, :, None]
    first_terms, second_terms = after((first_terms, second_terms), input_out)
    shared_grads = jnp.where(first_core, added(first_terms), added(second_terms))
    outward, inward = shared_grads[:, : 2 * width], shared_grads[:, 2 * width :]
    if sums:
        part = after(part, (first_terms, second_terms))
    up_sum, down_sum = placed(pieces + pieces_of(layer, at, part), last, sums)
    at = 2 * KW
    return (
        hidden_out[None, :, None],
        input_out,
        loss_value,
        inward[:, at + EXPERTS][None],
        outward[:, width:][None],
        inward[:, :at][None],
        outward[:, :width][None],
        inward[:, at + EXPERTS + 1][None],
        inward[:, at : at + EXPERTS][None],
        up_sum[None],
        down_sum[None],
    )


def solution(mesh):
    placed = (
        P(None, "fsdp", "ctx", None),
        P(None, "fsdp", "ctx", None),
        P(),
        P("section", None, "fsdp", "ctx", None),
        P("section", ("ctx", "fsdp")),
        P("section", ("ctx", "fsdp"), None),
        P("section", ("ctx", "fsdp"), None),
        P("section", ("ctx", "fsdp"), None),
        P("section", ("ctx", "fsdp")),
        P("section", ("ctx", "fsdp"), None),
        P("section", "ctx", "fsdp", None),
        P("section", "ctx", "fsdp", None),
    )
    return jax.shard_map(
        shards,
        mesh=mesh,
        in_specs=placed,
        out_specs=(
            P("section", None, "fsdp", "ctx", None),
            P("section", None, "fsdp", "ctx", None),
            P(),
            P("section", ("ctx", "fsdp")),
            P("section", ("ctx", "fsdp"), None),
            P("section", ("ctx", "fsdp"), None),
            P("section", ("ctx", "fsdp"), None),
            P("section", ("ctx", "fsdp")),
            P("section", ("ctx", "fsdp"), None),
            P("section", "ctx", "fsdp", None),
            P("section", "ctx", "fsdp", None),
        ),
        check_vma=False,
    )
```

```python
import functools
import math

import jax
import jax.numpy as jnp
from jax import lax
from jax.experimental import pallas as pl
from jax.experimental.pallas import tpu as pltpu
from jax.sharding import PartitionSpec as P

QH = 16
KVH = 8
HD = 64
EXPERTS = 32
FF_E = 512
TOPK = 8
KW = KVH * HD
EXT = 16

epsilon = 1e-06
rope_base = 10000.0
negative = -1e30
F32 = jnp.float32
BF16 = jnp.bfloat16
VMEM_LIMIT = 60 * 1024 * 1024


def params(grid_dims=0):
    return pltpu.CompilerParams(
        vmem_limit_bytes=VMEM_LIMIT,
        dimension_semantics=("arbitrary",) * grid_dims if grid_dims else None,
    )


def cost(flops, moved, exps=0, share=1.0):
    return pl.CostEstimate(
        flops=int(flops / share), bytes_accessed=int(moved), transcendentals=int(exps)
    )


def mm(a, b):
    return jnp.dot(a, b, preferred_element_type=F32)


def mm_nt(a, b):
    return lax.dot_general(a, b, (((1,), (1,)), ((), ())), preferred_element_type=F32)


def mm_tn(a, b):
    return lax.dot_general(a, b, (((0,), (0,)), ((), ())), preferred_element_type=F32)


def fixed(shape):
    return pl.BlockSpec(shape, lambda *_: (0,) * len(shape), pipeline_mode=pl.Buffered(1))


def resident(shape):
    return pl.BlockSpec(shape, lambda *_: (0,) * len(shape))


def lane_index(shape):
    return lax.broadcasted_iota(jnp.int32, shape, len(shape) - 1)


def turn(block, cosine, sine):
    low_half = lane_index(block.shape) % HD < HD // 2
    swapped = jnp.where(
        low_half, pltpu.roll(block, 128 - HD // 2, axis=1), pltpu.roll(block, HD // 2, axis=1)
    )
    return block * cosine + swapped * sine


def rolled(block):
    return pltpu.roll(block.astype(F32), HD, axis=1).astype(BF16)


def key_positions(device, half, devices, shape, dim):
    within = lax.broadcasted_iota(jnp.int32, shape, dim)
    return jnp.where(
        within < half, device * half + within, (2 * devices - 1 - device) * half + within - half
    )


def fill_bias(bias, scal, devices, rows):
    context, length = scal[0], scal[1]
    query_pos = key_positions(context, rows // 2, devices, (rows, rows), 1)
    for k in range(devices):
        key_pos = key_positions(context ^ k, rows // 2, devices, (rows, rows), 0)
        taken = (key_pos <= query_pos) & (key_pos < length)
        bias[k * rows : (k + 1) * rows, :] = jnp.where(taken, 0.0, negative)


def two_heads(block):
    even = lane_index(block.shape) < HD
    zero = jnp.zeros((), block.dtype)
    return jnp.concatenate([jnp.where(even, block, zero), jnp.where(even, zero, block)], axis=0)


def two_heads_doubled(block):
    even = lane_index(block.shape) < HD
    other = rolled(block)
    return jnp.concatenate([jnp.where(even, block, other), jnp.where(even, other, block)], axis=0)


def doubled(block, odd):
    even = lane_index(block.shape) < HD
    other = rolled(block)
    return jnp.where(even, other, block) if odd else jnp.where(even, block, other)


def one_hot(rank_row, slots):
    rows = rank_row.shape[-1]
    index = lax.broadcasted_iota(jnp.int32, (slots, rows), 0).astype(F32)
    return rank_row == index


def project_kernel(x, gain, wq, wm, cosine, sine, q_out, kv_out):
    values = x[...].astype(F32)
    factor = lax.rsqrt(jnp.mean(values * values, axis=-1, keepdims=True) + epsilon)
    normed = (values * factor * gain[...]).astype(BF16)
    cos, sin = cosine[...], sine[...]
    q0 = mm(normed, wq[...])
    for b in range(QH * HD // 128):
        at = slice(b * 128, (b + 1) * 128)
        q_out[:, at] = turn(q0[:, at], cos, sin).astype(BF16)
    kv0 = mm(normed, wm[...])
    for b in range(KW // 128):
        at = slice(b * 128, (b + 1) * 128)
        kv_out[0, :, at] = turn(kv0[:, at], cos, sin).astype(BF16)
    kv_out[1] = kv0[:, KW:].astype(BF16)


def project(x, gain, shared, cosine, sine):
    rows, width = x.shape
    return pl.pallas_call(
        project_kernel,
        name="project",
        grid=(1,),
        in_specs=[
            fixed((rows, width)),
            fixed((1, width)),
            pl.BlockSpec((width, QH * HD), lambda i: (0, 0), pipeline_mode=pl.Buffered(1)),
            pl.BlockSpec((width, 2 * KW), lambda i: (0, 1), pipeline_mode=pl.Buffered(1)),
            fixed((rows, 128)),
            fixed((rows, 128)),
        ],
        out_specs=[resident((rows, QH * HD)), resident((2, rows, KW))],
        out_shape=[
            jax.ShapeDtypeStruct((rows, QH * HD), BF16),
            jax.ShapeDtypeStruct((2, rows, KW), BF16),
        ],
        compiler_params=params(1),
        cost_estimate=cost(
            2 * rows * width * 2048, 2 * width * 2048 + 8 * rows * width, share=0.2
        ),
    )(x, gain, shared, shared, cosine, sine)


def attend_kernel(devices, scal, x, q, *rest):
    ks, vs, rest = rest[:devices], rest[devices : 2 * devices], rest[2 * devices :]
    wo, gain, router, mask, o_out, lse_out, mid_out, msg_out, bias, held = rest
    rows = x.shape[0]
    step = pl.program_id(0)

    @pl.when(step == 0)
    def _():
        fill_bias(bias, scal, devices, rows)

    keys = jnp.concatenate([r[0] for r in ks], axis=0)
    values = jnp.concatenate([r[0] for r in vs], axis=0)
    block_bias = bias[...]
    both_bias = jnp.concatenate([block_bias, block_bias], axis=1)
    for i in range(2):
        query = two_heads(q[:, i * 128 : (i + 1) * 128])
        scores = mm_nt(doubled(keys, i), query) * (1.0 / math.sqrt(HD)) + both_bias
        top = jnp.max(scores, axis=0, keepdims=True)
        raised = jnp.exp(scores - top)
        total = jnp.sum(raised, axis=0, keepdims=True)
        probs = (raised * (1.0 / total)).astype(BF16)
        lse_out[0, i : i + 1, :] = top + jnp.log(total)
        mixed = mm_tn(values, probs)[i * HD : (i + 1) * HD]
        pair = jnp.concatenate([mixed[:, :rows], mixed[:, rows:]], axis=0)
        at = pl.multiple_of(step * 256 + i * 128, 128)
        held[:, pl.ds(at, 128)] = jnp.transpose(pair).astype(BF16)

    @pl.when(step == pl.num_programs(0) - 1)
    def _():
        attended = held[...]
        o_out[...] = attended
        middle = x[...].astype(F32) + mm(attended, wo[...])
        mid_out[...] = middle
        factor = lax.rsqrt(jnp.mean(middle * middle, axis=-1, keepdims=True) + epsilon)
        normed = (middle * factor * gain[...]).astype(BF16)
        msg_out[:rows, :] = normed
        logits = mm_nt(router[...], normed)
        chosen = mask[...] > 0.5
        top = jnp.max(jnp.where(chosen, logits, negative), axis=0, keepdims=True)
        raised = jnp.where(chosen, jnp.exp(jnp.where(chosen, logits - top, 0.0)), 0.0)
        gates = raised / jnp.sum(raised, axis=0, keepdims=True)
        high = gates.astype(BF16)
        low = (gates - high.astype(F32)).astype(BF16)
        ext = [high[:EXT], high[EXT:], low[:EXT], low[EXT:]]
        if 4 * rows < x.shape[1]:
            ext.append(jnp.zeros((EXT, x.shape[1] - 4 * rows), BF16))
        msg_out[rows:, :] = jnp.concatenate(ext, axis=1)


def attend(scal, x, q, kvs, shared, gain, router, mask):
    rows, width = x.shape
    devices = len(kvs)
    keys = devices * rows
    kv_specs = [pl.BlockSpec((1, rows, 128), lambda h: (0, 0, h)) for _ in kvs] + [
        pl.BlockSpec((1, rows, 128), lambda h: (1, 0, h)) for _ in kvs
    ]
    return pl.pallas_call(
        functools.partial(attend_kernel, devices),
        name="attend",
        grid=(KVH // 2,),
        in_specs=[
            pl.BlockSpec(memory_space=pltpu.SMEM),
            fixed((rows, width)),
            pl.BlockSpec((rows, 256), lambda h: (0, h)),
            *kv_specs,
            pl.BlockSpec((QH * HD, width), lambda h: (0, 2), pipeline_mode=pl.Buffered(1)),
            fixed((1, width)),
            fixed((EXPERTS, width)),
            fixed((EXPERTS, rows)),
        ],
        out_specs=[
            resident((rows, QH * HD)),
            pl.BlockSpec((1, 2, 2 * rows), lambda h: (h, 0, 0)),
            resident((rows, width)),
            resident((rows + EXT, width)),
        ],
        out_shape=[
            jax.ShapeDtypeStruct((rows, QH * HD), BF16),
            jax.ShapeDtypeStruct((KVH // 2, 2, 2 * rows), F32),
            jax.ShapeDtypeStruct((rows, width), F32),
            jax.ShapeDtypeStruct((rows + EXT, width), BF16),
        ],
        scratch_shapes=[pltpu.VMEM((keys, rows), F32), pltpu.VMEM((rows, QH * HD), BF16)],
        compiler_params=params(1),
        cost_estimate=cost(
            4 * rows * keys * QH * HD * 2 + 2 * rows * width * width,
            2 * width * width + 4 * keys * width + 12 * rows * width,
            rows * keys * QH,
            0.17,
        ),
    )(scal, x, q, *kvs, *kvs, shared, gain, router, mask)


def hot_rows(rank, j, slots):
    local = rank.shape[1]
    return jnp.concatenate(
        [
            jnp.where(one_hot(rank[j, i : i + 1, :], slots), 1.0, 0.0).astype(BF16)
            for i in range(local)
        ],
        axis=0,
    )


def combine(rank, held, prior, outs, buffers, slots):
    held = held if isinstance(held, list) else [held]
    prior_buffer, out_buffer, prior_sems, out_sems = buffers
    width = held[0].shape[-1]
    depth = out_buffer.shape[0]
    count = len(outs)
    fetch = lambda j: pltpu.make_async_copy(
        prior[j], prior_buffer.at[j % depth], prior_sems.at[j % depth]
    )
    send = lambda j: pltpu.make_async_copy(
        out_buffer.at[j % depth], outs[j], out_sems.at[j % depth]
    )
    for j in range(min(depth - 1, count) if prior else 0):
        fetch(j).start()
    for j in range(count):
        rows = [part[:, j].reshape(part.shape[0] * slots, width) for part in held]
        rows = rows[0] if len(rows) == 1 else jnp.concatenate(rows, axis=0)
        total = mm_tn(hot_rows(rank, j, slots), rows)
        if prior:
            if j + depth - 1 < count:
                fetch(j + depth - 1).start()
            fetch(j).wait()
            total = total + prior_buffer[j % depth].astype(F32)
        if j >= depth:
            send(j - depth).wait()
        out_buffer[j % depth] = total.astype(BF16)
        send(j).start()
    for j in range(max(0, count - depth), count):
        send(j).wait()


def gate_columns(rank, values, step, sources, slots):
    columns = []
    for j in sources:
        hot = one_hot(rank[j, pl.ds(step, 1), :], slots)
        columns.append(jnp.sum(jnp.where(hot, values(j), 0.0), axis=1, keepdims=True))
    return jnp.concatenate(columns, axis=0)


def finish_kernel(count, routed, slots, *refs):
    terms, (middle, goal, valid, refs) = refs[:count], (*refs[count : count + 3], refs[count + 3 :])
    if routed:
        rank, refs = refs[0], refs[1:]
        arrived, refs = refs[:routed], refs[routed:]
    hidden, grad_out, message, refs = *refs[:3], refs[3:]
    rows, width = middle.shape
    mixed = terms[0][...].astype(F32)
    for term in terms[1:]:
        mixed = mixed + term[...].astype(F32)
    if routed:
        given = jnp.concatenate([ref[...].reshape(-1, width) for ref in arrived], axis=0)
        hots = [
            jnp.where(one_hot(rank[i : i + 1, :], slots), 1.0, 0.0).astype(BF16)
            for i in range(rank.shape[0])
        ]
        mixed = mixed + mm_tn(jnp.concatenate(hots, axis=0), given)
    output = middle[...] + mixed
    hidden[...] = output.astype(BF16)
    grad = (output - goal[...].astype(F32)) * valid[...]
    grad_out[...] = grad
    error = 0.5 * jnp.sum(jnp.sum(grad * grad, axis=1, keepdims=True), axis=0, keepdims=True)
    fill_message(message, grad, mixed, error)
    if routed:
        low = message[:rows, :]
        inner = message[rows:, :rows]
        for i, hot in enumerate(hots):
            spread = jnp.where(one_hot(rank[i : i + 1, :], 128), 1.0, 0.0).astype(BF16)
            below = jnp.concatenate(
                [mm_nt(inner, spread)[:8], jnp.zeros((8, width - 128), F32)], axis=1
            )
            refs[i // 2][i % 2] = jnp.concatenate(
                [mm(hot, low)[: slots - 8], below], axis=0
            ).astype(BF16)


def finish(terms, middle, goal, valid, rank=None, arrived=(), slots=0):
    rows, width = middle.shape
    messages = len(rank) // 2 if arrived else 0
    return pl.pallas_call(
        functools.partial(finish_kernel, len(terms), len(arrived), slots),
        name="finish",
        out_shape=[
            jax.ShapeDtypeStruct((rows, width), BF16),
            jax.ShapeDtypeStruct((rows, width), F32),
            jax.ShapeDtypeStruct((rows + EXT, width), BF16),
            *[jax.ShapeDtypeStruct((2, slots, width), BF16) for _ in range(messages)],
        ],
        compiler_params=params(),
        cost_estimate=cost(8 * rows * width, 24 * rows * width),
    )(*terms, middle, goal, valid, *([rank, *arrived] if arrived else []))


def fill_message(message, grad, mixed, error):
    rows, width = grad.shape
    message[:rows, :] = grad.astype(BF16)
    inner = jnp.transpose(
        jnp.broadcast_to(jnp.sum(grad * mixed, axis=1, keepdims=True), (rows, 128))
    )[:EXT]
    high = inner.astype(BF16)
    low = (inner - high.astype(F32)).astype(BF16)
    row = lax.broadcasted_iota(jnp.int32, (EXT, rows), 0)
    ext = jnp.where(row == 0, high.astype(F32), jnp.where(row == 1, low.astype(F32), 0.0))
    for at in range(2, 5):
        term = error.astype(BF16).astype(F32)
        ext = jnp.where(row == at, term, ext)
        error = error - term
    message[rows:, :rows] = ext.astype(BF16)
    message[rows:, rows:] = jnp.zeros((EXT, width - rows), BF16)


def message_kernel(grad, mixed, message):
    fill_message(message, grad[...], mixed[...], jnp.zeros((1, 1), F32))


def grad_message(grad, mixed):
    rows, width = grad.shape
    return pl.pallas_call(
        message_kernel,
        name="grad_message",
        out_shape=jax.ShapeDtypeStruct((rows + EXT, width), BF16),
        compiler_params=params(),
        cost_estimate=cost(4 * rows * width, 10 * rows * width),
    )(grad, mixed)


def dispatch_kernel(sources, slots, backward, scal, *rest):
    msgs, (rank, x_out, side_out, arrived, picked, in_sems, out_sems) = (
        rest[:sources],
        rest[sources:],
    )
    local, rows = rank.shape[1:]
    fetch = lambda j: pltpu.make_async_copy(msgs[j], arrived.at[j], in_sems.at[j])
    send = lambda j: pltpu.make_async_copy(picked.at[j], x_out.at[:, j], out_sems.at[j])
    for j in range(sources):
        fetch(j).start()
    pick_row = lax.broadcasted_iota(jnp.int32, (EXT, 4 * rows), 0)
    for j in range(sources):
        fetch(j).wait()
        taken = mm(hot_rows(rank, j, slots), arrived[j, :rows, :]).astype(BF16)
        for i in range(local):
            picked[j, i] = taken[i * slots : (i + 1) * slots]
        send(j).start()
        if backward:
            ext = arrived[j, rows:, :rows].astype(F32)
            side_out[j, 0:1, :] = ext[0:1, :] + ext[1:2, :]
            side_out[j, 1:2, :] = ext[2:3, :] + ext[3:4, :] + ext[4:5, :]
        else:
            ext = arrived[j, rows:, : 4 * rows].astype(F32)
            for i in range(local):
                expert = scal[0] + i
                row = jnp.sum(jnp.where(pick_row == expert % EXT, ext, 0.0), axis=0, keepdims=True)
                high = jnp.where(expert < EXT, row[:, :rows], row[:, rows : 2 * rows])
                low = jnp.where(expert < EXT, row[:, 2 * rows : 3 * rows], row[:, 3 * rows :])
                side_out[j, i : i + 1, :] = high + low
    for j in range(sources):
        send(j).wait()


def dispatch(scal, msgs, rank, slots, backward):
    sources, local, rows = rank.shape
    width = msgs[0].shape[1]
    anywhere = pl.BlockSpec(memory_space=pl.ANY)
    side = (sources, 2 if backward else local, rows)
    taken, beside = pl.pallas_call(
        functools.partial(dispatch_kernel, sources, slots, backward),
        name="dispatch",
        grid=(1,),
        in_specs=[
            pl.BlockSpec(memory_space=pltpu.SMEM),
            *[anywhere for _ in msgs],
            fixed(rank.shape),
        ],
        out_specs=[anywhere, resident(side)],
        out_shape=[
            jax.ShapeDtypeStruct((local, sources, slots, width), BF16),
            jax.ShapeDtypeStruct(side, F32),
        ],
        scratch_shapes=[
            pltpu.VMEM((sources, rows + EXT, width), BF16),
            pltpu.VMEM((sources, local, slots, width), BF16),
            pltpu.SemaphoreType.DMA((sources,)),
            pltpu.SemaphoreType.DMA((sources,)),
        ],
        compiler_params=params(1),
        cost_estimate=cost(
            2 * local * sources * slots * rows * width,
            2 * sources * width * (rows + local * slots),
            0,
            0.05 * local,
        ),
    )(scal, *msgs, rank)
    return taken.reshape(local, sources * slots, width), beside


def fill_weights(scal, blocks, w1, w2):
    up = w1.shape[0] // len(blocks)
    down = w2.shape[0] // len(blocks)
    for k, block in enumerate(blocks):
        at = scal[1 + k]
        w1[pl.ds(pl.multiple_of(at * up, up), up), :] = block[0, :up]
        w2[pl.ds(pl.multiple_of(at * down, down), down), :] = block[0, up:]


def experts_kernel(sources, depth, slots, chained, combined, scal, *rest):
    prior = ()
    if chained:
        prior, rest = rest[:sources], rest[sources:]
    rank, gates, xs, rest = *rest[:3], rest[3:]
    blocks, rest = rest[:depth], rest[depth:]
    gu_out, y_out, rest = *rest[:2], rest[2:]
    if combined:
        outs, rest = rest[:sources], rest[sources:]
        held, w1, w2 = rest[:3]
    else:
        outs, (w1, w2) = rest[:sources], rest[sources:]
    width = w1.shape[0]
    step, part = pl.program_id(0), pl.program_id(1)
    portions = sources // (xs.shape[1] // slots)
    portion = sources // portions

    @pl.when(part == 0)
    def _():
        fill_weights(scal, blocks, w1, w2)

    gate_up = mm(xs[0], w1[...])
    gu_out[0] = gate_up
    gate, up = gate_up[:, :FF_E], gate_up[:, FF_E:]
    activated = (gate * jax.nn.sigmoid(gate) * up).astype(BF16)
    out = mm(activated, w2[...]).astype(BF16)
    y_out[0] = out
    column = gate_columns(
        rank,
        lambda j: gates[j, pl.ds(step, 1), :],
        step,
        [part * portion + n for n in range(portion)],
        slots,
    )
    given = (column * out.astype(F32)).astype(BF16).reshape(portion, slots, width)
    if combined:
        held[step, pl.ds(part * portion, portion)] = given

        @pl.when((step == pl.num_programs(0) - 1) & (part == portions - 1))
        def _():
            combine(rank, held, prior, outs, rest[3:], slots)

    else:
        for j in range(sources):
            outs[j][...] = given[j]


def weight_specs(blocks, depth, base=0):
    arrays = blocks if len(blocks) == depth else blocks * depth
    rows = arrays[0].shape[1] // (depth // len(blocks))
    width = arrays[0].shape[2]
    specs = [
        pl.BlockSpec((1, rows, width), lambda e, r, f=(k if len(blocks) == 1 else 0): (e + base, f, 0))
        for k in range(depth)
    ]
    return arrays, specs


def combine_kernel(order, rank, *refs):
    parts, rest = refs[: len(order)], refs[len(order) :]
    outs, buffers = rest[:-4], rest[-4:]
    slots = parts[0].shape[2]
    combine(rank, [parts[o] for o in order], (), outs, buffers, slots)


def combine_rows(rank, parts, order, slots):
    sources, _, rows = rank.shape
    width = parts[0].shape[-1]
    parts = [part.reshape(part.shape[0], sources, slots, width) for part in parts]
    return list(
        pl.pallas_call(
            functools.partial(combine_kernel, order),
            name="combine_rows",
            grid=(1,),
            in_specs=[fixed(rank.shape), *[fixed(part.shape) for part in parts]],
            out_specs=[pl.BlockSpec(memory_space=pl.ANY)] * sources,
            out_shape=[jax.ShapeDtypeStruct((rows, width), BF16)] * sources,
            scratch_shapes=stream_scratch(rows, width),
            compiler_params=params(1),
            cost_estimate=cost(
                2 * sources * rows * width * rank.shape[1] * slots,
                4 * sources * width * rank.shape[1] * slots,
                share=0.2,
            ),
        )(rank, *parts)
    )


def stream_scratch(rows, width):
    return [
        pltpu.VMEM((4, rows, width), BF16),
        pltpu.VMEM((4, rows, width), BF16),
        pltpu.SemaphoreType.DMA((4,)),
        pltpu.SemaphoreType.DMA((4,)),
    ]


def experts_forward(scal, xs, rank, gates, blocks, depth, slots, first, prior=(), combined=True):
    sources, local, rows = rank.shape
    width = xs.shape[2]
    portions = max(1, sources // 8) if combined else 1
    count = sources * slots
    arrays, specs = weight_specs(blocks, depth)
    anywhere = pl.BlockSpec(memory_space=pl.ANY)
    each = lambda shape, base=0: pl.BlockSpec((1,) + shape, lambda e, r: (e + base, r, 0))
    outs = pl.pallas_call(
        functools.partial(experts_kernel, sources, depth, slots, bool(prior), combined),
        name="experts_forward",
        grid=(local, portions),
        in_specs=[
            pl.BlockSpec(memory_space=pltpu.SMEM),
            *[anywhere for _ in prior],
            fixed((sources, local, rows)),
            fixed((sources, local, rows)),
            each((count // portions, width), first),
            *specs,
        ],
        out_specs=[
            each((count // portions, 2 * FF_E)),
            each((count // portions, width)),
            *(
                [anywhere] * sources
                if combined
                else [resident((slots, width))] * sources
            ),
        ],
        out_shape=[
            jax.ShapeDtypeStruct((local, count, 2 * FF_E), F32),
            jax.ShapeDtypeStruct((local, count, width), BF16),
            *(
                [jax.ShapeDtypeStruct((rows, width), BF16)] * sources
                if combined
                else [jax.ShapeDtypeStruct((slots, width), BF16)] * sources
            ),
        ],
        scratch_shapes=[
            *([pltpu.VMEM((local, sources, slots, width), BF16)] if combined else []),
            pltpu.VMEM((width, 2 * FF_E), BF16),
            pltpu.VMEM((FF_E, width), BF16),
            *(stream_scratch(rows, width) if combined else []),
        ],
        compiler_params=params(2),
        cost_estimate=cost(
            2 * local * count * width * 3 * FF_E * 1.3,
            8 * local * count * width,
            local * count * FF_E,
            0.1 * (local + 1),
        ),
    )(scal, *prior, rank, gates, xs, *arrays)
    return outs[:2], list(outs[2:])


def experts_back_kernel(sources, depth, slots, mode, scal, *rest):
    last, order, direct = mode
    earlier = ()
    if last:
        full_rank, rest = rest[0], rest[1:]
        earlier, rest = rest[: len(order) - 1], rest[len(order) - 1 :]
    if direct:
        rank, gates, rest = *rest[:2], rest[2:]
        given_rows, rest = rest[:sources], rest[sources:]
    else:
        rank, gates, inners, grads, rest = *rest[:4], rest[4:]
    xs, gu, ys, router, rest = *rest[:4], rest[4:]
    blocks, rest = rest[:depth], rest[depth:]
    grad_out_ref, router_out, rest = *rest[:2], rest[2:]
    outs, rest = (rest[:sources], rest[sources:]) if last else (rest[:1], rest[1:])
    held, w1, w2, sum1, sum2 = rest[:5]
    width = w1.shape[0]
    step, part = pl.program_id(0), pl.program_id(1)
    portions = sources // (xs.shape[1] // slots)
    portion = sources // portions

    @pl.when(part == 0)
    def _():
        fill_weights(scal, blocks, w1, w2)

    mine = [part * portion + n for n in range(portion)]
    gate_column = gate_columns(rank, lambda j: gates[j, pl.ds(step, 1), :], step, mine, slots)
    if direct:
        blocks_of = [ref[0] if len(ref.shape) == 3 else ref[...] for ref in given_rows]
        blocks_of = [block.astype(F32) for block in blocks_of]
        grad_out = jnp.concatenate(blocks_of, axis=0)
        inner_column = jnp.concatenate(
            [
                jnp.transpose(block[slots - 8 :, :128])[:slots, :2].sum(axis=1, keepdims=True)
                for block in blocks_of
            ],
            axis=0,
        )
    else:
        inner_column = gate_columns(rank, lambda j: inners[j, 0:1, :], step, mine, slots)
        grad_out = grads[0].astype(F32)
    grad_y = (gate_column * grad_out).astype(BF16)
    given = jnp.sum(grad_out * ys[0].astype(F32), axis=1, keepdims=True)
    grad_logit = gate_column * (given - inner_column)
    gate, up = gu[0, :, :FF_E], gu[0, :, FF_E:]
    sigmoid = jax.nn.sigmoid(gate)
    silu = gate * sigmoid
    activated = (silu * up).astype(BF16)
    down_part = mm_tn(activated, grad_y)
    grad_act = mm_nt(grad_y, w2[...])
    grad_gate = grad_act * up * sigmoid * (1.0 + gate * (1.0 - sigmoid))
    grad_up = grad_act * silu
    grad_gate_up = jnp.concatenate([grad_gate.astype(BF16), grad_up.astype(BF16)], axis=1)
    taken = xs[0]
    up_part = mm_tn(taken, grad_gate_up)
    router_part = jnp.sum(taken.astype(F32) * grad_logit, axis=0, keepdims=True)
    grad_rows = mm_nt(grad_gate_up, w1[...]) + grad_logit * router[0]
    if last:
        held[step, pl.ds(part * portion, portion)] = grad_rows.astype(BF16).reshape(
            portion, slots, width
        )
    else:
        outs[0][0] = grad_rows.astype(BF16)

    def write(up_total, down_total):
        up_rows, down_rows = width // depth, FF_E // depth
        for f in range(depth):
            top = f * (up_rows + down_rows)
            grad_out_ref[0, top : top + up_rows, :] = up_total[
                f * up_rows : (f + 1) * up_rows
            ].astype(BF16)
            grad_out_ref[0, top + up_rows : top + up_rows + down_rows, :] = down_total[
                f * down_rows : (f + 1) * down_rows
            ].astype(BF16)

    if sum1 is None:
        write(up_part, down_part)
        router_out[0] = router_part
    else:

        @pl.when(part == 0)
        def _():
            sum1[...] = up_part
            sum2[...] = down_part
            router_out[0] = router_part

        @pl.when(part > 0)
        def _():
            sum1[...] += up_part
            sum2[...] += down_part
            router_out[0] += router_part

        @pl.when(part == portions - 1)
        def _():
            write(sum1, sum2)

    if last:

        @pl.when((step == pl.num_programs(0) - 1) & (part == portions - 1))
        def _():
            pieces = list(earlier) + [held]
            combine(full_rank, [pieces[o] for o in order], (), outs, rest[5:], slots)


def experts_backward(
    scal, grads, rank, gates, inners, xs, kept, router, blocks, depth, slots, first, base, begin, last
):
    direct = isinstance(grads, list)
    sources, local, rows = rank.shape
    width = xs.shape[2]
    portions = max(1, sources // 8)
    count = sources * slots
    gu, ys = kept
    arrays, specs = weight_specs(blocks, depth, base)
    merged = width + FF_E
    anywhere = pl.BlockSpec(memory_space=pl.ANY)
    each = lambda shape, base=0: pl.BlockSpec((1,) + shape, lambda e, r: (e + base, r, 0))
    whole = lambda shape: pl.BlockSpec((1,) + shape, lambda e, r: (e, 0, 0))
    before = []
    if last:
        before = [last[0]] + [
            part.reshape(part.shape[0], sources, slots, width) for part in last[1]
        ]
    mode = (bool(last), last[2] if last else (), direct)
    if direct:
        given = grads
        given_specs = [
            fixed(block.shape)
            if block.ndim == 2
            else pl.BlockSpec(
                (1,) + block.shape[1:], lambda *_: (0, 0, 0), pipeline_mode=pl.Buffered(1)
            )
            for block in grads
        ]
    else:
        given = [inners, grads]
        given_specs = [fixed((sources, 2, rows)), each((count // portions, width), begin)]

    def kernel(*refs):
        refs = list(refs)
        if portions == 1:
            at = len(refs) - (4 if last else 0)
            refs[at:at] = [None, None]
        if not last:
            refs[-4:-4] = [None]
        experts_back_kernel(sources, depth, slots, mode, *refs)

    sums = [pltpu.VMEM((width, 2 * FF_E), F32), pltpu.VMEM((FF_E, width), F32)]
    outs = pl.pallas_call(
        kernel,
        name="experts_backward",
        grid=(local, portions),
        in_specs=[
            pl.BlockSpec(memory_space=pltpu.SMEM),
            *[fixed(part.shape) for part in before],
            fixed((sources, local, rows)),
            fixed((sources, local, rows)),
            *given_specs,
            each((count // portions, width), first),
            each((count // portions, 2 * FF_E), base),
            each((count // portions, width), base),
            whole((1, width)),
            *specs,
        ],
        out_specs=[
            whole((merged, width)),
            whole((1, width)),
            *([anywhere] * sources if last else [each((count // portions, width))]),
        ],
        out_shape=[
            jax.ShapeDtypeStruct((local, merged, width), BF16),
            jax.ShapeDtypeStruct((local, 1, width), F32),
            *(
                [jax.ShapeDtypeStruct((rows, width), BF16)] * sources
                if last
                else [jax.ShapeDtypeStruct((local, count, width), BF16)]
            ),
        ],
        scratch_shapes=[
            *([pltpu.VMEM((local, sources, slots, width), BF16)] if last else []),
            pltpu.VMEM((width, 2 * FF_E), BF16),
            pltpu.VMEM((FF_E, width), BF16),
            *(sums if portions > 1 else []),
            *(stream_scratch(rows, width) if last else []),
        ],
        compiler_params=params(2),
        cost_estimate=cost(
            2 * local * count * width * 3 * FF_E * 2.3,
            14 * local * count * width,
            local * count * FF_E,
            0.37,
        ),
    )(scal, *before, rank, gates, *given, xs, gu, ys, router, *arrays)
    return outs[0], outs[1], list(outs[2:])


def place_kernel(places, number, aliased, scal, *refs):
    parts, (up_out, down_out) = refs[: -2 - aliased], refs[-2:]
    step = number(pl.program_id(0))
    up_rows = up_out.shape[1]

    def put(block):
        up_out[0] = block[0, :up_rows].astype(F32)
        down_out[0] = block[0, up_rows:].astype(F32)

    at = 0
    for place in places:
        core, base, count = place
        pl.when((scal[0] == core) & (step >= base) & (step < base + count))(
            functools.partial(put, parts[at])
        )
        at += 1


def place_experts(scal, pieces, held_experts, up_rows, experts, into=()):
    rows, width = pieces[0][2].shape[1:]
    run = next((i for i in range(1, len(experts)) if experts[i] != experts[0] + i), len(experts))
    skip = experts[run] - experts[run - 1] if run < len(experts) else 1
    number = lambda i: experts[0] + (i // run) * (run - 1 + skip) + i % run
    assert [number(i) for i in range(len(experts))] == list(experts)
    places = [(core, base, array.shape[0]) for core, base, array in pieces]
    arrays = [array for _, _, array in pieces]
    specs = [
        pl.BlockSpec(
            (1, rows, width),
            lambda i, scal, base=base, top=count - 1: (jnp.clip(number(i) - base, 0, top), 0, 0),
        )
        for _, base, count in places
    ]
    specs += [pl.BlockSpec(memory_space=pl.ANY) for _ in into]
    return pl.pallas_call(
        functools.partial(place_kernel, places, number, len(into)),
        name="place_experts",
        grid_spec=pltpu.PrefetchScalarGridSpec(
            num_scalar_prefetch=1,
            grid=(len(experts),),
            in_specs=specs,
            out_specs=[
                pl.BlockSpec((1, up_rows, width), lambda i, scal: (number(i), 0, 0)),
                pl.BlockSpec((1, rows - up_rows, width), lambda i, scal: (number(i), 0, 0)),
            ],
        ),
        out_shape=[
            jax.ShapeDtypeStruct((held_experts, up_rows, width), F32),
            jax.ShapeDtypeStruct((held_experts, rows - up_rows, width), F32),
        ],
        input_output_aliases={1 + len(arrays) + i: i for i in range(len(into))},
        compiler_params=params(1),
        cost_estimate=cost(0, 8 * len(experts) * rows * width),
    )(scal, *arrays, *into)


def pack_kernel(scal, up, down, out):
    up_rows = up.shape[1]
    out[0, :up_rows, :] = up[0]
    out[0, up_rows:, :] = down[0]


def pack_experts(half, up, down):
    experts, up_rows, width = up.shape
    rows = up_rows + down.shape[1]
    local = experts // 2
    take = lambda i, scal: (scal[0] * local + i, 0, 0)
    return pl.pallas_call(
        pack_kernel,
        name="pack_experts",
        grid_spec=pltpu.PrefetchScalarGridSpec(
            num_scalar_prefetch=1,
            grid=(local,),
            in_specs=[
                pl.BlockSpec((1, up_rows, width), take),
                pl.BlockSpec((1, rows - up_rows, width), take),
            ],
            out_specs=pl.BlockSpec((1, rows, width), lambda i, scal: (i, 0, 0)),
        ),
        out_shape=jax.ShapeDtypeStruct((local, rows, width), BF16),
        compiler_params=params(1),
        cost_estimate=cost(0, 4 * local * rows * width),
    )(half.astype(jnp.int32).reshape(1), up, down)


def assemble_kernel(devices, depth, scal, *refs):
    owns, others, whole, sem = refs[:devices], refs[devices : 2 * devices], refs[-2], refs[-1]
    piece = whole.shape[0] // (devices * depth)
    for home, blocks in ((1, owns), (0, others)):

        @pl.when(scal[0] == home)
        def _(blocks=blocks):
            for k in range(devices):
                for i in range(depth):
                    to = pl.multiple_of(((scal[1] ^ k) * depth + (scal[2] ^ i)) * piece, piece)
                    pltpu.make_async_copy(
                        blocks[k].at[pl.ds(i * piece, piece)], whole.at[pl.ds(to, piece)], sem
                    ).start()
            pltpu.make_async_copy(whole, whole, sem).wait()


def assemble(scal, owns, others, depth):
    devices = len(owns)
    rows, columns = owns[0].shape
    return pl.pallas_call(
        functools.partial(assemble_kernel, devices, depth),
        name="assemble",
        in_specs=[pl.BlockSpec(memory_space=pltpu.SMEM)]
        + [pl.BlockSpec(memory_space=pl.ANY)] * (2 * devices),
        out_specs=pl.BlockSpec(memory_space=pltpu.VMEM),
        out_shape=jax.ShapeDtypeStruct((rows * devices, columns), owns[0].dtype),
        scratch_shapes=[pltpu.SemaphoreType.DMA(())],
        compiler_params=params(),
        cost_estimate=cost(0, 4 * rows * devices * columns),
    )(scal, *owns, *others)


def attend_back_kernel(devices, arrived, scal, *rest):
    parts, rest = rest[:arrived], rest[arrived:]
    grad_out, middle, gain, attended, wo, q, lse, cosine, sine, x, gain_first = rest[:11]
    ks, vs, rest = rest[11 : 11 + devices], rest[11 + devices : 11 + 2 * devices], rest[11 + 2 * devices :]
    mid_out, weight_grads, gain_grad, dq_out = rest[:4]
    dkv_outs, (bias, held) = rest[4 : 4 + devices], rest[4 + devices :]
    width = middle.shape[1]
    rows = middle.shape[0]
    scale = 1.0 / math.sqrt(HD)
    step = pl.program_id(0)

    @pl.when(step == 0)
    def _():
        fill_bias(bias, scal, devices, rows)
        grad_mix = parts[0][...].astype(F32)
        for part in parts[1:]:
            grad_mix = grad_mix + part[...].astype(F32)
        mid = middle[...]
        factor = lax.rsqrt(jnp.mean(mid * mid, axis=-1, keepdims=True) + epsilon)
        scaled = grad_mix * gain[...]
        inner = jnp.mean(mid * scaled, axis=-1, keepdims=True)
        gain_grad[...] = jnp.sum(grad_mix * mid * factor, axis=0, keepdims=True)
        grad_mid = grad_out[...] + factor * scaled - mid * (factor * factor * factor * inner)
        mid_out[...] = grad_mid
        branch = grad_mid.astype(BF16)
        weight_grads[:, :width] = mm_tn(attended[...], branch).astype(BF16)
        held[...] = mm_nt(branch, wo[...]).astype(BF16)

    keys = jnp.concatenate([r[0] for r in ks], axis=0)
    values = jnp.concatenate([r[0] for r in vs], axis=0)
    block_bias = bias[...]
    both_bias = jnp.concatenate([block_bias, block_bias], axis=1)
    key_parts, value_parts = [], []
    for i in range(2):
        block = q[:, i * 128 : (i + 1) * 128]
        at = pl.multiple_of(step * 256 + i * 128, 128)
        grads = held[:, pl.ds(at, 128)]
        scores = mm_nt(doubled(keys, i), two_heads(block)) * scale + both_bias
        probs = jnp.exp(scores - lse[0, i : i + 1, :])
        grad_probs = mm_nt(doubled(values, i), two_heads(grads))
        product = probs * grad_probs
        dots = jnp.sum(product, axis=0, keepdims=True)
        grad_scores = (product - probs * dots).astype(BF16)
        key_parts.append(mm(grad_scores, two_heads_doubled(block)) * scale)
        value_parts.append(mm(probs.astype(BF16), two_heads_doubled(grads)))
        moved = mm_tn(keys, grad_scores)[i * HD : (i + 1) * HD] * scale
        pair = jnp.concatenate([moved[:, :rows], moved[:, rows:]], axis=0)
        dq_out[:, pl.ds(at, 128)] = turn(jnp.transpose(pair), cosine[...], sine[...]).astype(BF16)
    even = lane_index(key_parts[0].shape) < HD
    grad_keys = jnp.where(even, key_parts[0], key_parts[1]).astype(BF16)
    grad_values = jnp.where(even, value_parts[0], value_parts[1]).astype(BF16)
    for k in range(devices):
        dkv_outs[k][0] = grad_keys[k * rows : (k + 1) * rows]
        dkv_outs[k][1] = grad_values[k * rows : (k + 1) * rows]

    @pl.when(step == pl.num_programs(0) - 1)
    def _():
        values = x[...].astype(F32)
        factor = lax.rsqrt(jnp.mean(values * values, axis=-1, keepdims=True) + epsilon)
        normed = (values * factor * gain_first[...]).astype(BF16)
        weight_grads[:, width:] = mm_tn(normed, dq_out[...]).astype(BF16)


def attend_backward(
    scal, parts, grad_out, middle, gain, attended, shared, q, lse, cosine, sine, x, gain_first, kvs
):
    rows, width = middle.shape
    devices = len(kvs)
    keys = devices * rows
    kv_specs = [pl.BlockSpec((1, rows, 128), lambda h: (0, 0, h)) for _ in kvs] + [
        pl.BlockSpec((1, rows, 128), lambda h: (1, 0, h)) for _ in kvs
    ]
    return pl.pallas_call(
        functools.partial(attend_back_kernel, devices, len(parts)),
        name="attend_backward",
        grid=(KVH // 2,),
        in_specs=[
            pl.BlockSpec(memory_space=pltpu.SMEM),
            *[fixed((rows, width)) for _ in parts],
            fixed((rows, width)),
            fixed((rows, width)),
            fixed((1, width)),
            fixed((rows, QH * HD)),
            pl.BlockSpec((QH * HD, width), lambda h: (0, 2), pipeline_mode=pl.Buffered(1)),
            pl.BlockSpec((rows, 256), lambda h: (0, h)),
            pl.BlockSpec((1, 2, 2 * rows), lambda h: (h, 0, 0)),
            fixed((rows, 128)),
            fixed((rows, 128)),
            fixed((rows, width)),
            fixed((1, width)),
            *kv_specs,
        ],
        out_specs=[
            resident((rows, width)),
            resident((width, width + QH * HD)),
            resident((1, width)),
            resident((rows, QH * HD)),
            *[pl.BlockSpec((2, rows, 128), lambda h: (0, 0, h)) for _ in kvs],
        ],
        out_shape=[
            jax.ShapeDtypeStruct((rows, width), F32),
            jax.ShapeDtypeStruct((width, width + QH * HD), BF16),
            jax.ShapeDtypeStruct((1, width), F32),
            jax.ShapeDtypeStruct((rows, QH * HD), BF16),
            *[jax.ShapeDtypeStruct((2, rows, KW), BF16) for _ in kvs],
        ],
        scratch_shapes=[pltpu.VMEM((keys, rows), F32), pltpu.VMEM((rows, QH * HD), BF16)],
        compiler_params=params(1),
        cost_estimate=cost(
            10 * rows * keys * QH * HD * 2 + 4 * rows * width * width,
            6 * width * width + 8 * keys * width + 20 * rows * width,
            rows * keys * QH,
            0.23,
        ),
    )(
        scal,
        *parts,
        grad_out,
        middle,
        gain,
        attended,
        shared,
        q,
        lse,
        cosine,
        sine,
        x,
        gain_first,
        *kvs,
        *kvs,
    )


def project_back_kernel(devices, x, gain, dq, *rest):
    parts, rest = rest[:devices], rest[devices:]
    grad_mid, wq, wm, cosine, sine, small, dx_out, packed = rest
    values = x[...].astype(F32)
    width = values.shape[1]
    factor = lax.rsqrt(jnp.mean(values * values, axis=-1, keepdims=True) + epsilon)
    normed = (values * factor * gain[...]).astype(BF16)
    summed = parts[0][...].astype(F32)
    for part in parts[1:]:
        summed = summed + part[...].astype(F32)
    grad_keys = [
        turn(summed[0, :, b * 128 : (b + 1) * 128], cosine[...], sine[...]).astype(BF16)
        for b in range(KW // 128)
    ]
    grad_memory = jnp.concatenate(grad_keys + [summed[1].astype(BF16)], axis=1)
    grad_query = dq[...]
    packed[:, : 2 * KW] = mm_tn(normed, grad_memory).astype(BF16)
    grad_normed = mm_nt(grad_query, wq[...]) + mm_nt(grad_memory, wm[...])
    scaled = grad_normed * gain[...]
    inner = jnp.mean(values * scaled, axis=-1, keepdims=True)
    gain_grad = jnp.sum(grad_normed * values * factor, axis=0, keepdims=True)
    row = lax.broadcasted_iota(jnp.int32, (128, width), 0)
    packed[:, 2 * KW :] = jnp.transpose(
        jnp.where(row == EXPERTS, gain_grad, small[...])
    ).astype(BF16)
    dx_out[...] = (
        grad_mid[...] + factor * scaled - values * (factor * factor * factor * inner)
    )


def project_backward(x, gain, dq, parts, grad_mid, shared, cosine, sine, small):
    rows, width = x.shape
    columns = 2 * KW + 128
    return pl.pallas_call(
        functools.partial(project_back_kernel, len(parts)),
        name="project_backward",
        grid=(1,),
        in_specs=[
            fixed((rows, width)),
            fixed((1, width)),
            fixed((rows, QH * HD)),
            *[fixed((2, rows, KW)) for _ in parts],
            fixed((rows, width)),
            pl.BlockSpec((width, QH * HD), lambda i: (0, 0), pipeline_mode=pl.Buffered(1)),
            pl.BlockSpec((width, 2 * KW), lambda i: (0, 1), pipeline_mode=pl.Buffered(1)),
            fixed((rows, 128)),
            fixed((rows, 128)),
            fixed((128, width)),
        ],
        out_specs=[resident((rows, width)), resident((width, columns))],
        out_shape=[
            jax.ShapeDtypeStruct((rows, width), F32),
            jax.ShapeDtypeStruct((width, columns), BF16),
        ],
        compiler_params=params(1),
        cost_estimate=cost(
            6 * rows * width * 2048, 8 * width * 2048 + 16 * rows * width, share=0.35
        ),
    )(x, gain, dq, *parts, grad_mid, shared, shared, cosine, sine, small)


def pairs_within(axis, by, sections=(0, 1)):
    count = lax.axis_size(axis)
    return [(s * count + i, s * count + (i ^ by)) for s in sections for i in range(count)]


def exchanged(value, axis, by, sections=(0, 1)):
    return lax.ppermute(value, ("section", axis), pairs_within(axis, by, sections))


def swapped(value):
    return lax.ppermute(value, "section", [(0, 1), (1, 0)])


def from_all(value, axis, sections=(0, 1)):
    count = lax.axis_size(axis)
    return [value] + [exchanged(value, axis, k, sections) for k in range(1, count)]


def after(value, other):
    return lax.optimization_barrier((value, other))[0]


def scattered(blocks, axis, sections):
    return [blocks[0]] + [
        exchanged(blocks[k], axis, k, sections) for k in range(1, len(blocks))
    ]


def added(terms):
    return functools.reduce(lambda a, b: a + b, [term.astype(F32) for term in terms])


def shards(
    tokens,
    targets,
    lengths,
    routes,
    attention_gain,
    query_weight,
    memory_weight,
    output_weight,
    mixture_gain,
    router_weight,
    gate_up_weight,
    down_weight,
):
    section = lax.axis_index("section")
    context = lax.axis_index("ctx")
    line = lax.axis_index("fsdp")
    devices = lax.axis_size("ctx")
    depth = lax.axis_size("fsdp")
    first_core = section == 0
    rows, width = tokens.shape[2:]
    layers = 2
    held_experts = gate_up_weight.shape[1]
    half_held = held_experts // 2
    capacity = rows * TOPK * 9 // (EXPERTS * 8)
    slots = -(-capacity // 16) * 16
    up_rows, down_rows = gate_up_weight.shape[2], down_weight.shape[2]
    shard_rows = up_rows + down_rows

    column = context * held_experts
    plain = (column + section * half_held, half_held, 2 * devices)
    places = [plain, plain]

    pack = jnp.concatenate(
        [
            query_weight[0],
            memory_weight[0],
            output_weight[0],
            router_weight[0],
            attention_gain[0][:, None],
            mixture_gain[0][:, None],
            jnp.zeros((query_weight.shape[1], 128 - EXPERTS - 2), BF16),
        ],
        axis=1,
    )

    def shared_of_line(layer, ahead):
        mine = pack if ahead is None else after(pack, ahead)
        return jnp.concatenate(from_all(mine, "fsdp", (layer,)), axis=0)

    def shared_of_plane(layer, block, ahead):
        mine = block if ahead is None else after(block, ahead)
        owns = from_all(mine, "ctx", (layer,))
        others = [lax.ppermute(own, "section", [(layer, 1 - layer)]) for own in owns]
        scal = jnp.stack([(section == layer).astype(jnp.int32), context, line])
        whole = assemble(scal, owns, others, depth)
        small = whole[:, 3 * width :].T
        return (
            whole,
            small[:EXPERTS],
            small[EXPERTS : EXPERTS + 1].astype(F32),
            small[EXPERTS + 1 : EXPERTS + 2].astype(F32),
        )

    my_routes = jnp.swapaxes(routes[0, :, 0], 1, 2)
    other_routes = swapped(my_routes)
    layer_routes = jnp.where(
        first_core,
        jnp.stack([my_routes, other_routes]),
        jnp.stack([other_routes, my_routes])[:, ::-1],
    )
    all_routes = jnp.stack(from_all(layer_routes, "ctx"), axis=2).reshape(
        layers, 2 * devices, TOPK, rows
    )
    source_routes = [all_routes[0], all_routes[1]]
    earlier = (
        lax.broadcasted_iota(jnp.int32, (rows, rows), 0)
        < lax.broadcasted_iota(jnp.int32, (rows, rows), 1)
    ).astype(BF16)

    def ranked(layer):
        first, local, _ = places[layer]
        ids = first + jnp.arange(local, dtype=jnp.int32)
        named = jnp.any(source_routes[layer][:, None] == ids[None, :, None, None], axis=2)
        before = jnp.dot(
            named.astype(BF16).reshape(-1, rows), earlier, preferred_element_type=F32
        ).reshape(named.shape)
        return jnp.where(named, before, -1.0)

    ranks = [ranked(layer) for layer in range(layers)]
    masks = jnp.any(
        layer_routes[:, 0, None] == jnp.arange(EXPERTS, dtype=jnp.int32)[None, :, None, None], axis=2
    ).astype(F32)

    own_ranks = jnp.where(
        masks[1] > 0.5,
        jnp.dot(masks[1].astype(BF16), earlier, preferred_element_type=F32),
        -1.0,
    )
    last_rank = jnp.take(
        own_ranks,
        jnp.stack(
            [
                (context ^ k) * held_experts + (section ^ m) * half_held + half_held - 1
                for k in range(devices)
                for m in range(2)
            ]
        ),
        axis=0,
    )

    line_blocks = [after(shared_of_line(0, None), (ranks, masks, last_rank)), None]

    whole = [(0, half_held)]
    split = [(0, half_held - 1), (half_held - 1, 1)] if half_held > 1 else whole
    runs = [whole, split]
    back_runs = [split, split[::-1]]
    by_rows_fits = half_held > 1 and slots - capacity >= 8 and slots % 16 == 0

    arrived = swapped(pack_experts(1 - section, gate_up_weight[0], down_weight[0]))
    mine = pack_experts(section, gate_up_weight[0], down_weight[0])

    def gathered_experts(layer, ahead):
        own, other = (mine, arrived) if ahead is None else after((mine, arrived), ahead)
        parts = []
        for a, n in runs[layer]:
            shard = jnp.where(section == layer, own[a : a + n], other[a : a + n])
            parts.append([lax.all_gather(shard, "fsdp", axis=1, tiled=True)])
        return parts

    half = rows // 2
    within = jnp.arange(rows, dtype=jnp.int32)
    positions = jnp.where(
        within < half, context * half + within, (2 * devices - 1 - context) * half + within - half
    )
    inverse = rope_base ** (-2.0 * jnp.arange(HD // 2, dtype=F32) / HD)
    angles = positions.astype(F32)[:, None] * inverse[None, :]
    sine, cosine = jnp.sin(angles), jnp.cos(angles)
    cos_table = jnp.concatenate([cosine] * 4, axis=1)
    sin_table = jnp.concatenate([-sine, sine, -sine, sine], axis=1)
    length = lengths[section, line]
    attend_scalars = jnp.stack([context, length]).astype(jnp.int32)

    def dispatched(message):
        plane = from_all(message, "ctx")
        blocks = plane + [swapped(block) for block in plane]
        return blocks

    def returned(outs):
        own, other = outs[:devices], outs[devices : 2 * devices]
        crossed = [swapped(block) for block in other]
        near = [own[0], crossed[0]]
        for k in range(1, devices):
            chip = (own[k].astype(F32) + crossed[k].astype(F32)).astype(BF16)
            near.append(exchanged(chip, "ctx", k))
        return near

    my_targets = lax.dynamic_index_in_dim(targets[:, 0], section, 0, keepdims=False)
    layer_input = lax.dynamic_index_in_dim(tokens[:, 0], section, 0, keepdims=False)
    valid = (positions < length).astype(F32)[:, None]
    saved, hidden = [], []
    early_experts = gathered_experts(0, None)
    ahead = None
    for layer in range(layers):
        first, local, sources = places[layer]
        shared, router, gain_first, gain_second = shared_of_plane(
            layer, line_blocks[layer], ahead
        )
        q, kv = project(layer_input, gain_first, shared, cos_table, sin_table)
        if layer == 0:
            line_blocks[1] = shared_of_line(1, kv)
        kvs = from_all(kv, "ctx")
        attended, lse, middle, message = attend(
            attend_scalars, layer_input, q, kvs, shared, gain_second, router, masks[layer]
        )
        messages = dispatched(message)
        if layer == 0:
            ahead = messages
            weights = early_experts
            late_experts = gathered_experts(1, message)
        else:
            weights = late_experts
        kept, outs = [], ()
        xs, gates = dispatch(
            first.astype(jnp.int32).reshape(1), messages, ranks[layer], slots, False
        )
        sparse = layer == 1 and by_rows_fits
        for at, ((a, n), blocks) in enumerate(zip(runs[layer], weights)):
            scal = jnp.stack([first + a, *[jnp.asarray(k) for k in range(depth)]]).astype(jnp.int32)
            by_rows = sparse and at == len(runs[layer]) - 1
            if by_rows:
                terms = [added(terms)]
                scal = after(scal, terms)
            run, outs = experts_forward(
                scal,
                xs,
                ranks[layer][:, a : a + n],
                gates[:, a : a + n],
                blocks,
                depth,
                slots,
                a,
                () if by_rows else outs,
                not by_rows,
            )
            kept.append((a, n, scal, run, blocks))
            if not by_rows:
                terms = returned(outs)
        if layer == layers - 1:
            routed = [last_rank, [], slots] if sparse else []
            if sparse:
                near, far = outs[:devices], [swapped(block) for block in outs[devices:]]
                near = after(near, far)
                near, far = (
                    blocks[:1] + [exchanged(blocks[k], "ctx", k) for k in range(1, devices)]
                    for blocks in (near, far)
                )
                routed[1] = [block for pair in zip(near, far) for block in pair]
            mixed = None
            hidden_rows, grad_output, message, *row_messages = finish(
                terms, middle, my_targets, valid, *routed
            )
            hidden.append(hidden_rows)
        else:
            mixed = functools.reduce(lambda a, b: a + b, [t.astype(F32) for t in terms])
            hidden.append((middle + mixed).astype(BF16))
        saved.append(
            dict(
                x=layer_input,
                shared=shared,
                router=router,
                gain_first=gain_first,
                gain_second=gain_second,
                q=q,
                kvs=kvs,
                attended=attended,
                lse=lse,
                middle=middle,
                kept=kept,
                xs=xs,
                gates=gates,
                mixed=mixed,
            )
        )
        layer_input = hidden[-1]

    def home_blocks(packed, layer):
        arrived = lax.ppermute(packed, "section", [(1 - layer, layer)])
        size = packed.shape[0] // devices
        return [
            (
                lax.dynamic_slice_in_dim(packed, (context ^ k) * size, size, 0).astype(F32)
                + lax.dynamic_slice_in_dim(arrived, (context ^ k) * size, size, 0).astype(F32)
            ).astype(BF16)
            for k in range(devices)
        ]

    def home_plane(blocks, layer):
        return added(scattered(blocks, "ctx", (layer,))).astype(BF16)

    def home_line(plane, layer, ahead=None):
        size = plane.shape[0] // depth
        blocks = [
            lax.dynamic_slice_in_dim(plane, (line ^ k) * size, size, 0) for k in range(depth)
        ]
        if ahead is not None:
            blocks[-1] = after(blocks[-1], ahead)
        return scattered(blocks, "fsdp", (layer,))

    def placed_rows(values):
        home = jnp.where(first_core, values[0], values[1])
        arrived = swapped(jnp.where(first_core, values[1], values[0]))
        return jnp.stack(
            [jnp.where(first_core, home, arrived), jnp.where(first_core, arrived, home)]
        )

    input_grads, expert_grads = [None] * layers, [None] * layers
    waiting = None
    summed = {}
    for layer in reversed(range(layers)):
        held = saved[layer]
        first, local, sources = places[layer]
        if layer < layers - 1:
            message = grad_message(grad_output, held["mixed"])
        sparse = layer == 1 and by_rows_fits
        if sparse:
            plane = [row_messages[0]] + [
                exchanged(row_messages[k], "ctx", k) for k in range(1, devices)
            ]
            row_blocks = plane + [swapped(block[1]) for block in plane]
            message = after(message, plane[1])
        messages = dispatched(message)
        if waiting is not None:
            by = 1
            while by < depth:
                error = error + lax.ppermute(error, "fsdp", [(i, i ^ by) for i in range(depth)])
                by *= 2
            loss_value = error / jnp.sum(lengths).astype(F32)
            hidden_out = placed_rows(hidden)
            blocks_1 = [waiting[0], home_blocks(waiting[1], 1)]
            messages = after(messages, (blocks_1, loss_value, hidden_out))
            planes = [home_plane(blocks, 1) for blocks in after(blocks_1, messages)]
        own_router = lax.dynamic_slice_in_dim(held["router"], first, local, 0).astype(F32)
        small = jnp.zeros((128, width), F32)
        outs = ()
        gathered = []
        steps = back_runs[layer]
        spans = [a for a, _ in steps]
        for at, (a, n) in enumerate(steps):
            base, _, scal, run, blocks = next(
                kept for kept in held["kept"] if kept[0] <= a and a + n <= kept[0] + kept[1]
            )
            scal = jnp.concatenate([scal[:1] + (a - base), scal[1:]])
            last = None
            if at == len(steps) - 1 and not sparse:
                order = tuple(sorted(range(len(spans)), key=lambda i: spans[i]))
                last = (ranks[layer], [rows_of for rows_of in outs], order)
            if sparse and at == 0:
                grad_rows, inners, start = row_blocks, None, a
            elif not sparse:
                grad_rows, inners = dispatch(
                    scal[:1], messages, ranks[layer][:, a : a + n], slots, True
                )
                start = a
            elif at == 1:
                start = 0
                grad_rows, inners = dispatch(
                    scal[:1], messages, ranks[layer][:, : half_held - 1], slots, True
                )
            grads, router_grad, rows_out = experts_backward(
                scal,
                grad_rows,
                ranks[layer][:, a : a + n],
                held["gates"][:, a : a + n],
                inners,
                held["xs"],
                run,
                own_router[a : a + n, None, :],
                blocks,
                depth,
                slots,
                a,
                a - base,
                a - start,
                last,
            )
            outs = rows_out if last else list(outs) + rows_out
            if layer == 1 and inners is not None:
                error = jnp.sum(inners[:, 1, 0])
            small = lax.dynamic_update_slice_in_dim(small, router_grad[:, 0], first + a, 0)
            gathered.append(grads)
        if sparse:
            order = tuple(sorted(range(len(spans)), key=lambda i: spans[i]))
            outs = combine_rows(ranks[layer], outs, order, slots)
        over_line = lambda grads: lax.psum_scatter(
            grads, "fsdp", scatter_dimension=1, tiled=True
        )
        at_once = gathered if layer == 1 or len(gathered) == 1 else gathered[:-1]
        summed[layer] = [over_line(grads) for grads in at_once]
        if layer == 1:
            grad_output = after(grad_output, summed[1][0])
        else:
            grad_output = after(grad_output, summed[1][-1])
            outs = after(outs, planes)
        back = attend_backward(
            attend_scalars,
            returned(outs),
            grad_output,
            held["middle"],
            held["gain_second"],
            held["attended"],
            held["shared"],
            held["q"],
            held["lse"],
            cos_table,
            -sin_table,
            held["x"],
            held["gain_first"],
            held["kvs"],
        )
        grad_mid, weight_grads, gain_second_grad, dq = back[:4]
        dkv = back[4:]
        parts = [dkv[0]] + [exchanged(dkv[k], "ctx", k) for k in range(1, devices)]
        outward = home_blocks(weight_grads, layer)
        grad_mid = after(grad_mid, outward)
        small = lax.dynamic_update_slice_in_dim(small, gain_second_grad, EXPERTS + 1, 0)
        dx, packed = project_backward(
            held["x"],
            held["gain_first"],
            dq,
            parts,
            grad_mid,
            held["shared"],
            cos_table,
            -sin_table,
            small,
        )
        expert_grads[layer] = (spans, summed[layer])
        input_grads[layer] = dx
        grad_output = dx.astype(BF16).astype(F32)
        if layer == 1:
            waiting = (outward, packed)
        else:
            outward = after(outward, packed)
            summed[0] += [over_line(after(grads, packed)) for grads in gathered[len(at_once) :]]
            inward_plane = home_plane(home_blocks(packed, 0), 0)
            outward_plane = home_plane(outward, 0)

    def pieces_of(layer, at, part):
        arrived = lax.ppermute(part, "section", [(1 - layer, layer)])
        return [
            (layer, half * half_held + at, term)
            for half, term in ((layer, part), (1 - layer, arrived))
        ]

    def placed(pieces, experts, into):
        touched = [p for p in pieces if any(0 <= e - p[1] < p[2].shape[0] for e in experts)]
        return place_experts(
            section.astype(jnp.int32).reshape(1), touched, held_experts, up_rows, experts, into
        )

    parts = [(layer, at, part) for layer in (1, 0) for at, part in zip(*expert_grads[layer])]
    pieces = [piece for part in parts[:-1] for piece in pieces_of(*part)]
    layer, at, part = parts[-1]
    last = [half * half_held + at + i for half in range(2) for i in range(part.shape[0])]
    sums = ()
    if len(last) < held_experts:
        sums = placed(pieces, [e for e in range(held_experts) if e not in last], ())
    first_terms = home_line(
        jnp.concatenate([outward_plane, inward_plane], axis=1), 0, sums if sums else None
    )
    second_terms = home_line(jnp.concatenate(planes, axis=1), 1)
    input_out = placed_rows(after(input_grads, inward_plane))[None, :, None]
    first_terms, second_terms = after((first_terms, second_terms), input_out)
    shared_grads = jnp.where(first_core, added(first_terms), added(second_terms))
    outward, inward = shared_grads[:, : 2 * width], shared_grads[:, 2 * width :]
    if sums:
        part = after(part, (first_terms, second_terms))
    up_sum, down_sum = placed(pieces + pieces_of(layer, at, part), last, sums)
    at = 2 * KW
    return (
        hidden_out[None, :, None],
        input_out,
        loss_value,
        inward[:, at + EXPERTS][None],
        outward[:, width:][None],
        inward[:, :at][None],
        outward[:, :width][None],
        inward[:, at + EXPERTS + 1][None],
        inward[:, at : at + EXPERTS][None],
        up_sum[None],
        down_sum[None],
    )


def solution(mesh):
    placed = (
        P(None, "fsdp", "ctx", None),
        P(None, "fsdp", "ctx", None),
        P(),
        P("section", None, "fsdp", "ctx", None),
        P("section", ("ctx", "fsdp")),
        P("section", ("ctx", "fsdp"), None),
        P("section", ("ctx", "fsdp"), None),
        P("section", ("ctx", "fsdp"), None),
        P("section", ("ctx", "fsdp")),
        P("section", ("ctx", "fsdp"), None),
        P("section", "ctx", "fsdp", None),
        P("section", "ctx", "fsdp", None),
    )
    return jax.shard_map(
        shards,
        mesh=mesh,
        in_specs=placed,
        out_specs=(
            P("section", None, "fsdp", "ctx", None),
            P("section", None, "fsdp", "ctx", None),
            P(),
            P("section", ("ctx", "fsdp")),
            P("section", ("ctx", "fsdp"), None),
            P("section", ("ctx", "fsdp"), None),
            P("section", ("ctx", "fsdp"), None),
            P("section", ("ctx", "fsdp")),
            P("section", ("ctx", "fsdp"), None),
            P("section", "ctx", "fsdp", None),
            P("section", "ctx", "fsdp", None),
        ),
        check_vma=False,
    )
```
